128 devices in a mesh: tile: 32 (over x, z_hi, y), sub: 4 (over z_lo, core).
Axes of the slice: x: 4, y: 4, z: 4 (z_hi: 2, z_lo: 2; z = z_hi * 2 + z_lo), core: 2. Of those that a mesh axis runs over, the one named last changes fastest.
Arguments:
- field_in: bfloat16 [12, 64, 64, 128], P('sub', 'tile'), may hold values from -6 to 6
- grad_out: bfloat16 [12, 64, 64, 128], P('sub', 'tile'), may hold values from -6 to 6
- first_weight: bfloat16 [3, 3, 128, 128], replicated, may hold values from -0.1875 to 0.1875
- second_weight: bfloat16 [3, 3, 128, 128], replicated, may hold values from -0.1875 to 0.1875
- face_neighbour: int32 [12, 4], replicated, may hold values from 0 to 11, as said below
- seam_rotation: int32 [12, 4], replicated, may hold values from 0 to 7, as said below
- corner_fill: int32 [12, 4], replicated, may hold values from 0 to 47
Outputs:
- grad_in: bfloat16 [12, 64, 64, 128], P('sub', 'tile')
- first_grad: float32 [3, 3, 128, 128], replicated
- second_grad: float32 [3, 3, 128, 128], replicated
The draws below stay inside these ranges and needn't reach their ends.
Inputs may be any that keep to these rules, and one draw needn't show every extreme that they name: With seam_rotation: side s of face f borders side seam_rotation[f,s] % 4 of face face_neighbour[f,s], read in reverse when seam_rotation[f,s] // 4 = 1. The pairing is symmetric: that side names side s of face f back, with the same reversal; no side names itself. `seam_rotation`: see face_neighbour.
All inputs are finite; a program needn't handle non-finite values.
Results may differ from the reference program's by a relative error of at most 0.007.
Values may be sent and summed in bfloat16 or wider, within the bound.
No kernel may reach another device: no remote copies, remote signals or barrier semaphores. Data moves between devices by JAX's collectives and lax.ppermute only.
A program may use at most 64 MiB of HBM per device.

```python
import jax
import jax.numpy as jnp
from jax import lax

C = 128
FACES = 12
NSIDE = 64


def seam_pairs(key):
    key = jax.random.fold_in(key, 7)
    first_key, second_key = jax.random.split(key)
    slot_count = FACES * 4
    shuffled = jax.random.permutation(first_key, slot_count)
    left_slots = shuffled[0::2]
    right_slots = shuffled[1::2]
    partner = jnp.zeros((slot_count,), jnp.int32).at[left_slots].set(right_slots).at[right_slots].set(left_slots)
    coin_flips = jax.random.randint(second_key, (slot_count // 2,), 0, 2).astype(jnp.int32)
    reversed_bits = jnp.zeros((slot_count,), jnp.int32).at[left_slots].set(coin_flips).at[right_slots].set(coin_flips)
    slot_index = jnp.arange(slot_count, dtype=jnp.int32)
    reversed_bits = jnp.where((slot_index == 3) | (slot_index == partner[3]), 1, reversed_bits)
    zero_slot = jnp.where(partner[3] == 0, 4, 0)
    reversed_bits = jnp.where((slot_index == zero_slot) | (slot_index == partner[zero_slot]), 0, reversed_bits)
    return (partner, reversed_bits)


def draw_face_neighbour(key, part):
    partner, reversed_bits = seam_pairs(key)
    return (partner // 4).reshape(FACES, 4).astype(jnp.int32)


def draw_seam_rotation(key, part):
    partner, reversed_bits = seam_pairs(key)
    return (partner % 4 + 4 * reversed_bits).reshape(FACES, 4).astype(jnp.int32)


def with_ends(entries, rng, smallest, high):
    longest = entries.shape.index(max(entries.shape))
    spots = []
    for shift in (0, 1):
        where = [jax.random.randint(jax.random.fold_in(rng, axis), (), 0, length) for axis, length in enumerate(entries.shape)]
        where[longest] = (where[longest] + shift) % entries.shape[longest]
        spots.append(tuple(where))
    return entries.at[spots[0]].set(smallest).at[spots[1]].set(high)


def levels(stream_key, extent, cuts, least, top_value):
    level, own = 1.0, jax.random.fold_in(stream_key, 6)
    for dim, parts in cuts:
        draws = jnp.exp(jax.random.uniform(jax.random.fold_in(own, dim), (parts,), jnp.float32, least / len(cuts), top_value / len(cuts)))
        level = level * jnp.repeat(draws, extent[dim] // parts).reshape([-1 if axis == dim else 1 for axis in range(len(extent))])
    return level


def normal_values(rng, extent, width, reach, pieces=(), held_as=jnp.bfloat16):
    values = width * jax.random.normal(rng, extent, jnp.float32)
    if pieces:
        values = values * levels(rng, extent, pieces, -0.22, 0.18)
    return jnp.clip(values, -reach, reach).astype(held_as)


def setup_inputs(seed: int = 0) -> dict:
    arg_keys = jax.random.split(jax.random.key(seed), 8)
    field_in = normal_values(arg_keys[0], (FACES, NSIDE, NSIDE, C), 1.0, 6.0, ((0, 4), (1, 32)))
    grad_out = normal_values(arg_keys[1], (FACES, NSIDE, NSIDE, C), 1.0, 6.0, ((0, 4), (1, 32)))
    first_weight = normal_values(arg_keys[2], (3, 3, C, C), (9 * C) ** -0.5, 0.1875)
    second_weight = normal_values(arg_keys[3], (3, 3, C, C), (9 * C) ** -0.5, 0.1875)
    face_neighbour = draw_face_neighbour(jax.random.fold_in(arg_keys[7], 71), 0)
    seam_rotation = draw_seam_rotation(jax.random.fold_in(arg_keys[7], 71), 0)
    corner_fill = with_ends(jax.random.randint(arg_keys[6], (FACES, 4), 0, FACES * 4), jax.random.fold_in(arg_keys[6], 1), 0, (FACES * 4) - 1).astype(jnp.int32)
    return {"field_in": field_in, "grad_out": grad_out, "first_weight": first_weight, "second_weight": second_weight, "face_neighbour": face_neighbour, "seam_rotation": seam_rotation, "corner_fill": corner_fill}


def face_lines(field_data):
    return jnp.stack([field_data[:, 0], field_data[:, -1], field_data[:, :, 0], field_data[:, :, -1]], axis=1)


def seam_halos(edge_lines, face_neighbour, seam_rotation, corner_fill):
    faces_all = edge_lines.shape[0]
    line_length = edge_lines.shape[2]
    channels = edge_lines.shape[3]
    flat_lines = edge_lines.reshape(faces_all * 4, line_length, channels)
    source = (face_neighbour * 4 + seam_rotation % 4).reshape(-1).astype(jnp.int32)
    picked = flat_lines[source].reshape(faces_all, 4, line_length, channels)
    flipped = (seam_rotation // 4 == 1)[:, :, None, None]
    picked = jnp.where(flipped, picked[:, :, ::-1], picked)
    corners = jnp.stack([edge_lines[:, 0, 0], edge_lines[:, 0, -1], edge_lines[:, 1, 0], edge_lines[:, 1, -1]], axis=1)
    filled = corners.reshape(faces_all * 4, channels)[corner_fill.reshape(-1).astype(jnp.int32)]
    return picked, filled.reshape(faces_all, 4, channels)


def pad_face(field_data, picked, filled):
    upper = jnp.concatenate([filled[0:1], picked[0], filled[1:2]], axis=0)
    lower = jnp.concatenate([filled[2:3], picked[1], filled[3:4]], axis=0)
    middle = jnp.concatenate([picked[2][:, None], field_data, picked[3][:, None]], axis=1)
    return jnp.concatenate([upper[None], middle, lower[None]], axis=0)


def apply_taps(padded, weight):
    height = padded.shape[0] - 2
    breadth = padded.shape[1] - 2
    channels = padded.shape[2]
    running = jnp.zeros((height * breadth, weight.shape[3]), jnp.float32)
    for row_shift in range(3):
        for col_shift in range(3):
            window = padded[row_shift:row_shift + height, col_shift:col_shift + breadth].reshape(-1, channels)
            running = running + jnp.dot(window, weight[row_shift, col_shift], preferred_element_type=jnp.float32)
    return running.reshape(height, breadth, -1)


def weight_taps(padded, gradient):
    height = gradient.shape[0]
    breadth = gradient.shape[1]
    channels = padded.shape[2]
    flat_grad = gradient.reshape(-1, gradient.shape[2])
    result = []
    for row_shift in range(3):
        for col_shift in range(3):
            window = padded[row_shift:row_shift + height, col_shift:col_shift + breadth].reshape(-1, channels)
            result.append(jnp.dot(window.T, flat_grad, preferred_element_type=jnp.float32))
    return jnp.stack(result, axis=0).reshape(3, 3, channels, gradient.shape[2])


def transpose_taps(gradient, weight):
    widened = jnp.pad(gradient, ((2, 2), (2, 2), (0, 0)))
    return apply_taps(widened, jnp.transpose(weight[::-1, ::-1], (0, 1, 3, 2)))


def cycle_split(full_grad):
    interior = full_grad[1:-1, 1:-1]
    cycle_lines = jnp.stack([full_grad[0, 1:-1], full_grad[-1, 1:-1], full_grad[1:-1, 0], full_grad[1:-1, -1]], axis=0)
    cycle_corners = jnp.stack([full_grad[0, 0], full_grad[0, -1], full_grad[-1, 0], full_grad[-1, -1]], axis=0)
    return interior, cycle_lines, cycle_corners


def seam_adjoint(cycle_lines, cycle_corners, face_neighbour, seam_rotation, corner_fill):
    faces_all = cycle_lines.shape[0]
    line_length = cycle_lines.shape[2]
    channels = cycle_lines.shape[3]
    flipped = (seam_rotation // 4 == 1)[:, :, None, None]
    cycle_lines = jnp.where(flipped, cycle_lines[:, :, ::-1], cycle_lines)
    source = (face_neighbour * 4 + seam_rotation % 4).reshape(-1).astype(jnp.int32)
    spread = jnp.zeros((faces_all * 4, line_length, channels), jnp.float32)
    spread = spread.at[source].add(cycle_lines.reshape(faces_all * 4, line_length, channels))
    corner_spread = jnp.zeros((faces_all * 4, channels), jnp.float32)
    corner_spread = corner_spread.at[corner_fill.reshape(-1).astype(jnp.int32)].add(cycle_corners.reshape(faces_all * 4, channels))
    return spread.reshape(faces_all, 4, line_length, channels), corner_spread.reshape(faces_all, 4, channels)


def add_boundary(interior, line_grads, corner_grads):
    interior = interior.at[0].add(line_grads[0]).at[-1].add(line_grads[1])
    interior = interior.at[:, 0].add(line_grads[2]).at[:, -1].add(line_grads[3])
    interior = interior.at[0, 0].add(corner_grads[0]).at[0, -1].add(corner_grads[1])
    return interior.at[-1, 0].add(corner_grads[2]).at[-1, -1].add(corner_grads[3])


def sigmoid_slope(pre_act):
    logistic = jax.nn.sigmoid(pre_act)
    return logistic * (1.0 + pre_act * (1.0 - logistic))


def reference(field_in, grad_out, first_weight, second_weight, face_neighbour, seam_rotation, corner_fill):
    pick_in, fill_in = seam_halos(face_lines(field_in), face_neighbour, seam_rotation, corner_fill)

    def first_pass(item_set):
        return jax.nn.silu(apply_taps(pad_face(item_set[0], item_set[1], item_set[2]), first_weight)).astype(jnp.bfloat16)

    hidden = lax.map(first_pass, (field_in, pick_in, fill_in))
    pick_hidden, fill_hidden = seam_halos(face_lines(hidden), face_neighbour, seam_rotation, corner_fill)

    def second_pass(accum, item_set):
        padded = pad_face(item_set[0], item_set[1], item_set[2])
        accum = accum + weight_taps(padded, item_set[3])
        return accum, cycle_split(transpose_taps(item_set[3], second_weight))

    zero_grad = jnp.zeros((3, 3, C, C), jnp.float32)
    second_sum, (inner_hidden, lines_hidden, corners_hidden) = lax.scan(second_pass, zero_grad, (hidden, pick_hidden, fill_hidden, grad_out))
    seam_hidden, corner_hidden = seam_adjoint(lines_hidden, corners_hidden, face_neighbour, seam_rotation, corner_fill)

    def third_pass(accum, item_set):
        padded = pad_face(item_set[0], item_set[1], item_set[2])
        pre_act = apply_taps(padded, first_weight)
        grad_hidden = add_boundary(item_set[3], item_set[4], item_set[5])
        grad_pre = (grad_hidden * sigmoid_slope(pre_act)).astype(jnp.bfloat16)
        accum = accum + weight_taps(padded, grad_pre)
        return accum, cycle_split(transpose_taps(grad_pre, first_weight))

    first_sum, (inner_in, lines_in, corners_in) = lax.scan(third_pass, zero_grad, (field_in, pick_in, fill_in, inner_hidden, seam_hidden, corner_hidden))
    seam_in, corner_in = seam_adjoint(lines_in, corners_in, face_neighbour, seam_rotation, corner_fill)

    def last_pass(item_set):
        total_grad = item_set[0].astype(jnp.float32) + add_boundary(item_set[1], item_set[2], item_set[3])
        return total_grad.astype(jnp.bfloat16)

    grad_in = lax.map(last_pass, (grad_out, inner_in, seam_in, corner_in))
    factor = (1.0 * FACES * NSIDE * NSIDE) ** -0.5
    return grad_in, first_sum * factor, second_sum * factor
```

```python
import jax
import jax.numpy as jnp
import numpy as np
from jax import lax
from jax.experimental import pallas as pl
from jax.experimental.pallas import tpu as pltpu
from jax.sharding import PartitionSpec as P

BF = jnp.bfloat16
F32 = jnp.float32
I32 = jnp.int32
BOTH = ("tile", "sub")
BANDS = 32
GROUPS = 4
SPAN = 64
CH = 128
TAPS = [(a, b) for a in range(3) for b in range(3)]
POSITIONS = 10
ROWS_BLOCK = POSITIONS * 16
SLOT_ONE = ROWS_BLOCK + 48
CHUNK = 18
SLOT_TWO = 24
VMEM_BYTES = 48 * 1024 * 1024


def mm(left, right):
    return jnp.dot(left, right, preferred_element_type=F32)


def mm_t(left, right):
    return lax.dot_general(left, right, (((0,), (0,)), ((), ())), preferred_element_type=F32)


def call(kernel, outs, scratch, operands, smem_first=False):
    specs = [pl.BlockSpec(memory_space=pltpu.VMEM) for _ in operands]
    if smem_first:
        specs[0] = pl.BlockSpec(memory_space=pltpu.SMEM)
    many = isinstance(outs, (list, tuple))
    out_specs = [pl.BlockSpec(memory_space=pltpu.VMEM) for _ in outs] if many else pl.BlockSpec(memory_space=pltpu.VMEM)
    return pl.pallas_call(
        kernel,
        out_shape=outs,
        in_specs=specs,
        out_specs=out_specs,
        scratch_shapes=scratch,
        compiler_params=pltpu.CompilerParams(vmem_limit_bytes=VMEM_BYTES),
    )(*operands)


def pack_lines(f_ref, g_ref, out_ref, wide, ends):
    wide[...] = jnp.zeros_like(wide)
    for fld, ref in enumerate((f_ref, g_ref)):
        for row in range(2):
            for face in range(3):
                block = ref[face, row].astype(F32)
                wide[pl.ds(fld * 6 + row * 3 + face, SPAN, stride=16), :] = block
                for side, cols in enumerate(((0, 1), (63, 62))):
                    for depth, col in enumerate(cols):
                        place = row * 24 + fld * 12 + side * 6 + depth * 3 + face
                        ends[place : place + 1, :] = block[col : col + 1, :]
    tail = ends[...].astype(BF)
    for pos in range(SPAN):
        block = wide[pos * 16 : pos * 16 + 16, :].astype(BF)
        for d in range(BANDS):
            for j in range(POSITIONS):
                t = min(max(d - 2 + j if j < 5 else 56 - d + j, 0), SPAN - 1)
                if t == pos:
                    out_ref[d, j * 16 : j * 16 + 16, :] = block
    for d in range(BANDS):
        out_ref[d, ROWS_BLOCK:SLOT_ONE, :] = tail


def line_selector():
    select = np.zeros((2, 64, 80), np.float32)
    for parity in range(2):
        for fld in range(2):
            for depth in range(2):
                for face in range(3):
                    base = (fld * 2 + depth) * 16 + face
                    select[parity, base, fld * 6 + depth * 3 + face] = 1
                    select[parity, base + 3, 16 + fld * 6 + (1 - depth) * 3 + face] = 1
                    for side in range(2):
                        source = 32 + parity * 24 + fld * 12 + side * 6 + depth * 3 + face
                        select[parity, base + 6 + 3 * side, source] = 1
    return select


def gather_lines(sc_ref, sel_ref, in_ref, out_ref):
    band = sc_ref[0]
    for j in range(POSITIONS):
        t = band - 2 + j if j < 5 else 56 - band + j
        inside = jnp.logical_and(t >= 0, t < SPAN)
        t = jnp.clip(t, 0, SPAN - 1)
        ends = in_ref[t >> 1, ROWS_BLOCK:SLOT_ONE, :]
        rows = slice(j * 16, j * 16 + 16)
        pieces = jnp.concatenate([in_ref[0, rows, :], in_ref[BANDS - 1, rows, :], ends], axis=0)
        picked = mm(sel_ref[t & 1], pieces)
        out_ref[j] = jnp.where(inside, picked, 0.0).astype(BF)


def silu_parts(pre):
    logistic = 1.0 / (1.0 + jnp.exp(-pre))
    return pre * logistic, logistic * (1.0 + pre * (1.0 - logistic))


def side_frame(side, tap):
    dr, dc = tap[0] - 1, tap[1] - 1
    return ((dr, dc), (-dr, dc), (dc, dr), (-dc, dr))[side]


def main_kernel(
    sc_ref, idx_ref, a_ref, f_ref, fu_ref, fd_ref, g_ref, gu_ref, gd_ref, w1_ref, w2_ref,
    out_ref, gin_ref,
    f2, g2, w1t, w2t, xs, hal, lp, lg, lc, ob, ss, gp, gpu, acc,
):
    band = sc_ref[0]
    group = sc_ref[1]

    for k, (a, b) in enumerate(TAPS):
        w1t[k * CH : (k + 1) * CH, :] = w1_ref[a, b].T
        w2t[k * CH : (k + 1) * CH, :] = w2_ref[a, b].T

    for row in range(2):
        for face in range(3):
            for part, (fr, gr) in enumerate(((fu_ref, gu_ref), (f_ref, g_ref), (fd_ref, gd_ref))):
                start = (part * 2 + row) * 192 + face * 64
                f2[start : start + 64, :] = fr[face, row]
                g2[start : start + 64, :] = gr[face, row]

    def conv_weights(ref):
        return jnp.concatenate([ref[:, b].reshape(3 * CH, CH) for b in range(3)], axis=1)

    def back_weights(ref):
        columns = []
        for b in range(3):
            columns.append(jnp.concatenate([ref[(a * 3 + b) * CH : (a * 3 + b + 1) * CH, :] for a in (2, 1, 0)], axis=0))
        return jnp.concatenate(columns, axis=1)

    def up_one(value):
        return pltpu.roll(value, value.shape[0] - 1, 0)

    def down_one(value):
        return pltpu.roll(value, 1, 0)

    def three_rows(ref, first, count):
        return jnp.concatenate([ref[first + 192 * a : first + 192 * a + count, :] for a in range(3)], axis=1)

    y = mm(three_rows(f2, 0, 768), conv_weights(w1_ref))
    pre = down_one(y[:, :CH]) + y[:, CH : 2 * CH] + up_one(y[:, 2 * CH :])
    z = mm(three_rows(g2, 0, 768), back_weights(w2t))
    back = up_one(z[:, :CH]) + z[:, CH : 2 * CH] + down_one(z[:, 2 * CH :])
    hidden, slope = silu_parts(pre)
    index = lax.broadcasted_iota(I32, (768, CH), 0)
    step = (index >= 192).astype(I32) + (index >= 384).astype(I32) + (index >= 576).astype(I32)
    row = 2 * band - 1 + step
    col = index & 63
    inner = (row >= 1) & (row <= 62) & (col >= 1) & (col <= 62)
    gpre = jnp.where(inner, back * slope, 0.0).astype(BF)
    hid = jnp.where(inner, hidden, 0.0)[192:576].astype(BF)

    gown = gpre[192:576].astype(F32)
    gcat = jnp.concatenate([up_one(gown).astype(BF), gpre[192:576], down_one(gown).astype(BF)], axis=1)
    first = mm_t(three_rows(f2, 192, 384), gcat)
    hown = hid.astype(F32)
    hcat = jnp.concatenate([down_one(hown).astype(BF), hid, up_one(hown).astype(BF)], axis=1)
    gback = jnp.concatenate([g2[576:960, :], g2[384:768, :], g2[192:576, :]], axis=1)
    second = mm_t(hcat, gback)
    for k, (a, b) in enumerate(TAPS):
        acc[k * CH : (k + 1) * CH, :] = first[a * CH : (a + 1) * CH, b * CH : (b + 1) * CH]
        acc[1152 + k * CH : 1152 + (k + 1) * CH, :] = second[b * CH : (b + 1) * CH, a * CH : (a + 1) * CH]

    gthree = jnp.concatenate([gpre[0:384], gpre[192:576], gpre[384:768]], axis=1)
    z = mm(gthree, back_weights(w1t))
    gin_ref[...] = up_one(z[:, :CH]) + z[:, CH : 2 * CH] + down_one(z[:, 2 * CH :])

    line = lax.broadcasted_iota(I32, (64, 1), 0)
    place = line & 15
    side = (place >= 3).astype(I32) + (place >= 6).astype(I32) + (place >= 9).astype(I32)
    face = place - 3 * side
    home = line - place
    real = place < 12
    lane = lax.broadcasted_iota(I32, (64, 64), 1)

    def one_hot(target, keep):
        return (jnp.where(keep & real, target, -1) == lane).astype(F32).astype(BF)

    fn = idx_ref[:, 0:1]
    rot = idx_ref[:, 1:2]
    fn_group = (fn * 43) >> 7
    partner = fn_group * 16 + (rot & 3) * 3 + (fn - 3 * fn_group)
    straight = one_hot(partner, (rot >> 2) == 0)
    turned = one_hot(partner, (rot >> 2) == 1)
    fills = []
    for column in (2, 3):
        m = idx_ref[:, column : column + 1]
        mf = m >> 2
        mg = (mf * 43) >> 7
        target = mg * 16 + ((m >> 1) & 1) * 3 + (mf - 3 * mg)
        fills.append((one_hot(target, (m & 1) == 0), one_hot(target, (m & 1) == 1)))
    (lo_zero, lo_end), (hi_zero, hi_end) = fills
    even = (side & 1) == 0
    low_side = jnp.where(side < 2, 2, 0)
    high_side = jnp.where(side < 2, 3, 1)
    near = [one_hot(home + low_side * 3 + face, even), one_hot(home + low_side * 3 + face, ~even)]
    far = [one_hot(home + high_side * 3 + face, even), one_hot(home + high_side * 3 + face, ~even)]
    side_mask = [jnp.broadcast_to((side == s).astype(F32), (64, CH)).astype(BF) for s in range(4)]
    row_line = (side < 2).astype(F32)

    for j in range(POSITIONS):
        for block in range(4):
            xs[block, j] = jnp.concatenate([a_ref[g, j, block * 16 : block * 16 + 16, :] for g in range(4)], axis=0)
    for j in range(POSITIONS):
        hal[j] = (mm(straight, xs[0, j]) + mm(turned, xs[0, 9 - j])).astype(BF)

    start = 2 - band
    stop = 7 + band

    @pl.when(band < 2)
    def _():
        for depth in range(2):
            head = hal[start + depth]
            tail = hal[stop - depth]
            xs[depth, start - 1] = (mm(near[0], head) + mm(near[1], tail)).astype(BF)
            xs[depth, stop + 1] = (mm(far[0], head) + mm(far[1], tail)).astype(BF)
        head = xs[0, start]
        tail = xs[0, stop]
        hal[start - 1] = (mm(lo_zero, head) + mm(lo_end, tail)).astype(BF)
        hal[stop + 1] = (mm(hi_zero, head) + mm(hi_end, tail)).astype(BF)

    def choose(options):
        total = None
        for s, option in enumerate(options):
            if option is None:
                continue
            term = option * side_mask[s]
            total = term if total is None else total + term
        return jnp.zeros((64, CH), BF) if total is None else total

    def fill(target, block, source):
        for k, tap in enumerate(TAPS):
            target[block * 64 : block * 64 + 64, k * CH : (k + 1) * CH] = choose(
                [source(*side_frame(s, tap)) for s in range(4)]
            )

    def field_source(j):
        def source(delta, dt):
            return hal[j + dt] if delta == -1 else xs[delta, j + dt]
        return source

    def grad_source(e, j, depths):
        def source(delta, dt):
            depth, at = e - delta, j - dt
            if depth not in depths or not 0 <= at < POSITIONS:
                return None
            return depths[depth](at)
        return source

    order_pre = (2, 7, 1, 3, 6, 8)
    for block, j in enumerate(order_pre):
        fill(lp, block, field_source(j))
    order_back = [(0, 2), (0, 7), (-1, 2), (-1, 7), (-1, 1), (-1, 8), (0, 1), (0, 3), (0, 6), (0, 8), (-1, 0), (-1, 3), (-1, 6), (-1, 9)]
    given = {0: lambda at: xs[2, at], 1: lambda at: xs[3, at]}
    for block, (e, j) in enumerate(order_back):
        fill(lg, block, grad_source(e, j, given))

    pre = mm(lp[...], w1_ref[...].reshape(9 * CH, CH))
    back = mm(lg[...], w2t[...])

    def back_block(e, j):
        block = order_back.index((e, j))
        return back[block * 64 : block * 64 + 64]

    for j in (0, 1, 2, 3, 6, 7, 8, 9):
        ob[j] = back_block(-1, j).astype(BF)
    for j in (1, 2, 3, 6, 7, 8):
        ss[j] = mm(straight, ob[j]) + mm(turned, ob[9 - j])

    def corner_sums(low, high):
        low = (low.astype(F32) * row_line).astype(BF)
        high = (high.astype(F32) * row_line).astype(BF)
        return mm_t(lo_zero, low) + mm_t(hi_zero, high), mm_t(lo_end, low) + mm_t(hi_end, high)

    @pl.when(band < 2)
    def _():
        at_zero, at_end = corner_sums(ob[start - 1], ob[stop + 1])
        head = ss[start] + at_zero
        tail = ss[stop] + at_end
        head_b, tail_b = head.astype(BF), tail.astype(BF)
        ss[start] = head + mm(near[0], head_b) + mm(near[1], tail_b)
        ss[stop] = tail + mm(far[0], head_b) + mm(far[1], tail_b)

    def spot(j):
        return band - 2 + j if j < 5 else 56 - band + j

    unique = {}
    hid = {}
    for j in (0, 9):
        gp[j] = jnp.zeros((64, CH), BF)
        gpu[j] = jnp.zeros((64, CH), BF)
    for block, j in enumerate(order_pre):
        value = pre[block * 64 : block * 64 + 64]
        hidden, slope = silu_parts(value)
        t = spot(j)
        inside = jnp.logical_and(t >= 0, t < SPAN)
        corner = jnp.logical_or(t == 0, t == SPAN - 1)
        keep = jnp.where(corner, row_line, jnp.ones_like(row_line))
        unique[j] = keep
        grad = jnp.where(inside, (back_block(0, j) + ss[j]) * slope, 0.0).astype(BF)
        gp[j] = grad
        gpu[j] = (grad.astype(F32) * keep).astype(BF)
        if j in (2, 7):
            hid[j] = hidden.astype(BF)

    mine = (home == group * 16).astype(F32)
    edge = jnp.where(band == 0, 1.0, 0.0) * mine * row_line

    def scaled(value, factor):
        return (value.astype(F32) * factor).astype(BF)

    cells = jnp.concatenate([
        scaled(hid[2], mine * unique[2]),
        scaled(hid[7], mine * unique[7]),
        scaled(mm(straight, hid[2]) + mm(turned, hid[7]), mine),
        scaled(mm(straight, hid[7]) + mm(turned, hid[2]), mine),
        scaled(mm(lo_zero, hid[2]) + mm(lo_end, hid[7]), edge),
        scaled(mm(hi_zero, hid[2]) + mm(hi_end, hid[7]), edge),
    ], axis=0)
    second = mm_t(cells, lg[0:384, :])
    own = jnp.concatenate([scaled(gpu[2], mine), scaled(gpu[7], mine)], axis=0)
    first = mm_t(lp[0:128, :], own)
    acc[0:1152, :] += first
    for k in range(9):
        acc[1152 + k * CH : 1152 + (k + 1) * CH, :] += second[:, k * CH : (k + 1) * CH]

    order_in = [(0, 2), (0, 7), (1, 2), (1, 7), (-1, 1), (-1, 2), (-1, 7), (-1, 8)]
    for block, (e, j) in enumerate(order_in):
        depths = {0: (lambda at: gp[at]) if e == -1 else (lambda at: gpu[at])}
        fill(lc, block, grad_source(e, j, depths))
    back = mm(lc[...], w1t[...])
    part = [back[k * 64 : k * 64 + 64] for k in range(8)]
    o1, o2, o7, o8 = [p.astype(BF) for p in part[4:]]
    at_zero, at_end = corner_sums(o1, o8)
    at_edge = jnp.where(band == 0, 1.0, 0.0)
    owed = [
        part[0] + mm(straight, o2) + mm(turned, o7) + at_zero * at_edge,
        part[2],
        part[1] + mm(straight, o7) + mm(turned, o2) + at_end * at_edge,
        part[3],
    ]

    acc[2304:2312, :] = jnp.zeros((8, CH), F32)
    slot_row = lax.broadcasted_iota(I32, (SLOT_TWO, 64), 0)
    slot_lane = lax.broadcasted_iota(I32, (SLOT_TWO, 64), 1)
    head_row = lax.broadcasted_iota(I32, (SLOT_TWO, CH), 0) < CHUNK
    tails = {}
    for half in range(2):
        for g in range(4):
            tile = jnp.concatenate([o[g * 16 : g * 16 + 16] for o in owed], axis=0).astype(BF)
            row_target = group * 16 + half * 3 + (slot_row - 18)
            col_target = (half * 2 + (group & 1)) * 16 + 6 + 3 * (group >> 1) + (slot_row - 21)
            target = jnp.where(slot_row < 18, -1, jnp.where(slot_row < 21, row_target, col_target))
            tails[half, g] = mm((target == slot_lane).astype(F32).astype(BF), tile)
    for i in range(BANDS * GROUPS):
        piece = acc[CHUNK * i : CHUNK * i + SLOT_TWO, :]
        tail = tails[int(i // 4 >= 16), i % 4]
        out_ref[i] = jnp.where(head_row, piece, tail).astype(BF)


def reverse_selector():
    select = np.zeros((64, 64), np.float32)
    for b in range(32):
        select[b, b] = 1
        select[63 - b, 32 + b] = 1
    return select


def reduce_kernel(factor, sc_ref, in_ref, sum_ref):
    total = jnp.zeros((SLOT_TWO, CH), F32)
    for i in range(BANDS * GROUPS):
        total = total + in_ref[i].astype(F32)
    total = (total * factor).astype(BF)
    for i in range(BANDS * GROUPS):
        sum_ref[i] = total


def grad_kernel(sc_ref, rev_ref, in_ref, gin_ref, g_ref, out_ref, wide, total):
    band = sc_ref[0]
    for row in range(2):
        for face in range(3):
            start = row * 192 + face * 64
            total[row, face] = gin_ref[start : start + 64, :] + g_ref[face, row].astype(F32)
    low = band < 16
    for row in range(2):
        source = jnp.where(low, 2 * band + row, 63 - 2 * band - row)
        for sub in range(4):
            tile = in_ref[source * 4 + sub].astype(F32)
            depth, side = sub % 2, sub // 2
            column = depth if side == 0 else 63 - depth
            for face in range(3):
                total[row, face, column : column + 1, :] += tile[21 + face : 22 + face, :]

    @pl.when((band == 0) | (band == BANDS - 1))
    def _():
        for i in range(BANDS * GROUPS):
            wide[i * SLOT_TWO : (i + 1) * SLOT_TWO, :] = in_ref[i].astype(F32)
        for depth in range(2):
            for face in range(3):
                halves = [
                    wide[pl.ds((pos * 2 + depth) * SLOT_TWO + 18 + face, BANDS, stride=4 * SLOT_TWO), :]
                    for pos in range(2)
                ]
                extra = mm(rev_ref[...], jnp.concatenate(halves, axis=0).astype(BF))
                row = jnp.where(band == 0, depth, 1 - depth)
                total[row, face] += extra

    for row in range(2):
        for face in range(3):
            out_ref[face, row] = total[row, face].astype(BF)


def spread_kernel(in_ref, first_ref, second_ref):
    for i in range(BANDS * GROUPS):
        piece = in_ref[i].astype(F32)[0:CHUNK, :]
        ref = first_ref if i < 64 else second_ref
        start = CHUNK * (i % 64)
        ref[start : start + CHUNK, :] = piece


def by_line(table):
    return jnp.pad(table.reshape(4, 3, 4).transpose(0, 2, 1).reshape(4, 12), ((0, 0), (0, 4))).reshape(64)


def body(field_in, grad_out, first_weight, second_weight, face_neighbour, seam_rotation, corner_fill):
    band = lax.axis_index("tile")
    group = lax.axis_index("sub")
    scalars = jnp.stack([band, group]).astype(I32)
    factor = (1.0 * 12 * SPAN * SPAN) ** -0.5

    pair = jnp.stack([field_in, grad_out], axis=0)
    up = [(i, i + 1) for i in range(BANDS - 1)]
    down = [(j, i) for i, j in up]
    above = lax.ppermute(pair, "tile", up)
    below = lax.ppermute(pair, "tile", down)

    fill_low = jnp.stack([corner_fill[:, k] for k in (0, 2, 0, 1)], axis=1)
    fill_high = jnp.stack([corner_fill[:, k] for k in (1, 3, 2, 3)], axis=1)
    table = jnp.stack([by_line(t) for t in (face_neighbour, seam_rotation, fill_low, fill_high)], axis=1)

    slots = call(
        pack_lines,
        jax.ShapeDtypeStruct((BANDS, SLOT_ONE, CH), BF),
        [pltpu.VMEM((SPAN * 16, CH), F32), pltpu.VMEM((48, CH), F32)],
        (field_in, grad_out),
    )
    slots = lax.all_to_all(slots, "tile", 0, 0, tiled=True)
    lines = call(
        gather_lines,
        jax.ShapeDtypeStruct((POSITIONS, 64, CH), BF),
        [],
        (scalars, jnp.asarray(line_selector(), BF), slots),
        smem_first=True,
    )
    lines = lax.all_gather(lines, "sub", axis=0)

    slots, gin = call(
        main_kernel,
        [jax.ShapeDtypeStruct((BANDS * GROUPS, SLOT_TWO, CH), BF), jax.ShapeDtypeStruct((384, CH), F32)],
        [
            pltpu.VMEM((1152, CH), BF),
            pltpu.VMEM((1152, CH), BF),
            pltpu.VMEM((1152, CH), BF),
            pltpu.VMEM((1152, CH), BF),
            pltpu.VMEM((4, POSITIONS, 64, CH), BF),
            pltpu.VMEM((POSITIONS, 64, CH), BF),
            pltpu.VMEM((384, 1152), BF),
            pltpu.VMEM((896, 1152), BF),
            pltpu.VMEM((512, 1152), BF),
            pltpu.VMEM((POSITIONS, 64, CH), BF),
            pltpu.VMEM((POSITIONS, 64, CH), F32),
            pltpu.VMEM((POSITIONS, 64, CH), BF),
            pltpu.VMEM((POSITIONS, 64, CH), BF),
            pltpu.VMEM((2312, CH), F32),
        ],
        (
            scalars, table, lines, field_in, above[0], below[0], grad_out, above[1], below[1],
            first_weight, second_weight,
        ),
        smem_first=True,
    )
    slots = lax.all_to_all(slots, BOTH, 0, 0, tiled=True)
    reduced = call(
        lambda *refs: reduce_kernel(factor, *refs),
        jax.ShapeDtypeStruct((BANDS * GROUPS, SLOT_TWO, CH), BF),
        [],
        (scalars, slots),
        smem_first=True,
    )
    reduced = lax.all_to_all(reduced, BOTH, 0, 0, tiled=True)
    grad_in = call(
        grad_kernel,
        jax.ShapeDtypeStruct((3, 2, SPAN, CH), BF),
        [pltpu.VMEM((BANDS * GROUPS * SLOT_TWO, CH), F32), pltpu.VMEM((2, 3, SPAN, CH), F32)],
        (scalars, jnp.asarray(reverse_selector(), BF), slots, gin, grad_out),
        smem_first=True,
    )
    first, second = call(
        spread_kernel,
        [jax.ShapeDtypeStruct((1152, CH), F32), jax.ShapeDtypeStruct((1152, CH), F32)],
        [],
        (reduced,),
    )
    return grad_in, first.reshape(3, 3, CH, CH), second.reshape(3, 3, CH, CH)


def solution(mesh):
    return jax.shard_map(
        body,
        mesh=mesh,
        in_specs=(P("sub", "tile", None, None), P("sub", "tile", None, None), P(), P(), P(), P(), P()),
        out_specs=(P("sub", "tile", None, None), P(), P()),
        check_vma=False,
    )
```

```python
import jax
import jax.numpy as jnp
import numpy as np
from jax import lax
from jax.experimental import pallas as pl
from jax.experimental.pallas import tpu as pltpu
from jax.sharding import PartitionSpec as P

BF = jnp.bfloat16
F32 = jnp.float32
I32 = jnp.int32
BANDS = 32
SPAN = 64
CH = 128
TAPS = [(a, b) for a in range(3) for b in range(3)]
WINDOW = 6
ENDS = 48
STRIP = 12 * WINDOW
SLOT_ONE = 2 * STRIP
CHUNK = 72
TAIL = 48
SLOT_TWO = CHUNK + TAIL
VMEM_BYTES = 48 * 1024 * 1024


def mm(left, right):
    return jnp.dot(left, right, preferred_element_type=F32)


def mm_t(left, right):
    return lax.dot_general(left, right, (((0,), (0,)), ((), ())), preferred_element_type=F32)


def call(kernel, outs, scratch, operands, places=(), aliases=None):
    kinds = {"v": pltpu.VMEM, "s": pltpu.SMEM, "a": pl.ANY}
    places = dict(places)
    many = isinstance(outs, (list, tuple))
    out_specs = [pl.BlockSpec(memory_space=kinds[places.get(f"o{k}", "v")]) for k in range(len(outs) if many else 1)]
    return pl.pallas_call(
        kernel,
        out_shape=outs,
        in_specs=[pl.BlockSpec(memory_space=kinds[places.get(k, "v")]) for k in range(len(operands))],
        out_specs=out_specs if many else out_specs[0],
        scratch_shapes=scratch,
        input_output_aliases=aliases or {},
        compiler_params=pltpu.CompilerParams(vmem_limit_bytes=VMEM_BYTES),
    )(*operands)


def here():
    return lax.axis_index("tile"), lax.axis_index("sub")


def is_mirrored(fn_ref, rot_ref, face, side):
    rot = rot_ref[face, side]
    partner = 4 * fn_ref[face, side] + (rot & 3)
    return jnp.where(4 * face + side > partner, rot >> 2, 0)


def is_mirrored(fn_ref, rot_ref, face, side):
    rot = rot_ref[side, face]
    partner = 4 * fn_ref[side, face] + (rot & 3)
    return jnp.where(4 * face + side > partner, rot >> 2, 0)


def pack_lines(f_hbm, g_hbm, out_ref, buf, wide, ends, sems):
    copies = [pltpu.make_async_copy(src, buf.at[k], sems.at[k]) for k, src in enumerate((f_hbm, g_hbm))]
    for copy in copies:
        copy.start()
    band, _ = here()
    ends[ENDS:STRIP, :] = jnp.zeros((STRIP - ENDS, CH), F32)
    for fld in range(2):
        copies[fld].wait()
        for row in range(2):
            for face in range(3):
                block = buf[fld, face, row].astype(F32)
                wide[pl.ds(24 + fld * 6 + row * 3 + face, SPAN, stride=12), :] = block
                for edge, cols in enumerate(((0, 1), (63, 62))):
                    for depth, col in enumerate(cols):
                        place = row * 24 + fld * 12 + edge * 6 + depth * 3 + face
                        ends[place : place + 1, :] = block[col : col + 1, :]
    wide[0:24, :] = wide[SPAN * 12 : SPAN * 12 + 24, :]
    wide[SPAN * 12 + 24 : SPAN * 12 + 48, :] = wide[24:48, :]
    outer = (band == 0) | (band == BANDS - 1)
    strips = [wide[24 * d : 24 * d + STRIP, :] for d in range(BANDS)]
    for d in range(BANDS):
        rest = jnp.where(outer, strips[BANDS - 1 - d], ends[...])
        out_ref[d] = jnp.concatenate([strips[d], rest], axis=0).astype(BF)


def line_selector():
    select = np.zeros((2, WINDOW * 64, 4 * STRIP + 6 * ENDS), np.float32)
    for mirrored in range(2):
        for j in range(WINDOW):
            part, parity = j // 2, j % 2
            for fld in range(2):
                for depth in range(2):
                    for face in range(3):
                        base = j * 64 + (fld * 2 + depth) * 16 + face
                        column = STRIP * mirrored + (5 - j if mirrored else j) * 12 + fld * 6 + face
                        select[mirrored, base, column + depth * 3] = 1
                        select[mirrored, base + 3, 2 * STRIP + column + (1 - depth) * 3] = 1
                        for side in range(2):
                            source = 4 * STRIP + (3 * mirrored + part) * ENDS + (1 - parity if mirrored else parity) * 24
                            select[mirrored, base + 6 + 3 * side, source + fld * 12 + side * 6 + depth * 3 + face] = 1
    return select


def ends_selector():
    select = np.zeros((4, ENDS, SLOT_ONE), np.float32)
    for k, d in enumerate((0, 1, 30, 31)):
        for row in range(2):
            for fld in range(2):
                for side in range(2):
                    for depth in range(2):
                        col = 63 - depth if side else depth
                        at = (col - 2 * d + 2) % SPAN
                        other = (col - 60 + 2 * d) % SPAN
                        base = at * 12 if at < WINDOW else STRIP + other * 12
                        for face in range(3):
                            place = row * 24 + fld * 12 + side * 6 + depth * 3 + face
                            select[k, place, base + fld * 6 + row * 3 + face] = 1
    return select


def gather_lines(fn_ref, rot_ref, sel_ref, ends_ref, in_ref, out_ref):
    band, group = here()
    first, last = in_ref[0], in_ref[BANDS - 1]
    pick_ends = ends_ref[(band & 1) + 2 * (band >> 4)]
    first_ends, last_ends = mm(pick_ends, first), mm(pick_ends, last)
    ends = []
    for source in [band + 31 + part for part in range(3)] + [64 - band - part for part in range(3)]:
        source = source & 31
        block = in_ref[source].astype(F32)[STRIP : STRIP + ENDS]
        ends.append(jnp.where(source == 0, first_ends, jnp.where(source == BANDS - 1, last_ends, block)))
    pieces = jnp.concatenate([first.astype(F32), last.astype(F32)] + ends, axis=0).astype(BF)
    place = lax.broadcasted_iota(I32, (WINDOW * 64, CH), 0) & 15
    flip = jnp.zeros((WINDOW * 64, CH), I32)
    for side in range(4):
        for face in range(3):
            flip = jnp.where(place == side * 3 + face, is_mirrored(fn_ref, rot_ref, 3 * group + face, side), flip)
    picked = jnp.where(flip == 1, mm(sel_ref[1], pieces), mm(sel_ref[0], pieces)).astype(BF)
    for j in range(WINDOW):
        out_ref[j] = picked[j * 64 : j * 64 + 64]


def silu_parts(pre):
    logistic = 1.0 / (1.0 + jnp.exp(-pre))
    return pre * logistic, logistic * (1.0 + pre * (1.0 - logistic))


def side_frame(side, tap):
    dr, dc = tap[0] - 1, tap[1] - 1
    return ((dr, dc), (-dr, dc), (dc, dr), (-dc, dr))[side]


def transpose_weights(ref, out):
    for k, (a, b) in enumerate(TAPS):
        out[k * CH : (k + 1) * CH, :] = ref[a, b].T


def interior(band, in_ref, w1_ref, w1t, w2t, f2, g2, wide, acc, done):
    for s in range(BANDS):
        wide[s * STRIP : (s + 1) * STRIP, :] = in_ref[s].astype(F32)[0:STRIP]
    for q in range(WINDOW):
        for fld, target in enumerate((f2, g2)):
            for row in range(2):
                for face in range(3):
                    piece = wide[pl.ds(q * 12 + fld * 6 + row * 3 + face, BANDS, stride=STRIP), :]
                    target[pl.ds(q * 192 + face * 64 + row, BANDS, stride=2), :] = piece

    def conv_weights(ref):
        return jnp.concatenate([ref[a].reshape(3 * CH, CH) for a in range(3)], axis=1)

    def back_weights(ref):
        columns = []
        for a in range(3):
            columns.append(jnp.concatenate([ref[(a * 3 + b) * CH : (a * 3 + b + 1) * CH, :] for b in (2, 1, 0)], axis=0))
        return jnp.concatenate(columns, axis=1)

    def up_one(value):
        return pltpu.roll(value, value.shape[0] - 1, 0)

    def down_one(value):
        return pltpu.roll(value, 1, 0)

    def three_columns(ref, first, count):
        return jnp.concatenate([ref[first + 192 * b : first + 192 * b + count, :].astype(BF) for b in range(3)], axis=1)

    y = mm(three_columns(f2, 0, 768), conv_weights(w1_ref))
    pre = down_one(y[:, :CH]) + y[:, CH : 2 * CH] + up_one(y[:, 2 * CH :])
    z = mm(three_columns(g2, 0, 768), back_weights(w2t))
    back = up_one(z[:, :CH]) + z[:, CH : 2 * CH] + down_one(z[:, 2 * CH :])
    hidden, slope = silu_parts(pre)
    index = lax.broadcasted_iota(I32, (768, CH), 0)
    step = (index >= 192).astype(I32) + (index >= 384).astype(I32) + (index >= 576).astype(I32)
    col = 2 * band - 1 + step
    row = index & 63
    inner = (row >= 1) & (row <= 62) & (col >= 1) & (col <= 62)
    gpre = jnp.where(inner, back * slope, 0.0).astype(BF)
    hid = jnp.where(inner, hidden, 0.0)[192:576].astype(BF)

    gown = gpre[192:576].astype(F32)
    gcat = jnp.concatenate([up_one(gown).astype(BF), gpre[192:576], down_one(gown).astype(BF)], axis=1)
    first = mm_t(three_columns(f2, 192, 384), gcat)
    hown = hid.astype(F32)
    hcat = jnp.concatenate([down_one(hown).astype(BF), hid, up_one(hown).astype(BF)], axis=1)
    gback = jnp.concatenate([g2[start : start + 384, :].astype(BF) for start in (576, 384, 192)], axis=1)
    second = mm_t(hcat, gback)
    for k, (a, b) in enumerate(TAPS):
        top, low = k * CH, 1152 + k * CH
        acc[top : top + CH, :] = first[b * CH : (b + 1) * CH, a * CH : (a + 1) * CH]
        acc[low : low + CH, :] = second[a * CH : (a + 1) * CH, b * CH : (b + 1) * CH]

    gthree = jnp.concatenate([gpre[0:384], gpre[192:576], gpre[384:768]], axis=1)
    z = mm(gthree, back_weights(w1t))
    done[...] = up_one(z[:, :CH]) + z[:, CH : 2 * CH] + down_one(z[:, 2 * CH :]) + g2[384:768, :]


def main_kernel(
    fn_ref, rot_ref, fill_ref, sel_ref, a_ref, in_ref, w1_ref, w2_ref,
    out_ref,
    f2, g2, wide, total, done, sent, w1t, w2t, xs, hal, nb, cg, lp, lg, lc, ss, gp, gpu, owe,
):
    band, group = here()
    transpose_weights(w1_ref, w1t)
    transpose_weights(w2_ref, w2t)
    interior(band, in_ref, w1_ref, w1t, w2t, f2, g2, wide, total, done)

    line = lax.broadcasted_iota(I32, (64, 1), 0)
    place = line & 15
    side = (place >= 3).astype(I32) + (place >= 6).astype(I32) + (place >= 9).astype(I32)
    face = place - 3 * side
    home = line - place
    real = place < 12
    lane = lax.broadcasted_iota(I32, (64, 64), 1)

    def one_hot(target, keep):
        return (jnp.where(keep & real, target, -1) == lane).astype(F32).astype(BF)

    face_lane = lax.broadcasted_iota(I32, (64, 12), 1)
    faces = (jnp.where(real, 3 * (line >> 4) + face, -1) == face_lane).astype(F32).astype(BF)

    def by_line(ref, columns):
        table = ref[...].astype(F32).astype(BF)
        rows = lax.dot_general(faces, table, (((1,), (1,)), ((), ())), preferred_element_type=F32).astype(I32)
        value = rows[:, columns[0] : columns[0] + 1]
        for s in range(1, 4):
            value = jnp.where(side == s, rows[:, columns[s] : columns[s] + 1], value)
        return value

    fn = by_line(fn_ref, (0, 1, 2, 3))
    rot = by_line(rot_ref, (0, 1, 2, 3))
    fn_group = (fn * 43) >> 7
    partner = one_hot(fn_group * 16 + (rot & 3) * 3 + (fn - 3 * fn_group), real)
    number = 4 * (3 * (line >> 4) + face) + side
    flip = ((rot >> 2) == 1) & (number > 4 * fn + (rot & 3)) & real
    fills = []
    for columns in ((0, 2, 0, 1), (1, 3, 2, 3)):
        m = by_line(fill_ref, columns)
        mf = m >> 2
        mg = (mf * 43) >> 7
        target = mg * 16 + ((m >> 1) & 1) * 3 + (mf - 3 * mg)
        fills.append((one_hot(target, (m & 1) == 0), one_hot(target, (m & 1) == 1)))
    (lo_zero, lo_end), (hi_zero, hi_end) = fills
    even = (side & 1) == 0
    low_side = jnp.where(side < 2, 2, 0)
    high_side = jnp.where(side < 2, 3, 1)
    near = [one_hot(home + low_side * 3 + face, even), one_hot(home + low_side * 3 + face, ~even)]
    far = [one_hot(home + high_side * 3 + face, even), one_hot(home + high_side * 3 + face, ~even)]
    side_mask = [jnp.broadcast_to((side == s).astype(F32), (64, CH)).astype(BF) for s in range(4)]
    row_line = (side < 2).astype(F32)
    flip_f = jnp.broadcast_to(flip.astype(F32), (64, CH))
    flip_b, keep_b = flip_f.astype(BF), (1.0 - flip_f).astype(BF)

    def pick(plain, mirrored):
        return plain * keep_b + mirrored * flip_b

    def pick_f(plain, mirrored):
        return jnp.where(flip_f > 0.5, mirrored, plain)

    for j in range(WINDOW):
        for block in range(4):
            xs[block, j] = jnp.concatenate([a_ref[g, j, block * 16 : block * 16 + 16, :] for g in range(4)], axis=0)
    for j in range(WINDOW):
        hal[j] = mm(partner, xs[0, j]).astype(BF)

    def block_at(block, j):
        return hal[j] if block == 0 else xs[block - 1, j]

    for block in range(5):
        for j in range(1, 5):
            before, after = block_at(block, j - 1), block_at(block, j + 1)
            nb[0, block, j] = pick(before, after)
            nb[1, block, j] = pick(after, before)
    cg[...] = jnp.zeros_like(cg)

    def line_ends(zero, end, shift):
        lower, upper = zero + shift, end - shift
        return lambda value: (pick(value(lower), value(upper)), pick(value(upper), value(lower)))

    def fill_ends(zero, end):
        first = line_ends(zero, end, 0)
        second = line_ends(zero, end, 1)
        h_zero, h_end = first(lambda j: hal[j])
        h_one, h_last = second(lambda j: hal[j])
        f_zero, f_end = first(lambda j: xs[0, j])
        none = jnp.zeros((64, CH), BF)
        low = [
            (mm(lo_zero, f_zero) + mm(lo_end, f_end)).astype(BF),
            (mm(near[0], h_zero) + mm(near[1], h_end)).astype(BF),
            (mm(near[0], h_one) + mm(near[1], h_last)).astype(BF),
            none, none,
        ]
        high = [
            (mm(hi_zero, f_zero) + mm(hi_end, f_end)).astype(BF),
            (mm(far[0], h_zero) + mm(far[1], h_end)).astype(BF),
            (mm(far[0], h_one) + mm(far[1], h_last)).astype(BF),
            none, none,
        ]
        for block in range(5):
            nb[0, block, zero] = pick(low[block], nb[0, block, zero])
            nb[1, block, zero] = pick(nb[1, block, zero], high[block])
            nb[0, block, end] = pick(nb[0, block, end], low[block])
            nb[1, block, end] = pick(high[block], nb[1, block, end])
        cg[0], cg[1] = first(lambda j: xs[2, j])

    @pl.when(band == 0)
    def _():
        fill_ends(2, 1)

    @pl.when(band == BANDS - 1)
    def _():
        fill_ends(4, 3)

    def choose(options):
        result = None
        for s, option in enumerate(options):
            if option is None:
                continue
            term = option * side_mask[s]
            result = term if result is None else result + term
        return jnp.zeros((64, CH), BF) if result is None else result

    def fill(target, block, source):
        for k, tap in enumerate(TAPS):
            target[block * 64 : block * 64 + 64, k * CH : (k + 1) * CH] = choose(
                [source(*side_frame(s, tap)) for s in range(4)]
            )

    def field_source(j):
        def source(delta, dt):
            return block_at(delta + 1, j) if dt == 0 else nb[(dt + 1) // 2, delta + 1, j]
        return source

    def grad_source(e, j):
        def source(delta, dt):
            depth = e - delta
            if depth not in (0, 1):
                return None
            return xs[2 + depth, j] if dt == 0 else nb[(1 - dt) // 2, 3 + depth, j]
        return source

    def corner_source(which, value):
        def source(delta, dt):
            return value if (delta, dt) == (-1, 2 * which - 1) else None
        return source

    order_pre = (2, 3, 1, 4)
    for block, j in enumerate(order_pre):
        fill(lp, block, field_source(j))
    order_back = [(0, 2), (0, 3), (-1, 2), (-1, 3), None, None, (0, 1), (0, 4), (-1, 1), (-1, 4)]
    for block, at in enumerate(order_back):
        fill(lg, block, corner_source(block - 4, cg[block - 4]) if at is None else grad_source(*at))

    pre = mm(lp[...], w1_ref[...].reshape(9 * CH, CH))
    back = mm(lg[...], w2t[...])

    def back_block(e, j):
        block = order_back.index((e, j))
        return back[block * 64 : block * 64 + 64]

    for j in range(1, 5):
        ss[j] = mm(partner, back_block(-1, j).astype(BF))

    def corner_sums(low, high):
        low = (low * row_line).astype(BF)
        high = (high * row_line).astype(BF)
        return mm_t(lo_zero, low) + mm_t(hi_zero, high), mm_t(lo_end, low) + mm_t(hi_end, high)

    corner_low, corner_high = back[256:320], back[320:384]

    def close_ends(zero, end):
        at_zero, at_end = corner_sums(corner_low, corner_high)
        head = pick_f(ss[zero], ss[end]) + at_zero
        tail = pick_f(ss[end], ss[zero]) + at_end
        head_b, tail_b = head.astype(BF), tail.astype(BF)
        head += mm(near[0], head_b) + mm(near[1], tail_b)
        tail += mm(far[0], head_b) + mm(far[1], tail_b)
        ss[zero] = pick_f(head, tail)
        ss[end] = pick_f(tail, head)

    @pl.when(band == 0)
    def _():
        close_ends(2, 1)

    @pl.when(band == BANDS - 1)
    def _():
        close_ends(4, 3)

    unique = {}
    hid = {}
    for block, j in enumerate(order_pre):
        value = pre[block * 64 : block * 64 + 64]
        hidden, slope = silu_parts(value)
        t = (2 * band - 2 + j) & (SPAN - 1)
        corner = jnp.logical_or(t == 0, t == SPAN - 1)
        unique[j] = jnp.where(corner, row_line, jnp.ones_like(row_line))
        grad = ((back_block(0, j) + ss[j]) * slope).astype(BF)
        gp[j] = grad
        gpu[j] = (grad.astype(F32) * unique[j]).astype(BF)
        hid[j] = hidden.astype(BF)

    mine = (home == group * 16).astype(F32)
    edge = jnp.where(band == 0, 1.0, 0.0) * mine * row_line

    def scaled(value, factor):
        return (value.astype(F32) * factor).astype(BF)

    h_zero, h_end = pick(hid[2], hid[1]), pick(hid[1], hid[2])
    cells = jnp.concatenate([
        scaled(hid[2], mine * unique[2]),
        scaled(hid[3], mine * unique[3]),
        scaled(mm(partner, hid[2]), mine),
        scaled(mm(partner, hid[3]), mine),
        scaled(mm(lo_zero, h_zero) + mm(lo_end, h_end), edge),
        scaled(mm(hi_zero, h_zero) + mm(hi_end, h_end), edge),
    ], axis=0)
    second = mm_t(cells, lg[0:384, :])
    own = jnp.concatenate([scaled(gpu[2], mine), scaled(gpu[3], mine)], axis=0)
    first = mm_t(lp[0:128, :], own)

    at_first, at_last = band == 0, band == BANDS - 1
    inner_low = jnp.where(at_first, 0.0, 1.0)
    inner_high = jnp.where(at_last, 0.0, 1.0)

    def spread_source(e, j, ref):
        def source(delta, dt):
            if e - delta != 0:
                return None
            if dt == 0:
                return ref[j]
            before = scaled(ref[1], inner_low) if j == 2 else ref[2]
            after = ref[3] if j == 2 else scaled(ref[4], inner_high)
            return pick(before, after) if dt == 1 else pick(after, before)
        return source

    g_zero = jnp.where(at_first, gp[2], gp[4])
    g_end = jnp.where(at_first, gp[1], gp[3])
    g_zero, g_end = pick(g_zero, g_end), pick(g_end, g_zero)
    order_in = [(0, 2), (0, 3), (1, 2), (1, 3), (-1, 2), (-1, 3), None, None]
    for block, at in enumerate(order_in):
        if at is None:
            fill(lc, block, corner_source(block - 6, (g_zero, g_end)[block - 6]))
        else:
            fill(lc, block, spread_source(*at, gp if at[0] == -1 else gpu))
    back = mm(lc[...], w1t[...])
    part = [back[k * 64 : k * 64 + 64] for k in range(8)]
    at_zero, at_end = corner_sums(part[6], part[7])
    owe[0] = part[0] + mm(partner, part[4].astype(BF)) + pick_f(at_zero, at_end) * (1.0 - inner_low)
    owe[1] = part[2]
    owe[2] = part[1] + mm(partner, part[5].astype(BF)) + pick_f(at_end, at_zero) * (1.0 - inner_high)
    owe[3] = part[3]

    tile = jnp.concatenate([owe[k, pl.ds(pl.multiple_of(group * 16, 16), 16), :] for k in range(4)], axis=0)
    tails = mm(sel_ref[...], tile.astype(BF))
    total[0:1152, :] += first
    for k in range(9):
        total[1152 + k * CH : 1152 + (k + 1) * CH, :] += second[:, k * CH : (k + 1) * CH]
    sent[...] = jnp.zeros_like(sent)
    for q in range(2):
        for face in range(3):
            for row in range(2):
                piece = done[pl.ds(q * 192 + face * 64 + row, BANDS, stride=2), :]
                sent[pl.ds((q * 3 + face) * 2 + row, BANDS, stride=16), :] = piece
    for i in range(BANDS):
        half = i // 16
        tail = tails[half * 40 : half * 40 + 40]
        pixels = jnp.concatenate([sent[i * 16 : i * 16 + 16, :], jnp.zeros((32, CH), F32)], axis=0)
        shifted = jnp.concatenate([jnp.zeros((8, CH), F32), tail], axis=0)
        out_ref[i] = jnp.concatenate([total[CHUNK * i : CHUNK * i + CHUNK, :], pixels + shifted], axis=0).astype(BF)


def tail_selector():
    select = np.zeros((80, 64), np.float32)
    for half in range(2):
        for pos in range(2):
            for depth in range(2):
                for face in range(3):
                    lane = (pos * 2 + depth) * 16 + face
                    select[half * 40 + 4 + (pos * 2 + depth) * 3 + face, lane + half * 3] = 1
                    for side in range(2):
                        row = 16 + ((pos * 2 + side) * 2 + depth) * 3 + face
                        select[half * 40 + row, lane + 6 + 3 * side] = 1
    return select


def order_selector():
    select = np.zeros((2, 64, 64), np.float32)
    for pos in range(2):
        for b in range(BANDS):
            select[0, 2 * b + pos, pos * 32 + b] = 1
            select[1, 63 - 2 * b - pos, pos * 32 + b] = 1
    return select


def reduce_kernel(in_ref, sum_ref):
    total = in_ref[0].astype(F32)
    for i in range(1, BANDS):
        total = total + in_ref[i].astype(F32)
    sum_ref[...] = total[0:CHUNK]


def spread_kernel(factor, in_ref, out_ref):
    total = (in_ref[0] + in_ref[1]) + (in_ref[2] + in_ref[3])
    total = (total * factor).astype(BF)
    for i in range(BANDS):
        out_ref[i] = total


def final_kernel(fn_ref, rot_ref, sel_ref, in_ref, sum_ref, out_ref, first_ref, second_ref, wide, total):
    first_ref[...] = sum_ref[0:16].astype(F32).reshape(1152, CH)
    second_ref[...] = sum_ref[16:32].astype(F32).reshape(1152, CH)
    band, group = here()
    for i in range(BANDS):
        wide[i * TAIL : (i + 1) * TAIL, :] = in_ref[i].astype(F32)[CHUNK:SLOT_TWO]
    for q in range(2):
        for face in range(3):
            for row in range(2):
                piece = wide[pl.ds((q * 3 + face) * 2 + row, BANDS, stride=TAIL), :]
                total[row, face, pl.ds(q, BANDS, stride=2), :] = piece
    tiles = [wide[pl.ds(pl.multiple_of(src * TAIL, TAIL), TAIL), :] for src in (band, BANDS - 1 - band)]
    for side in range(2):
        for face in range(3):
            flip = is_mirrored(fn_ref, rot_ref, 3 * group + face, 2 + side) == 1
            for row in range(2):
                for depth in range(2):
                    column = depth if side == 0 else 63 - depth
                    k, m = [24 + ((pos * 2 + side) * 2 + depth) * 3 + face for pos in (row, 1 - row)]
                    extra = jnp.where(flip, tiles[1][m : m + 1, :], tiles[0][k : k + 1, :])
                    total[row, face, column : column + 1, :] += extra

    @pl.when((band == 0) | (band == BANDS - 1))
    def _():
        side = jnp.where(band == 0, 0, 1)
        for face in range(3):
            order = sel_ref[is_mirrored(fn_ref, rot_ref, 3 * group + face, side)]
            for depth in range(2):
                halves = [wide[pl.ds(12 + (pos * 2 + depth) * 3 + face, BANDS, stride=TAIL), :] for pos in range(2)]
                extra = mm(order, jnp.concatenate(halves, axis=0).astype(BF))
                row = jnp.where(band == 0, depth, 1 - depth)
                total[row, face] += extra

    for row in range(2):
        for face in range(3):
            out_ref[face, row] = total[row, face].astype(BF)


def body(field_in, grad_out, first_weight, second_weight, face_neighbour, seam_rotation, corner_fill):
    factor = (1.0 * 12 * SPAN * SPAN) ** -0.5
    seams = (face_neighbour.T, seam_rotation.T)
    in_smem = {0: "s", 1: "s"}

    slots = call(
        pack_lines,
        jax.ShapeDtypeStruct((BANDS, SLOT_ONE, CH), BF),
        [
            pltpu.VMEM((2, 3, 2, SPAN, CH), BF),
            pltpu.VMEM(((SPAN + 4) * 12, CH), F32),
            pltpu.VMEM((STRIP, CH), F32),
            pltpu.SemaphoreType.DMA((2,)),
        ],
        (field_in, grad_out),
        {0: "a", 1: "a"},
    )
    strips = lax.all_to_all(slots, "tile", 0, 0, tiled=True)
    lines = call(
        gather_lines,
        jax.ShapeDtypeStruct((WINDOW, 64, CH), BF),
        [],
        (*seams, jnp.asarray(line_selector(), BF), jnp.asarray(ends_selector(), BF), strips),
        in_smem,
    )
    lines = lax.all_gather(lines, "sub", axis=0)

    slots = call(
        main_kernel,
        jax.ShapeDtypeStruct((BANDS, SLOT_TWO, CH), BF),
        [
            pltpu.VMEM((1152, CH), F32),
            pltpu.VMEM((1152, CH), F32),
            pltpu.VMEM((BANDS * STRIP, CH), F32),
            pltpu.VMEM((2304, CH), F32),
            pltpu.VMEM((384, CH), F32),
            pltpu.VMEM((BANDS * 16, CH), F32),
            pltpu.VMEM((1152, CH), BF),
            pltpu.VMEM((1152, CH), BF),
            pltpu.VMEM((4, WINDOW, 64, CH), BF),
            pltpu.VMEM((WINDOW, 64, CH), BF),
            pltpu.VMEM((2, 5, 5, 64, CH), BF),
            pltpu.VMEM((2, 64, CH), BF),
            pltpu.VMEM((256, 1152), BF),
            pltpu.VMEM((640, 1152), BF),
            pltpu.VMEM((512, 1152), BF),
            pltpu.VMEM((5, 64, CH), F32),
            pltpu.VMEM((5, 64, CH), BF),
            pltpu.VMEM((5, 64, CH), BF),
            pltpu.VMEM((4, 64, CH), F32),
        ],
        (*seams, corner_fill.T, jnp.asarray(tail_selector(), BF), lines, strips, first_weight, second_weight),
    )
    slots = lax.all_to_all(slots, "tile", 0, 0, tiled=True)
    part = call(reduce_kernel, jax.ShapeDtypeStruct((CHUNK, CH), F32), [], (slots,))
    part = lax.all_gather(part, "sub", axis=0)
    reduced = call(
        lambda *refs: spread_kernel(factor, *refs),
        jax.ShapeDtypeStruct((BANDS, CHUNK, CH), BF),
        [],
        (part,),
    )
    reduced = lax.all_to_all(reduced, "tile", 0, 0, tiled=True)
    grad_in, first, second = call(
        final_kernel,
        [
            jax.ShapeDtypeStruct((3, 2, SPAN, CH), BF),
            jax.ShapeDtypeStruct((1152, CH), F32),
            jax.ShapeDtypeStruct((1152, CH), F32),
        ],
        [pltpu.VMEM((BANDS * TAIL, CH), F32), pltpu.VMEM((2, 3, SPAN, CH), F32)],
        (*seams, jnp.asarray(order_selector(), BF), slots, reduced),
        in_smem,
    )
    return grad_in, first.reshape(3, 3, CH, CH), second.reshape(3, 3, CH, CH)


def solution(mesh):
    return jax.shard_map(
        body,
        mesh=mesh,
        in_specs=(P("sub", "tile", None, None), P("sub", "tile", None, None), P(), P(), P(), P(), P()),
        out_specs=(P("sub", "tile", None, None), P(), P()),
        check_vma=False,
    )
```

```python
import jax
import jax.numpy as jnp
import numpy as np
from jax import lax
from jax.experimental import pallas as pl
from jax.experimental.pallas import tpu as pltpu
from jax.sharding import PartitionSpec as P

BF = jnp.bfloat16
F32 = jnp.float32
I32 = jnp.int32
BANDS = 32
SPAN = 64
CH = 128
TAPS = [(a, b) for a in range(3) for b in range(3)]
WINDOW = 6
ENDS = 48
STRIP = 12 * WINDOW
SLOT_ONE = 2 * STRIP
CHUNK = 72
TAIL = 48
SLOT_TWO = CHUNK + TAIL
VMEM_BYTES = 48 * 1024 * 1024


def mm(left, right):
    return jnp.dot(left, right, preferred_element_type=F32)


def mm_t(left, right):
    return lax.dot_general(left, right, (((0,), (0,)), ((), ())), preferred_element_type=F32)


def call(kernel, outs, scratch, operands, places=(), aliases=None):
    kinds = {"v": pltpu.VMEM, "s": pltpu.SMEM, "h": pltpu.HBM}
    places = dict(places)
    many = isinstance(outs, (list, tuple))
    out_specs = [pl.BlockSpec(memory_space=kinds[places.get(f"o{k}", "v")]) for k in range(len(outs) if many else 1)]
    return pl.pallas_call(
        kernel,
        out_shape=outs,
        in_specs=[pl.BlockSpec(memory_space=kinds[places.get(k, "v")]) for k in range(len(operands))],
        out_specs=out_specs if many else out_specs[0],
        scratch_shapes=scratch,
        input_output_aliases=aliases or {},
        compiler_params=pltpu.CompilerParams(vmem_limit_bytes=VMEM_BYTES),
    )(*operands)


def here():
    return lax.axis_index("tile"), lax.axis_index("sub")


def is_mirrored(fn_ref, rot_ref, face, side):
    rot = rot_ref[face, side]
    partner = 4 * fn_ref[face, side] + (rot & 3)
    return jnp.where(4 * face + side > partner, rot >> 2, 0)


def is_mirrored(fn_ref, rot_ref, face, side):
    rot = rot_ref[side, face]
    partner = 4 * fn_ref[side, face] + (rot & 3)
    return jnp.where(4 * face + side > partner, rot >> 2, 0)


def pack_lines(f_hbm, g_hbm, out_ref, buf, wide, ends, sems):
    copies = [pltpu.make_async_copy(src, buf.at[k], sems.at[k]) for k, src in enumerate((f_hbm, g_hbm))]
    for copy in copies:
        copy.start()
    band, _ = here()
    ends[ENDS:STRIP, :] = jnp.zeros((STRIP - ENDS, CH), F32)
    for fld in range(2):
        copies[fld].wait()
        for row in range(2):
            for face in range(3):
                block = buf[fld, face, row].astype(F32)
                wide[pl.ds(24 + fld * 6 + row * 3 + face, SPAN, stride=12), :] = block
                for edge, cols in enumerate(((0, 1), (63, 62))):
                    for depth, col in enumerate(cols):
                        place = row * 24 + fld * 12 + edge * 6 + depth * 3 + face
                        ends[place : place + 1, :] = block[col : col + 1, :]
    wide[0:24, :] = wide[SPAN * 12 : SPAN * 12 + 24, :]
    wide[SPAN * 12 + 24 : SPAN * 12 + 48, :] = wide[24:48, :]
    outer = (band == 0) | (band == BANDS - 1)
    strips = [wide[24 * d : 24 * d + STRIP, :] for d in range(BANDS)]
    for d in range(BANDS):
        rest = jnp.where(outer, strips[BANDS - 1 - d], ends[...])
        out_ref[d] = jnp.concatenate([strips[d], rest], axis=0).astype(BF)


def line_selector():
    select = np.zeros((2, WINDOW * 64, 4 * STRIP + 6 * ENDS), np.float32)
    for mirrored in range(2):
        for j in range(WINDOW):
            part, parity = j // 2, j % 2
            for fld in range(2):
                for depth in range(2):
                    for face in range(3):
                        base = j * 64 + (fld * 2 + depth) * 16 + face
                        column = STRIP * mirrored + (5 - j if mirrored else j) * 12 + fld * 6 + face
                        select[mirrored, base, column + depth * 3] = 1
                        select[mirrored, base + 3, 2 * STRIP + column + (1 - depth) * 3] = 1
                        for side in range(2):
                            source = 4 * STRIP + (3 * mirrored + part) * ENDS + (1 - parity if mirrored else parity) * 24
                            select[mirrored, base + 6 + 3 * side, source + fld * 12 + side * 6 + depth * 3 + face] = 1
    return select


def ends_selector():
    select = np.zeros((4, ENDS, SLOT_ONE), np.float32)
    for k, d in enumerate((0, 1, 30, 31)):
        for row in range(2):
            for fld in range(2):
                for side in range(2):
                    for depth in range(2):
                        col = 63 - depth if side else depth
                        at = (col - 2 * d + 2) % SPAN
                        other = (col - 60 + 2 * d) % SPAN
                        base = at * 12 if at < WINDOW else STRIP + other * 12
                        for face in range(3):
                            place = row * 24 + fld * 12 + side * 6 + depth * 3 + face
                            select[k, place, base + fld * 6 + row * 3 + face] = 1
    return select


def gather_lines(fn_ref, rot_ref, sel_ref, ends_ref, in_ref, out_ref):
    band, group = here()
    first, last = in_ref[0], in_ref[BANDS - 1]
    pick_ends = ends_ref[(band & 1) + 2 * (band >> 4)]
    first_ends, last_ends = mm(pick_ends, first), mm(pick_ends, last)
    ends = []
    for source in [band + 31 + part for part in range(3)] + [64 - band - part for part in range(3)]:
        source = source & 31
        block = in_ref[source].astype(F32)[STRIP : STRIP + ENDS]
        ends.append(jnp.where(source == 0, first_ends, jnp.where(source == BANDS - 1, last_ends, block)))
    pieces = jnp.concatenate([first.astype(F32), last.astype(F32)] + ends, axis=0).astype(BF)
    place = lax.broadcasted_iota(I32, (WINDOW * 64, 1), 0) & 15
    flip = jnp.zeros((WINDOW * 64, 1), I32)
    for side in range(4):
        for face in range(3):
            flip = jnp.where(place == side * 3 + face, is_mirrored(fn_ref, rot_ref, 3 * group + face, side), flip)
    flip = jnp.broadcast_to(flip.astype(F32), sel_ref.shape[1:]).astype(BF)
    picked = mm(sel_ref[0] * (1 - flip) + sel_ref[1] * flip, pieces).astype(BF)
    for j in range(WINDOW):
        out_ref[j] = picked[j * 64 : j * 64 + 64]


def silu_parts(pre):
    logistic = 1.0 / (1.0 + jnp.exp(-pre))
    return pre * logistic, logistic * (1.0 + pre * (1.0 - logistic))


def side_frame(side, tap):
    dr, dc = tap[0] - 1, tap[1] - 1
    return ((dr, dc), (-dr, dc), (dc, dr), (-dc, dr))[side]


def transpose_weights(ref, out):
    for k, (a, b) in enumerate(TAPS):
        out[k * CH : (k + 1) * CH, :] = ref[a, b].T


def interior_kernel(in_ref, w1_ref, w2_ref, acc, done, w1t, w2t, f2, g2, wide):
    band, _ = here()
    transpose_weights(w1_ref, w1t)
    transpose_weights(w2_ref, w2t)
    for s in range(BANDS):
        wide[s * STRIP : (s + 1) * STRIP, :] = in_ref[s].astype(F32)[0:STRIP]
    for q in range(WINDOW):
        for fld, target in enumerate((f2, g2)):
            for row in range(2):
                for face in range(3):
                    piece = wide[pl.ds(q * 12 + fld * 6 + row * 3 + face, BANDS, stride=STRIP), :]
                    target[pl.ds(q * 192 + face * 64 + row, BANDS, stride=2), :] = piece

    def conv_weights(ref):
        return jnp.concatenate([ref[a].reshape(3 * CH, CH) for a in range(3)], axis=1)

    def back_weights(ref):
        columns = []
        for a in range(3):
            columns.append(jnp.concatenate([ref[(a * 3 + b) * CH : (a * 3 + b + 1) * CH, :] for b in (2, 1, 0)], axis=0))
        return jnp.concatenate(columns, axis=1)

    def up_one(value):
        return pltpu.roll(value, value.shape[0] - 1, 0)

    def down_one(value):
        return pltpu.roll(value, 1, 0)

    def three_columns(ref, first, count):
        return jnp.concatenate([ref[first + 192 * b : first + 192 * b + count, :].astype(BF) for b in range(3)], axis=1)

    y = mm(three_columns(f2, 0, 768), conv_weights(w1_ref))
    pre = down_one(y[:, :CH]) + y[:, CH : 2 * CH] + up_one(y[:, 2 * CH :])
    z = mm(three_columns(g2, 0, 768), back_weights(w2t))
    back = up_one(z[:, :CH]) + z[:, CH : 2 * CH] + down_one(z[:, 2 * CH :])
    hidden, slope = silu_parts(pre)
    index = lax.broadcasted_iota(I32, (768, CH), 0)
    step = (index >= 192).astype(I32) + (index >= 384).astype(I32) + (index >= 576).astype(I32)
    col = 2 * band - 1 + step
    row = index & 63
    inner = (row >= 1) & (row <= 62) & (col >= 1) & (col <= 62)
    gpre = jnp.where(inner, back * slope, 0.0).astype(BF)
    hid = jnp.where(inner, hidden, 0.0)[192:576].astype(BF)

    gown = gpre[192:576].astype(F32)
    gcat = jnp.concatenate([up_one(gown).astype(BF), gpre[192:576], down_one(gown).astype(BF)], axis=1)
    first = mm_t(three_columns(f2, 192, 384), gcat)
    hown = hid.astype(F32)
    hcat = jnp.concatenate([down_one(hown).astype(BF), hid, up_one(hown).astype(BF)], axis=1)
    gback = jnp.concatenate([g2[start : start + 384, :].astype(BF) for start in (576, 384, 192)], axis=1)
    second = mm_t(hcat, gback)
    for k, (a, b) in enumerate(TAPS):
        top, low = k * CH, 1152 + k * CH
        acc[top : top + CH, :] = first[b * CH : (b + 1) * CH, a * CH : (a + 1) * CH]
        acc[low : low + CH, :] = second[a * CH : (a + 1) * CH, b * CH : (b + 1) * CH]

    gthree = jnp.concatenate([gpre[0:384], gpre[192:576], gpre[384:768]], axis=1)
    z = mm(gthree, back_weights(w1t))
    done[...] = up_one(z[:, :CH]) + z[:, CH : 2 * CH] + down_one(z[:, 2 * CH :]) + g2[384:768, :]


def main_kernel(
    fn_ref, rot_ref, fill_ref, sel_ref, own_ref, one_ref, two_ref, three_ref, acc, done, w1_ref, w2_ref,
    out_ref,
    total, sent, w1t, w2t, xs, hal, nb, cg, lp, lg, lc, ss, gp, gpu, owe,
):
    band, group = here()
    transpose_weights(w1_ref, w1t)
    transpose_weights(w2_ref, w2t)

    line = lax.broadcasted_iota(I32, (64, 1), 0)
    place = line & 15
    side = (place >= 3).astype(I32) + (place >= 6).astype(I32) + (place >= 9).astype(I32)
    face = place - 3 * side
    home = line - place
    real = place < 12
    lane = lax.broadcasted_iota(I32, (64, 64), 1)

    def one_hot(target, keep):
        return (jnp.where(keep & real, target, -1) == lane).astype(F32).astype(BF)

    face_lane = lax.broadcasted_iota(I32, (64, 12), 1)
    faces = (jnp.where(real, 3 * (line >> 4) + face, -1) == face_lane).astype(F32).astype(BF)

    def by_line(ref, columns):
        table = ref[...].astype(F32).astype(BF)
        rows = lax.dot_general(faces, table, (((1,), (1,)), ((), ())), preferred_element_type=F32).astype(I32)
        value = rows[:, columns[0] : columns[0] + 1]
        for s in range(1, 4):
            value = jnp.where(side == s, rows[:, columns[s] : columns[s] + 1], value)
        return value

    fn = by_line(fn_ref, (0, 1, 2, 3))
    rot = by_line(rot_ref, (0, 1, 2, 3))
    fn_group = (fn * 43) >> 7
    partner = one_hot(fn_group * 16 + (rot & 3) * 3 + (fn - 3 * fn_group), real)
    number = 4 * (3 * (line >> 4) + face) + side
    flip = ((rot >> 2) == 1) & (number > 4 * fn + (rot & 3)) & real
    fills = []
    for columns in ((0, 2, 0, 1), (1, 3, 2, 3)):
        m = by_line(fill_ref, columns)
        mf = m >> 2
        mg = (mf * 43) >> 7
        target = mg * 16 + ((m >> 1) & 1) * 3 + (mf - 3 * mg)
        fills.append((one_hot(target, (m & 1) == 0), one_hot(target, (m & 1) == 1)))
    (lo_zero, lo_end), (hi_zero, hi_end) = fills
    even = (side & 1) == 0
    low_side = jnp.where(side < 2, 2, 0)
    high_side = jnp.where(side < 2, 3, 1)
    near = [one_hot(home + low_side * 3 + face, even), one_hot(home + low_side * 3 + face, ~even)]
    far = [one_hot(home + high_side * 3 + face, even), one_hot(home + high_side * 3 + face, ~even)]
    side_mask = [jnp.broadcast_to((side == s).astype(F32), (64, CH)).astype(BF) for s in range(4)]
    row_line = (side < 2).astype(F32)
    flip_f = jnp.broadcast_to(flip.astype(F32), (64, CH))
    flip_b, keep_b = flip_f.astype(BF), (1.0 - flip_f).astype(BF)

    def pick(plain, mirrored):
        return plain * keep_b + mirrored * flip_b

    def pick_f(plain, mirrored):
        return jnp.where(flip_f > 0.5, mirrored, plain)

    for step, ref in enumerate((own_ref, one_ref, two_ref, three_ref)):
        start = pl.multiple_of(((group - step) & 3) * 16, 16)
        for j in range(WINDOW):
            for block in range(4):
                xs[block, j, pl.ds(start, 16), :] = ref[j, block * 16 : block * 16 + 16, :]
    for j in range(WINDOW):
        hal[j] = mm(partner, xs[0, j]).astype(BF)

    def block_at(block, j):
        return hal[j] if block == 0 else xs[block - 1, j]

    for block in range(5):
        for j in range(1, 5):
            before, after = block_at(block, j - 1), block_at(block, j + 1)
            nb[0, block, j] = pick(before, after)
            nb[1, block, j] = pick(after, before)
    cg[...] = jnp.zeros_like(cg)

    def line_ends(zero, end, shift):
        lower, upper = zero + shift, end - shift
        return lambda value: (pick(value(lower), value(upper)), pick(value(upper), value(lower)))

    def fill_ends(zero, end):
        first = line_ends(zero, end, 0)
        second = line_ends(zero, end, 1)
        h_zero, h_end = first(lambda j: hal[j])
        h_one, h_last = second(lambda j: hal[j])
        f_zero, f_end = first(lambda j: xs[0, j])
        none = jnp.zeros((64, CH), BF)
        low = [
            (mm(lo_zero, f_zero) + mm(lo_end, f_end)).astype(BF),
            (mm(near[0], h_zero) + mm(near[1], h_end)).astype(BF),
            (mm(near[0], h_one) + mm(near[1], h_last)).astype(BF),
            none, none,
        ]
        high = [
            (mm(hi_zero, f_zero) + mm(hi_end, f_end)).astype(BF),
            (mm(far[0], h_zero) + mm(far[1], h_end)).astype(BF),
            (mm(far[0], h_one) + mm(far[1], h_last)).astype(BF),
            none, none,
        ]
        for block in range(5):
            nb[0, block, zero] = pick(low[block], nb[0, block, zero])
            nb[1, block, zero] = pick(nb[1, block, zero], high[block])
            nb[0, block, end] = pick(nb[0, block, end], low[block])
            nb[1, block, end] = pick(high[block], nb[1, block, end])
        cg[0], cg[1] = first(lambda j: xs[2, j])

    @pl.when(band == 0)
    def _():
        fill_ends(2, 1)

    @pl.when(band == BANDS - 1)
    def _():
        fill_ends(4, 3)

    def choose(options):
        result = None
        for s, option in enumerate(options):
            if option is None:
                continue
            term = option * side_mask[s]
            result = term if result is None else result + term
        return jnp.zeros((64, CH), BF) if result is None else result

    def fill(target, block, source):
        for k, tap in enumerate(TAPS):
            target[block * 64 : block * 64 + 64, k * CH : (k + 1) * CH] = choose(
                [source(*side_frame(s, tap)) for s in range(4)]
            )

    def field_source(j):
        def source(delta, dt):
            return block_at(delta + 1, j) if dt == 0 else nb[(dt + 1) // 2, delta + 1, j]
        return source

    def grad_source(e, j):
        def source(delta, dt):
            depth = e - delta
            if depth not in (0, 1):
                return None
            return xs[2 + depth, j] if dt == 0 else nb[(1 - dt) // 2, 3 + depth, j]
        return source

    def corner_source(which, value):
        def source(delta, dt):
            return value if (delta, dt) == (-1, 2 * which - 1) else None
        return source

    order_pre = (2, 3, 1, 4)
    for block, j in enumerate(order_pre):
        fill(lp, block, field_source(j))
    order_back = [(0, 2), (0, 3), (-1, 2), (-1, 3), None, None, (0, 1), (0, 4), (-1, 1), (-1, 4)]
    for block, at in enumerate(order_back):
        fill(lg, block, corner_source(block - 4, cg[block - 4]) if at is None else grad_source(*at))

    pre = mm(lp[...], w1_ref[...].reshape(9 * CH, CH))
    back = mm(lg[...], w2t[...])

    def back_block(e, j):
        block = order_back.index((e, j))
        return back[block * 64 : block * 64 + 64]

    for j in range(1, 5):
        ss[j] = mm(partner, back_block(-1, j).astype(BF))

    def corner_sums(low, high):
        low = (low * row_line).astype(BF)
        high = (high * row_line).astype(BF)
        return mm_t(lo_zero, low) + mm_t(hi_zero, high), mm_t(lo_end, low) + mm_t(hi_end, high)

    corner_low, corner_high = back[256:320], back[320:384]

    def close_ends(zero, end):
        at_zero, at_end = corner_sums(corner_low, corner_high)
        head = pick_f(ss[zero], ss[end]) + at_zero
        tail = pick_f(ss[end], ss[zero]) + at_end
        head_b, tail_b = head.astype(BF), tail.astype(BF)
        head += mm(near[0], head_b) + mm(near[1], tail_b)
        tail += mm(far[0], head_b) + mm(far[1], tail_b)
        ss[zero] = pick_f(head, tail)
        ss[end] = pick_f(tail, head)

    @pl.when(band == 0)
    def _():
        close_ends(2, 1)

    @pl.when(band == BANDS - 1)
    def _():
        close_ends(4, 3)

    unique = {}
    hid = {}
    for block, j in enumerate(order_pre):
        value = pre[block * 64 : block * 64 + 64]
        hidden, slope = silu_parts(value)
        t = (2 * band - 2 + j) & (SPAN - 1)
        corner = jnp.logical_or(t == 0, t == SPAN - 1)
        unique[j] = jnp.where(corner, row_line, jnp.ones_like(row_line))
        grad = ((back_block(0, j) + ss[j]) * slope).astype(BF)
        gp[j] = grad
        gpu[j] = (grad.astype(F32) * unique[j]).astype(BF)
        hid[j] = hidden.astype(BF)

    mine = (home == group * 16).astype(F32)
    edge = jnp.where(band == 0, 1.0, 0.0) * mine * row_line

    def scaled(value, factor):
        return (value.astype(F32) * factor).astype(BF)

    h_zero, h_end = pick(hid[2], hid[1]), pick(hid[1], hid[2])
    cells = jnp.concatenate([
        scaled(hid[2], mine * unique[2]),
        scaled(hid[3], mine * unique[3]),
        scaled(mm(partner, hid[2]), mine),
        scaled(mm(partner, hid[3]), mine),
        scaled(mm(lo_zero, h_zero) + mm(lo_end, h_end), edge),
        scaled(mm(hi_zero, h_zero) + mm(hi_end, h_end), edge),
    ], axis=0)
    second = mm_t(cells, lg[0:384, :])
    own = jnp.concatenate([scaled(gpu[2], mine), scaled(gpu[3], mine)], axis=0)
    first = mm_t(lp[0:128, :], own)

    at_first, at_last = band == 0, band == BANDS - 1
    inner_low = jnp.where(at_first, 0.0, 1.0)
    inner_high = jnp.where(at_last, 0.0, 1.0)

    def spread_source(e, j, ref):
        def source(delta, dt):
            if e - delta != 0:
                return None
            if dt == 0:
                return ref[j]
            before = scaled(ref[1], inner_low) if j == 2 else ref[2]
            after = ref[3] if j == 2 else scaled(ref[4], inner_high)
            return pick(before, after) if dt == 1 else pick(after, before)
        return source

    g_zero = jnp.where(at_first, gp[2], gp[4])
    g_end = jnp.where(at_first, gp[1], gp[3])
    g_zero, g_end = pick(g_zero, g_end), pick(g_end, g_zero)
    order_in = [(0, 2), (0, 3), (1, 2), (1, 3), (-1, 2), (-1, 3), None, None]
    for block, at in enumerate(order_in):
        if at is None:
            fill(lc, block, corner_source(block - 6, (g_zero, g_end)[block - 6]))
        else:
            fill(lc, block, spread_source(*at, gp if at[0] == -1 else gpu))
    back = mm(lc[...], w1t[...])
    part = [back[k * 64 : k * 64 + 64] for k in range(8)]
    at_zero, at_end = corner_sums(part[6], part[7])
    owe[0] = part[0] + mm(partner, part[4].astype(BF)) + pick_f(at_zero, at_end) * (1.0 - inner_low)
    owe[1] = part[2]
    owe[2] = part[1] + mm(partner, part[5].astype(BF)) + pick_f(at_end, at_zero) * (1.0 - inner_high)
    owe[3] = part[3]

    tile = jnp.concatenate([owe[k, pl.ds(pl.multiple_of(group * 16, 16), 16), :] for k in range(4)], axis=0)
    tails = mm(sel_ref[...], tile.astype(BF))
    total[0:1152, :] = acc[0:1152, :] + first
    for k in range(9):
        low = 1152 + k * CH
        total[low : low + CH, :] = acc[low : low + CH, :] + second[:, k * CH : (k + 1) * CH]
    sent[...] = jnp.zeros_like(sent)
    for q in range(2):
        for face in range(3):
            for row in range(2):
                piece = done[pl.ds(q * 192 + face * 64 + row, BANDS, stride=2), :]
                sent[pl.ds((q * 3 + face) * 2 + row, BANDS, stride=16), :] = piece
    for i in range(BANDS):
        half = i // 16
        tail = tails[half * 40 : half * 40 + 40]
        pixels = jnp.concatenate([sent[i * 16 : i * 16 + 16, :], jnp.zeros((32, CH), F32)], axis=0)
        shifted = jnp.concatenate([jnp.zeros((8, CH), F32), tail], axis=0)
        out_ref[i] = jnp.concatenate([total[CHUNK * i : CHUNK * i + CHUNK, :], pixels + shifted], axis=0).astype(BF)


def tail_selector():
    select = np.zeros((80, 64), np.float32)
    for half in range(2):
        for pos in range(2):
            for depth in range(2):
                for face in range(3):
                    lane = (pos * 2 + depth) * 16 + face
                    select[half * 40 + 4 + (pos * 2 + depth) * 3 + face, lane + half * 3] = 1
                    for side in range(2):
                        row = 16 + ((pos * 2 + side) * 2 + depth) * 3 + face
                        select[half * 40 + row, lane + 6 + 3 * side] = 1
    return select


def order_selector():
    select = np.zeros((2, 64, 64), np.float32)
    for pos in range(2):
        for b in range(BANDS):
            select[0, 2 * b + pos, pos * 32 + b] = 1
            select[1, 63 - 2 * b - pos, pos * 32 + b] = 1
    return select


def reduce_kernel(in_ref, sum_ref):
    total = in_ref[0].astype(F32)
    for i in range(1, BANDS):
        total = total + in_ref[i].astype(F32)
    sum_ref[...] = total[0:CHUNK]


def spread_kernel(factor, own_ref, one_ref, two_ref, three_ref, out_ref, parts):
    _, group = here()
    for step, ref in enumerate((own_ref, one_ref, two_ref, three_ref)):
        parts[(group - step) & 3] = ref[...]
    total = (parts[0] + parts[1]) + (parts[2] + parts[3])
    total = (total * factor).astype(BF)
    for i in range(BANDS):
        out_ref[i] = total


def final_kernel(fn_ref, rot_ref, sel_ref, in_ref, sum_ref, out_ref, first_ref, second_ref, wide, total):
    first_ref[...] = sum_ref[0:16].astype(F32).reshape(1152, CH)
    second_ref[...] = sum_ref[16:32].astype(F32).reshape(1152, CH)
    band, group = here()
    for i in range(BANDS):
        wide[i * TAIL : (i + 1) * TAIL, :] = in_ref[i].astype(F32)[CHUNK:SLOT_TWO]
    for q in range(2):
        for face in range(3):
            for row in range(2):
                piece = wide[pl.ds((q * 3 + face) * 2 + row, BANDS, stride=TAIL), :]
                total[row, face, pl.ds(q, BANDS, stride=2), :] = piece
    tiles = [wide[pl.ds(pl.multiple_of(src * TAIL, TAIL), TAIL), :] for src in (band, BANDS - 1 - band)]
    for side in range(2):
        for face in range(3):
            flip = is_mirrored(fn_ref, rot_ref, 3 * group + face, 2 + side) == 1
            for row in range(2):
                for depth in range(2):
                    column = depth if side == 0 else 63 - depth
                    k, m = [24 + ((pos * 2 + side) * 2 + depth) * 3 + face for pos in (row, 1 - row)]
                    extra = jnp.where(flip, tiles[1][m : m + 1, :], tiles[0][k : k + 1, :])
                    total[row, face, column : column + 1, :] += extra

    @pl.when((band == 0) | (band == BANDS - 1))
    def _():
        side = jnp.where(band == 0, 0, 1)
        for face in range(3):
            order = sel_ref[is_mirrored(fn_ref, rot_ref, 3 * group + face, side)]
            for depth in range(2):
                halves = [wide[pl.ds(12 + (pos * 2 + depth) * 3 + face, BANDS, stride=TAIL), :] for pos in range(2)]
                extra = mm(order, jnp.concatenate(halves, axis=0).astype(BF))
                row = jnp.where(band == 0, depth, 1 - depth)
                total[row, face] += extra

    for row in range(2):
        for face in range(3):
            out_ref[face, row] = total[row, face].astype(BF)


def around(value):
    moved = [lax.ppermute(value, "sub", [(i, (i + step) % 4) for i in range(4)]) for step in (1, 2, 3)]
    return (value, *moved)


def body(field_in, grad_out, first_weight, second_weight, face_neighbour, seam_rotation, corner_fill):
    factor = (1.0 * 12 * SPAN * SPAN) ** -0.5
    seams = (face_neighbour.T, seam_rotation.T)
    in_smem = {0: "s", 1: "s"}

    slots = call(
        pack_lines,
        jax.ShapeDtypeStruct((BANDS, SLOT_ONE, CH), BF),
        [
            pltpu.VMEM((2, 3, 2, SPAN, CH), BF),
            pltpu.VMEM(((SPAN + 4) * 12, CH), F32),
            pltpu.VMEM((STRIP, CH), F32),
            pltpu.SemaphoreType.DMA((2,)),
        ],
        tuple(pltpu.with_memory_space_constraint(value, pltpu.HBM) for value in (field_in, grad_out)),
        {0: "h", 1: "h"},
    )
    strips = lax.all_to_all(slots, "tile", 0, 0, tiled=True)
    lines = call(
        gather_lines,
        jax.ShapeDtypeStruct((WINDOW, 64, CH), BF),
        [],
        (*seams, jnp.asarray(line_selector(), BF), jnp.asarray(ends_selector(), BF), strips),
        in_smem,
    )
    lines = around(lines)
    acc, done = call(
        interior_kernel,
        [jax.ShapeDtypeStruct((2304, CH), F32), jax.ShapeDtypeStruct((384, CH), F32)],
        [
            pltpu.VMEM((1152, CH), BF),
            pltpu.VMEM((1152, CH), BF),
            pltpu.VMEM((1152, CH), F32),
            pltpu.VMEM((1152, CH), F32),
            pltpu.VMEM((BANDS * STRIP, CH), F32),
        ],
        (strips, first_weight, second_weight),
    )

    slots = call(
        main_kernel,
        jax.ShapeDtypeStruct((BANDS, SLOT_TWO, CH), BF),
        [
            pltpu.VMEM((2304, CH), F32),
            pltpu.VMEM((BANDS * 16, CH), F32),
            pltpu.VMEM((1152, CH), BF),
            pltpu.VMEM((1152, CH), BF),
            pltpu.VMEM((4, WINDOW, 64, CH), BF),
            pltpu.VMEM((WINDOW, 64, CH), BF),
            pltpu.VMEM((2, 5, 5, 64, CH), BF),
            pltpu.VMEM((2, 64, CH), BF),
            pltpu.VMEM((256, 1152), BF),
            pltpu.VMEM((640, 1152), BF),
            pltpu.VMEM((512, 1152), BF),
            pltpu.VMEM((5, 64, CH), F32),
            pltpu.VMEM((5, 64, CH), BF),
            pltpu.VMEM((5, 64, CH), BF),
            pltpu.VMEM((4, 64, CH), F32),
        ],
        (*seams, corner_fill.T, jnp.asarray(tail_selector(), BF), *lines, acc, done, first_weight, second_weight),
    )
    slots = lax.all_to_all(slots, "tile", 0, 0, tiled=True)
    part = call(reduce_kernel, jax.ShapeDtypeStruct((CHUNK, CH), F32), [], (slots,))
    part = around(part)
    reduced = call(
        lambda *refs: spread_kernel(factor, *refs),
        jax.ShapeDtypeStruct((BANDS, CHUNK, CH), BF),
        [pltpu.VMEM((4, CHUNK, CH), F32)],
        part,
    )
    reduced = lax.all_to_all(reduced, "tile", 0, 0, tiled=True)
    grad_in, first, second = call(
        final_kernel,
        [
            jax.ShapeDtypeStruct((3, 2, SPAN, CH), BF),
            jax.ShapeDtypeStruct((1152, CH), F32),
            jax.ShapeDtypeStruct((1152, CH), F32),
        ],
        [
            pltpu.VMEM((BANDS * TAIL, CH), F32),
            pltpu.VMEM((2, 3, SPAN, CH), F32),
        ],
        (*seams, jnp.asarray(order_selector(), BF), slots, reduced),
        in_smem,
    )
    return grad_in, first.reshape(3, 3, CH, CH), second.reshape(3, 3, CH, CH)


def solution(mesh):
    return jax.shard_map(
        body,
        mesh=mesh,
        in_specs=(P("sub", "tile", None, None), P("sub", "tile", None, None), P(), P(), P(), P(), P()),
        out_specs=(P("sub", "tile", None, None), P(), P()),
        check_vma=False,
    )
```

```python
import jax
import jax.numpy as jnp
import numpy as np
from jax import lax
from jax.experimental import pallas as pl
from jax.experimental.pallas import tpu as pltpu
from jax.sharding import PartitionSpec as P

BF = jnp.bfloat16
F32 = jnp.float32
I32 = jnp.int32
BANDS = 32
SPAN = 64
CH = 128
TAPS = [(a, b) for a in range(3) for b in range(3)]
WINDOW = 6
ENDS = 48
STRIP = 12 * WINDOW
SLOT_ONE = 2 * STRIP
HALF = 9 * CH
CHUNK = 40
TAIL = 48
SLOT_TWO = CHUNK + TAIL
VMEM_BYTES = 48 * 1024 * 1024


def mm(left, right):
    return jnp.dot(left, right, preferred_element_type=F32)


def mm_t(left, right):
    return lax.dot_general(left, right, (((0,), (0,)), ((), ())), preferred_element_type=F32)


def call(kernel, outs, scratch, operands, places=(), aliases=None):
    kinds = {"v": pltpu.VMEM, "s": pltpu.SMEM, "h": pltpu.HBM, "a": pl.ANY}
    places = dict(places)
    many = isinstance(outs, (list, tuple))
    out_specs = [pl.BlockSpec(memory_space=kinds[places.get(f"o{k}", "v")]) for k in range(len(outs) if many else 1)]
    return pl.pallas_call(
        kernel,
        out_shape=outs,
        in_specs=[pl.BlockSpec(memory_space=kinds[places.get(k, "v")]) for k in range(len(operands))],
        out_specs=out_specs if many else out_specs[0],
        scratch_shapes=scratch,
        input_output_aliases=aliases or {},
        compiler_params=pltpu.CompilerParams(vmem_limit_bytes=VMEM_BYTES),
    )(*operands)


def here():
    return lax.axis_index("tile"), lax.axis_index("sub")


def is_mirrored(fn_ref, rot_ref, face, side):
    rot = rot_ref[face, side]
    partner = 4 * fn_ref[face, side] + (rot & 3)
    return jnp.where(4 * face + side > partner, rot >> 2, 0)


def is_mirrored(fn_ref, rot_ref, face, side):
    rot = rot_ref[side, face]
    partner = 4 * fn_ref[side, face] + (rot & 3)
    return jnp.where(4 * face + side > partner, rot >> 2, 0)


def pack_lines(f_hbm, g_hbm, out_ref, buf, wide, ends, sems):
    copies = [pltpu.make_async_copy(src, buf.at[k], sems.at[k]) for k, src in enumerate((f_hbm, g_hbm))]
    for copy in copies:
        copy.start()
    band, _ = here()
    ends[ENDS:STRIP, :] = jnp.zeros((STRIP - ENDS, CH), F32)
    for fld in range(2):
        copies[fld].wait()
        for row in range(2):
            for face in range(3):
                block = buf[fld, face, row].astype(F32)
                wide[pl.ds(24 + fld * 6 + row * 3 + face, SPAN, stride=12), :] = block
                for edge, cols in enumerate(((0, 1), (63, 62))):
                    for depth, col in enumerate(cols):
                        place = row * 24 + fld * 12 + edge * 6 + depth * 3 + face
                        ends[place : place + 1, :] = block[col : col + 1, :]
    wide[0:24, :] = wide[SPAN * 12 : SPAN * 12 + 24, :]
    wide[SPAN * 12 + 24 : SPAN * 12 + 48, :] = wide[24:48, :]
    outer = (band == 0) | (band == BANDS - 1)
    strips = [wide[24 * d : 24 * d + STRIP, :] for d in range(BANDS)]
    for d in range(BANDS):
        rest = jnp.where(outer, strips[BANDS - 1 - d], ends[...])
        out_ref[d] = jnp.concatenate([strips[d], rest], axis=0).astype(BF)


def line_selector():
    select = np.zeros((2, WINDOW * 64, 4 * STRIP + 6 * ENDS), np.float32)
    for mirrored in range(2):
        for j in range(WINDOW):
            part, parity = j // 2, j % 2
            for fld in range(2):
                for depth in range(2):
                    for face in range(3):
                        base = j * 64 + (fld * 2 + depth) * 16 + face
                        column = STRIP * mirrored + (5 - j if mirrored else j) * 12 + fld * 6 + face
                        select[mirrored, base, column + depth * 3] = 1
                        select[mirrored, base + 3, 2 * STRIP + column + (1 - depth) * 3] = 1
                        for side in range(2):
                            source = 4 * STRIP + (3 * mirrored + part) * ENDS + (1 - parity if mirrored else parity) * 24
                            select[mirrored, base + 6 + 3 * side, source + fld * 12 + side * 6 + depth * 3 + face] = 1
    return select


def ends_selector():
    select = np.zeros((4, ENDS, SLOT_ONE), np.float32)
    for k, d in enumerate((0, 1, 30, 31)):
        for row in range(2):
            for fld in range(2):
                for side in range(2):
                    for depth in range(2):
                        col = 63 - depth if side else depth
                        at = (col - 2 * d + 2) % SPAN
                        other = (col - 60 + 2 * d) % SPAN
                        base = at * 12 if at < WINDOW else STRIP + other * 12
                        for face in range(3):
                            place = row * 24 + fld * 12 + side * 6 + depth * 3 + face
                            select[k, place, base + fld * 6 + row * 3 + face] = 1
    return select


def gather_lines(fn_ref, rot_ref, sel_ref, ends_ref, in_ref, out_ref):
    band, group = here()
    first, last = in_ref[0], in_ref[BANDS - 1]
    pick_ends = ends_ref[(band & 1) + 2 * (band >> 4)]
    first_ends, last_ends = mm(pick_ends, first), mm(pick_ends, last)
    ends = []
    for source in [band + 31 + part for part in range(3)] + [64 - band - part for part in range(3)]:
        source = source & 31
        block = in_ref[source].astype(F32)[STRIP : STRIP + ENDS]
        ends.append(jnp.where(source == 0, first_ends, jnp.where(source == BANDS - 1, last_ends, block)))
    pieces = jnp.concatenate([first.astype(F32), last.astype(F32)] + ends, axis=0).astype(BF)
    place = lax.broadcasted_iota(I32, (WINDOW * 64, 1), 0) & 15
    flip = jnp.zeros((WINDOW * 64, 1), I32)
    for side in range(4):
        for face in range(3):
            flip = jnp.where(place == side * 3 + face, is_mirrored(fn_ref, rot_ref, 3 * group + face, side), flip)
    flip = jnp.broadcast_to(flip.astype(F32), sel_ref.shape[1:]).astype(BF)
    picked = mm(sel_ref[0] * (1 - flip) + sel_ref[1] * flip, pieces).astype(BF)
    for j in range(WINDOW):
        out_ref[j] = picked[j * 64 : j * 64 + 64]


def silu_parts(pre):
    logistic = 1.0 / (1.0 + jnp.exp(-pre))
    return pre * logistic, logistic * (1.0 + pre * (1.0 - logistic))


def side_frame(side, tap):
    dr, dc = tap[0] - 1, tap[1] - 1
    return ((dr, dc), (-dr, dc), (dc, dr), (-dc, dr))[side]


def transpose_weights(ref, out):
    for k, (a, b) in enumerate(TAPS):
        out[k * CH : (k + 1) * CH, :] = ref[a, b].T


def interior_kernel(
    in_ref, w1_ref, w2_ref, own_ref, away_ref, sent, acc, done, w1t, w2t, f2, g2, wide
):
    band, group = here()
    transpose_weights(w1_ref, w1t)
    transpose_weights(w2_ref, w2t)
    for s in range(BANDS):
        wide[s * STRIP : (s + 1) * STRIP, :] = in_ref[s].astype(F32)[0:STRIP]
    for q in range(WINDOW):
        for fld, target in enumerate((f2, g2)):
            for row in range(2):
                for face in range(3):
                    piece = wide[pl.ds(q * 12 + fld * 6 + row * 3 + face, BANDS, stride=STRIP), :]
                    target[pl.ds(q * 192 + face * 64 + row, BANDS, stride=2), :] = piece

    def conv_weights(ref):
        return jnp.concatenate([ref[a].reshape(3 * CH, CH) for a in range(3)], axis=1)

    def back_weights(ref):
        columns = []
        for a in range(3):
            columns.append(jnp.concatenate([ref[(a * 3 + b) * CH : (a * 3 + b + 1) * CH, :] for b in (2, 1, 0)], axis=0))
        return jnp.concatenate(columns, axis=1)

    def up_one(value):
        return pltpu.roll(value, value.shape[0] - 1, 0)

    def down_one(value):
        return pltpu.roll(value, 1, 0)

    def three_columns(ref, first, count):
        return jnp.concatenate([ref[first + 192 * b : first + 192 * b + count, :].astype(BF) for b in range(3)], axis=1)

    y = mm(three_columns(f2, 0, 768), conv_weights(w1_ref))
    pre = down_one(y[:, :CH]) + y[:, CH : 2 * CH] + up_one(y[:, 2 * CH :])
    z = mm(three_columns(g2, 0, 768), back_weights(w2t))
    back = up_one(z[:, :CH]) + z[:, CH : 2 * CH] + down_one(z[:, 2 * CH :])
    hidden, slope = silu_parts(pre)
    index = lax.broadcasted_iota(I32, (768, CH), 0)
    step = (index >= 192).astype(I32) + (index >= 384).astype(I32) + (index >= 576).astype(I32)
    col = 2 * band - 1 + step
    row = index & 63
    inner = (row >= 1) & (row <= 62) & (col >= 1) & (col <= 62)
    gpre = jnp.where(inner, back * slope, 0.0).astype(BF)
    hid = jnp.where(inner, hidden, 0.0)[192:576].astype(BF)

    gown = gpre[192:576].astype(F32)
    gcat = jnp.concatenate([up_one(gown).astype(BF), gpre[192:576], down_one(gown).astype(BF)], axis=1)
    first = mm_t(three_columns(f2, 192, 384), gcat)
    hown = hid.astype(F32)
    hcat = jnp.concatenate([down_one(hown).astype(BF), hid, up_one(hown).astype(BF)], axis=1)
    gback = jnp.concatenate([g2[start : start + 384, :].astype(BF) for start in (576, 384, 192)], axis=1)
    second = mm_t(hcat, gback)
    for k, (a, b) in enumerate(TAPS):
        top, low = k * CH, 1152 + k * CH
        acc[top : top + CH, :] = first[b * CH : (b + 1) * CH, a * CH : (a + 1) * CH]
        acc[low : low + CH, :] = second[a * CH : (a + 1) * CH, b * CH : (b + 1) * CH]
    core = group & 1
    own_ref[...] = acc[pl.ds(pl.multiple_of(core * HALF, CH), HALF), :]
    away_ref[...] = acc[pl.ds(pl.multiple_of((1 - core) * HALF, CH), HALF), :].astype(BF)

    gthree = jnp.concatenate([gpre[0:384], gpre[192:576], gpre[384:768]], axis=1)
    z = mm(gthree, back_weights(w1t))
    done[...] = up_one(z[:, :CH]) + z[:, CH : 2 * CH] + down_one(z[:, 2 * CH :]) + g2[384:768, :]
    sent[...] = jnp.zeros_like(sent)
    for q in range(2):
        for face in range(3):
            for row in range(2):
                piece = done[pl.ds(q * 192 + face * 64 + row, BANDS, stride=2), :]
                sent[pl.ds((q * 3 + face) * 2 + row, BANDS, stride=16), :] = piece


def main_kernel(
    fn_ref, rot_ref, fill_ref, sel_ref, own_ref, one_ref, two_ref, three_ref, w1_ref, w2_ref,
    share_ref, tail_ref,
    w1t, w2t, xs, hal, nb, cg, lp, lg, lc, ss, gp, gpu, owe,
):
    band, group = here()
    transpose_weights(w1_ref, w1t)
    transpose_weights(w2_ref, w2t)

    line = lax.broadcasted_iota(I32, (64, 1), 0)
    place = line & 15
    side = (place >= 3).astype(I32) + (place >= 6).astype(I32) + (place >= 9).astype(I32)
    face = place - 3 * side
    home = line - place
    real = place < 12
    lane = lax.broadcasted_iota(I32, (64, 64), 1)

    def one_hot(target, keep):
        return (jnp.where(keep & real, target, -1) == lane).astype(F32).astype(BF)

    face_lane = lax.broadcasted_iota(I32, (64, 12), 1)
    faces = (jnp.where(real, 3 * (line >> 4) + face, -1) == face_lane).astype(F32).astype(BF)

    def by_line(ref, columns):
        table = ref[...].astype(F32).astype(BF)
        rows = lax.dot_general(faces, table, (((1,), (1,)), ((), ())), preferred_element_type=F32).astype(I32)
        value = rows[:, columns[0] : columns[0] + 1]
        for s in range(1, 4):
            value = jnp.where(side == s, rows[:, columns[s] : columns[s] + 1], value)
        return value

    fn = by_line(fn_ref, (0, 1, 2, 3))
    rot = by_line(rot_ref, (0, 1, 2, 3))
    fn_group = (fn * 43) >> 7
    partner = one_hot(fn_group * 16 + (rot & 3) * 3 + (fn - 3 * fn_group), real)
    number = 4 * (3 * (line >> 4) + face) + side
    flip = ((rot >> 2) == 1) & (number > 4 * fn + (rot & 3)) & real
    fills = []
    for columns in ((0, 2, 0, 1), (1, 3, 2, 3)):
        m = by_line(fill_ref, columns)
        mf = m >> 2
        mg = (mf * 43) >> 7
        target = mg * 16 + ((m >> 1) & 1) * 3 + (mf - 3 * mg)
        fills.append((one_hot(target, (m & 1) == 0), one_hot(target, (m & 1) == 1)))
    corner_cells = jnp.concatenate([jnp.concatenate(pair, axis=1) for pair in fills], axis=0)
    corner_back = corner_cells.astype(F32).T.astype(BF)
    even = (side & 1) == 0
    low_side = jnp.where(side < 2, 2, 0)
    high_side = jnp.where(side < 2, 3, 1)
    beside = jnp.concatenate([
        jnp.concatenate([one_hot(home + other * 3 + face, even), one_hot(home + other * 3 + face, ~even)], axis=1)
        for other in (low_side, high_side)
    ], axis=0)
    side_mask = [jnp.broadcast_to((side == s).astype(F32), (64, CH)).astype(BF) for s in range(4)]
    row_line = (side < 2).astype(F32)
    flip_f = jnp.broadcast_to(flip.astype(F32), (64, CH))
    flip_b, keep_b = flip_f.astype(BF), (1.0 - flip_f).astype(BF)

    def pick(plain, mirrored):
        return plain * keep_b + mirrored * flip_b

    def pick_f(plain, mirrored):
        return jnp.where(flip_f > 0.5, mirrored, plain)

    for step, ref in enumerate((own_ref, one_ref, two_ref, three_ref)):
        start = pl.multiple_of((group ^ step) * 16, 16)
        for j in range(WINDOW):
            for block in range(4):
                xs[block, j, pl.ds(start, 16), :] = ref[j, block * 16 : block * 16 + 16, :]
    halos = mm(partner, jnp.concatenate([xs[0, j] for j in range(WINDOW)], axis=1)).astype(BF)
    for j in range(WINDOW):
        hal[j] = halos[:, j * CH : (j + 1) * CH]

    def block_at(block, j):
        return hal[j] if block == 0 else xs[block - 1, j]

    for block in range(5):
        for j in range(1, 5):
            before, after = block_at(block, j - 1), block_at(block, j + 1)
            nb[0, block, j] = pick(before, after)
            nb[1, block, j] = pick(after, before)
    cg[...] = jnp.zeros_like(cg)

    def line_ends(zero, end, shift):
        lower, upper = zero + shift, end - shift
        return lambda value: (pick(value(lower), value(upper)), pick(value(upper), value(lower)))

    def fill_ends(zero, end):
        first = line_ends(zero, end, 0)
        second = line_ends(zero, end, 1)
        h_zero, h_end = first(lambda j: hal[j])
        h_one, h_last = second(lambda j: hal[j])
        f_zero, f_end = first(lambda j: xs[0, j])
        none = jnp.zeros((64, CH), BF)
        cells = mm(corner_cells, jnp.concatenate([f_zero, f_end], axis=0)).astype(BF)
        sides = jnp.concatenate([
            jnp.concatenate([h_zero, h_one], axis=1), jnp.concatenate([h_end, h_last], axis=1)
        ], axis=0)
        sides = mm(beside, sides).astype(BF)
        low = [cells[:64], sides[:64, :CH], sides[:64, CH:], none, none]
        high = [cells[64:], sides[64:, :CH], sides[64:, CH:], none, none]
        for block in range(5):
            nb[0, block, zero] = pick(low[block], nb[0, block, zero])
            nb[1, block, zero] = pick(nb[1, block, zero], high[block])
            nb[0, block, end] = pick(nb[0, block, end], low[block])
            nb[1, block, end] = pick(high[block], nb[1, block, end])
        cg[0], cg[1] = first(lambda j: xs[2, j])

    @pl.when(band == 0)
    def _():
        fill_ends(2, 1)

    @pl.when(band == BANDS - 1)
    def _():
        fill_ends(4, 3)

    def choose(options):
        result = None
        for s, option in enumerate(options):
            if option is None:
                continue
            term = option * side_mask[s]
            result = term if result is None else result + term
        return jnp.zeros((64, CH), BF) if result is None else result

    def fill(target, block, source):
        for k, tap in enumerate(TAPS):
            target[block * 64 : block * 64 + 64, k * CH : (k + 1) * CH] = choose(
                [source(*side_frame(s, tap)) for s in range(4)]
            )

    def field_source(j):
        def source(delta, dt):
            return block_at(delta + 1, j) if dt == 0 else nb[(dt + 1) // 2, delta + 1, j]
        return source

    def grad_source(e, j):
        def source(delta, dt):
            depth = e - delta
            if depth not in (0, 1):
                return None
            return xs[2 + depth, j] if dt == 0 else nb[(1 - dt) // 2, 3 + depth, j]
        return source

    def corner_source(which, value):
        def source(delta, dt):
            return value if (delta, dt) == (-1, 2 * which - 1) else None
        return source

    order_pre = (2, 3, 1, 4)
    for block, j in enumerate(order_pre):
        fill(lp, block, field_source(j))
    order_back = [(0, 2), (0, 3), (-1, 2), (-1, 3), None, None, (0, 1), (0, 4), (-1, 1), (-1, 4)]
    for block, at in enumerate(order_back):
        fill(lg, block, corner_source(block - 4, cg[block - 4]) if at is None else grad_source(*at))

    pre = mm(lp[...], w1_ref[...].reshape(9 * CH, CH))
    back = mm(lg[...], w2t[...])

    def back_block(e, j):
        block = order_back.index((e, j))
        return back[block * 64 : block * 64 + 64]

    seams = jnp.concatenate([back_block(-1, j).astype(BF) for j in range(1, 5)], axis=1)
    seams = mm(partner, seams)
    for j in range(1, 5):
        ss[j] = seams[:, (j - 1) * CH : j * CH]
    both_rows = jnp.concatenate([row_line, row_line], axis=0)

    def corner_sums(both):
        sums = mm(corner_back, (both * both_rows).astype(BF))
        return sums[:64], sums[64:]


    def close_ends(zero, end):
        at_zero, at_end = corner_sums(back[256:384])
        head = pick_f(ss[zero], ss[end]) + at_zero
        tail = pick_f(ss[end], ss[zero]) + at_end
        sides = mm(beside, jnp.concatenate([head, tail], axis=0).astype(BF))
        head += sides[:64]
        tail += sides[64:]
        ss[zero] = pick_f(head, tail)
        ss[end] = pick_f(tail, head)

    @pl.when(band == 0)
    def _():
        close_ends(2, 1)

    @pl.when(band == BANDS - 1)
    def _():
        close_ends(4, 3)

    unique = {}
    hid = {}
    for block, j in enumerate(order_pre):
        value = pre[block * 64 : block * 64 + 64]
        hidden, slope = silu_parts(value)
        t = (2 * band - 2 + j) & (SPAN - 1)
        corner = jnp.logical_or(t == 0, t == SPAN - 1)
        unique[j] = jnp.where(corner, row_line, jnp.ones_like(row_line))
        grad = ((back_block(0, j) + ss[j]) * slope).astype(BF)
        gp[j] = grad
        gpu[j] = (grad.astype(F32) * unique[j]).astype(BF)
        hid[j] = hidden.astype(BF)

    mine = ((line >> 5) == (group >> 1)).astype(F32)
    edge = jnp.where(band == 0, 1.0, 0.0) * mine * row_line

    def scaled(value, factor):
        return (value.astype(F32) * factor).astype(BF)

    h_zero, h_end = pick(hid[2], hid[1]), pick(hid[1], hid[2])
    halos = mm(partner, jnp.concatenate([hid[2], hid[3]], axis=1))
    ends = mm(corner_cells, jnp.concatenate([h_zero, h_end], axis=0))
    cells = jnp.concatenate([
        scaled(hid[2], mine * unique[2]),
        scaled(hid[3], mine * unique[3]),
        scaled(halos[:, :CH], mine),
        scaled(halos[:, CH:], mine),
        scaled(ends[:64], edge),
        scaled(ends[64:], edge),
    ], axis=0)
    @pl.when((group & 1) == 0)
    def _():
        own = jnp.concatenate([scaled(gpu[2], mine), scaled(gpu[3], mine)], axis=0)
        share_ref[...] = mm_t(lp[0:128, :], own)

    @pl.when((group & 1) == 1)
    def _():
        second = mm_t(cells, lg[0:384, :])
        for k in range(9):
            share_ref[k * CH : (k + 1) * CH, :] = second[:, k * CH : (k + 1) * CH]

    at_first, at_last = band == 0, band == BANDS - 1
    inner_low = jnp.where(at_first, 0.0, 1.0)
    inner_high = jnp.where(at_last, 0.0, 1.0)

    def spread_source(e, j, ref):
        def source(delta, dt):
            if e - delta != 0:
                return None
            if dt == 0:
                return ref[j]
            before = scaled(ref[1], inner_low) if j == 2 else ref[2]
            after = ref[3] if j == 2 else scaled(ref[4], inner_high)
            return pick(before, after) if dt == 1 else pick(after, before)
        return source

    g_zero = jnp.where(at_first, gp[2], gp[4])
    g_end = jnp.where(at_first, gp[1], gp[3])
    g_zero, g_end = pick(g_zero, g_end), pick(g_end, g_zero)
    order_in = [(0, 2), (0, 3), (1, 2), (1, 3), (-1, 2), (-1, 3), None, None]
    for block, at in enumerate(order_in):
        if at is None:
            fill(lc, block, corner_source(block - 6, (g_zero, g_end)[block - 6]))
        else:
            fill(lc, block, spread_source(*at, gp if at[0] == -1 else gpu))
    back = mm(lc[...], w1t[...])
    part = [back[k * 64 : k * 64 + 64] for k in range(8)]
    at_zero, at_end = corner_sums(back[384:512])
    seams = mm(partner, jnp.concatenate([part[4], part[5]], axis=1).astype(BF))
    owe[0] = part[0] + seams[:, :CH] + pick_f(at_zero, at_end) * (1.0 - inner_low)
    owe[1] = part[2]
    owe[2] = part[1] + seams[:, CH:] + pick_f(at_end, at_zero) * (1.0 - inner_high)
    owe[3] = part[3]

    tile = jnp.concatenate([owe[k, pl.ds(pl.multiple_of(group * 16, 16), 16), :] for k in range(4)], axis=0)
    tail_ref[...] = mm(sel_ref[...], tile.astype(BF))


def after_kernel(*refs):
    pass


def share_kernel(own_ref, other_ref, line_ref, tail_ref, sent, out_ref, total):
    total[0:HALF, :] = own_ref[...] + other_ref[...].astype(F32) + line_ref[...]
    total[HALF : BANDS * CHUNK, :] = jnp.zeros((BANDS * CHUNK - HALF, CH), F32)
    for i in range(BANDS):
        half = i // 16
        tail = tail_ref[half * 40 : half * 40 + 40, :]
        pixels = jnp.concatenate([sent[i * 16 : i * 16 + 16, :], jnp.zeros((32, CH), F32)], axis=0)
        shifted = jnp.concatenate([jnp.zeros((8, CH), F32), tail], axis=0)
        out_ref[i] = jnp.concatenate([total[CHUNK * i : CHUNK * i + CHUNK, :], pixels + shifted], axis=0).astype(BF)


def tail_selector():
    select = np.zeros((80, 64), np.float32)
    for half in range(2):
        for pos in range(2):
            for depth in range(2):
                for face in range(3):
                    lane = (pos * 2 + depth) * 16 + face
                    select[half * 40 + 4 + (pos * 2 + depth) * 3 + face, lane + half * 3] = 1
                    for side in range(2):
                        row = 16 + ((pos * 2 + side) * 2 + depth) * 3 + face
                        select[half * 40 + row, lane + 6 + 3 * side] = 1
    return select


def order_selector():
    select = np.zeros((2, 64, 64), np.float32)
    for pos in range(2):
        for b in range(BANDS):
            select[0, 2 * b + pos, pos * 32 + b] = 1
            select[1, 63 - 2 * b - pos, pos * 32 + b] = 1
    return select


def reduce_kernel(in_ref, out_ref):
    total = in_ref[0, 0:48, :].astype(F32)
    for i in range(1, BANDS):
        total = total + in_ref[i, 0:48, :].astype(F32)
    out_ref[...] = total[0:CHUNK]


def spread_kernel(factor, own_ref, other_ref, out_ref):
    total = ((own_ref[...] + other_ref[...]) * factor).astype(BF)
    for i in range(BANDS):
        out_ref[i] = total


def unpack_kernel(own_ref, other_ref, first_ref, second_ref):
    _, group = here()
    core = group & 1
    for i in range(29):
        own, other = own_ref[i].astype(F32), other_ref[i].astype(F32)
        rows = min(CHUNK, HALF - CHUNK * i)
        first_ref[CHUNK * i : CHUNK * i + rows, :] = jnp.where(core == 0, own, other)[0:rows]
        second_ref[CHUNK * i : CHUNK * i + rows, :] = jnp.where(core == 0, other, own)[0:rows]


def grad_kernel(fn_ref, rot_ref, sel_ref, in_ref, out_ref, wide, total):
    band, group = here()
    for i in range(BANDS):
        wide[i * TAIL : (i + 1) * TAIL, :] = in_ref[i].astype(F32)[CHUNK:SLOT_TWO]
    for q in range(2):
        for face in range(3):
            for row in range(2):
                piece = wide[pl.ds((q * 3 + face) * 2 + row, BANDS, stride=TAIL), :]
                total[row, face, pl.ds(q, BANDS, stride=2), :] = piece
    tiles = [wide[pl.ds(pl.multiple_of(src * TAIL, TAIL), TAIL), :] for src in (band, BANDS - 1 - band)]
    for side in range(2):
        for face in range(3):
            flip = is_mirrored(fn_ref, rot_ref, 3 * group + face, 2 + side) == 1
            for row in range(2):
                for depth in range(2):
                    column = depth if side == 0 else 63 - depth
                    k, m = [24 + ((pos * 2 + side) * 2 + depth) * 3 + face for pos in (row, 1 - row)]
                    extra = jnp.where(flip, tiles[1][m : m + 1, :], tiles[0][k : k + 1, :])
                    total[row, face, column : column + 1, :] += extra

    @pl.when((band == 0) | (band == BANDS - 1))
    def _():
        side = jnp.where(band == 0, 0, 1)
        for face in range(3):
            order = sel_ref[is_mirrored(fn_ref, rot_ref, 3 * group + face, side)]
            for depth in range(2):
                halves = [wide[pl.ds(12 + (pos * 2 + depth) * 3 + face, BANDS, stride=TAIL), :] for pos in range(2)]
                extra = mm(order, jnp.concatenate(halves, axis=0).astype(BF))
                row = jnp.where(band == 0, depth, 1 - depth)
                total[row, face] += extra

    for row in range(2):
        for face in range(3):
            out_ref[face, row] = total[row, face].astype(BF)


def swapped(value, step):
    return lax.ppermute(value, "sub", [(i, i ^ step) for i in range(4)])


def body(field_in, grad_out, first_weight, second_weight, face_neighbour, seam_rotation, corner_fill):
    factor = (1.0 * 12 * SPAN * SPAN) ** -0.5
    seams = (face_neighbour.T, seam_rotation.T)
    in_smem = {0: "s", 1: "s"}

    slots = call(
        pack_lines,
        jax.ShapeDtypeStruct((BANDS, SLOT_ONE, CH), BF),
        [
            pltpu.VMEM((2, 3, 2, SPAN, CH), BF),
            pltpu.VMEM(((SPAN + 4) * 12, CH), F32),
            pltpu.VMEM((STRIP, CH), F32),
            pltpu.SemaphoreType.DMA((2,)),
        ],
        tuple(pltpu.with_memory_space_constraint(value, pltpu.HBM) for value in (field_in, grad_out)),
        {0: "h", 1: "h"},
    )
    strips = lax.all_to_all(slots, "tile", 0, 0, tiled=True)
    lines = call(
        gather_lines,
        jax.ShapeDtypeStruct((WINDOW, 64, CH), BF),
        [],
        (*seams, jnp.asarray(line_selector(), BF), jnp.asarray(ends_selector(), BF), strips),
        in_smem,
    )
    lines = (lines, *[swapped(lines, step) for step in (1, 2, 3)])
    share = jax.ShapeDtypeStruct((HALF, CH), F32)
    own, away, sent = call(
        interior_kernel,
        [share, jax.ShapeDtypeStruct((HALF, CH), BF), jax.ShapeDtypeStruct((BANDS * 16, CH), F32)],
        [
            pltpu.VMEM((2304, CH), F32),
            pltpu.VMEM((384, CH), F32),
            pltpu.VMEM((1152, CH), BF),
            pltpu.VMEM((1152, CH), BF),
            pltpu.VMEM((1152, CH), F32),
            pltpu.VMEM((1152, CH), F32),
            pltpu.VMEM((BANDS * STRIP, CH), F32),
        ],
        (strips, first_weight, second_weight),
    )
    away = call(after_kernel, jax.ShapeDtypeStruct((HALF, CH), BF), [], (away, *lines[1:]), dict.fromkeys((0, 1, 2, 3, "o0"), "a"), {0: 0})
    other = swapped(away, 1)

    line, tails = call(
        main_kernel,
        [share, jax.ShapeDtypeStruct((80, CH), F32)],
        [
            pltpu.VMEM((1152, CH), BF),
            pltpu.VMEM((1152, CH), BF),
            pltpu.VMEM((4, WINDOW, 64, CH), BF),
            pltpu.VMEM((WINDOW, 64, CH), BF),
            pltpu.VMEM((2, 5, 5, 64, CH), BF),
            pltpu.VMEM((2, 64, CH), BF),
            pltpu.VMEM((256, 1152), BF),
            pltpu.VMEM((640, 1152), BF),
            pltpu.VMEM((512, 1152), BF),
            pltpu.VMEM((5, 64, CH), F32),
            pltpu.VMEM((5, 64, CH), BF),
            pltpu.VMEM((5, 64, CH), BF),
            pltpu.VMEM((4, 64, CH), F32),
        ],
        (*seams, corner_fill.T, jnp.asarray(tail_selector(), BF), *lines, first_weight, second_weight),
    )
    slots = call(
        share_kernel,
        jax.ShapeDtypeStruct((BANDS, SLOT_TWO, CH), BF),
        [pltpu.VMEM((BANDS * CHUNK, CH), F32)],
        (own, other, line, tails, sent),
    )
    slots = lax.all_to_all(slots, "tile", 0, 0, tiled=True)
    part = call(reduce_kernel, jax.ShapeDtypeStruct((CHUNK, CH), F32), [], (slots,))
    reduced = call(
        lambda *refs: spread_kernel(factor, *refs),
        jax.ShapeDtypeStruct((BANDS, CHUNK, CH), BF),
        [],
        (part, swapped(part, 2)),
    )
    reduced = lax.all_to_all(reduced, "tile", 0, 0, tiled=True)
    swap = swapped(reduced, 1)
    grad_in = call(
        grad_kernel,
        jax.ShapeDtypeStruct((3, 2, SPAN, CH), BF),
        [pltpu.VMEM((BANDS * TAIL, CH), F32), pltpu.VMEM((2, 3, SPAN, CH), F32)],
        (*seams, jnp.asarray(order_selector(), BF), slots),
        in_smem,
    )
    first, second = call(
        unpack_kernel,
        [jax.ShapeDtypeStruct((1152, CH), F32), jax.ShapeDtypeStruct((1152, CH), F32)],
        [],
        (reduced, swap),
    )
    return grad_in, first.reshape(3, 3, CH, CH), second.reshape(3, 3, CH, CH)


def solution(mesh):
    return jax.shard_map(
        body,
        mesh=mesh,
        in_specs=(P("sub", "tile", None, None), P("sub", "tile", None, None), P(), P(), P(), P(), P()),
        out_specs=(P("sub", "tile", None, None), P(), P()),
        check_vma=False,
    )
```

```python
import jax
import jax.numpy as jnp
import numpy as np
from jax import lax
from jax.experimental import pallas as pl
from jax.experimental.pallas import tpu as pltpu
from jax.sharding import PartitionSpec as P

BF = jnp.bfloat16
F32 = jnp.float32
I32 = jnp.int32
BANDS = 32
SPAN = 64
CH = 128
TAPS = [(a, b) for a in range(3) for b in range(3)]
WINDOW = 6
ENDS = 48
STRIP = 12 * WINDOW
SLOT_ONE = 2 * STRIP
HALF = 9 * CH
CHUNK = 36
TAIL = 36
SLOT_TWO = CHUNK + TAIL
SLOT_THREE = 40
VMEM_BYTES = 48 * 1024 * 1024


def mm(left, right):
    return jnp.dot(left, right, preferred_element_type=F32)


def mm_t(left, right):
    return lax.dot_general(left, right, (((0,), (0,)), ((), ())), preferred_element_type=F32)


def call(kernel, outs, scratch, operands, places=(), aliases=None):
    kinds = {"v": pltpu.VMEM, "s": pltpu.SMEM, "h": pltpu.HBM, "a": pl.ANY}
    places = dict(places)
    many = isinstance(outs, (list, tuple))
    out_specs = [pl.BlockSpec(memory_space=kinds[places.get(f"o{k}", "v")]) for k in range(len(outs) if many else 1)]
    return pl.pallas_call(
        kernel,
        out_shape=outs,
        in_specs=[pl.BlockSpec(memory_space=kinds[places.get(k, "v")]) for k in range(len(operands))],
        out_specs=out_specs if many else out_specs[0],
        scratch_shapes=scratch,
        input_output_aliases=aliases or {},
        compiler_params=pltpu.CompilerParams(vmem_limit_bytes=VMEM_BYTES),
    )(*operands)


def here():
    return lax.axis_index("tile"), lax.axis_index("sub")


def is_mirrored(fn_ref, rot_ref, face, side):
    rot = rot_ref[face, side]
    partner = 4 * fn_ref[face, side] + (rot & 3)
    return jnp.where(4 * face + side > partner, rot >> 2, 0)


def is_mirrored(fn_ref, rot_ref, face, side):
    rot = rot_ref[side, face]
    partner = 4 * fn_ref[side, face] + (rot & 3)
    return jnp.where(4 * face + side > partner, rot >> 2, 0)


def mirrored_in(fn_ref, rot_ref, face, side):
    lane = lax.broadcasted_iota(I32, (1, 12), 1) == face
    rot = jnp.sum(jnp.where(lane, rot_ref[side : side + 1, :], 0))
    partner = 4 * jnp.sum(jnp.where(lane, fn_ref[side : side + 1, :], 0)) + (rot & 3)
    return jnp.where(4 * face + side > partner, rot >> 2, 0)


def pack_lines(f_hbm, g_hbm, out_ref, buf, wide, ends, sems):
    copies = [pltpu.make_async_copy(src, buf.at[k], sems.at[k]) for k, src in enumerate((f_hbm, g_hbm))]
    for copy in copies:
        copy.start()
    band, _ = here()
    ends[ENDS:STRIP, :] = jnp.zeros((STRIP - ENDS, CH), F32)
    for fld in range(2):
        copies[fld].wait()
        for row in range(2):
            for face in range(3):
                block = buf[fld, face, row].astype(F32)
                wide[pl.ds(24 + fld * 6 + row * 3 + face, SPAN, stride=12), :] = block
                for edge, cols in enumerate(((0, 1), (63, 62))):
                    for depth, col in enumerate(cols):
                        place = row * 24 + fld * 12 + edge * 6 + depth * 3 + face
                        ends[place : place + 1, :] = block[col : col + 1, :]
    wide[0:24, :] = wide[SPAN * 12 : SPAN * 12 + 24, :]
    wide[SPAN * 12 + 24 : SPAN * 12 + 48, :] = wide[24:48, :]
    outer = (band == 0) | (band == BANDS - 1)
    strips = [wide[24 * d : 24 * d + STRIP, :] for d in range(BANDS)]
    for d in range(BANDS):
        rest = jnp.where(outer, strips[BANDS - 1 - d], ends[...])
        out_ref[d] = jnp.concatenate([strips[d], rest], axis=0).astype(BF)


def line_selector():
    select = np.zeros((2, WINDOW * 64, 4 * STRIP + 6 * ENDS), np.float32)
    for mirrored in range(2):
        for j in range(WINDOW):
            part, parity = j // 2, j % 2
            for fld in range(2):
                for depth in range(2):
                    for face in range(3):
                        base = j * 64 + (fld * 2 + depth) * 16 + face
                        column = STRIP * mirrored + (5 - j if mirrored else j) * 12 + fld * 6 + face
                        select[mirrored, base, column + depth * 3] = 1
                        select[mirrored, base + 3, 2 * STRIP + column + (1 - depth) * 3] = 1
                        for side in range(2):
                            source = 4 * STRIP + (3 * mirrored + part) * ENDS + (1 - parity if mirrored else parity) * 24
                            select[mirrored, base + 6 + 3 * side, source + fld * 12 + side * 6 + depth * 3 + face] = 1
    return select


def ends_selector():
    select = np.zeros((4, ENDS, SLOT_ONE), np.float32)
    for k, d in enumerate((0, 1, 30, 31)):
        for row in range(2):
            for fld in range(2):
                for side in range(2):
                    for depth in range(2):
                        col = 63 - depth if side else depth
                        at = (col - 2 * d + 2) % SPAN
                        other = (col - 60 + 2 * d) % SPAN
                        base = at * 12 if at < WINDOW else STRIP + other * 12
                        for face in range(3):
                            place = row * 24 + fld * 12 + side * 6 + depth * 3 + face
                            select[k, place, base + fld * 6 + row * 3 + face] = 1
    return select


def gather_lines(fn_ref, rot_ref, sel_ref, ends_ref, in_ref, out_ref):
    band, group = here()
    first, last = in_ref[0], in_ref[BANDS - 1]
    pick_ends = ends_ref[(band & 1) + 2 * (band >> 4)]
    first_ends, last_ends = mm(pick_ends, first), mm(pick_ends, last)
    ends = []
    for source in [band + 31 + part for part in range(3)] + [64 - band - part for part in range(3)]:
        source = source & 31
        block = in_ref[source].astype(F32)[STRIP : STRIP + ENDS]
        ends.append(jnp.where(source == 0, first_ends, jnp.where(source == BANDS - 1, last_ends, block)))
    pieces = jnp.concatenate([first.astype(F32), last.astype(F32)] + ends, axis=0).astype(BF)
    place = lax.broadcasted_iota(I32, (WINDOW * 64, 1), 0) & 15
    flip = jnp.zeros((WINDOW * 64, 1), I32)
    for side in range(4):
        for face in range(3):
            flip = jnp.where(place == side * 3 + face, is_mirrored(fn_ref, rot_ref, 3 * group + face, side), flip)
    flip = jnp.broadcast_to(flip.astype(F32), sel_ref.shape[1:]).astype(BF)
    picked = mm(sel_ref[0] * (1 - flip) + sel_ref[1] * flip, pieces).astype(BF)
    for j in range(WINDOW):
        out_ref[j] = picked[j * 64 : j * 64 + 64]


def silu_parts(pre):
    logistic = 1.0 / (1.0 + jnp.exp(-pre))
    return pre * logistic, logistic * (1.0 + pre * (1.0 - logistic))


def side_frame(side, tap):
    dr, dc = tap[0] - 1, tap[1] - 1
    return ((dr, dc), (-dr, dc), (dc, dr), (-dc, dr))[side]


def transpose_weights(ref, out):
    for k, (a, b) in enumerate(TAPS):
        out[k * CH : (k + 1) * CH, :] = ref[a, b].T


def interior_kernel(
    in_ref, w1_ref, w2_ref, own_ref, away_ref, sent, acc, done, w1t, w2t, f2, g2, wide
):
    band, group = here()
    transpose_weights(w1_ref, w1t)
    transpose_weights(w2_ref, w2t)
    for s in range(BANDS):
        wide[s * STRIP : (s + 1) * STRIP, :] = in_ref[s].astype(F32)[0:STRIP]
    for q in range(WINDOW):
        for fld, target in enumerate((f2, g2)):
            for row in range(2):
                for face in range(3):
                    piece = wide[pl.ds(q * 12 + fld * 6 + row * 3 + face, BANDS, stride=STRIP), :]
                    target[pl.ds(q * 192 + face * 64 + row, BANDS, stride=2), :] = piece

    def conv_weights(ref):
        return jnp.concatenate([ref[a].reshape(3 * CH, CH) for a in range(3)], axis=1)

    def back_weights(ref):
        columns = []
        for a in range(3):
            columns.append(jnp.concatenate([ref[(a * 3 + b) * CH : (a * 3 + b + 1) * CH, :] for b in (2, 1, 0)], axis=0))
        return jnp.concatenate(columns, axis=1)

    def up_one(value):
        return pltpu.roll(value, value.shape[0] - 1, 0)

    def down_one(value):
        return pltpu.roll(value, 1, 0)

    def three_columns(ref, first, count):
        return jnp.concatenate([ref[first + 192 * b : first + 192 * b + count, :].astype(BF) for b in range(3)], axis=1)

    y = mm(three_columns(f2, 0, 768), conv_weights(w1_ref))
    pre = down_one(y[:, :CH]) + y[:, CH : 2 * CH] + up_one(y[:, 2 * CH :])
    z = mm(three_columns(g2, 0, 768), back_weights(w2t))
    back = up_one(z[:, :CH]) + z[:, CH : 2 * CH] + down_one(z[:, 2 * CH :])
    hidden, slope = silu_parts(pre)
    index = lax.broadcasted_iota(I32, (768, CH), 0)
    step = (index >= 192).astype(I32) + (index >= 384).astype(I32) + (index >= 576).astype(I32)
    col = 2 * band - 1 + step
    row = index & 63
    inner = (row >= 1) & (row <= 62) & (col >= 1) & (col <= 62)
    gpre = jnp.where(inner, back * slope, 0.0).astype(BF)
    hid = jnp.where(inner, hidden, 0.0)[192:576].astype(BF)

    gown = gpre[192:576].astype(F32)
    gcat = jnp.concatenate([up_one(gown).astype(BF), gpre[192:576], down_one(gown).astype(BF)], axis=1)
    first = mm_t(three_columns(f2, 192, 384), gcat)
    hown = hid.astype(F32)
    hcat = jnp.concatenate([down_one(hown).astype(BF), hid, up_one(hown).astype(BF)], axis=1)
    gback = jnp.concatenate([g2[start : start + 384, :].astype(BF) for start in (576, 384, 192)], axis=1)
    second = mm_t(hcat, gback)
    for k, (a, b) in enumerate(TAPS):
        top, low = k * CH, 1152 + k * CH
        acc[top : top + CH, :] = first[b * CH : (b + 1) * CH, a * CH : (a + 1) * CH]
        acc[low : low + CH, :] = second[a * CH : (a + 1) * CH, b * CH : (b + 1) * CH]
    core = group & 1
    own_ref[...] = acc[pl.ds(pl.multiple_of(core * HALF, CH), HALF), :]
    away_ref[...] = acc[pl.ds(pl.multiple_of((1 - core) * HALF, CH), HALF), :].astype(BF)

    gthree = jnp.concatenate([gpre[0:384], gpre[192:576], gpre[384:768]], axis=1)
    z = mm(gthree, back_weights(w1t))
    done[...] = up_one(z[:, :CH]) + z[:, CH : 2 * CH] + down_one(z[:, 2 * CH :]) + g2[384:768, :]
    sent[...] = jnp.zeros_like(sent)
    for q in range(2):
        for face in range(3):
            for row in range(2):
                piece = done[pl.ds(q * 192 + face * 64 + row, BANDS, stride=2), :]
                sent[pl.ds((q * 3 + face) * 2 + row, BANDS, stride=16), :] = piece


def main_kernel(
    fn_ref, rot_ref, fill_ref, plan_ref, sel_ref, own_ref, one_ref, two_ref, three_ref, w1_ref, w2_ref,
    share_ref, tail_ref,
    w1t, w2t, xs, hal, nb, cg, lp, lg, lc, ss, gp, gpu, owe,
):
    band, group = here()
    transpose_weights(w1_ref, w1t)
    transpose_weights(w2_ref, w2t)

    line = lax.broadcasted_iota(I32, (64, 1), 0)
    place = line & 15
    side = (place >= 3).astype(I32) + (place >= 6).astype(I32) + (place >= 9).astype(I32)
    face = place - 3 * side
    home = line - place
    real = place < 12
    lane = lax.broadcasted_iota(I32, (64, 64), 1)

    def one_hot(target, keep):
        return (jnp.where(keep & real, target, -1) == lane).astype(F32).astype(BF)

    face_lane = lax.broadcasted_iota(I32, (64, 12), 1)
    faces = (jnp.where(real, 3 * (line >> 4) + face, -1) == face_lane).astype(F32).astype(BF)

    def by_line(ref, columns):
        table = ref[...].astype(F32).astype(BF)
        rows = lax.dot_general(faces, table, (((1,), (1,)), ((), ())), preferred_element_type=F32).astype(I32)
        value = rows[:, columns[0] : columns[0] + 1]
        for s in range(1, 4):
            value = jnp.where(side == s, rows[:, columns[s] : columns[s] + 1], value)
        return value

    fn = by_line(fn_ref, (0, 1, 2, 3))
    rot = by_line(rot_ref, (0, 1, 2, 3))
    fn_group = (fn * 43) >> 7
    partner = one_hot(fn_group * 16 + (rot & 3) * 3 + (fn - 3 * fn_group), real)
    number = 4 * (3 * (line >> 4) + face) + side
    flip = ((rot >> 2) == 1) & (number > 4 * fn + (rot & 3)) & real
    fills = []
    for columns in ((0, 2, 0, 1), (1, 3, 2, 3)):
        m = by_line(fill_ref, columns)
        mf = m >> 2
        mg = (mf * 43) >> 7
        target = mg * 16 + ((m >> 1) & 1) * 3 + (mf - 3 * mg)
        fills.append((one_hot(target, (m & 1) == 0), one_hot(target, (m & 1) == 1)))
    corner_cells = jnp.concatenate([jnp.concatenate(pair, axis=1) for pair in fills], axis=0)
    corner_back = corner_cells.astype(F32).T.astype(BF)
    even = (side & 1) == 0
    low_side = jnp.where(side < 2, 2, 0)
    high_side = jnp.where(side < 2, 3, 1)
    beside = jnp.concatenate([
        jnp.concatenate([one_hot(home + other * 3 + face, even), one_hot(home + other * 3 + face, ~even)], axis=1)
        for other in (low_side, high_side)
    ], axis=0)
    side_mask = [jnp.broadcast_to((side == s).astype(F32), (64, CH)).astype(BF) > 0.5 for s in range(4)]
    row_line = (side < 2).astype(F32)
    flip_f = jnp.broadcast_to(flip.astype(F32), (64, CH))
    flip_b = flip_f.astype(BF) > 0.5

    def pick(plain, mirrored):
        return jnp.where(flip_b, mirrored, plain)

    def pick_f(plain, mirrored):
        return jnp.where(flip_f > 0.5, mirrored, plain)

    for step, ref in enumerate((own_ref, one_ref, two_ref, three_ref)):
        start = pl.multiple_of((group ^ step) * 16, 16)
        for j in range(WINDOW):
            for block in range(4):
                xs[block, j, pl.ds(start, 16), :] = ref[j, block * 16 : block * 16 + 16, :]
    halos = mm(partner, jnp.concatenate([xs[0, j] for j in range(WINDOW)], axis=1)).astype(BF)
    for j in range(WINDOW):
        hal[j] = halos[:, j * CH : (j + 1) * CH]

    def block_at(block, j):
        return hal[j] if block == 0 else xs[block - 1, j]

    for block in range(5):
        for j in range(1, 5):
            before, after = block_at(block, j - 1), block_at(block, j + 1)
            nb[0, block, j] = pick(before, after)
            nb[1, block, j] = pick(after, before)
    cg[...] = jnp.zeros_like(cg)

    def line_ends(zero, end, shift):
        lower, upper = zero + shift, end - shift
        return lambda value: (pick(value(lower), value(upper)), pick(value(upper), value(lower)))

    def fill_ends(zero, end):
        first = line_ends(zero, end, 0)
        second = line_ends(zero, end, 1)
        h_zero, h_end = first(lambda j: hal[j])
        h_one, h_last = second(lambda j: hal[j])
        f_zero, f_end = first(lambda j: xs[0, j])
        none = jnp.zeros((64, CH), BF)
        cells = mm(corner_cells, jnp.concatenate([f_zero, f_end], axis=0)).astype(BF)
        sides = jnp.concatenate([
            jnp.concatenate([h_zero, h_one], axis=1), jnp.concatenate([h_end, h_last], axis=1)
        ], axis=0)
        sides = mm(beside, sides).astype(BF)
        low = [cells[:64], sides[:64, :CH], sides[:64, CH:], none, none]
        high = [cells[64:], sides[64:, :CH], sides[64:, CH:], none, none]
        for block in range(5):
            nb[0, block, zero] = pick(low[block], nb[0, block, zero])
            nb[1, block, zero] = pick(nb[1, block, zero], high[block])
            nb[0, block, end] = pick(nb[0, block, end], low[block])
            nb[1, block, end] = pick(high[block], nb[1, block, end])
        cg[0], cg[1] = first(lambda j: xs[2, j])

    @pl.when(band == 0)
    def _():
        fill_ends(2, 1)

    @pl.when(band == BANDS - 1)
    def _():
        fill_ends(4, 3)

    def choose(options):
        whole = all(option is not None for option in options)
        result = options[0] if whole else jnp.zeros((64, CH), BF)
        for s, option in enumerate(options):
            if option is not None and not (whole and s == 0):
                result = jnp.where(side_mask[s], option, result)
        return result

    def fill(target, block, source):
        for k, tap in enumerate(TAPS):
            target[block * 64 : block * 64 + 64, k * CH : (k + 1) * CH] = choose(
                [source(*side_frame(s, tap)) for s in range(4)]
            )

    def field_source(j):
        def source(delta, dt):
            return block_at(delta + 1, j) if dt == 0 else nb[(dt + 1) // 2, delta + 1, j]
        return source

    def grad_source(e, j):
        def source(delta, dt):
            depth = e - delta
            if depth not in (0, 1):
                return None
            return xs[2 + depth, j] if dt == 0 else nb[(1 - dt) // 2, 3 + depth, j]
        return source

    def corner_source(which, value):
        def source(delta, dt):
            return value if (delta, dt) == (-1, 2 * which - 1) else None
        return source

    order_pre = (2, 3, 1, 4)
    for block, j in enumerate(order_pre):
        fill(lp, block, field_source(j))
    order_back = [(0, 2), (0, 3), (-1, 2), (-1, 3), None, None, (0, 1), (0, 4), (-1, 1), (-1, 4)]
    for block, at in enumerate(order_back):
        fill(lg, block, corner_source(block - 4, cg[block - 4]) if at is None else grad_source(*at))

    pre = mm(lp[...], w1_ref[...].reshape(9 * CH, CH))
    back = mm(lg[...], w2t[...])

    def back_block(e, j):
        block = order_back.index((e, j))
        return back[block * 64 : block * 64 + 64]

    seams = jnp.concatenate([back_block(-1, j).astype(BF) for j in range(1, 5)], axis=1)
    seams = mm(partner, seams)
    for j in range(1, 5):
        ss[j] = seams[:, (j - 1) * CH : j * CH]
    both_rows = jnp.concatenate([row_line, row_line], axis=0)

    def corner_sums(both):
        sums = mm(corner_back, (both * both_rows).astype(BF))
        return sums[:64], sums[64:]


    def close_ends(zero, end):
        at_zero, at_end = corner_sums(back[256:384])
        head = pick_f(ss[zero], ss[end]) + at_zero
        tail = pick_f(ss[end], ss[zero]) + at_end
        sides = mm(beside, jnp.concatenate([head, tail], axis=0).astype(BF))
        head += sides[:64]
        tail += sides[64:]
        ss[zero] = pick_f(head, tail)
        ss[end] = pick_f(tail, head)

    @pl.when(band == 0)
    def _():
        close_ends(2, 1)

    @pl.when(band == BANDS - 1)
    def _():
        close_ends(4, 3)

    unique = {}
    hid = {}
    for block, j in enumerate(order_pre):
        value = pre[block * 64 : block * 64 + 64]
        hidden, slope = silu_parts(value)
        t = (2 * band - 2 + j) & (SPAN - 1)
        corner = jnp.logical_or(t == 0, t == SPAN - 1)
        unique[j] = jnp.where(corner, row_line, jnp.ones_like(row_line))
        grad = ((back_block(0, j) + ss[j]) * slope).astype(BF)
        gp[j] = grad
        gpu[j] = (grad.astype(F32) * unique[j]).astype(BF)
        hid[j] = hidden.astype(BF)

    mine = ((line >> 5) == (group >> 1)).astype(F32)
    edge = jnp.where(band == 0, 1.0, 0.0) * mine * row_line

    def scaled(value, factor):
        return (value.astype(F32) * factor).astype(BF)

    h_zero, h_end = pick(hid[2], hid[1]), pick(hid[1], hid[2])
    halos = mm(partner, jnp.concatenate([hid[2], hid[3]], axis=1))
    ends = mm(corner_cells, jnp.concatenate([h_zero, h_end], axis=0))
    cells = jnp.concatenate([
        scaled(hid[2], mine * unique[2]),
        scaled(hid[3], mine * unique[3]),
        scaled(halos[:, :CH], mine),
        scaled(halos[:, CH:], mine),
        scaled(ends[:64], edge),
        scaled(ends[64:], edge),
    ], axis=0)
    @pl.when((group & 1) == 0)
    def _():
        own = jnp.concatenate([scaled(gpu[2], mine), scaled(gpu[3], mine)], axis=0)
        share_ref[...] = mm_t(lp[0:128, :], own)

    @pl.when((group & 1) == 1)
    def _():
        second = mm_t(cells, lg[0:384, :])
        for k in range(9):
            share_ref[k * CH : (k + 1) * CH, :] = second[:, k * CH : (k + 1) * CH]

    at_first, at_last = band == 0, band == BANDS - 1
    inner_low = jnp.where(at_first, 0.0, 1.0)
    inner_high = jnp.where(at_last, 0.0, 1.0)

    def spread_source(e, j, ref):
        def source(delta, dt):
            if e - delta != 0:
                return None
            if dt == 0:
                return ref[j]
            before = scaled(ref[1], inner_low) if j == 2 else ref[2]
            after = ref[3] if j == 2 else scaled(ref[4], inner_high)
            return pick(before, after) if dt == 1 else pick(after, before)
        return source

    g_zero = jnp.where(at_first, gp[2], gp[4])
    g_end = jnp.where(at_first, gp[1], gp[3])
    g_zero, g_end = pick(g_zero, g_end), pick(g_end, g_zero)
    order_in = [(0, 2), (0, 3), (1, 2), (1, 3), (-1, 2), (-1, 3), None, None]
    for block, at in enumerate(order_in):
        if at is None:
            fill(lc, block, corner_source(block - 6, (g_zero, g_end)[block - 6]))
        else:
            fill(lc, block, spread_source(*at, gp if at[0] == -1 else gpu))
    back = mm(lc[...], w1t[...])
    part = [back[k * 64 : k * 64 + 64] for k in range(8)]
    at_zero, at_end = corner_sums(back[384:512])
    seams = mm(partner, jnp.concatenate([part[4], part[5]], axis=1).astype(BF))
    owe[0] = part[0] + seams[:, :CH] + pick_f(at_zero, at_end) * (1.0 - inner_low)
    owe[1] = part[2]
    owe[2] = part[1] + seams[:, CH:] + pick_f(at_end, at_zero) * (1.0 - inner_high)
    owe[3] = part[3]

    tile = jnp.concatenate([owe[k, pl.ds(pl.multiple_of(group * 16, 16), 16), :] for k in range(4)], axis=0)
    plan = [plan_ref[:, k : k + 1] for k in range(8)]
    flips = [jnp.zeros((48, 1), I32) for _ in range(2)]
    for which in range(4):
        for face_index in range(3):
            value = mirrored_in(fn_ref, rot_ref, 3 * group + face_index, which)
            for k in range(2):
                flips[k] = jnp.where(plan[6 + k] == which * 3 + face_index, value, flips[k])
    last = jnp.where(at_last, 1, 0)
    outer = jnp.logical_or(at_first, at_last)
    row_lane = jnp.where(flips[0] ^ last == plan[4], jnp.where(at_last, plan[1], plan[0]), -1)
    col_lane = jnp.where(flips[1] ^ last == plan[5], jnp.where(at_last, plan[3], plan[2]), -1)
    lanes = lax.broadcasted_iota(I32, (48, 64), 1)
    patch = (row_lane == lanes).astype(F32) + (col_lane == lanes).astype(F32)
    select = jnp.concatenate([jnp.where(outer, patch, sel_ref[0:48, :]), sel_ref[48:72, :]], axis=0)
    tail_ref[...] = mm(select.astype(BF), tile.astype(BF))


def tail_plan():
    select = np.zeros((72, 64), np.float32)
    plan = np.zeros((48, 8), np.int32)
    for pos in range(2):
        for depth in range(2):
            for face in range(3):
                lane = (pos * 2 + depth) * 16 + face
                for half in range(2):
                    select[half * 24 + (pos * 2 + depth) * 3 + face, lane + half * 3] = 1
                for side in range(2):
                    select[48 + ((pos * 2 + side) * 2 + depth) * 3 + face, lane + 6 + 3 * side] = 1
    for half in range(2):
        for side in range(2):
            for face in range(3):
                for row in range(2):
                    for col in range(2):
                        place = half * 24 + ((side * 3 + face) * 2 + row) * 2 + col
                        for last in range(2):
                            plan[place, last] = ((col ^ last) * 2 + row) * 16 + half * 3 + face
                            plan[place, 2 + last] = ((row ^ last) * 2 + col) * 16 + (2 + side) * 3 + face
                        plan[place, 4:] = side, half, half * 3 + face, (2 + side) * 3 + face
    return select, plan


def after_kernel(*refs):
    pass


def share_kernel(own_ref, other_ref, line_ref, tail_ref, sent, out_ref, total):
    total[...] = own_ref[...] + other_ref[...].astype(F32) + line_ref[...]
    for i in range(BANDS):
        start = 0 if i == 0 else 24 if i == BANDS - 1 else 48
        parts = [total[CHUNK * i : CHUNK * i + CHUNK, :], sent[i * 16 : i * 16 + 12, :], tail_ref[start : start + 24, :]]
        out_ref[i] = jnp.concatenate(parts, axis=0).astype(BF)


def order_selector():
    select = np.zeros((2, 64, 64), np.float32)
    for pos in range(2):
        for b in range(BANDS):
            select[0, 2 * b + pos, pos * 32 + b] = 1
            select[1, 63 - 2 * b - pos, pos * 32 + b] = 1
    return select


def reduce_kernel(in_ref, out_ref):
    total = in_ref[0, 0:48, :].astype(F32)
    for i in range(1, BANDS):
        total = total + in_ref[i, 0:48, :].astype(F32)
    out_ref[...] = total[0:SLOT_THREE]


def spread_kernel(factor, own_ref, other_ref, out_ref):
    total = ((own_ref[...] + other_ref[...]) * factor).astype(BF)
    for i in range(BANDS):
        out_ref[i] = total


def unpack_kernel(own_ref, other_ref, first_ref, second_ref):
    _, group = here()
    core = group & 1
    for i in range(BANDS):
        own, other = own_ref[i].astype(F32), other_ref[i].astype(F32)
        rows = slice(CHUNK * i, CHUNK * i + CHUNK)
        first_ref[rows, :] = jnp.where(core == 0, own, other)[0:CHUNK]
        second_ref[rows, :] = jnp.where(core == 0, other, own)[0:CHUNK]


def grad_kernel(fn_ref, rot_ref, sel_ref, in_ref, out_ref, wide, total):
    band, group = here()
    for i in range(BANDS):
        wide[i * 40 : i * 40 + 40, :] = in_ref[i].astype(F32)[32:SLOT_TWO]
    for q in range(2):
        for face in range(3):
            for row in range(2):
                piece = wide[pl.ds(4 + (q * 3 + face) * 2 + row, BANDS, stride=40), :]
                total[row, face, pl.ds(q, BANDS, stride=2), :] = piece
    tiles = [wide[pl.ds(pl.multiple_of(src * 40, 8), 40), :] for src in (band, BANDS - 1 - band)]
    outer = (band == 0) | (band == BANDS - 1)

    @pl.when(~outer)
    def _():
        for side in range(2):
            for face in range(3):
                flip = is_mirrored(fn_ref, rot_ref, 3 * group + face, 2 + side) == 1
                for row in range(2):
                    for depth in range(2):
                        column = depth if side == 0 else 63 - depth
                        k, m = [16 + ((pos * 2 + side) * 2 + depth) * 3 + face for pos in (row, 1 - row)]
                        extra = jnp.where(flip, tiles[1][m : m + 1, :], tiles[0][k : k + 1, :])
                        total[row, face, column : column + 1, :] += extra

    @pl.when(outer)
    def _():
        half = jnp.where(band == 0, 0, 1)
        patches = tiles[0] + tiles[1]
        place = lax.broadcasted_iota(I32, (SPAN, CH), 0)
        inner = (place >= 2) & (place < SPAN - 2)
        for face in range(3):
            order = sel_ref[is_mirrored(fn_ref, rot_ref, 3 * group + face, half)]
            for depth in range(2):
                halves = [wide[pl.ds(16 + (pos * 2 + depth) * 3 + face, BANDS, stride=40), :] for pos in range(2)]
                extra = mm(order, jnp.concatenate(halves, axis=0).astype(BF))
                total[depth ^ half, face] += jnp.where(inner, extra, 0.0)
                for side in range(2):
                    for col in range(2):
                        k = 16 + ((side * 3 + face) * 2 + depth) * 2 + col
                        column = 63 - col if side else col
                        total[depth ^ half, face, column : column + 1, :] += patches[k : k + 1, :]

    for row in range(2):
        for face in range(3):
            out_ref[face, row] = total[row, face].astype(BF)


def swapped(value, step):
    return lax.ppermute(value, "sub", [(i, i ^ step) for i in range(4)])


def body(field_in, grad_out, first_weight, second_weight, face_neighbour, seam_rotation, corner_fill):
    factor = (1.0 * 12 * SPAN * SPAN) ** -0.5
    seams = (face_neighbour.T, seam_rotation.T)
    in_smem = {0: "s", 1: "s"}
    select, plan = tail_plan()

    slots = call(
        pack_lines,
        jax.ShapeDtypeStruct((BANDS, SLOT_ONE, CH), BF),
        [
            pltpu.VMEM((2, 3, 2, SPAN, CH), BF),
            pltpu.VMEM(((SPAN + 4) * 12, CH), F32),
            pltpu.VMEM((STRIP, CH), F32),
            pltpu.SemaphoreType.DMA((2,)),
        ],
        tuple(pltpu.with_memory_space_constraint(value, pltpu.HBM) for value in (field_in, grad_out)),
        {0: "h", 1: "h"},
    )
    strips = lax.all_to_all(slots, "tile", 0, 0, tiled=True)
    lines = call(
        gather_lines,
        jax.ShapeDtypeStruct((WINDOW, 64, CH), BF),
        [],
        (*seams, jnp.asarray(line_selector(), BF), jnp.asarray(ends_selector(), BF), strips),
        in_smem,
    )
    lines = (lines, *[swapped(lines, step) for step in (1, 2, 3)])
    share = jax.ShapeDtypeStruct((HALF, CH), F32)
    own, away, sent = call(
        interior_kernel,
        [share, jax.ShapeDtypeStruct((HALF, CH), BF), jax.ShapeDtypeStruct((BANDS * 16, CH), F32)],
        [
            pltpu.VMEM((2304, CH), F32),
            pltpu.VMEM((384, CH), F32),
            pltpu.VMEM((1152, CH), BF),
            pltpu.VMEM((1152, CH), BF),
            pltpu.VMEM((1152, CH), F32),
            pltpu.VMEM((1152, CH), F32),
            pltpu.VMEM((BANDS * STRIP, CH), F32),
        ],
        (strips, first_weight, second_weight),
    )
    away = call(after_kernel, jax.ShapeDtypeStruct((HALF, CH), BF), [], (away, *lines[1:]), dict.fromkeys((0, 1, 2, 3, "o0"), "a"), {0: 0})
    other = swapped(away, 1)

    line, tails = call(
        main_kernel,
        [share, jax.ShapeDtypeStruct((72, CH), F32)],
        [
            pltpu.VMEM((1152, CH), BF),
            pltpu.VMEM((1152, CH), BF),
            pltpu.VMEM((4, WINDOW, 64, CH), BF),
            pltpu.VMEM((WINDOW, 64, CH), BF),
            pltpu.VMEM((2, 5, 5, 64, CH), BF),
            pltpu.VMEM((2, 64, CH), BF),
            pltpu.VMEM((256, 1152), BF),
            pltpu.VMEM((640, 1152), BF),
            pltpu.VMEM((512, 1152), BF),
            pltpu.VMEM((5, 64, CH), F32),
            pltpu.VMEM((5, 64, CH), BF),
            pltpu.VMEM((5, 64, CH), BF),
            pltpu.VMEM((4, 64, CH), F32),
        ],
        (*seams, corner_fill.T, jnp.asarray(plan), jnp.asarray(select, F32), *lines, first_weight, second_weight),
    )
    slots = call(
        share_kernel,
        jax.ShapeDtypeStruct((BANDS, SLOT_TWO, CH), BF),
        [pltpu.VMEM((HALF, CH), F32)],
        (own, other, line, tails, sent),
    )
    slots = lax.all_to_all(slots, "tile", 0, 0, tiled=True)
    part = call(reduce_kernel, jax.ShapeDtypeStruct((SLOT_THREE, CH), F32), [], (slots,))
    reduced = call(
        lambda *refs: spread_kernel(factor, *refs),
        jax.ShapeDtypeStruct((BANDS, SLOT_THREE, CH), BF),
        [],
        (part, swapped(part, 2)),
    )
    reduced = lax.all_to_all(reduced, "tile", 0, 0, tiled=True)
    swap = swapped(reduced, 1)
    grad_in = call(
        grad_kernel,
        jax.ShapeDtypeStruct((3, 2, SPAN, CH), BF),
        [pltpu.VMEM((BANDS * 40, CH), F32), pltpu.VMEM((2, 3, SPAN, CH), F32)],
        (*seams, jnp.asarray(order_selector(), BF), slots),
        in_smem,
    )
    first, second = call(
        unpack_kernel,
        [jax.ShapeDtypeStruct((1152, CH), F32), jax.ShapeDtypeStruct((1152, CH), F32)],
        [],
        (reduced, swap),
    )
    return grad_in, first.reshape(3, 3, CH, CH), second.reshape(3, 3, CH, CH)


def solution(mesh):
    return jax.shard_map(
        body,
        mesh=mesh,
        in_specs=(P("sub", "tile", None, None), P("sub", "tile", None, None), P(), P(), P(), P(), P()),
        out_specs=(P("sub", "tile", None, None), P(), P()),
        check_vma=False,
    )
```

```python
import jax
import jax.numpy as jnp
import numpy as np
from jax import lax
from jax.experimental import pallas as pl
from jax.experimental.pallas import tpu as pltpu
from jax.sharding import PartitionSpec as P

BF = jnp.bfloat16
F32 = jnp.float32
I32 = jnp.int32
BANDS = 32
SPAN = 64
CH = 128
TAPS = [(a, b) for a in range(3) for b in range(3)]
WINDOW = 6
ENDS = 48
STRIP = 12 * WINDOW
SLOT_ONE = 2 * STRIP
HALF = 9 * CH
CHUNK = 36
TAIL = 36
SLOT_TWO = CHUNK + TAIL
SLOT_THREE = 40
VMEM_BYTES = 48 * 1024 * 1024


def mm(left, right):
    return jnp.dot(left, right, preferred_element_type=F32)


def mm_t(left, right):
    return lax.dot_general(left, right, (((0,), (0,)), ((), ())), preferred_element_type=F32)


def call(kernel, outs, scratch, operands, places=(), aliases=None):
    kinds = {"v": pltpu.VMEM, "s": pltpu.SMEM, "h": pltpu.HBM, "a": pl.ANY}
    places = dict(places)
    many = isinstance(outs, (list, tuple))
    out_specs = [pl.BlockSpec(memory_space=kinds[places.get(f"o{k}", "v")]) for k in range(len(outs) if many else 1)]
    return pl.pallas_call(
        kernel,
        out_shape=outs,
        in_specs=[pl.BlockSpec(memory_space=kinds[places.get(k, "v")]) for k in range(len(operands))],
        out_specs=out_specs if many else out_specs[0],
        scratch_shapes=scratch,
        input_output_aliases=aliases or {},
        compiler_params=pltpu.CompilerParams(vmem_limit_bytes=VMEM_BYTES),
    )(*operands)


def here():
    return lax.axis_index("tile"), lax.axis_index("sub")


def is_mirrored(fn_ref, rot_ref, face, side):
    rot = rot_ref[face, side]
    partner = 4 * fn_ref[face, side] + (rot & 3)
    return jnp.where(4 * face + side > partner, rot >> 2, 0)


def is_mirrored(fn_ref, rot_ref, face, side):
    rot = rot_ref[side, face]
    partner = 4 * fn_ref[side, face] + (rot & 3)
    return jnp.where(4 * face + side > partner, rot >> 2, 0)


def mirrored_in(fn_ref, rot_ref, face, side):
    lane = lax.broadcasted_iota(I32, (1, 12), 1) == face
    rot = jnp.sum(jnp.where(lane, rot_ref[side : side + 1, :], 0))
    partner = 4 * jnp.sum(jnp.where(lane, fn_ref[side : side + 1, :], 0)) + (rot & 3)
    return jnp.where(4 * face + side > partner, rot >> 2, 0)


def pack_lines(f_hbm, g_hbm, out_ref, buf, wide, ends, sems):
    copies = [pltpu.make_async_copy(src, buf.at[k], sems.at[k]) for k, src in enumerate((f_hbm, g_hbm))]
    for copy in copies:
        copy.start()
    band, _ = here()
    ends[ENDS:STRIP, :] = jnp.zeros((STRIP - ENDS, CH), F32)
    for fld in range(2):
        copies[fld].wait()
        for row in range(2):
            for face in range(3):
                block = buf[fld, face, row].astype(F32)
                wide[pl.ds(24 + fld * 6 + row * 3 + face, SPAN, stride=12), :] = block
                for edge, cols in enumerate(((0, 1), (63, 62))):
                    for depth, col in enumerate(cols):
                        place = row * 24 + fld * 12 + edge * 6 + depth * 3 + face
                        ends[place : place + 1, :] = block[col : col + 1, :]
    wide[0:24, :] = wide[SPAN * 12 : SPAN * 12 + 24, :]
    wide[SPAN * 12 + 24 : SPAN * 12 + 48, :] = wide[24:48, :]
    outer = (band == 0) | (band == BANDS - 1)
    strips = [wide[24 * d : 24 * d + STRIP, :] for d in range(BANDS)]
    for d in range(BANDS):
        rest = jnp.where(outer, strips[BANDS - 1 - d], ends[...])
        out_ref[d] = jnp.concatenate([strips[d], rest], axis=0).astype(BF)


def line_selector():
    select = np.zeros((2, WINDOW * ENDS, 4 * STRIP + 6 * ENDS), np.float32)
    for mirrored in range(2):
        for j in range(WINDOW):
            part, parity = j // 2, j % 2
            for fld in range(2):
                for depth in range(2):
                    for face in range(3):
                        base = j * ENDS + (fld * 2 + depth) * 12 + face
                        column = STRIP * mirrored + (5 - j if mirrored else j) * 12 + fld * 6 + face
                        select[mirrored, base, column + depth * 3] = 1
                        select[mirrored, base + 3, 2 * STRIP + column + (1 - depth) * 3] = 1
                        for side in range(2):
                            source = 4 * STRIP + (3 * mirrored + part) * ENDS + (1 - parity if mirrored else parity) * 24
                            select[mirrored, base + 6 + 3 * side, source + fld * 12 + side * 6 + depth * 3 + face] = 1
    return select


def ends_selector():
    select = np.zeros((4, ENDS, SLOT_ONE), np.float32)
    for k, d in enumerate((0, 1, 30, 31)):
        for row in range(2):
            for fld in range(2):
                for side in range(2):
                    for depth in range(2):
                        col = 63 - depth if side else depth
                        at = (col - 2 * d + 2) % SPAN
                        other = (col - 60 + 2 * d) % SPAN
                        base = at * 12 if at < WINDOW else STRIP + other * 12
                        for face in range(3):
                            place = row * 24 + fld * 12 + side * 6 + depth * 3 + face
                            select[k, place, base + fld * 6 + row * 3 + face] = 1
    return select


def gather_lines(fn_ref, rot_ref, sel_ref, ends_ref, in_ref, out_ref):
    band, group = here()
    first, last = in_ref[0], in_ref[BANDS - 1]
    pick_ends = ends_ref[(band & 1) + 2 * (band >> 4)]
    first_ends, last_ends = mm(pick_ends, first), mm(pick_ends, last)
    ends = []
    for source in [band + 31 + part for part in range(3)] + [64 - band - part for part in range(3)]:
        source = source & 31
        block = in_ref[source].astype(F32)[STRIP : STRIP + ENDS]
        ends.append(jnp.where(source == 0, first_ends, jnp.where(source == BANDS - 1, last_ends, block)))
    pieces = jnp.concatenate([first.astype(F32), last.astype(F32)] + ends, axis=0).astype(BF)
    place = lax.broadcasted_iota(I32, (WINDOW * ENDS, 1), 0)
    place = place - 12 * ((place * 171) >> 11)
    flip = jnp.zeros((WINDOW * ENDS, 1), I32)
    for side in range(4):
        for face in range(3):
            flip = jnp.where(place == side * 3 + face, is_mirrored(fn_ref, rot_ref, 3 * group + face, side), flip)
    flip = jnp.broadcast_to(flip.astype(F32), sel_ref.shape[1:]).astype(BF)
    picked = mm(sel_ref[0] * (1 - flip) + sel_ref[1] * flip, pieces).astype(BF)
    for j in range(WINDOW):
        out_ref[j] = picked[j * ENDS : (j + 1) * ENDS]


def silu_parts(pre):
    logistic = 1.0 / (1.0 + jnp.exp(-pre))
    return pre * logistic, logistic * (1.0 + pre * (1.0 - logistic))


def side_frame(side, tap):
    dr, dc = tap[0] - 1, tap[1] - 1
    return ((dr, dc), (-dr, dc), (dc, dr), (-dc, dr))[side]


def transpose_weights(ref, out):
    for k, (a, b) in enumerate(TAPS):
        out[k * CH : (k + 1) * CH, :] = ref[a, b].T


def interior_kernel(
    in_ref, w1_ref, w2_ref, own_ref, away_ref, sent, acc, done, w1t, w2t, f2, g2, wide
):
    band, group = here()
    transpose_weights(w1_ref, w1t)
    transpose_weights(w2_ref, w2t)
    for s in range(BANDS):
        wide[s * STRIP : (s + 1) * STRIP, :] = in_ref[s].astype(F32)[0:STRIP]
    for q in range(WINDOW):
        for fld, target in enumerate((f2, g2)):
            for row in range(2):
                for face in range(3):
                    piece = wide[pl.ds(q * 12 + fld * 6 + row * 3 + face, BANDS, stride=STRIP), :]
                    target[pl.ds(q * 192 + face * 64 + row, BANDS, stride=2), :] = piece

    def conv_weights(ref):
        return jnp.concatenate([ref[a].reshape(3 * CH, CH) for a in range(3)], axis=1)

    def back_weights(ref):
        columns = []
        for a in range(3):
            columns.append(jnp.concatenate([ref[(a * 3 + b) * CH : (a * 3 + b + 1) * CH, :] for b in (2, 1, 0)], axis=0))
        return jnp.concatenate(columns, axis=1)

    def up_one(value):
        return pltpu.roll(value, value.shape[0] - 1, 0)

    def down_one(value):
        return pltpu.roll(value, 1, 0)

    def three_columns(ref, first, count):
        return jnp.concatenate([ref[first + 192 * b : first + 192 * b + count, :].astype(BF) for b in range(3)], axis=1)

    y = mm(three_columns(f2, 0, 768), conv_weights(w1_ref))
    pre = down_one(y[:, :CH]) + y[:, CH : 2 * CH] + up_one(y[:, 2 * CH :])
    z = mm(three_columns(g2, 0, 768), back_weights(w2t))
    back = up_one(z[:, :CH]) + z[:, CH : 2 * CH] + down_one(z[:, 2 * CH :])
    hidden, slope = silu_parts(pre)
    index = lax.broadcasted_iota(I32, (768, CH), 0)
    step = (index >= 192).astype(I32) + (index >= 384).astype(I32) + (index >= 576).astype(I32)
    col = 2 * band - 1 + step
    row = index & 63
    inner = (row >= 1) & (row <= 62) & (col >= 1) & (col <= 62)
    gpre = jnp.where(inner, back * slope, 0.0).astype(BF)
    hid = jnp.where(inner, hidden, 0.0)[192:576].astype(BF)

    gown = gpre[192:576].astype(F32)
    gcat = jnp.concatenate([up_one(gown).astype(BF), gpre[192:576], down_one(gown).astype(BF)], axis=1)
    first = mm_t(three_columns(f2, 192, 384), gcat)
    hown = hid.astype(F32)
    hcat = jnp.concatenate([down_one(hown).astype(BF), hid, up_one(hown).astype(BF)], axis=1)
    gback = jnp.concatenate([g2[start : start + 384, :].astype(BF) for start in (576, 384, 192)], axis=1)
    second = mm_t(hcat, gback)
    for k, (a, b) in enumerate(TAPS):
        top, low = k * CH, 1152 + k * CH
        acc[top : top + CH, :] = first[b * CH : (b + 1) * CH, a * CH : (a + 1) * CH]
        acc[low : low + CH, :] = second[a * CH : (a + 1) * CH, b * CH : (b + 1) * CH]
    core = group & 1
    own_ref[...] = acc[pl.ds(pl.multiple_of(core * HALF, CH), HALF), :]
    away_ref[...] = acc[pl.ds(pl.multiple_of((1 - core) * HALF, CH), HALF), :].astype(BF)

    gthree = jnp.concatenate([gpre[0:384], gpre[192:576], gpre[384:768]], axis=1)
    z = mm(gthree, back_weights(w1t))
    done[...] = up_one(z[:, :CH]) + z[:, CH : 2 * CH] + down_one(z[:, 2 * CH :]) + g2[384:768, :]
    sent[...] = jnp.zeros_like(sent)
    for q in range(2):
        for face in range(3):
            for row in range(2):
                piece = done[pl.ds(q * 192 + face * 64 + row, BANDS, stride=2), :]
                sent[pl.ds((q * 3 + face) * 2 + row, BANDS, stride=16), :] = piece


def main_kernel(
    fn_ref, rot_ref, fill_ref, plan_ref, sel_ref, own_ref, one_ref, two_ref, three_ref, w1_ref, w2_ref,
    share_ref, tail_ref,
    w1t, w2t, xs, hal, nb, lp, lg, lc, ss, gp, gpu, owe,
):
    band, group = here()
    transpose_weights(w1_ref, w1t)
    transpose_weights(w2_ref, w2t)

    line = lax.broadcasted_iota(I32, (64, 1), 0)
    place = line & 15
    side = (place >= 3).astype(I32) + (place >= 6).astype(I32) + (place >= 9).astype(I32)
    face = place - 3 * side
    home = line - place
    real = place < 12
    lane = lax.broadcasted_iota(I32, (64, 64), 1)

    def one_hot(target, keep):
        return (jnp.where(keep & real, target, -1) == lane).astype(F32).astype(BF)

    face_lane = lax.broadcasted_iota(I32, (64, 12), 1)
    faces = (jnp.where(real, 3 * (line >> 4) + face, -1) == face_lane).astype(F32).astype(BF)

    def by_line(ref, columns):
        table = ref[...].astype(F32).astype(BF)
        rows = lax.dot_general(faces, table, (((1,), (1,)), ((), ())), preferred_element_type=F32).astype(I32)
        value = rows[:, columns[0] : columns[0] + 1]
        for s in range(1, 4):
            value = jnp.where(side == s, rows[:, columns[s] : columns[s] + 1], value)
        return value

    fn = by_line(fn_ref, (0, 1, 2, 3))
    rot = by_line(rot_ref, (0, 1, 2, 3))
    fn_group = (fn * 43) >> 7
    partner = one_hot(fn_group * 16 + (rot & 3) * 3 + (fn - 3 * fn_group), real)
    number = 4 * (3 * (line >> 4) + face) + side
    flip = ((rot >> 2) == 1) & (number > 4 * fn + (rot & 3)) & real
    fills = []
    for columns in ((0, 2, 0, 1), (1, 3, 2, 3)):
        m = by_line(fill_ref, columns)
        mf = m >> 2
        mg = (mf * 43) >> 7
        target = mg * 16 + ((m >> 1) & 1) * 3 + (mf - 3 * mg)
        fills.append((one_hot(target, (m & 1) == 0), one_hot(target, (m & 1) == 1)))
    corner_cells = jnp.concatenate([jnp.concatenate(pair, axis=1) for pair in fills], axis=0)
    corner_back = corner_cells.astype(F32).T.astype(BF)
    even = (side & 1) == 0
    low_side = jnp.where(side < 2, 2, 0)
    high_side = jnp.where(side < 2, 3, 1)
    beside = jnp.concatenate([
        jnp.concatenate([one_hot(home + other * 3 + face, even), one_hot(home + other * 3 + face, ~even)], axis=1)
        for other in (low_side, high_side)
    ], axis=0)
    side_mask = [jnp.broadcast_to((side == s).astype(F32), (64, CH)).astype(BF) > 0.5 for s in range(4)]
    row_line = (side < 2).astype(F32)
    flip_f = jnp.broadcast_to(flip.astype(F32), (64, CH))
    flip_b = flip_f.astype(BF) > 0.5

    def pick(plain, mirrored):
        return jnp.where(flip_b, mirrored, plain)

    def pick_f(plain, mirrored):
        return jnp.where(flip_f > 0.5, mirrored, plain)

    arrived = (own_ref, one_ref, two_ref, three_ref)
    arrived = [jnp.concatenate([ref[j] for ref in arrived], axis=0) for j in range(WINDOW)]
    row = lax.broadcasted_iota(I32, (256, 1), 0)
    source = (((row >> 4) & 3) ^ group) * ENDS + (row >> 6) * 12 + (row & 15)
    source = jnp.where((row & 15) < 12, source, -1)
    expand = (source == lax.broadcasted_iota(I32, (256, 4 * ENDS), 1)).astype(F32).astype(BF)
    arrived = mm(expand, jnp.concatenate(arrived, axis=1)).astype(BF)
    for j in range(WINDOW):
        for block in range(4):
            xs[block, j] = arrived[block * 64 : block * 64 + 64, j * CH : (j + 1) * CH]
    halos = mm(partner, jnp.concatenate([xs[0, j] for j in range(WINDOW)], axis=1)).astype(BF)
    for j in range(WINDOW):
        hal[j] = halos[:, j * CH : (j + 1) * CH]

    def block_at(block, j):
        return hal[j] if block == 0 else xs[block - 1, j]

    for block in range(5):
        for j in range(1, 5):
            before, after = block_at(block, j - 1), block_at(block, j + 1)
            nb[0, block, j] = pick(before, after)
            nb[1, block, j] = pick(after, before)
    at_first, at_last = band == 0, band == BANDS - 1

    def line_ends(value, lower, upper, choice):
        zero = jnp.where(at_last, value(lower + 2), value(lower))
        end = jnp.where(at_last, value(upper + 2), value(upper))
        return choice(zero, end), choice(end, zero)

    h_zero, h_end = line_ends(lambda j: hal[j], 2, 1, pick)
    h_one, h_last = line_ends(lambda j: hal[j], 3, 0, pick)
    f_zero, f_end = line_ends(lambda j: xs[0, j], 2, 1, pick)
    none = jnp.zeros((64, CH), BF)
    cells = mm(corner_cells, jnp.concatenate([f_zero, f_end], axis=0)).astype(BF)
    sides = jnp.concatenate([jnp.concatenate([h_zero, h_one], axis=1), jnp.concatenate([h_end, h_last], axis=1)], axis=0)
    sides = mm(beside, sides).astype(BF)
    low = [cells[:64], sides[:64, :CH], sides[:64, CH:], none, none]
    high = [cells[64:], sides[64:, :CH], sides[64:, CH:], none, none]
    for block in range(5):
        for slot, here_now in ((2, at_first), (4, at_last)):
            before, after = nb[0, block, slot], nb[1, block, slot]
            nb[0, block, slot] = jnp.where(here_now, pick(low[block], before), before)
            nb[1, block, slot] = jnp.where(here_now, pick(after, high[block]), after)
            before, after = nb[0, block, slot - 1], nb[1, block, slot - 1]
            nb[0, block, slot - 1] = jnp.where(here_now, pick(before, low[block]), before)
            nb[1, block, slot - 1] = jnp.where(here_now, pick(high[block], after), after)
    corner_grad = line_ends(lambda j: xs[2, j], 2, 1, pick)

    def choose(options):
        whole = all(option is not None for option in options)
        result = options[0] if whole else jnp.zeros((64, CH), BF)
        for s, option in enumerate(options):
            if option is not None and not (whole and s == 0):
                result = jnp.where(side_mask[s], option, result)
        return result

    def fill(target, block, source):
        for k, tap in enumerate(TAPS):
            target[block * 64 : block * 64 + 64, k * CH : (k + 1) * CH] = choose(
                [source(*side_frame(s, tap)) for s in range(4)]
            )

    def field_source(j):
        def source(delta, dt):
            return block_at(delta + 1, j) if dt == 0 else nb[(dt + 1) // 2, delta + 1, j]
        return source

    def grad_source(e, j):
        def source(delta, dt):
            depth = e - delta
            if depth not in (0, 1):
                return None
            return xs[2 + depth, j] if dt == 0 else nb[(1 - dt) // 2, 3 + depth, j]
        return source

    def corner_source(which, value):
        def source(delta, dt):
            return value if (delta, dt) == (-1, 2 * which - 1) else None
        return source

    order_pre = (2, 3, 1, 4)
    for block, j in enumerate(order_pre):
        fill(lp, block, field_source(j))
    order_back = [(0, 2), (0, 3), (-1, 2), (-1, 3), None, None, (0, 1), (0, 4), (-1, 1), (-1, 4)]
    for block, at in enumerate(order_back):
        fill(lg, block, corner_source(block - 4, corner_grad[block - 4]) if at is None else grad_source(*at))

    pre = mm(lp[...], w1_ref[...].reshape(9 * CH, CH))
    back = mm(lg[...], w2t[...])

    def back_block(e, j):
        block = order_back.index((e, j))
        return back[block * 64 : block * 64 + 64]

    seams = jnp.concatenate([back_block(-1, j).astype(BF) for j in range(1, 5)], axis=1)
    seams = mm(partner, seams)
    for j in range(1, 5):
        ss[j] = seams[:, (j - 1) * CH : j * CH]
    both_rows = jnp.concatenate([row_line, row_line], axis=0)

    def corner_sums(both):
        sums = mm(corner_back, (both * both_rows).astype(BF))
        return sums[:64], sums[64:]


    at_zero, at_end = corner_sums(back[256:384])
    head, tail = line_ends(lambda j: ss[j], 2, 1, pick_f)
    head, tail = head + at_zero, tail + at_end
    sides = mm(beside, jnp.concatenate([head, tail], axis=0).astype(BF))
    head, tail = head + sides[:64], tail + sides[64:]
    for slot, here_now in ((2, at_first), (4, at_last)):
        ss[slot] = jnp.where(here_now, pick_f(head, tail), ss[slot])
        ss[slot - 1] = jnp.where(here_now, pick_f(tail, head), ss[slot - 1])

    unique = {}
    hid = {}
    for block, j in enumerate(order_pre):
        value = pre[block * 64 : block * 64 + 64]
        hidden, slope = silu_parts(value)
        t = (2 * band - 2 + j) & (SPAN - 1)
        corner = jnp.logical_or(t == 0, t == SPAN - 1)
        unique[j] = jnp.where(corner, row_line, jnp.ones_like(row_line))
        grad = ((back_block(0, j) + ss[j]) * slope).astype(BF)
        gp[j] = grad
        gpu[j] = (grad.astype(F32) * unique[j]).astype(BF)
        hid[j] = hidden.astype(BF)

    mine = ((line >> 5) == (group >> 1)).astype(F32)
    edge = jnp.where(band == 0, 1.0, 0.0) * mine * row_line

    def scaled(value, factor):
        return (value.astype(F32) * factor).astype(BF)

    h_zero, h_end = pick(hid[2], hid[1]), pick(hid[1], hid[2])
    halos = mm(partner, jnp.concatenate([hid[2], hid[3]], axis=1))
    ends = mm(corner_cells, jnp.concatenate([h_zero, h_end], axis=0))
    cells = jnp.concatenate([
        scaled(hid[2], mine * unique[2]),
        scaled(hid[3], mine * unique[3]),
        scaled(halos[:, :CH], mine),
        scaled(halos[:, CH:], mine),
        scaled(ends[:64], edge),
        scaled(ends[64:], edge),
    ], axis=0)
    @pl.when((group & 1) == 0)
    def _():
        own = jnp.concatenate([scaled(gpu[2], mine), scaled(gpu[3], mine)], axis=0)
        share_ref[...] = mm_t(lp[0:128, :], own)

    @pl.when((group & 1) == 1)
    def _():
        second = mm_t(cells, lg[0:384, :])
        for k in range(9):
            share_ref[k * CH : (k + 1) * CH, :] = second[:, k * CH : (k + 1) * CH]

    inner_low = jnp.where(at_first, 0.0, 1.0)
    inner_high = jnp.where(at_last, 0.0, 1.0)

    def spread_source(e, j, ref):
        def source(delta, dt):
            if e - delta != 0:
                return None
            if dt == 0:
                return ref[j]
            before = scaled(ref[1], inner_low) if j == 2 else ref[2]
            after = ref[3] if j == 2 else scaled(ref[4], inner_high)
            return pick(before, after) if dt == 1 else pick(after, before)
        return source

    g_zero = jnp.where(at_first, gp[2], gp[4])
    g_end = jnp.where(at_first, gp[1], gp[3])
    g_zero, g_end = pick(g_zero, g_end), pick(g_end, g_zero)
    order_in = [(0, 2), (0, 3), (1, 2), (1, 3), (-1, 2), (-1, 3), None, None]
    for block, at in enumerate(order_in):
        if at is None:
            fill(lc, block, corner_source(block - 6, (g_zero, g_end)[block - 6]))
        else:
            fill(lc, block, spread_source(*at, gp if at[0] == -1 else gpu))
    back = mm(lc[...], w1t[...])
    part = [back[k * 64 : k * 64 + 64] for k in range(8)]
    at_zero, at_end = corner_sums(back[384:512])
    seams = mm(partner, jnp.concatenate([part[4], part[5]], axis=1).astype(BF))
    owe[0] = part[0] + seams[:, :CH] + pick_f(at_zero, at_end) * (1.0 - inner_low)
    owe[1] = part[2]
    owe[2] = part[1] + seams[:, CH:] + pick_f(at_end, at_zero) * (1.0 - inner_high)
    owe[3] = part[3]

    tile = jnp.concatenate([owe[k, pl.ds(pl.multiple_of(group * 16, 16), 16), :] for k in range(4)], axis=0)
    plan = [plan_ref[:, k : k + 1] for k in range(8)]
    flips = [jnp.zeros((48, 1), I32) for _ in range(2)]
    for which in range(4):
        for face_index in range(3):
            value = mirrored_in(fn_ref, rot_ref, 3 * group + face_index, which)
            for k in range(2):
                flips[k] = jnp.where(plan[6 + k] == which * 3 + face_index, value, flips[k])
    last = jnp.where(at_last, 1, 0)
    outer = jnp.logical_or(at_first, at_last)
    row_lane = jnp.where(flips[0] ^ last == plan[4], jnp.where(at_last, plan[1], plan[0]), -1)
    col_lane = jnp.where(flips[1] ^ last == plan[5], jnp.where(at_last, plan[3], plan[2]), -1)
    lanes = lax.broadcasted_iota(I32, (48, 64), 1)
    patch = (row_lane == lanes).astype(F32) + (col_lane == lanes).astype(F32)
    select = jnp.concatenate([jnp.where(outer, patch, sel_ref[0:48, :]), sel_ref[48:72, :]], axis=0)
    tail_ref[...] = mm(select.astype(BF), tile.astype(BF))


def tail_plan():
    select = np.zeros((72, 64), np.float32)
    plan = np.zeros((48, 8), np.int32)
    for pos in range(2):
        for depth in range(2):
            for face in range(3):
                lane = (pos * 2 + depth) * 16 + face
                for half in range(2):
                    select[half * 24 + (pos * 2 + depth) * 3 + face, lane + half * 3] = 1
                for side in range(2):
                    select[48 + ((pos * 2 + side) * 2 + depth) * 3 + face, lane + 6 + 3 * side] = 1
    for half in range(2):
        for side in range(2):
            for face in range(3):
                for row in range(2):
                    for col in range(2):
                        place = half * 24 + ((side * 3 + face) * 2 + row) * 2 + col
                        for last in range(2):
                            plan[place, last] = ((col ^ last) * 2 + row) * 16 + half * 3 + face
                            plan[place, 2 + last] = ((row ^ last) * 2 + col) * 16 + (2 + side) * 3 + face
                        plan[place, 4:] = side, half, half * 3 + face, (2 + side) * 3 + face
    return select, plan


def after_kernel(*refs):
    pass


def share_kernel(own_ref, other_ref, line_ref, tail_ref, sent, out_ref, total):
    total[...] = own_ref[...] + other_ref[...].astype(F32) + line_ref[...]
    for i in range(BANDS):
        start = 0 if i == 0 else 24 if i == BANDS - 1 else 48
        parts = [total[CHUNK * i : CHUNK * i + CHUNK, :], sent[i * 16 : i * 16 + 12, :], tail_ref[start : start + 24, :]]
        out_ref[i] = jnp.concatenate(parts, axis=0).astype(BF)


def order_selector():
    select = np.zeros((2, 64, 64), np.float32)
    for pos in range(2):
        for b in range(BANDS):
            select[0, 2 * b + pos, pos * 32 + b] = 1
            select[1, 63 - 2 * b - pos, pos * 32 + b] = 1
    return select


def reduce_kernel(in_ref, out_ref):
    total = in_ref[0, 0:48, :].astype(F32)
    for i in range(1, BANDS):
        total = total + in_ref[i, 0:48, :].astype(F32)
    out_ref[...] = total[0:SLOT_THREE]


def spread_kernel(factor, own_ref, other_ref, out_ref):
    total = ((own_ref[...] + other_ref[...]) * factor).astype(BF)
    for i in range(BANDS):
        out_ref[i] = total


def unpack_kernel(own_ref, other_ref, first_ref, second_ref):
    _, group = here()
    core = group & 1
    for i in range(BANDS):
        own, other = own_ref[i].astype(F32), other_ref[i].astype(F32)
        rows = slice(CHUNK * i, CHUNK * i + CHUNK)
        first_ref[rows, :] = jnp.where(core == 0, own, other)[0:CHUNK]
        second_ref[rows, :] = jnp.where(core == 0, other, own)[0:CHUNK]


def grad_kernel(fn_ref, rot_ref, sel_ref, in_ref, out_ref, wide, total):
    band, group = here()
    for i in range(BANDS):
        wide[i * 40 : i * 40 + 40, :] = in_ref[i].astype(F32)[32:SLOT_TWO]
    for q in range(2):
        for face in range(3):
            for row in range(2):
                piece = wide[pl.ds(4 + (q * 3 + face) * 2 + row, BANDS, stride=40), :]
                total[row, face, pl.ds(q, BANDS, stride=2), :] = piece
    tiles = [wide[pl.ds(pl.multiple_of(src * 40, 8), 40), :] for src in (band, BANDS - 1 - band)]
    outer = (band == 0) | (band == BANDS - 1)

    @pl.when(~outer)
    def _():
        for side in range(2):
            for face in range(3):
                flip = is_mirrored(fn_ref, rot_ref, 3 * group + face, 2 + side) == 1
                for row in range(2):
                    for depth in range(2):
                        column = depth if side == 0 else 63 - depth
                        k, m = [16 + ((pos * 2 + side) * 2 + depth) * 3 + face for pos in (row, 1 - row)]
                        extra = jnp.where(flip, tiles[1][m : m + 1, :], tiles[0][k : k + 1, :])
                        total[row, face, column : column + 1, :] += extra

    @pl.when(outer)
    def _():
        half = jnp.where(band == 0, 0, 1)
        patches = tiles[0] + tiles[1]
        place = lax.broadcasted_iota(I32, (SPAN, CH), 0)
        inner = (place >= 2) & (place < SPAN - 2)
        for face in range(3):
            order = sel_ref[is_mirrored(fn_ref, rot_ref, 3 * group + face, half)]
            for depth in range(2):
                halves = [wide[pl.ds(16 + (pos * 2 + depth) * 3 + face, BANDS, stride=40), :] for pos in range(2)]
                extra = mm(order, jnp.concatenate(halves, axis=0).astype(BF))
                total[depth ^ half, face] += jnp.where(inner, extra, 0.0)
                for side in range(2):
                    for col in range(2):
                        k = 16 + ((side * 3 + face) * 2 + depth) * 2 + col
                        column = 63 - col if side else col
                        total[depth ^ half, face, column : column + 1, :] += patches[k : k + 1, :]

    for row in range(2):
        for face in range(3):
            out_ref[face, row] = total[row, face].astype(BF)


def swapped(value, step):
    return lax.ppermute(value, "sub", [(i, i ^ step) for i in range(4)])


def body(field_in, grad_out, first_weight, second_weight, face_neighbour, seam_rotation, corner_fill):
    factor = (1.0 * 12 * SPAN * SPAN) ** -0.5
    seams = (face_neighbour.T, seam_rotation.T)
    in_smem = {0: "s", 1: "s"}
    select, plan = tail_plan()

    slots = call(
        pack_lines,
        jax.ShapeDtypeStruct((BANDS, SLOT_ONE, CH), BF),
        [
            pltpu.VMEM((2, 3, 2, SPAN, CH), BF),
            pltpu.VMEM(((SPAN + 4) * 12, CH), F32),
            pltpu.VMEM((STRIP, CH), F32),
            pltpu.SemaphoreType.DMA((2,)),
        ],
        tuple(pltpu.with_memory_space_constraint(value, pltpu.HBM) for value in (field_in, grad_out)),
        {0: "h", 1: "h"},
    )
    strips = lax.all_to_all(slots, "tile", 0, 0, tiled=True)
    lines = call(
        gather_lines,
        jax.ShapeDtypeStruct((WINDOW, ENDS, CH), BF),
        [],
        (*seams, jnp.asarray(line_selector(), BF), jnp.asarray(ends_selector(), BF), strips),
        in_smem,
    )
    lines = (lines, *[swapped(lines, step) for step in (1, 2, 3)])
    share = jax.ShapeDtypeStruct((HALF, CH), F32)
    own, away, sent = call(
        interior_kernel,
        [share, jax.ShapeDtypeStruct((HALF, CH), BF), jax.ShapeDtypeStruct((BANDS * 16, CH), F32)],
        [
            pltpu.VMEM((2304, CH), F32),
            pltpu.VMEM((384, CH), F32),
            pltpu.VMEM((1152, CH), BF),
            pltpu.VMEM((1152, CH), BF),
            pltpu.VMEM((1152, CH), F32),
            pltpu.VMEM((1152, CH), F32),
            pltpu.VMEM((BANDS * STRIP, CH), F32),
        ],
        (strips, first_weight, second_weight),
    )
    away = call(after_kernel, jax.ShapeDtypeStruct((HALF, CH), BF), [], (away, *lines[1:]), dict.fromkeys((0, 1, 2, 3, "o0"), "a"), {0: 0})
    other = swapped(away, 1)

    line, tails = call(
        main_kernel,
        [share, jax.ShapeDtypeStruct((72, CH), F32)],
        [
            pltpu.VMEM((1152, CH), BF),
            pltpu.VMEM((1152, CH), BF),
            pltpu.VMEM((4, WINDOW, 64, CH), BF),
            pltpu.VMEM((WINDOW, 64, CH), BF),
            pltpu.VMEM((2, 5, 5, 64, CH), BF),
            pltpu.VMEM((256, 1152), BF),
            pltpu.VMEM((640, 1152), BF),
            pltpu.VMEM((512, 1152), BF),
            pltpu.VMEM((5, 64, CH), F32),
            pltpu.VMEM((5, 64, CH), BF),
            pltpu.VMEM((5, 64, CH), BF),
            pltpu.VMEM((4, 64, CH), F32),
        ],
        (*seams, corner_fill.T, jnp.asarray(plan), jnp.asarray(select, F32), *lines, first_weight, second_weight),
    )
    slots = call(
        share_kernel,
        jax.ShapeDtypeStruct((BANDS, SLOT_TWO, CH), BF),
        [pltpu.VMEM((HALF, CH), F32)],
        (own, other, line, tails, sent),
    )
    slots = lax.all_to_all(slots, "tile", 0, 0, tiled=True)
    part = call(reduce_kernel, jax.ShapeDtypeStruct((SLOT_THREE, CH), F32), [], (slots,))
    reduced = call(
        lambda *refs: spread_kernel(factor, *refs),
        jax.ShapeDtypeStruct((BANDS, SLOT_THREE, CH), BF),
        [],
        (part, swapped(part, 2)),
    )
    reduced = lax.all_to_all(reduced, "tile", 0, 0, tiled=True)
    swap = swapped(reduced, 1)
    grad_in = call(
        grad_kernel,
        jax.ShapeDtypeStruct((3, 2, SPAN, CH), BF),
        [pltpu.VMEM((BANDS * 40, CH), F32), pltpu.VMEM((2, 3, SPAN, CH), F32)],
        (*seams, jnp.asarray(order_selector(), BF), slots),
        in_smem,
    )
    first, second = call(
        unpack_kernel,
        [jax.ShapeDtypeStruct((1152, CH), F32), jax.ShapeDtypeStruct((1152, CH), F32)],
        [],
        (reduced, swap),
    )
    return grad_in, first.reshape(3, 3, CH, CH), second.reshape(3, 3, CH, CH)


def solution(mesh):
    return jax.shard_map(
        body,
        mesh=mesh,
        in_specs=(P("sub", "tile", None, None), P("sub", "tile", None, None), P(), P(), P(), P(), P()),
        out_specs=(P("sub", "tile", None, None), P(), P()),
        check_vma=False,
    )
```

```python
import jax
import jax.numpy as jnp
import numpy as np
from jax import lax
from jax.experimental import pallas as pl
from jax.experimental.pallas import tpu as pltpu
from jax.sharding import PartitionSpec as P

BF = jnp.bfloat16
F32 = jnp.float32
I32 = jnp.int32
BANDS = 32
SPAN = 64
CH = 128
TAPS = [(a, b) for a in range(3) for b in range(3)]
WINDOW = 6
ENDS = 48
STRIP = 12 * WINDOW
UNIT = 48
SLOT_ONE = UNIT + STRIP
HALF = 9 * CH
CHUNK = 36
SLOT_TWO = 80
SLOT_THREE = 40
VMEM_BYTES = 48 * 1024 * 1024


def mm(left, right):
    return jnp.dot(left, right, preferred_element_type=F32)


def mm_t(left, right):
    return lax.dot_general(left, right, (((0,), (0,)), ((), ())), preferred_element_type=F32)


def call(kernel, outs, scratch, operands, places=(), aliases=None):
    kinds = {"v": pltpu.VMEM, "s": pltpu.SMEM, "h": pltpu.HBM, "a": pl.ANY}
    places = dict(places)
    many = isinstance(outs, (list, tuple))
    out_specs = [pl.BlockSpec(memory_space=kinds[places.get(f"o{k}", "v")]) for k in range(len(outs) if many else 1)]
    return pl.pallas_call(
        kernel,
        out_shape=outs,
        in_specs=[pl.BlockSpec(memory_space=kinds[places.get(k, "v")]) for k in range(len(operands))],
        out_specs=out_specs if many else out_specs[0],
        scratch_shapes=scratch,
        input_output_aliases=aliases or {},
        compiler_params=pltpu.CompilerParams(vmem_limit_bytes=VMEM_BYTES),
    )(*operands)


def here():
    return lax.axis_index("tile"), lax.axis_index("sub")


def is_mirrored(fn_ref, rot_ref, face, side):
    rot = rot_ref[face, side]
    partner = 4 * fn_ref[face, side] + (rot & 3)
    return jnp.where(4 * face + side > partner, rot >> 2, 0)


def is_mirrored(fn_ref, rot_ref, face, side):
    rot = rot_ref[side, face]
    partner = 4 * fn_ref[side, face] + (rot & 3)
    return jnp.where(4 * face + side > partner, rot >> 2, 0)


def mirrored_in(fn_ref, rot_ref, face, side):
    lane = lax.broadcasted_iota(I32, (1, 12), 1) == face
    rot = jnp.sum(jnp.where(lane, rot_ref[side : side + 1, :], 0))
    partner = 4 * jnp.sum(jnp.where(lane, fn_ref[side : side + 1, :], 0)) + (rot & 3)
    return jnp.where(4 * face + side > partner, rot >> 2, 0)


def unit_of(band):
    unit = band - 4
    strip = (unit * 43) >> 7
    return strip, unit - 3 * strip


def pack_lines(f_hbm, g_hbm, fn_hbm, rot_hbm, out_ref, buf, fn_ref, rot_ref, wide, ends, sems):
    moves = ((f_hbm, buf.at[0]), (g_hbm, buf.at[1]), (fn_hbm, fn_ref), (rot_hbm, rot_ref))
    copies = [pltpu.make_async_copy(src, dst, sems.at[k]) for k, (src, dst) in enumerate(moves)]
    for copy in copies:
        copy.start()
    band, group = here()
    ends[ENDS:STRIP, :] = jnp.zeros((STRIP - ENDS, CH), F32)
    for fld in range(2):
        copies[fld].wait()
        for row in range(2):
            for face in range(3):
                block = buf[fld, face, row].astype(F32)
                wide[pl.ds(24 + fld * 6 + row * 3 + face, SPAN, stride=12), :] = block
                for edge, cols in enumerate(((0, 1), (63, 62))):
                    for depth, col in enumerate(cols):
                        place = row * 24 + fld * 12 + edge * 6 + depth * 3 + face
                        ends[place : place + 1, :] = block[col : col + 1, :]
    wide[0:24, :] = wide[SPAN * 12 : SPAN * 12 + 24, :]
    wide[SPAN * 12 + 24 : SPAN * 12 + 48, :] = wide[24:48, :]
    for copy in copies[2:]:
        copy.wait()
    side = jnp.where(band == 0, 0, 1)
    row = lax.broadcasted_iota(I32, (STRIP, CH), 0)
    row = row - 3 * ((row * 43) >> 7)
    flip = jnp.zeros((STRIP, CH), I32)
    for face in range(3):
        flip = jnp.where(row == face, is_mirrored(fn_ref, rot_ref, 3 * group + face, side), flip)
    outer = (band == 0) | (band == BANDS - 1)
    strips = [wide[24 * d : 24 * d + STRIP, :] for d in range(BANDS)]
    for d in range(BANDS):
        strip, face = unit_of(d)
        unit = wide[pl.ds(96 * strip + face, UNIT, stride=3), :] if 4 <= d < 28 else ends[0:ENDS, :]
        line = jnp.where(flip == 1, strips[BANDS - 1 - d], strips[d])
        out_ref[d] = jnp.concatenate([unit, jnp.where(outer, line, ends[...])], axis=0).astype(BF)


def line_selector():
    select = np.zeros((2, WINDOW * ENDS, 2 * STRIP + 6 * ENDS), np.float32)
    for mirrored in range(2):
        for j in range(WINDOW):
            part, parity = j // 2, j % 2
            for fld in range(2):
                for depth in range(2):
                    for face in range(3):
                        base = j * ENDS + (fld * 2 + depth) * 12 + face
                        column = (5 - j if mirrored else j) * 12 + fld * 6 + face
                        select[mirrored, base, column + depth * 3] = 1
                        select[mirrored, base + 3, STRIP + column + (1 - depth) * 3] = 1
                        for side in range(2):
                            source = 2 * STRIP + (3 * mirrored + part) * ENDS + (1 - parity if mirrored else parity) * 24
                            select[mirrored, base + 6 + 3 * side, source + fld * 12 + side * 6 + depth * 3 + face] = 1
    return select


def gather_lines(fn_ref, rot_ref, sel_ref, in_ref, out_ref):
    band, group = here()
    pieces = [in_ref[d].astype(F32)[UNIT:SLOT_ONE] for d in (0, BANDS - 1)]
    for source in [band + 31 + part for part in range(3)] + [64 - band - part for part in range(3)]:
        source = source & 31
        outer = (source == 0) | (source == BANDS - 1)
        pieces.append(jnp.where(outer, in_ref[source, 0:ENDS, :], in_ref[source, UNIT : UNIT + ENDS, :]).astype(F32))
    pieces = jnp.concatenate(pieces, axis=0).astype(BF)
    place = lax.broadcasted_iota(I32, (WINDOW * ENDS, 1), 0)
    place = place - 12 * ((place * 171) >> 11)
    flip = jnp.zeros((WINDOW * ENDS, 1), I32)
    for side in range(4):
        for face in range(3):
            flip = jnp.where(place == side * 3 + face, is_mirrored(fn_ref, rot_ref, 3 * group + face, side), flip)
    flip = jnp.broadcast_to(flip.astype(F32), sel_ref.shape[1:]).astype(BF)
    picked = mm(sel_ref[0] * (1 - flip) + sel_ref[1] * flip, pieces).astype(BF)
    for j in range(WINDOW):
        out_ref[j] = picked[j * ENDS : (j + 1) * ENDS]


def silu_parts(pre):
    logistic = 1.0 / (1.0 + jnp.exp(-pre))
    return pre * logistic, logistic * (1.0 + pre * (1.0 - logistic))


def side_frame(side, tap):
    dr, dc = tap[0] - 1, tap[1] - 1
    return ((dr, dc), (-dr, dc), (dc, dr), (-dc, dr))[side]


def transpose_weights(ref, out):
    for k, (a, b) in enumerate(TAPS):
        out[k * CH : (k + 1) * CH, :] = ref[a, b].T


def interior_kernel(
    in_ref, w1_ref, w2_ref, own_ref, away_ref, sent, acc, done, w1t, w2t, f2, g2, wide
):
    band, group = here()
    strip, _ = unit_of(band)
    transpose_weights(w1_ref, w1t)
    transpose_weights(w2_ref, w2t)
    for s in range(BANDS):
        wide[s * UNIT : (s + 1) * UNIT, :] = in_ref[s, 0:UNIT, :].astype(F32)
    for q in range(12):
        for fld, target in enumerate((f2, g2)):
            for row in range(2):
                piece = wide[pl.ds(q * 4 + fld * 2 + row, BANDS, stride=UNIT), :]
                target[pl.ds(q * 64 + row, BANDS, stride=2), :] = piece

    def conv_weights(ref):
        return jnp.concatenate([ref[a].reshape(3 * CH, CH) for a in range(3)], axis=1)

    def back_weights(ref):
        columns = []
        for a in range(3):
            columns.append(jnp.concatenate([ref[(a * 3 + b) * CH : (a * 3 + b + 1) * CH, :] for b in (2, 1, 0)], axis=0))
        return jnp.concatenate(columns, axis=1)

    def up_one(value):
        return pltpu.roll(value, value.shape[0] - 1, 0)

    def down_one(value):
        return pltpu.roll(value, 1, 0)

    def three_columns(ref, first, count):
        return jnp.concatenate([ref[first + 64 * b : first + 64 * b + count, :].astype(BF) for b in range(3)], axis=1)

    y = mm(three_columns(f2, 0, 640), conv_weights(w1_ref))
    pre = down_one(y[:, :CH]) + y[:, CH : 2 * CH] + up_one(y[:, 2 * CH :])
    z = mm(three_columns(g2, 0, 640), back_weights(w2t))
    back = up_one(z[:, :CH]) + z[:, CH : 2 * CH] + down_one(z[:, 2 * CH :])
    hidden, slope = silu_parts(pre)
    index = lax.broadcasted_iota(I32, (640, CH), 0)
    col = 8 * strip - 1 + (index >> 6)
    row = index & 63
    inner = (row >= 1) & (row <= 62) & (col >= 1) & (col <= 62) & (band >= 4) & (band < 28)
    gpre = jnp.where(inner, back * slope, 0.0).astype(BF)
    hid = jnp.where(inner, hidden, 0.0)[64:576].astype(BF)

    gown = gpre[64:576].astype(F32)
    gcat = jnp.concatenate([up_one(gown).astype(BF), gpre[64:576], down_one(gown).astype(BF)], axis=1)
    first = mm_t(three_columns(f2, 64, 512), gcat)
    hown = hid.astype(F32)
    hcat = jnp.concatenate([down_one(hown).astype(BF), hid, up_one(hown).astype(BF)], axis=1)
    gback = jnp.concatenate([g2[start : start + 512, :].astype(BF) for start in (192, 128, 64)], axis=1)
    second = mm_t(hcat, gback)
    for k, (a, b) in enumerate(TAPS):
        top, low = k * CH, 1152 + k * CH
        acc[top : top + CH, :] = first[b * CH : (b + 1) * CH, a * CH : (a + 1) * CH]
        acc[low : low + CH, :] = second[a * CH : (a + 1) * CH, b * CH : (b + 1) * CH]
    core = group & 1
    own_ref[...] = acc[pl.ds(pl.multiple_of(core * HALF, CH), HALF), :]
    away_ref[...] = acc[pl.ds(pl.multiple_of((1 - core) * HALF, CH), HALF), :].astype(BF)

    gthree = jnp.concatenate([gpre[0:512], gpre[64:576], gpre[128:640]], axis=1)
    z = mm(gthree, back_weights(w1t))
    done[...] = up_one(z[:, :CH]) + z[:, CH : 2 * CH] + down_one(z[:, 2 * CH :]) + g2[128:640, :]
    for q in range(8):
        for row in range(2):
            sent[pl.ds(q * 2 + row, BANDS, stride=16), :] = done[pl.ds(q * 64 + row, BANDS, stride=2), :]


def main_kernel(
    fn_ref, rot_ref, fill_ref, plan_ref, sel_ref, own_ref, one_ref, two_ref, three_ref, w1_ref, w2_ref,
    share_ref, tail_ref,
    w1t, w2t, xs, hal, nb, lp, lg, lc, ss, gp, gpu, owe,
):
    band, group = here()
    transpose_weights(w1_ref, w1t)
    transpose_weights(w2_ref, w2t)

    line = lax.broadcasted_iota(I32, (64, 1), 0)
    place = line & 15
    side = (place >= 3).astype(I32) + (place >= 6).astype(I32) + (place >= 9).astype(I32)
    face = place - 3 * side
    home = line - place
    real = place < 12
    lane = lax.broadcasted_iota(I32, (64, 64), 1)

    def one_hot(target, keep):
        return (jnp.where(keep & real, target, -1) == lane).astype(F32).astype(BF)

    face_lane = lax.broadcasted_iota(I32, (64, 12), 1)
    faces = (jnp.where(real, 3 * (line >> 4) + face, -1) == face_lane).astype(F32).astype(BF)

    def by_line(ref, columns):
        table = ref[...].astype(F32).astype(BF)
        rows = lax.dot_general(faces, table, (((1,), (1,)), ((), ())), preferred_element_type=F32).astype(I32)
        value = rows[:, columns[0] : columns[0] + 1]
        for s in range(1, 4):
            value = jnp.where(side == s, rows[:, columns[s] : columns[s] + 1], value)
        return value

    fn = by_line(fn_ref, (0, 1, 2, 3))
    rot = by_line(rot_ref, (0, 1, 2, 3))
    fn_group = (fn * 43) >> 7
    partner = one_hot(fn_group * 16 + (rot & 3) * 3 + (fn - 3 * fn_group), real)
    number = 4 * (3 * (line >> 4) + face) + side
    flip = ((rot >> 2) == 1) & (number > 4 * fn + (rot & 3)) & real
    fills = []
    for columns in ((0, 2, 0, 1), (1, 3, 2, 3)):
        m = by_line(fill_ref, columns)
        mf = m >> 2
        mg = (mf * 43) >> 7
        target = mg * 16 + ((m >> 1) & 1) * 3 + (mf - 3 * mg)
        fills.append((one_hot(target, (m & 1) == 0), one_hot(target, (m & 1) == 1)))
    corner_cells = jnp.concatenate([jnp.concatenate(pair, axis=1) for pair in fills], axis=0)
    corner_back = corner_cells.astype(F32).T.astype(BF)
    even = (side & 1) == 0
    low_side = jnp.where(side < 2, 2, 0)
    high_side = jnp.where(side < 2, 3, 1)
    beside = jnp.concatenate([
        jnp.concatenate([one_hot(home + other * 3 + face, even), one_hot(home + other * 3 + face, ~even)], axis=1)
        for other in (low_side, high_side)
    ], axis=0)
    side_mask = [jnp.broadcast_to((side == s).astype(F32), (64, CH)).astype(BF) > 0.5 for s in range(4)]
    row_line = (side < 2).astype(F32)
    flip_f = jnp.broadcast_to(flip.astype(F32), (64, CH))
    flip_b = flip_f.astype(BF) > 0.5

    def pick(plain, mirrored):
        return jnp.where(flip_b, mirrored, plain)

    def pick_f(plain, mirrored):
        return jnp.where(flip_f > 0.5, mirrored, plain)

    arrived = (own_ref, one_ref, two_ref, three_ref)
    arrived = [jnp.concatenate([ref[j] for ref in arrived], axis=0) for j in range(WINDOW)]
    row = lax.broadcasted_iota(I32, (256, 1), 0)
    source = (((row >> 4) & 3) ^ group) * ENDS + (row >> 6) * 12 + (row & 15)
    source = jnp.where((row & 15) < 12, source, -1)
    expand = (source == lax.broadcasted_iota(I32, (256, 4 * ENDS), 1)).astype(F32).astype(BF)
    arrived = mm(expand, jnp.concatenate(arrived, axis=1)).astype(BF)
    for j in range(WINDOW):
        for block in range(4):
            xs[block, j] = arrived[block * 64 : block * 64 + 64, j * CH : (j + 1) * CH]
    halos = mm(partner, jnp.concatenate([xs[0, j] for j in range(WINDOW)], axis=1)).astype(BF)
    for j in range(WINDOW):
        hal[j] = halos[:, j * CH : (j + 1) * CH]

    def block_at(block, j):
        return hal[j] if block == 0 else xs[block - 1, j]

    for block in range(5):
        for j in range(1, 5):
            before, after = block_at(block, j - 1), block_at(block, j + 1)
            nb[0, block, j] = pick(before, after)
            nb[1, block, j] = pick(after, before)
    at_first, at_last = band == 0, band == BANDS - 1

    def line_ends(value, lower, upper, choice):
        zero = jnp.where(at_last, value(lower + 2), value(lower))
        end = jnp.where(at_last, value(upper + 2), value(upper))
        return choice(zero, end), choice(end, zero)

    h_zero, h_end = line_ends(lambda j: hal[j], 2, 1, pick)
    h_one, h_last = line_ends(lambda j: hal[j], 3, 0, pick)
    f_zero, f_end = line_ends(lambda j: xs[0, j], 2, 1, pick)
    none = jnp.zeros((64, CH), BF)
    cells = mm(corner_cells, jnp.concatenate([f_zero, f_end], axis=0)).astype(BF)
    sides = jnp.concatenate([jnp.concatenate([h_zero, h_one], axis=1), jnp.concatenate([h_end, h_last], axis=1)], axis=0)
    sides = mm(beside, sides).astype(BF)
    low = [cells[:64], sides[:64, :CH], sides[:64, CH:], none, none]
    high = [cells[64:], sides[64:, :CH], sides[64:, CH:], none, none]
    for block in range(5):
        for slot, here_now in ((2, at_first), (4, at_last)):
            before, after = nb[0, block, slot], nb[1, block, slot]
            nb[0, block, slot] = jnp.where(here_now, pick(low[block], before), before)
            nb[1, block, slot] = jnp.where(here_now, pick(after, high[block]), after)
            before, after = nb[0, block, slot - 1], nb[1, block, slot - 1]
            nb[0, block, slot - 1] = jnp.where(here_now, pick(before, low[block]), before)
            nb[1, block, slot - 1] = jnp.where(here_now, pick(high[block], after), after)
    corner_grad = line_ends(lambda j: xs[2, j], 2, 1, pick)

    def choose(options):
        whole = all(option is not None for option in options)
        result = options[0] if whole else jnp.zeros((64, CH), BF)
        for s, option in enumerate(options):
            if option is not None and not (whole and s == 0):
                result = jnp.where(side_mask[s], option, result)
        return result

    def fill(target, block, source):
        for k, tap in enumerate(TAPS):
            target[block * 64 : block * 64 + 64, k * CH : (k + 1) * CH] = choose(
                [source(*side_frame(s, tap)) for s in range(4)]
            )

    def field_source(j):
        def source(delta, dt):
            return block_at(delta + 1, j) if dt == 0 else nb[(dt + 1) // 2, delta + 1, j]
        return source

    def grad_source(e, j):
        def source(delta, dt):
            depth = e - delta
            if depth not in (0, 1):
                return None
            return xs[2 + depth, j] if dt == 0 else nb[(1 - dt) // 2, 3 + depth, j]
        return source

    def corner_source(which, value):
        def source(delta, dt):
            return value if (delta, dt) == (-1, 2 * which - 1) else None
        return source

    order_pre = (2, 3, 1, 4)
    for block, j in enumerate(order_pre):
        fill(lp, block, field_source(j))
    order_back = [(0, 2), (0, 3), (-1, 2), (-1, 3), None, None, (0, 1), (0, 4), (-1, 1), (-1, 4)]
    for block, at in enumerate(order_back):
        fill(lg, block, corner_source(block - 4, corner_grad[block - 4]) if at is None else grad_source(*at))

    pre = mm(lp[...], w1_ref[...].reshape(9 * CH, CH))
    back = mm(lg[...], w2t[...])

    def back_block(e, j):
        block = order_back.index((e, j))
        return back[block * 64 : block * 64 + 64]

    seams = jnp.concatenate([back_block(-1, j).astype(BF) for j in range(1, 5)], axis=1)
    seams = mm(partner, seams)
    for j in range(1, 5):
        ss[j] = seams[:, (j - 1) * CH : j * CH]
    both_rows = jnp.concatenate([row_line, row_line], axis=0)

    def corner_sums(both):
        sums = mm(corner_back, (both * both_rows).astype(BF))
        return sums[:64], sums[64:]


    at_zero, at_end = corner_sums(back[256:384])
    head, tail = line_ends(lambda j: ss[j], 2, 1, pick_f)
    head, tail = head + at_zero, tail + at_end
    sides = mm(beside, jnp.concatenate([head, tail], axis=0).astype(BF))
    head, tail = head + sides[:64], tail + sides[64:]
    for slot, here_now in ((2, at_first), (4, at_last)):
        ss[slot] = jnp.where(here_now, pick_f(head, tail), ss[slot])
        ss[slot - 1] = jnp.where(here_now, pick_f(tail, head), ss[slot - 1])

    unique = {}
    hid = {}
    for block, j in enumerate(order_pre):
        value = pre[block * 64 : block * 64 + 64]
        hidden, slope = silu_parts(value)
        t = (2 * band - 2 + j) & (SPAN - 1)
        corner = jnp.logical_or(t == 0, t == SPAN - 1)
        unique[j] = jnp.where(corner, row_line, jnp.ones_like(row_line))
        grad = ((back_block(0, j) + ss[j]) * slope).astype(BF)
        gp[j] = grad
        gpu[j] = (grad.astype(F32) * unique[j]).astype(BF)
        hid[j] = hidden.astype(BF)

    mine = ((line >> 5) == (group >> 1)).astype(F32)
    edge = jnp.where(band == 0, 1.0, 0.0) * mine * row_line

    def scaled(value, factor):
        return (value.astype(F32) * factor).astype(BF)

    h_zero, h_end = pick(hid[2], hid[1]), pick(hid[1], hid[2])
    halos = mm(partner, jnp.concatenate([hid[2], hid[3]], axis=1))
    ends = mm(corner_cells, jnp.concatenate([h_zero, h_end], axis=0))
    cells = jnp.concatenate([
        scaled(hid[2], mine * unique[2]),
        scaled(hid[3], mine * unique[3]),
        scaled(halos[:, :CH], mine),
        scaled(halos[:, CH:], mine),
        scaled(ends[:64], edge),
        scaled(ends[64:], edge),
    ], axis=0)
    @pl.when((group & 1) == 0)
    def _():
        own = jnp.concatenate([scaled(gpu[2], mine), scaled(gpu[3], mine)], axis=0)
        share_ref[...] = mm_t(lp[0:128, :], own)

    @pl.when((group & 1) == 1)
    def _():
        second = mm_t(cells, lg[0:384, :])
        for k in range(9):
            share_ref[k * CH : (k + 1) * CH, :] = second[:, k * CH : (k + 1) * CH]

    inner_low = jnp.where(at_first, 0.0, 1.0)
    inner_high = jnp.where(at_last, 0.0, 1.0)

    def spread_source(e, j, ref):
        def source(delta, dt):
            if e - delta != 0:
                return None
            if dt == 0:
                return ref[j]
            before = scaled(ref[1], inner_low) if j == 2 else ref[2]
            after = ref[3] if j == 2 else scaled(ref[4], inner_high)
            return pick(before, after) if dt == 1 else pick(after, before)
        return source

    g_zero = jnp.where(at_first, gp[2], gp[4])
    g_end = jnp.where(at_first, gp[1], gp[3])
    g_zero, g_end = pick(g_zero, g_end), pick(g_end, g_zero)
    order_in = [(0, 2), (0, 3), (1, 2), (1, 3), (-1, 2), (-1, 3), None, None]
    for block, at in enumerate(order_in):
        if at is None:
            fill(lc, block, corner_source(block - 6, (g_zero, g_end)[block - 6]))
        else:
            fill(lc, block, spread_source(*at, gp if at[0] == -1 else gpu))
    back = mm(lc[...], w1t[...])
    part = [back[k * 64 : k * 64 + 64] for k in range(8)]
    at_zero, at_end = corner_sums(back[384:512])
    seams = mm(partner, jnp.concatenate([part[4], part[5]], axis=1).astype(BF))
    owe[0] = part[0] + seams[:, :CH] + pick_f(at_zero, at_end) * (1.0 - inner_low)
    owe[1] = part[2]
    owe[2] = part[1] + seams[:, CH:] + pick_f(at_end, at_zero) * (1.0 - inner_high)
    owe[3] = part[3]

    tile = jnp.concatenate([owe[k, pl.ds(pl.multiple_of(group * 16, 16), 16), :] for k in range(4)], axis=0)
    plan = [plan_ref[:, k : k + 1] for k in range(8)]
    flips = [jnp.zeros((48, 1), I32) for _ in range(2)]
    for which in range(4):
        for face_index in range(3):
            value = mirrored_in(fn_ref, rot_ref, 3 * group + face_index, which)
            for k in range(2):
                flips[k] = jnp.where(plan[6 + k] == which * 3 + face_index, value, flips[k])
    last = jnp.where(at_last, 1, 0)
    outer = jnp.logical_or(at_first, at_last)
    row_lane = jnp.where(flips[0] ^ last == plan[4], jnp.where(at_last, plan[1], plan[0]), -1)
    col_lane = jnp.where(flips[1] ^ last == plan[5], jnp.where(at_last, plan[3], plan[2]), -1)
    lanes = lax.broadcasted_iota(I32, (48, 64), 1)
    patch = (row_lane == lanes).astype(F32) + (col_lane == lanes).astype(F32)
    select = jnp.concatenate([jnp.where(outer, patch, sel_ref[0:48, :]), sel_ref[48:72, :]], axis=0)
    tail_ref[...] = mm(select.astype(BF), tile.astype(BF))


def tail_plan():
    select = np.zeros((72, 64), np.float32)
    plan = np.zeros((48, 8), np.int32)
    for pos in range(2):
        for depth in range(2):
            for face in range(3):
                lane = (pos * 2 + depth) * 16 + face
                for half in range(2):
                    select[half * 24 + (pos * 2 + depth) * 3 + face, lane + half * 3] = 1
                for side in range(2):
                    select[48 + ((pos * 2 + side) * 2 + depth) * 3 + face, lane + 6 + 3 * side] = 1
    for half in range(2):
        for side in range(2):
            for face in range(3):
                for row in range(2):
                    for col in range(2):
                        place = half * 24 + ((side * 3 + face) * 2 + row) * 2 + col
                        for last in range(2):
                            plan[place, last] = ((col ^ last) * 2 + row) * 16 + half * 3 + face
                            plan[place, 2 + last] = ((row ^ last) * 2 + col) * 16 + (2 + side) * 3 + face
                        plan[place, 4:] = side, half, half * 3 + face, (2 + side) * 3 + face
    return select, plan


def after_kernel(*refs):
    pass


def share_kernel(own_ref, other_ref, line_ref, tail_ref, sent, out_ref, total):
    total[...] = own_ref[...] + other_ref[...].astype(F32) + line_ref[...]
    for i in range(BANDS):
        start = 0 if i == 0 else 24 if i == BANDS - 1 else 48
        parts = [total[CHUNK * i : CHUNK * i + CHUNK, :], sent[i * 16 : i * 16 + 16, :], tail_ref[start : start + 24, :]]
        parts.append(jnp.zeros((4, CH), F32))
        out_ref[i] = jnp.concatenate(parts, axis=0).astype(BF)


def order_selector():
    select = np.zeros((2, 64, 64), np.float32)
    for pos in range(2):
        for b in range(BANDS):
            select[0, 2 * b + pos, pos * 32 + b] = 1
            select[1, 63 - 2 * b - pos, pos * 32 + b] = 1
    return select


def reduce_kernel(in_ref, out_ref):
    total = in_ref[0, 0:48, :].astype(F32)
    for i in range(1, BANDS):
        total = total + in_ref[i, 0:48, :].astype(F32)
    out_ref[...] = total[0:SLOT_THREE]


def spread_kernel(factor, own_ref, other_ref, out_ref):
    total = ((own_ref[...] + other_ref[...]) * factor).astype(BF)
    for i in range(BANDS):
        out_ref[i] = total


def unpack_kernel(own_ref, other_ref, first_ref, second_ref):
    _, group = here()
    core = group & 1
    for i in range(BANDS):
        own, other = own_ref[i].astype(F32), other_ref[i].astype(F32)
        rows = slice(CHUNK * i, CHUNK * i + CHUNK)
        first_ref[rows, :] = jnp.where(core == 0, own, other)[0:CHUNK]
        second_ref[rows, :] = jnp.where(core == 0, other, own)[0:CHUNK]


def grad_kernel(fn_ref, rot_ref, sel_ref, in_ref, out_ref, wide, total):
    band, group = here()
    for i in range(BANDS):
        wide[i * 48 : i * 48 + 48, :] = in_ref[i, 32:SLOT_TWO, :].astype(F32)
    for face in range(3):
        for row in range(2):
            for q in range(8):
                piece = wide[pl.ds((4 + face) * 48 + 4 + q * 2 + row, 8, stride=144), :]
                total[row, face, pl.ds(q, 8, stride=8), :] = piece
    tiles = [wide[pl.ds(pl.multiple_of(src * 48, 16), 48), :] for src in (band, BANDS - 1 - band)]
    outer = (band == 0) | (band == BANDS - 1)

    @pl.when(~outer)
    def _():
        for side in range(2):
            for face in range(3):
                flip = is_mirrored(fn_ref, rot_ref, 3 * group + face, 2 + side) == 1
                for row in range(2):
                    for depth in range(2):
                        column = depth if side == 0 else 63 - depth
                        k, m = [20 + ((pos * 2 + side) * 2 + depth) * 3 + face for pos in (row, 1 - row)]
                        extra = jnp.where(flip, tiles[1][m : m + 1, :], tiles[0][k : k + 1, :])
                        total[row, face, column : column + 1, :] += extra

    @pl.when(outer)
    def _():
        half = jnp.where(band == 0, 0, 1)
        patches = tiles[0] + tiles[1]
        place = lax.broadcasted_iota(I32, (SPAN, CH), 0)
        inner = (place >= 2) & (place < SPAN - 2)
        for face in range(3):
            order = sel_ref[is_mirrored(fn_ref, rot_ref, 3 * group + face, half)]
            for depth in range(2):
                halves = [wide[pl.ds(20 + (pos * 2 + depth) * 3 + face, BANDS, stride=48), :] for pos in range(2)]
                extra = mm(order, jnp.concatenate(halves, axis=0).astype(BF))
                total[depth ^ half, face] += jnp.where(inner, extra, 0.0)
                for side in range(2):
                    for col in range(2):
                        k = 20 + ((side * 3 + face) * 2 + depth) * 2 + col
                        column = 63 - col if side else col
                        total[depth ^ half, face, column : column + 1, :] += patches[k : k + 1, :]

    for row in range(2):
        for face in range(3):
            out_ref[face, row] = total[row, face].astype(BF)


def swapped(value, step):
    return lax.ppermute(value, "sub", [(i, i ^ step) for i in range(4)])


def body(field_in, grad_out, first_weight, second_weight, face_neighbour, seam_rotation, corner_fill):
    factor = (1.0 * 12 * SPAN * SPAN) ** -0.5
    seams = (face_neighbour.T, seam_rotation.T)
    in_smem = {0: "s", 1: "s"}
    select, plan = tail_plan()

    slots = call(
        pack_lines,
        jax.ShapeDtypeStruct((BANDS, SLOT_ONE, CH), BF),
        [
            pltpu.VMEM((2, 3, 2, SPAN, CH), BF),
            pltpu.SMEM((4, 12), I32),
            pltpu.SMEM((4, 12), I32),
            pltpu.VMEM(((SPAN + 4) * 12, CH), F32),
            pltpu.VMEM((STRIP, CH), F32),
            pltpu.SemaphoreType.DMA((4,)),
        ],
        tuple(pltpu.with_memory_space_constraint(value, pltpu.HBM) for value in (field_in, grad_out, *seams)),
        dict.fromkeys(range(4), "h"),
    )
    strips = lax.all_to_all(slots, "tile", 0, 0, tiled=True)
    lines = call(
        gather_lines,
        jax.ShapeDtypeStruct((WINDOW, ENDS, CH), BF),
        [],
        (*seams, jnp.asarray(line_selector(), BF), strips),
        in_smem,
    )
    lines = (lines, *[swapped(lines, step) for step in (1, 2, 3)])
    share = jax.ShapeDtypeStruct((HALF, CH), F32)
    own, away, sent = call(
        interior_kernel,
        [share, jax.ShapeDtypeStruct((HALF, CH), BF), jax.ShapeDtypeStruct((BANDS * 16, CH), F32)],
        [
            pltpu.VMEM((2304, CH), F32),
            pltpu.VMEM((512, CH), F32),
            pltpu.VMEM((1152, CH), BF),
            pltpu.VMEM((1152, CH), BF),
            pltpu.VMEM((768, CH), F32),
            pltpu.VMEM((768, CH), F32),
            pltpu.VMEM((BANDS * UNIT, CH), F32),
        ],
        (strips, first_weight, second_weight),
    )
    away = call(after_kernel, jax.ShapeDtypeStruct((HALF, CH), BF), [], (away, *lines[1:]), dict.fromkeys((0, 1, 2, 3, "o0"), "a"), {0: 0})
    other = swapped(away, 1)

    line, tails = call(
        main_kernel,
        [share, jax.ShapeDtypeStruct((72, CH), F32)],
        [
            pltpu.VMEM((1152, CH), BF),
            pltpu.VMEM((1152, CH), BF),
            pltpu.VMEM((4, WINDOW, 64, CH), BF),
            pltpu.VMEM((WINDOW, 64, CH), BF),
            pltpu.VMEM((2, 5, 5, 64, CH), BF),
            pltpu.VMEM((256, 1152), BF),
            pltpu.VMEM((640, 1152), BF),
            pltpu.VMEM((512, 1152), BF),
            pltpu.VMEM((5, 64, CH), F32),
            pltpu.VMEM((5, 64, CH), BF),
            pltpu.VMEM((5, 64, CH), BF),
            pltpu.VMEM((4, 64, CH), F32),
        ],
        (*seams, corner_fill.T, jnp.asarray(plan), jnp.asarray(select, F32), *lines, first_weight, second_weight),
    )
    slots = call(
        share_kernel,
        jax.ShapeDtypeStruct((BANDS, SLOT_TWO, CH), BF),
        [pltpu.VMEM((HALF, CH), F32)],
        (own, other, line, tails, sent),
    )
    slots = lax.all_to_all(slots, "tile", 0, 0, tiled=True)
    part = call(reduce_kernel, jax.ShapeDtypeStruct((SLOT_THREE, CH), F32), [], (slots,))
    reduced = call(
        lambda *refs: spread_kernel(factor, *refs),
        jax.ShapeDtypeStruct((BANDS, SLOT_THREE, CH), BF),
        [],
        (part, swapped(part, 2)),
    )
    reduced = lax.all_to_all(reduced, "tile", 0, 0, tiled=True)
    swap = swapped(reduced, 1)
    grad_in = call(
        grad_kernel,
        jax.ShapeDtypeStruct((3, 2, SPAN, CH), BF),
        [pltpu.VMEM((BANDS * 48, CH), F32), pltpu.VMEM((2, 3, SPAN, CH), F32)],
        (*seams, jnp.asarray(order_selector(), BF), slots),
        in_smem,
    )
    first, second = call(
        unpack_kernel,
        [jax.ShapeDtypeStruct((1152, CH), F32), jax.ShapeDtypeStruct((1152, CH), F32)],
        [],
        (reduced, swap),
    )
    return grad_in, first.reshape(3, 3, CH, CH), second.reshape(3, 3, CH, CH)


def solution(mesh):
    return jax.shard_map(
        body,
        mesh=mesh,
        in_specs=(P("sub", "tile", None, None), P("sub", "tile", None, None), P(), P(), P(), P(), P()),
        out_specs=(P("sub", "tile", None, None), P(), P()),
        check_vma=False,
    )
```

```python
import jax
import jax.numpy as jnp
import numpy as np
from jax import lax
from jax.experimental import pallas as pl
from jax.experimental.pallas import tpu as pltpu
from jax.sharding import PartitionSpec as P

BF = jnp.bfloat16
F32 = jnp.float32
I32 = jnp.int32
BANDS = 32
SPAN = 64
CH = 128
TAPS = [(a, b) for a in range(3) for b in range(3)]
WINDOW = 6
ENDS = 48
STRIP = 12 * WINDOW
UNIT = 48
SLOT_ONE = UNIT + STRIP
HALF = 9 * CH
CHUNK = 36
SLOT_TWO = 40
SLOT_THREE = 80
VMEM_BYTES = 48 * 1024 * 1024


def mm(left, right):
    return jnp.dot(left, right, preferred_element_type=F32)


def mm_t(left, right):
    return lax.dot_general(left, right, (((0,), (0,)), ((), ())), preferred_element_type=F32)


def call(kernel, outs, scratch, operands, places=(), aliases=None):
    kinds = {"v": pltpu.VMEM, "s": pltpu.SMEM, "h": pltpu.HBM, "a": pl.ANY}
    places = dict(places)
    many = isinstance(outs, (list, tuple))
    out_specs = [pl.BlockSpec(memory_space=kinds[places.get(f"o{k}", "v")]) for k in range(len(outs) if many else 1)]
    return pl.pallas_call(
        kernel,
        out_shape=outs,
        in_specs=[pl.BlockSpec(memory_space=kinds[places.get(k, "v")]) for k in range(len(operands))],
        out_specs=out_specs if many else out_specs[0],
        scratch_shapes=scratch,
        input_output_aliases=aliases or {},
        compiler_params=pltpu.CompilerParams(vmem_limit_bytes=VMEM_BYTES),
    )(*operands)


def here():
    return lax.axis_index("tile"), lax.axis_index("sub")


def is_mirrored(fn_ref, rot_ref, face, side):
    rot = rot_ref[face, side]
    partner = 4 * fn_ref[face, side] + (rot & 3)
    return jnp.where(4 * face + side > partner, rot >> 2, 0)


def is_mirrored(fn_ref, rot_ref, face, side):
    rot = rot_ref[side, face]
    partner = 4 * fn_ref[side, face] + (rot & 3)
    return jnp.where(4 * face + side > partner, rot >> 2, 0)


def mirrored_in(fn_ref, rot_ref, face, side):
    lane = lax.broadcasted_iota(I32, (1, 12), 1) == face
    rot = jnp.sum(jnp.where(lane, rot_ref[side : side + 1, :], 0))
    partner = 4 * jnp.sum(jnp.where(lane, fn_ref[side : side + 1, :], 0)) + (rot & 3)
    return jnp.where(4 * face + side > partner, rot >> 2, 0)


def unit_of(band):
    unit = band - 4
    strip = (unit * 43) >> 7
    return strip, unit - 3 * strip


def pack_lines(f_hbm, g_hbm, fn_hbm, rot_hbm, out_ref, buf, fn_ref, rot_ref, wide, ends, sems):
    moves = ((f_hbm, buf.at[0]), (g_hbm, buf.at[1]), (fn_hbm, fn_ref), (rot_hbm, rot_ref))
    copies = [pltpu.make_async_copy(src, dst, sems.at[k]) for k, (src, dst) in enumerate(moves)]
    for copy in copies:
        copy.start()
    band, group = here()
    ends[ENDS:STRIP, :] = jnp.zeros((STRIP - ENDS, CH), F32)
    for fld in range(2):
        copies[fld].wait()
        for row in range(2):
            for face in range(3):
                block = buf[fld, face, row].astype(F32)
                wide[pl.ds(24 + fld * 6 + row * 3 + face, SPAN, stride=12), :] = block
                for edge, cols in enumerate(((0, 1), (63, 62))):
                    for depth, col in enumerate(cols):
                        place = row * 24 + fld * 12 + edge * 6 + depth * 3 + face
                        ends[place : place + 1, :] = block[col : col + 1, :]
    wide[0:24, :] = wide[SPAN * 12 : SPAN * 12 + 24, :]
    wide[SPAN * 12 + 24 : SPAN * 12 + 48, :] = wide[24:48, :]
    for copy in copies[2:]:
        copy.wait()
    side = jnp.where(band == 0, 0, 1)
    row = lax.broadcasted_iota(I32, (STRIP, CH), 0)
    row = row - 3 * ((row * 43) >> 7)
    flip = jnp.zeros((STRIP, CH), I32)
    for face in range(3):
        flip = jnp.where(row == face, is_mirrored(fn_ref, rot_ref, 3 * group + face, side), flip)
    outer = (band == 0) | (band == BANDS - 1)
    strips = [wide[24 * d : 24 * d + STRIP, :] for d in range(BANDS)]
    for d in range(BANDS):
        strip, face = unit_of(d)
        unit = wide[pl.ds(96 * strip + face, UNIT, stride=3), :] if 4 <= d < 28 else ends[0:ENDS, :]
        line = jnp.where(flip == 1, strips[BANDS - 1 - d], strips[d])
        out_ref[d] = jnp.concatenate([unit, jnp.where(outer, line, ends[...])], axis=0).astype(BF)


def line_selector():
    select = np.zeros((2, WINDOW * ENDS, 2 * STRIP + 6 * ENDS), np.float32)
    for mirrored in range(2):
        for j in range(WINDOW):
            part, parity = j // 2, j % 2
            for fld in range(2):
                for depth in range(2):
                    for face in range(3):
                        base = j * ENDS + (fld * 2 + depth) * 12 + face
                        column = (5 - j if mirrored else j) * 12 + fld * 6 + face
                        select[mirrored, base, column + depth * 3] = 1
                        select[mirrored, base + 3, STRIP + column + (1 - depth) * 3] = 1
                        for side in range(2):
                            source = 2 * STRIP + (3 * mirrored + part) * ENDS + (1 - parity if mirrored else parity) * 24
                            select[mirrored, base + 6 + 3 * side, source + fld * 12 + side * 6 + depth * 3 + face] = 1
    return select


def gather_lines(fn_ref, rot_ref, sel_ref, in_ref, out_ref):
    band, group = here()
    pieces = [in_ref[d].astype(F32)[UNIT:SLOT_ONE] for d in (0, BANDS - 1)]
    for source in [band + 31 + part for part in range(3)] + [64 - band - part for part in range(3)]:
        source = source & 31
        outer = (source == 0) | (source == BANDS - 1)
        pieces.append(jnp.where(outer, in_ref[source, 0:ENDS, :], in_ref[source, UNIT : UNIT + ENDS, :]).astype(F32))
    pieces = jnp.concatenate(pieces, axis=0).astype(BF)
    place = lax.broadcasted_iota(I32, (WINDOW * ENDS, 1), 0)
    place = place - 12 * ((place * 171) >> 11)
    flip = jnp.zeros((WINDOW * ENDS, 1), I32)
    for side in range(4):
        for face in range(3):
            flip = jnp.where(place == side * 3 + face, is_mirrored(fn_ref, rot_ref, 3 * group + face, side), flip)
    flip = jnp.broadcast_to(flip.astype(F32), sel_ref.shape[1:]).astype(BF)
    picked = mm(sel_ref[0] * (1 - flip) + sel_ref[1] * flip, pieces).astype(BF)
    for j in range(WINDOW):
        out_ref[j] = picked[j * ENDS : (j + 1) * ENDS]


def silu_parts(pre):
    logistic = 1.0 / (1.0 + jnp.exp(-pre))
    return pre * logistic, logistic * (1.0 + pre * (1.0 - logistic))


def side_frame(side, tap):
    dr, dc = tap[0] - 1, tap[1] - 1
    return ((dr, dc), (-dr, dc), (dc, dr), (-dc, dr))[side]


def transpose_weights(ref, out):
    for k, (a, b) in enumerate(TAPS):
        out[k * CH : (k + 1) * CH, :] = ref[a, b].T


def interior_kernel(
    _fill, _plan, _select, in_ref, w1_ref, w2_ref, own_ref, away_ref, sent, acc, done, w1t, w2t, f2, g2, wide
):
    band, group = here()
    strip, _ = unit_of(band)
    transpose_weights(w1_ref, w1t)
    transpose_weights(w2_ref, w2t)
    for s in range(BANDS):
        wide[s * UNIT : (s + 1) * UNIT, :] = in_ref[s, 0:UNIT, :].astype(F32)
    for q in range(12):
        for fld, target in enumerate((f2, g2)):
            for row in range(2):
                piece = wide[pl.ds(q * 4 + fld * 2 + row, BANDS, stride=UNIT), :]
                target[pl.ds(q * 64 + row, BANDS, stride=2), :] = piece

    def conv_weights(ref):
        return jnp.concatenate([ref[a].reshape(3 * CH, CH) for a in range(3)], axis=1)

    def back_weights(ref):
        columns = []
        for a in range(3):
            columns.append(jnp.concatenate([ref[(a * 3 + b) * CH : (a * 3 + b + 1) * CH, :] for b in (2, 1, 0)], axis=0))
        return jnp.concatenate(columns, axis=1)

    def up_one(value):
        return pltpu.roll(value, value.shape[0] - 1, 0)

    def down_one(value):
        return pltpu.roll(value, 1, 0)

    def three_columns(ref, first, count):
        return jnp.concatenate([ref[first + 64 * b : first + 64 * b + count, :].astype(BF) for b in range(3)], axis=1)

    y = mm(three_columns(f2, 0, 640), conv_weights(w1_ref))
    pre = down_one(y[:, :CH]) + y[:, CH : 2 * CH] + up_one(y[:, 2 * CH :])
    z = mm(three_columns(g2, 0, 640), back_weights(w2t))
    back = up_one(z[:, :CH]) + z[:, CH : 2 * CH] + down_one(z[:, 2 * CH :])
    hidden, slope = silu_parts(pre)
    index = lax.broadcasted_iota(I32, (640, CH), 0)
    col = 8 * strip - 1 + (index >> 6)
    row = index & 63
    inner = (row >= 1) & (row <= 62) & (col >= 1) & (col <= 62) & (band >= 4) & (band < 28)
    gpre = jnp.where(inner, back * slope, 0.0).astype(BF)
    hid = jnp.where(inner, hidden, 0.0)[64:576].astype(BF)

    gown = gpre[64:576].astype(F32)
    gcat = jnp.concatenate([up_one(gown).astype(BF), gpre[64:576], down_one(gown).astype(BF)], axis=1)
    first = mm_t(three_columns(f2, 64, 512), gcat)
    hown = hid.astype(F32)
    hcat = jnp.concatenate([down_one(hown).astype(BF), hid, up_one(hown).astype(BF)], axis=1)
    gback = jnp.concatenate([g2[start : start + 512, :].astype(BF) for start in (192, 128, 64)], axis=1)
    second = mm_t(hcat, gback)
    for k, (a, b) in enumerate(TAPS):
        top, low = k * CH, 1152 + k * CH
        acc[top : top + CH, :] = first[b * CH : (b + 1) * CH, a * CH : (a + 1) * CH]
        acc[low : low + CH, :] = second[a * CH : (a + 1) * CH, b * CH : (b + 1) * CH]
    core = group & 1
    own_ref[...] = acc[pl.ds(pl.multiple_of(core * HALF, CH), HALF), :]
    away_ref[...] = acc[pl.ds(pl.multiple_of((1 - core) * HALF, CH), HALF), :].astype(BF)

    gthree = jnp.concatenate([gpre[0:512], gpre[64:576], gpre[128:640]], axis=1)
    z = mm(gthree, back_weights(w1t))
    done[...] = up_one(z[:, :CH]) + z[:, CH : 2 * CH] + down_one(z[:, 2 * CH :]) + g2[128:640, :]
    for q in range(8):
        for row in range(2):
            sent[pl.ds(q * 2 + row, BANDS, stride=16), :] = done[pl.ds(q * 64 + row, BANDS, stride=2), :]


def main_kernel(
    fn_ref, rot_ref, fill_ref, plan_ref, sel_ref, own_ref, one_ref, two_ref, three_ref, w1_ref, w2_ref,
    share_ref, tail_ref,
    w1t, w2t, xs, hal, nb, lp, lg, lc, ss, gp, gpu, owe,
):
    band, group = here()
    transpose_weights(w1_ref, w1t)
    transpose_weights(w2_ref, w2t)

    line = lax.broadcasted_iota(I32, (64, 1), 0)
    place = line & 15
    side = (place >= 3).astype(I32) + (place >= 6).astype(I32) + (place >= 9).astype(I32)
    face = place - 3 * side
    home = line - place
    real = place < 12
    lane = lax.broadcasted_iota(I32, (64, 64), 1)

    def one_hot(target, keep):
        return (jnp.where(keep & real, target, -1) == lane).astype(F32).astype(BF)

    face_lane = lax.broadcasted_iota(I32, (64, 12), 1)
    faces = (jnp.where(real, 3 * (line >> 4) + face, -1) == face_lane).astype(F32).astype(BF)

    def by_line(ref, columns):
        table = ref[...].astype(F32).astype(BF)
        rows = lax.dot_general(faces, table, (((1,), (1,)), ((), ())), preferred_element_type=F32).astype(I32)
        value = rows[:, columns[0] : columns[0] + 1]
        for s in range(1, 4):
            value = jnp.where(side == s, rows[:, columns[s] : columns[s] + 1], value)
        return value

    fn = by_line(fn_ref, (0, 1, 2, 3))
    rot = by_line(rot_ref, (0, 1, 2, 3))
    fn_group = (fn * 43) >> 7
    partner = one_hot(fn_group * 16 + (rot & 3) * 3 + (fn - 3 * fn_group), real)
    number = 4 * (3 * (line >> 4) + face) + side
    flip = ((rot >> 2) == 1) & (number > 4 * fn + (rot & 3)) & real
    fills = []
    for columns in ((0, 2, 0, 1), (1, 3, 2, 3)):
        m = by_line(fill_ref, columns)
        mf = m >> 2
        mg = (mf * 43) >> 7
        target = mg * 16 + ((m >> 1) & 1) * 3 + (mf - 3 * mg)
        fills.append((one_hot(target, (m & 1) == 0), one_hot(target, (m & 1) == 1)))
    corner_cells = jnp.concatenate([jnp.concatenate(pair, axis=1) for pair in fills], axis=0)
    corner_back = corner_cells.astype(F32).T.astype(BF)
    even = (side & 1) == 0
    low_side = jnp.where(side < 2, 2, 0)
    high_side = jnp.where(side < 2, 3, 1)
    beside = jnp.concatenate([
        jnp.concatenate([one_hot(home + other * 3 + face, even), one_hot(home + other * 3 + face, ~even)], axis=1)
        for other in (low_side, high_side)
    ], axis=0)
    side_mask = [jnp.broadcast_to((side == s).astype(F32), (64, CH)).astype(BF) > 0.5 for s in range(4)]
    row_line = (side < 2).astype(F32)
    flip_f = jnp.broadcast_to(flip.astype(F32), (64, CH))
    flip_b = flip_f.astype(BF) > 0.5

    def pick(plain, mirrored):
        return jnp.where(flip_b, mirrored, plain)

    def pick_f(plain, mirrored):
        return jnp.where(flip_f > 0.5, mirrored, plain)

    arrived = (own_ref, one_ref, two_ref, three_ref)
    arrived = [jnp.concatenate([ref[j] for ref in arrived], axis=0) for j in range(WINDOW)]
    row = lax.broadcasted_iota(I32, (256, 1), 0)
    source = (((row >> 4) & 3) ^ group) * ENDS + (row >> 6) * 12 + (row & 15)
    source = jnp.where((row & 15) < 12, source, -1)
    expand = (source == lax.broadcasted_iota(I32, (256, 4 * ENDS), 1)).astype(F32).astype(BF)
    arrived = mm(expand, jnp.concatenate(arrived, axis=1)).astype(BF)
    for j in range(WINDOW):
        for block in range(4):
            xs[block, j] = arrived[block * 64 : block * 64 + 64, j * CH : (j + 1) * CH]
    halos = mm(partner, jnp.concatenate([xs[0, j] for j in range(WINDOW)], axis=1)).astype(BF)
    for j in range(WINDOW):
        hal[j] = halos[:, j * CH : (j + 1) * CH]

    def block_at(block, j):
        return hal[j] if block == 0 else xs[block - 1, j]

    for block in range(5):
        for j in range(1, 5):
            before, after = block_at(block, j - 1), block_at(block, j + 1)
            nb[0, block, j] = pick(before, after)
            nb[1, block, j] = pick(after, before)
    at_first, at_last = band == 0, band == BANDS - 1

    def line_ends(value, lower, upper, choice):
        zero = jnp.where(at_last, value(lower + 2), value(lower))
        end = jnp.where(at_last, value(upper + 2), value(upper))
        return choice(zero, end), choice(end, zero)

    h_zero, h_end = line_ends(lambda j: hal[j], 2, 1, pick)
    h_one, h_last = line_ends(lambda j: hal[j], 3, 0, pick)
    f_zero, f_end = line_ends(lambda j: xs[0, j], 2, 1, pick)
    none = jnp.zeros((64, CH), BF)
    cells = mm(corner_cells, jnp.concatenate([f_zero, f_end], axis=0)).astype(BF)
    sides = jnp.concatenate([jnp.concatenate([h_zero, h_one], axis=1), jnp.concatenate([h_end, h_last], axis=1)], axis=0)
    sides = mm(beside, sides).astype(BF)
    low = [cells[:64], sides[:64, :CH], sides[:64, CH:], none, none]
    high = [cells[64:], sides[64:, :CH], sides[64:, CH:], none, none]
    for block in range(5):
        for slot, here_now in ((2, at_first), (4, at_last)):
            before, after = nb[0, block, slot], nb[1, block, slot]
            nb[0, block, slot] = jnp.where(here_now, pick(low[block], before), before)
            nb[1, block, slot] = jnp.where(here_now, pick(after, high[block]), after)
            before, after = nb[0, block, slot - 1], nb[1, block, slot - 1]
            nb[0, block, slot - 1] = jnp.where(here_now, pick(before, low[block]), before)
            nb[1, block, slot - 1] = jnp.where(here_now, pick(high[block], after), after)
    corner_grad = line_ends(lambda j: xs[2, j], 2, 1, pick)

    def choose(options):
        whole = all(option is not None for option in options)
        result = options[0] if whole else jnp.zeros((64, CH), BF)
        for s, option in enumerate(options):
            if option is not None and not (whole and s == 0):
                result = jnp.where(side_mask[s], option, result)
        return result

    def fill(target, block, source):
        for k, tap in enumerate(TAPS):
            target[block * 64 : block * 64 + 64, k * CH : (k + 1) * CH] = choose(
                [source(*side_frame(s, tap)) for s in range(4)]
            )

    def field_source(j):
        def source(delta, dt):
            return block_at(delta + 1, j) if dt == 0 else nb[(dt + 1) // 2, delta + 1, j]
        return source

    def grad_source(e, j):
        def source(delta, dt):
            depth = e - delta
            if depth not in (0, 1):
                return None
            return xs[2 + depth, j] if dt == 0 else nb[(1 - dt) // 2, 3 + depth, j]
        return source

    def corner_source(which, value):
        def source(delta, dt):
            return value if (delta, dt) == (-1, 2 * which - 1) else None
        return source

    order_pre = (2, 3, 1, 4)
    for block, j in enumerate(order_pre):
        fill(lp, block, field_source(j))
    order_back = [(0, 2), (0, 3), (-1, 2), (-1, 3), None, None, (0, 1), (0, 4), (-1, 1), (-1, 4)]
    for block, at in enumerate(order_back):
        fill(lg, block, corner_source(block - 4, corner_grad[block - 4]) if at is None else grad_source(*at))

    pre = mm(lp[...], w1_ref[...].reshape(9 * CH, CH))
    back = mm(lg[...], w2t[...])

    def back_block(e, j):
        block = order_back.index((e, j))
        return back[block * 64 : block * 64 + 64]

    seams = jnp.concatenate([back_block(-1, j).astype(BF) for j in range(1, 5)], axis=1)
    seams = mm(partner, seams)
    for j in range(1, 5):
        ss[j] = seams[:, (j - 1) * CH : j * CH]
    both_rows = jnp.concatenate([row_line, row_line], axis=0)

    def corner_sums(both):
        sums = mm(corner_back, (both * both_rows).astype(BF))
        return sums[:64], sums[64:]


    at_zero, at_end = corner_sums(back[256:384])
    head, tail = line_ends(lambda j: ss[j], 2, 1, pick_f)
    head, tail = head + at_zero, tail + at_end
    sides = mm(beside, jnp.concatenate([head, tail], axis=0).astype(BF))
    head, tail = head + sides[:64], tail + sides[64:]
    for slot, here_now in ((2, at_first), (4, at_last)):
        ss[slot] = jnp.where(here_now, pick_f(head, tail), ss[slot])
        ss[slot - 1] = jnp.where(here_now, pick_f(tail, head), ss[slot - 1])

    unique = {}
    hid = {}
    for block, j in enumerate(order_pre):
        value = pre[block * 64 : block * 64 + 64]
        hidden, slope = silu_parts(value)
        t = (2 * band - 2 + j) & (SPAN - 1)
        corner = jnp.logical_or(t == 0, t == SPAN - 1)
        unique[j] = jnp.where(corner, row_line, jnp.ones_like(row_line))
        grad = ((back_block(0, j) + ss[j]) * slope).astype(BF)
        gp[j] = grad
        gpu[j] = (grad.astype(F32) * unique[j]).astype(BF)
        hid[j] = hidden.astype(BF)

    mine = ((line >> 5) == (group >> 1)).astype(F32)
    edge = jnp.where(band == 0, 1.0, 0.0) * mine * row_line

    def scaled(value, factor):
        return (value.astype(F32) * factor).astype(BF)

    h_zero, h_end = pick(hid[2], hid[1]), pick(hid[1], hid[2])
    halos = mm(partner, jnp.concatenate([hid[2], hid[3]], axis=1))
    ends = mm(corner_cells, jnp.concatenate([h_zero, h_end], axis=0))
    cells = jnp.concatenate([
        scaled(hid[2], mine * unique[2]),
        scaled(hid[3], mine * unique[3]),
        scaled(halos[:, :CH], mine),
        scaled(halos[:, CH:], mine),
        scaled(ends[:64], edge),
        scaled(ends[64:], edge),
    ], axis=0)
    @pl.when((group & 1) == 0)
    def _():
        own = jnp.concatenate([scaled(gpu[2], mine), scaled(gpu[3], mine)], axis=0)
        share_ref[...] = mm_t(lp[0:128, :], own)

    @pl.when((group & 1) == 1)
    def _():
        second = mm_t(cells, lg[0:384, :])
        for k in range(9):
            share_ref[k * CH : (k + 1) * CH, :] = second[:, k * CH : (k + 1) * CH]

    inner_low = jnp.where(at_first, 0.0, 1.0)
    inner_high = jnp.where(at_last, 0.0, 1.0)

    def spread_source(e, j, ref):
        def source(delta, dt):
            if e - delta != 0:
                return None
            if dt == 0:
                return ref[j]
            before = scaled(ref[1], inner_low) if j == 2 else ref[2]
            after = ref[3] if j == 2 else scaled(ref[4], inner_high)
            return pick(before, after) if dt == 1 else pick(after, before)
        return source

    g_zero = jnp.where(at_first, gp[2], gp[4])
    g_end = jnp.where(at_first, gp[1], gp[3])
    g_zero, g_end = pick(g_zero, g_end), pick(g_end, g_zero)
    order_in = [(0, 2), (0, 3), (1, 2), (1, 3), (-1, 2), (-1, 3), None, None]
    for block, at in enumerate(order_in):
        if at is None:
            fill(lc, block, corner_source(block - 6, (g_zero, g_end)[block - 6]))
        else:
            fill(lc, block, spread_source(*at, gp if at[0] == -1 else gpu))
    back = mm(lc[...], w1t[...])
    part = [back[k * 64 : k * 64 + 64] for k in range(8)]
    at_zero, at_end = corner_sums(back[384:512])
    seams = mm(partner, jnp.concatenate([part[4], part[5]], axis=1).astype(BF))
    owe[0] = part[0] + seams[:, :CH] + pick_f(at_zero, at_end) * (1.0 - inner_low)
    owe[1] = part[2]
    owe[2] = part[1] + seams[:, CH:] + pick_f(at_end, at_zero) * (1.0 - inner_high)
    owe[3] = part[3]

    tile = jnp.concatenate([owe[k, pl.ds(pl.multiple_of(group * 16, 16), 16), :] for k in range(4)], axis=0)
    plan = [plan_ref[:, k : k + 1] for k in range(8)]
    flips = [jnp.zeros((48, 1), I32) for _ in range(2)]
    for which in range(4):
        for face_index in range(3):
            value = mirrored_in(fn_ref, rot_ref, 3 * group + face_index, which)
            for k in range(2):
                flips[k] = jnp.where(plan[6 + k] == which * 3 + face_index, value, flips[k])
    last = jnp.where(at_last, 1, 0)
    outer = jnp.logical_or(at_first, at_last)
    row_lane = jnp.where(flips[0] ^ last == plan[4], jnp.where(at_last, plan[1], plan[0]), -1)
    col_lane = jnp.where(flips[1] ^ last == plan[5], jnp.where(at_last, plan[3], plan[2]), -1)
    lanes = lax.broadcasted_iota(I32, (48, 64), 1)
    patch = (row_lane == lanes).astype(F32) + (col_lane == lanes).astype(F32)
    select = jnp.concatenate([jnp.where(outer, patch, sel_ref[0:48, :]), sel_ref[48:72, :]], axis=0)
    tail_ref[...] = mm(select.astype(BF), tile.astype(BF))


def tail_plan():
    select = np.zeros((72, 64), np.float32)
    plan = np.zeros((48, 8), np.int32)
    for pos in range(2):
        for depth in range(2):
            for face in range(3):
                lane = (pos * 2 + depth) * 16 + face
                for half in range(2):
                    select[half * 24 + (pos * 2 + depth) * 3 + face, lane + half * 3] = 1
                for side in range(2):
                    select[48 + ((pos * 2 + side) * 2 + depth) * 3 + face, lane + 6 + 3 * side] = 1
    for half in range(2):
        for side in range(2):
            for face in range(3):
                for row in range(2):
                    for col in range(2):
                        place = half * 24 + ((side * 3 + face) * 2 + row) * 2 + col
                        for last in range(2):
                            plan[place, last] = ((col ^ last) * 2 + row) * 16 + half * 3 + face
                            plan[place, 2 + last] = ((row ^ last) * 2 + col) * 16 + (2 + side) * 3 + face
                        plan[place, 4:] = side, half, half * 3 + face, (2 + side) * 3 + face
    return select, plan


def after_kernel(*refs):
    pass


def share_kernel(own_ref, other_ref, line_ref, out_ref, total):
    total[...] = own_ref[...] + other_ref[...].astype(F32) + line_ref[...]
    for i in range(BANDS):
        rows = [total[CHUNK * i : CHUNK * i + CHUNK, :], jnp.zeros((SLOT_TWO - CHUNK, CH), F32)]
        out_ref[i] = jnp.concatenate(rows, axis=0).astype(BF)


def order_selector():
    select = np.zeros((2, 64, 64), np.float32)
    for pos in range(2):
        for b in range(BANDS):
            select[0, 2 * b + pos, pos * 32 + b] = 1
            select[1, 63 - 2 * b - pos, pos * 32 + b] = 1
    return select


def reduce_kernel(in_ref, out_ref):
    total = in_ref[0].astype(F32)
    for i in range(1, BANDS):
        total = total + in_ref[i].astype(F32)
    out_ref[...] = total


def spread_kernel(factor, _order, own_ref, other_ref, tail_ref, sent, out_ref):
    total = (own_ref[...] + other_ref[...]) * factor
    for i in range(BANDS):
        start = 0 if i == 0 else 24 if i == BANDS - 1 else 48
        parts = [total, sent[i * 16 : i * 16 + 16, :], tail_ref[start : start + 24, :]]
        out_ref[i] = jnp.concatenate(parts, axis=0).astype(BF)


def sums_kernel(in_ref, out_ref):
    for i in range(BANDS):
        out_ref[i] = in_ref[i, 0:48, :].astype(F32)[0:SLOT_TWO].astype(BF)


def unpack_kernel(own_ref, other_ref, first_ref, second_ref):
    _, group = here()
    core = group & 1
    for i in range(BANDS):
        own, other = own_ref[i].astype(F32), other_ref[i].astype(F32)
        rows = slice(CHUNK * i, CHUNK * i + CHUNK)
        first_ref[rows, :] = jnp.where(core == 0, own, other)[0:CHUNK]
        second_ref[rows, :] = jnp.where(core == 0, other, own)[0:CHUNK]


def grad_kernel(fn_ref, rot_ref, sel_ref, in_ref, out_ref, wide, total):
    band, group = here()
    for i in range(BANDS):
        wide[i * 48 : i * 48 + 48, :] = in_ref[i, 32:SLOT_THREE, :].astype(F32)
    for face in range(3):
        for row in range(2):
            for q in range(8):
                piece = wide[pl.ds((4 + face) * 48 + 8 + q * 2 + row, 8, stride=144), :]
                total[row, face, pl.ds(q, 8, stride=8), :] = piece
    tiles = [wide[pl.ds(pl.multiple_of(src * 48, 16), 48), :] for src in (band, BANDS - 1 - band)]
    outer = (band == 0) | (band == BANDS - 1)

    @pl.when(~outer)
    def _():
        for side in range(2):
            for face in range(3):
                flip = is_mirrored(fn_ref, rot_ref, 3 * group + face, 2 + side) == 1
                for row in range(2):
                    for depth in range(2):
                        column = depth if side == 0 else 63 - depth
                        k, m = [24 + ((pos * 2 + side) * 2 + depth) * 3 + face for pos in (row, 1 - row)]
                        extra = jnp.where(flip, tiles[1][m : m + 1, :], tiles[0][k : k + 1, :])
                        total[row, face, column : column + 1, :] += extra

    @pl.when(outer)
    def _():
        half = jnp.where(band == 0, 0, 1)
        patches = tiles[0] + tiles[1]
        place = lax.broadcasted_iota(I32, (SPAN, CH), 0)
        inner = (place >= 2) & (place < SPAN - 2)
        for face in range(3):
            order = sel_ref[is_mirrored(fn_ref, rot_ref, 3 * group + face, half)]
            for depth in range(2):
                halves = [wide[pl.ds(24 + (pos * 2 + depth) * 3 + face, BANDS, stride=48), :] for pos in range(2)]
                extra = mm(order, jnp.concatenate(halves, axis=0).astype(BF))
                total[depth ^ half, face] += jnp.where(inner, extra, 0.0)
                for side in range(2):
                    for col in range(2):
                        k = 24 + ((side * 3 + face) * 2 + depth) * 2 + col
                        column = 63 - col if side else col
                        total[depth ^ half, face, column : column + 1, :] += patches[k : k + 1, :]

    for row in range(2):
        for face in range(3):
            out_ref[face, row] = total[row, face].astype(BF)


def swapped(value, step):
    return lax.ppermute(value, "sub", [(i, i ^ step) for i in range(4)])


def body(field_in, grad_out, first_weight, second_weight, face_neighbour, seam_rotation, corner_fill):
    factor = (1.0 * 12 * SPAN * SPAN) ** -0.5
    seams = (face_neighbour.T, seam_rotation.T)
    in_smem = {0: "s", 1: "s"}
    select, plan = tail_plan()

    slots = call(
        pack_lines,
        jax.ShapeDtypeStruct((BANDS, SLOT_ONE, CH), BF),
        [
            pltpu.VMEM((2, 3, 2, SPAN, CH), BF),
            pltpu.SMEM((4, 12), I32),
            pltpu.SMEM((4, 12), I32),
            pltpu.VMEM(((SPAN + 4) * 12, CH), F32),
            pltpu.VMEM((STRIP, CH), F32),
            pltpu.SemaphoreType.DMA((4,)),
        ],
        tuple(pltpu.with_memory_space_constraint(value, pltpu.HBM) for value in (field_in, grad_out, *seams)),
        dict.fromkeys(range(4), "h"),
    )
    strips = lax.all_to_all(slots, "tile", 0, 0, tiled=True)
    lines = call(
        gather_lines,
        jax.ShapeDtypeStruct((WINDOW, ENDS, CH), BF),
        [],
        (*seams, jnp.asarray(line_selector(), BF), strips),
        in_smem,
    )
    lines = (lines, *[swapped(lines, step) for step in (1, 2, 3)])
    tables = (corner_fill.T, jnp.asarray(plan), jnp.asarray(select, F32))
    share = jax.ShapeDtypeStruct((HALF, CH), F32)
    own, away, sent = call(
        interior_kernel,
        [share, jax.ShapeDtypeStruct((HALF, CH), BF), jax.ShapeDtypeStruct((BANDS * 16, CH), F32)],
        [
            pltpu.VMEM((2304, CH), F32),
            pltpu.VMEM((512, CH), F32),
            pltpu.VMEM((1152, CH), BF),
            pltpu.VMEM((1152, CH), BF),
            pltpu.VMEM((768, CH), F32),
            pltpu.VMEM((768, CH), F32),
            pltpu.VMEM((BANDS * UNIT, CH), F32),
        ],
        (*tables, strips, first_weight, second_weight),
    )
    away = call(after_kernel, jax.ShapeDtypeStruct((HALF, CH), BF), [], (away, *lines[1:]), dict.fromkeys((0, 1, 2, 3, "o0"), "a"), {0: 0})
    other = swapped(away, 1)

    line, tails = call(
        main_kernel,
        [share, jax.ShapeDtypeStruct((72, CH), F32)],
        [
            pltpu.VMEM((1152, CH), BF),
            pltpu.VMEM((1152, CH), BF),
            pltpu.VMEM((4, WINDOW, 64, CH), BF),
            pltpu.VMEM((WINDOW, 64, CH), BF),
            pltpu.VMEM((2, 5, 5, 64, CH), BF),
            pltpu.VMEM((256, 1152), BF),
            pltpu.VMEM((640, 1152), BF),
            pltpu.VMEM((512, 1152), BF),
            pltpu.VMEM((5, 64, CH), F32),
            pltpu.VMEM((5, 64, CH), BF),
            pltpu.VMEM((5, 64, CH), BF),
            pltpu.VMEM((4, 64, CH), F32),
        ],
        (*seams, *tables, *lines, first_weight, second_weight),
    )
    slots = call(
        share_kernel,
        jax.ShapeDtypeStruct((BANDS, SLOT_TWO, CH), BF),
        [pltpu.VMEM((HALF, CH), F32)],
        (own, other, line),
    )
    slots = lax.all_to_all(slots, "tile", 0, 0, tiled=True)
    order = jnp.asarray(order_selector(), BF)
    part = call(reduce_kernel, jax.ShapeDtypeStruct((SLOT_TWO, CH), F32), [], (slots,))
    reduced = call(
        lambda *refs: spread_kernel(factor, *refs),
        jax.ShapeDtypeStruct((BANDS, SLOT_THREE, CH), BF),
        [],
        (order, part, swapped(part, 2), tails, sent),
    )
    reduced = lax.all_to_all(reduced, "tile", 0, 0, tiled=True)
    sums = call(sums_kernel, jax.ShapeDtypeStruct((BANDS, SLOT_TWO, CH), BF), [], (reduced,))
    swap = swapped(sums, 1)
    grad_in = call(
        grad_kernel,
        jax.ShapeDtypeStruct((3, 2, SPAN, CH), BF),
        [pltpu.VMEM((BANDS * 48, CH), F32), pltpu.VMEM((2, 3, SPAN, CH), F32)],
        (*seams, order, reduced),
        in_smem,
    )
    first, second = call(
        unpack_kernel,
        [jax.ShapeDtypeStruct((1152, CH), F32), jax.ShapeDtypeStruct((1152, CH), F32)],
        [],
        (sums, swap),
    )
    return grad_in, first.reshape(3, 3, CH, CH), second.reshape(3, 3, CH, CH)


def solution(mesh):
    return jax.shard_map(
        body,
        mesh=mesh,
        in_specs=(P("sub", "tile", None, None), P("sub", "tile", None, None), P(), P(), P(), P(), P()),
        out_specs=(P("sub", "tile", None, None), P(), P()),
        check_vma=False,
    )
```

```python
import jax
import jax.numpy as jnp
import numpy as np
from jax import lax
from jax.experimental import pallas as pl
from jax.experimental.pallas import tpu as pltpu
from jax.sharding import PartitionSpec as P

BF = jnp.bfloat16
F32 = jnp.float32
I32 = jnp.int32
BANDS = 32
SPAN = 64
CH = 128
TAPS = [(a, b) for a in range(3) for b in range(3)]
WINDOW = 6
ENDS = 48
STRIP = 12 * WINDOW
UNIT = 48
SLOT_ONE = UNIT + STRIP
HALF = 9 * CH
CHUNK = 36
SLOT_TWO = 40
SLOT_THREE = 80
VMEM_BYTES = 48 * 1024 * 1024


def mm(left, right):
    return jnp.dot(left, right, preferred_element_type=F32)


def mm_t(left, right):
    return lax.dot_general(left, right, (((0,), (0,)), ((), ())), preferred_element_type=F32)


def call(kernel, outs, scratch, operands, places=(), aliases=None):
    kinds = {"v": pltpu.VMEM, "s": pltpu.SMEM, "h": pltpu.HBM, "a": pl.ANY}
    places = dict(places)
    many = isinstance(outs, (list, tuple))
    out_specs = [pl.BlockSpec(memory_space=kinds[places.get(f"o{k}", "v")]) for k in range(len(outs) if many else 1)]
    return pl.pallas_call(
        kernel,
        out_shape=outs,
        in_specs=[pl.BlockSpec(memory_space=kinds[places.get(k, "v")]) for k in range(len(operands))],
        out_specs=out_specs if many else out_specs[0],
        scratch_shapes=scratch,
        input_output_aliases=aliases or {},
        compiler_params=pltpu.CompilerParams(vmem_limit_bytes=VMEM_BYTES),
    )(*operands)


def here():
    return lax.axis_index("tile"), lax.axis_index("sub")


def is_mirrored(fn_ref, rot_ref, face, side):
    rot = rot_ref[face, side]
    partner = 4 * fn_ref[face, side] + (rot & 3)
    return jnp.where(4 * face + side > partner, rot >> 2, 0)


def is_mirrored(fn_ref, rot_ref, face, side):
    rot = rot_ref[side, face]
    partner = 4 * fn_ref[side, face] + (rot & 3)
    return jnp.where(4 * face + side > partner, rot >> 2, 0)


def mirrored_in(fn_ref, rot_ref, face, side):
    lane = lax.broadcasted_iota(I32, (1, 12), 1) == face
    rot = jnp.sum(jnp.where(lane, rot_ref[side : side + 1, :], 0))
    partner = 4 * jnp.sum(jnp.where(lane, fn_ref[side : side + 1, :], 0)) + (rot & 3)
    return jnp.where(4 * face + side > partner, rot >> 2, 0)


def unit_of(band):
    unit = band - 4
    strip = (unit * 43) >> 7
    return strip, unit - 3 * strip


def pack_lines(f_hbm, g_hbm, fn_hbm, rot_hbm, out_ref, buf, fn_ref, rot_ref, wide, ends, sems):
    moves = ((f_hbm, buf.at[0]), (g_hbm, buf.at[1]), (fn_hbm, fn_ref), (rot_hbm, rot_ref))
    copies = [pltpu.make_async_copy(src, dst, sems.at[k]) for k, (src, dst) in enumerate(moves)]
    for copy in copies:
        copy.start()
    band, group = here()
    ends[ENDS:STRIP, :] = jnp.zeros((STRIP - ENDS, CH), F32)
    for fld in range(2):
        copies[fld].wait()
        for row in range(2):
            for face in range(3):
                block = buf[fld, face, row].astype(F32)
                wide[pl.ds(24 + fld * 6 + row * 3 + face, SPAN, stride=12), :] = block
                for edge, cols in enumerate(((0, 1), (63, 62))):
                    for depth, col in enumerate(cols):
                        place = row * 24 + fld * 12 + edge * 6 + depth * 3 + face
                        ends[place : place + 1, :] = block[col : col + 1, :]
    wide[0:24, :] = wide[SPAN * 12 : SPAN * 12 + 24, :]
    wide[SPAN * 12 + 24 : SPAN * 12 + 48, :] = wide[24:48, :]
    for copy in copies[2:]:
        copy.wait()
    side = jnp.where(band == 0, 0, 1)
    row = lax.broadcasted_iota(I32, (STRIP, CH), 0)
    row = row - 3 * ((row * 43) >> 7)
    flip = jnp.zeros((STRIP, CH), I32)
    for face in range(3):
        flip = jnp.where(row == face, is_mirrored(fn_ref, rot_ref, 3 * group + face, side), flip)
    outer = (band == 0) | (band == BANDS - 1)
    strips = [wide[24 * d : 24 * d + STRIP, :] for d in range(BANDS)]
    for d in range(BANDS):
        strip, face = unit_of(d)
        unit = wide[pl.ds(96 * strip + face, UNIT, stride=3), :] if 4 <= d < 28 else ends[0:ENDS, :]
        line = jnp.where(flip == 1, strips[BANDS - 1 - d], strips[d])
        out_ref[d] = jnp.concatenate([unit, jnp.where(outer, line, ends[...])], axis=0).astype(BF)


def line_selector():
    select = np.zeros((2, WINDOW * ENDS, 2 * STRIP + 6 * ENDS), np.float32)
    for mirrored in range(2):
        for j in range(WINDOW):
            part, parity = j // 2, j % 2
            for fld in range(2):
                for depth in range(2):
                    for face in range(3):
                        base = j * ENDS + (fld * 2 + depth) * 12 + face
                        column = (5 - j if mirrored else j) * 12 + fld * 6 + face
                        select[mirrored, base, column + depth * 3] = 1
                        select[mirrored, base + 3, STRIP + column + (1 - depth) * 3] = 1
                        for side in range(2):
                            source = 2 * STRIP + (3 * mirrored + part) * ENDS + (1 - parity if mirrored else parity) * 24
                            select[mirrored, base + 6 + 3 * side, source + fld * 12 + side * 6 + depth * 3 + face] = 1
    return select


def gather_lines(fn_ref, rot_ref, sel_ref, in_ref, out_ref):
    band, group = here()
    pieces = [in_ref[d].astype(F32)[UNIT:SLOT_ONE] for d in (0, BANDS - 1)]
    for source in [band + 31 + part for part in range(3)] + [64 - band - part for part in range(3)]:
        source = source & 31
        outer = (source == 0) | (source == BANDS - 1)
        pieces.append(jnp.where(outer, in_ref[source, 0:ENDS, :], in_ref[source, UNIT : UNIT + ENDS, :]).astype(F32))
    pieces = jnp.concatenate(pieces, axis=0).astype(BF)
    place = lax.broadcasted_iota(I32, (24, CH), 0)
    place = jnp.where(place < 12, place, place - 12)
    flip = jnp.zeros((24, CH), I32)
    lane = lax.broadcasted_iota(I32, (4, 12), 1)
    rot = rot_ref[...]
    partner = 4 * fn_ref[...] + (rot & 3)
    table = jnp.where(4 * lane + lax.broadcasted_iota(I32, (4, 12), 0) > partner, rot >> 2, 0)
    for face in range(3):
        values = jnp.sum(jnp.where(lane == 3 * group + face, table, 0), axis=1, keepdims=True)
        for side in range(4):
            flip = jnp.where(place == side * 3 + face, jnp.broadcast_to(values[side : side + 1], (24, CH)), flip)
    flip = jnp.concatenate([flip.astype(F32)] * (WINDOW * ENDS // 24), axis=0).astype(BF)
    flip = jnp.concatenate([flip] * 4, axis=1)[:, 0 : sel_ref.shape[2]] > 0.5
    picked = mm(jnp.where(flip, sel_ref[1], sel_ref[0]), pieces).astype(BF)
    for j in range(WINDOW):
        out_ref[j] = picked[j * ENDS : (j + 1) * ENDS]


def silu_parts(pre):
    logistic = 1.0 / (1.0 + jnp.exp(-pre))
    return pre * logistic, logistic * (1.0 + pre * (1.0 - logistic))


def side_frame(side, tap):
    dr, dc = tap[0] - 1, tap[1] - 1
    return ((dr, dc), (-dr, dc), (dc, dr), (-dc, dr))[side]


def transpose_weights(ref, out):
    for k, (a, b) in enumerate(TAPS):
        out[k * CH : (k + 1) * CH, :] = ref[a, b].T


def interior_kernel(
    _fill, _plan, _select, in_ref, w1_ref, w2_ref, own_ref, away_ref, sent, acc, done, w1t, w2t, f2, g2, wide
):
    band, group = here()
    strip, _ = unit_of(band)
    transpose_weights(w1_ref, w1t)
    transpose_weights(w2_ref, w2t)
    for s in range(BANDS):
        wide[s * UNIT : (s + 1) * UNIT, :] = in_ref[s, 0:UNIT, :].astype(F32)
    for q in range(12):
        for fld, target in enumerate((f2, g2)):
            for row in range(2):
                piece = wide[pl.ds(q * 4 + fld * 2 + row, BANDS, stride=UNIT), :]
                target[pl.ds(q * 64 + row, BANDS, stride=2), :] = piece

    def conv_weights(ref):
        return jnp.concatenate([ref[a].reshape(3 * CH, CH) for a in range(3)], axis=1)

    def back_weights(ref):
        columns = []
        for a in range(3):
            columns.append(jnp.concatenate([ref[(a * 3 + b) * CH : (a * 3 + b + 1) * CH, :] for b in (2, 1, 0)], axis=0))
        return jnp.concatenate(columns, axis=1)

    def up_one(value):
        return pltpu.roll(value, value.shape[0] - 1, 0)

    def down_one(value):
        return pltpu.roll(value, 1, 0)

    def three_columns(ref, first, count):
        return jnp.concatenate([ref[first + 64 * b : first + 64 * b + count, :].astype(BF) for b in range(3)], axis=1)

    y = mm(three_columns(f2, 0, 640), conv_weights(w1_ref))
    pre = down_one(y[:, :CH]) + y[:, CH : 2 * CH] + up_one(y[:, 2 * CH :])
    z = mm(three_columns(g2, 0, 640), back_weights(w2t))
    back = up_one(z[:, :CH]) + z[:, CH : 2 * CH] + down_one(z[:, 2 * CH :])
    hidden, slope = silu_parts(pre)
    index = lax.broadcasted_iota(I32, (640, CH), 0)
    col = 8 * strip - 1 + (index >> 6)
    row = index & 63
    inner = (row >= 1) & (row <= 62) & (col >= 1) & (col <= 62) & (band >= 4) & (band < 28)
    gpre = jnp.where(inner, back * slope, 0.0).astype(BF)
    hid = jnp.where(inner, hidden, 0.0)[64:576].astype(BF)

    gown = gpre[64:576].astype(F32)
    gcat = jnp.concatenate([up_one(gown).astype(BF), gpre[64:576], down_one(gown).astype(BF)], axis=1)
    first = mm_t(three_columns(f2, 64, 512), gcat)
    hown = hid.astype(F32)
    hcat = jnp.concatenate([down_one(hown).astype(BF), hid, up_one(hown).astype(BF)], axis=1)
    gback = jnp.concatenate([g2[start : start + 512, :].astype(BF) for start in (192, 128, 64)], axis=1)
    second = mm_t(hcat, gback)
    for k, (a, b) in enumerate(TAPS):
        top, low = k * CH, 1152 + k * CH
        acc[top : top + CH, :] = first[b * CH : (b + 1) * CH, a * CH : (a + 1) * CH]
        acc[low : low + CH, :] = second[a * CH : (a + 1) * CH, b * CH : (b + 1) * CH]
    core = group & 1
    own_ref[...] = acc[pl.ds(pl.multiple_of(core * HALF, CH), HALF), :]
    away_ref[...] = acc[pl.ds(pl.multiple_of((1 - core) * HALF, CH), HALF), :].astype(BF)

    gthree = jnp.concatenate([gpre[0:512], gpre[64:576], gpre[128:640]], axis=1)
    z = mm(gthree, back_weights(w1t))
    done[...] = up_one(z[:, :CH]) + z[:, CH : 2 * CH] + down_one(z[:, 2 * CH :]) + g2[128:640, :]
    for q in range(8):
        for row in range(2):
            sent[pl.ds(q * 2 + row, BANDS, stride=16), :] = done[pl.ds(q * 64 + row, BANDS, stride=2), :]


def main_kernel(
    fn_ref, rot_ref, fill_ref, plan_ref, sel_ref, own_ref, one_ref, two_ref, three_ref, w1_ref, w2_ref,
    share_ref, tail_ref,
    w1t, w2t, xs, hal, nb, lp, lg, lc, ss, gp, gpu, owe,
):
    band, group = here()
    transpose_weights(w1_ref, w1t)
    transpose_weights(w2_ref, w2t)

    line = lax.broadcasted_iota(I32, (64, 1), 0)
    place = line & 15
    side = (place >= 3).astype(I32) + (place >= 6).astype(I32) + (place >= 9).astype(I32)
    face = place - 3 * side
    home = line - place
    real = place < 12
    lane = lax.broadcasted_iota(I32, (64, 64), 1)

    def one_hot(target, keep):
        return (jnp.where(keep & real, target, -1) == lane).astype(F32).astype(BF)

    face_lane = lax.broadcasted_iota(I32, (64, 12), 1)
    faces = (jnp.where(real, 3 * (line >> 4) + face, -1) == face_lane).astype(F32).astype(BF)

    def by_line(ref, columns):
        table = ref[...].astype(F32).astype(BF)
        rows = lax.dot_general(faces, table, (((1,), (1,)), ((), ())), preferred_element_type=F32).astype(I32)
        value = rows[:, columns[0] : columns[0] + 1]
        for s in range(1, 4):
            value = jnp.where(side == s, rows[:, columns[s] : columns[s] + 1], value)
        return value

    fn = by_line(fn_ref, (0, 1, 2, 3))
    rot = by_line(rot_ref, (0, 1, 2, 3))
    fn_group = (fn * 43) >> 7
    partner = one_hot(fn_group * 16 + (rot & 3) * 3 + (fn - 3 * fn_group), real)
    number = 4 * (3 * (line >> 4) + face) + side
    flip = ((rot >> 2) == 1) & (number > 4 * fn + (rot & 3)) & real
    fills = []
    for columns in ((0, 2, 0, 1), (1, 3, 2, 3)):
        m = by_line(fill_ref, columns)
        mf = m >> 2
        mg = (mf * 43) >> 7
        target = mg * 16 + ((m >> 1) & 1) * 3 + (mf - 3 * mg)
        fills.append((one_hot(target, (m & 1) == 0), one_hot(target, (m & 1) == 1)))
    corner_cells = jnp.concatenate([jnp.concatenate(pair, axis=1) for pair in fills], axis=0)
    corner_back = corner_cells.astype(F32).T.astype(BF)
    even = (side & 1) == 0
    low_side = jnp.where(side < 2, 2, 0)
    high_side = jnp.where(side < 2, 3, 1)
    beside = jnp.concatenate([
        jnp.concatenate([one_hot(home + other * 3 + face, even), one_hot(home + other * 3 + face, ~even)], axis=1)
        for other in (low_side, high_side)
    ], axis=0)
    side_mask = [jnp.broadcast_to((side == s).astype(F32), (64, CH)).astype(BF) > 0.5 for s in range(4)]
    row_line = (side < 2).astype(F32)
    flip_f = jnp.broadcast_to(flip.astype(F32), (64, CH))
    flip_b = flip_f.astype(BF) > 0.5

    def pick(plain, mirrored):
        return jnp.where(flip_b, mirrored, plain)

    def pick_f(plain, mirrored):
        return jnp.where(flip_f > 0.5, mirrored, plain)

    arrived = (own_ref, one_ref, two_ref, three_ref)
    arrived = [jnp.concatenate([ref[j] for ref in arrived], axis=0) for j in range(WINDOW)]
    row = lax.broadcasted_iota(I32, (256, 1), 0)
    source = (((row >> 4) & 3) ^ group) * ENDS + (row >> 6) * 12 + (row & 15)
    source = jnp.where((row & 15) < 12, source, -1)
    expand = (source == lax.broadcasted_iota(I32, (256, 4 * ENDS), 1)).astype(F32).astype(BF)
    arrived = mm(expand, jnp.concatenate(arrived, axis=1)).astype(BF)
    for j in range(WINDOW):
        for block in range(4):
            xs[block, j] = arrived[block * 64 : block * 64 + 64, j * CH : (j + 1) * CH]
    halos = mm(partner, jnp.concatenate([xs[0, j] for j in range(WINDOW)], axis=1)).astype(BF)
    for j in range(WINDOW):
        hal[j] = halos[:, j * CH : (j + 1) * CH]

    def block_at(block, j):
        return hal[j] if block == 0 else xs[block - 1, j]

    for block in range(5):
        for j in range(1, 5):
            before, after = block_at(block, j - 1), block_at(block, j + 1)
            nb[0, block, j] = pick(before, after)
            nb[1, block, j] = pick(after, before)
    at_first, at_last = band == 0, band == BANDS - 1

    def line_ends(value, lower, upper, choice):
        zero = jnp.where(at_last, value(lower + 2), value(lower))
        end = jnp.where(at_last, value(upper + 2), value(upper))
        return choice(zero, end), choice(end, zero)

    h_zero, h_end = line_ends(lambda j: hal[j], 2, 1, pick)
    h_one, h_last = line_ends(lambda j: hal[j], 3, 0, pick)
    f_zero, f_end = line_ends(lambda j: xs[0, j], 2, 1, pick)
    none = jnp.zeros((64, CH), BF)
    cells = mm(corner_cells, jnp.concatenate([f_zero, f_end], axis=0)).astype(BF)
    sides = jnp.concatenate([jnp.concatenate([h_zero, h_one], axis=1), jnp.concatenate([h_end, h_last], axis=1)], axis=0)
    sides = mm(beside, sides).astype(BF)
    low = [cells[:64], sides[:64, :CH], sides[:64, CH:], none, none]
    high = [cells[64:], sides[64:, :CH], sides[64:, CH:], none, none]
    for block in range(5):
        for slot, here_now in ((2, at_first), (4, at_last)):
            before, after = nb[0, block, slot], nb[1, block, slot]
            nb[0, block, slot] = jnp.where(here_now, pick(low[block], before), before)
            nb[1, block, slot] = jnp.where(here_now, pick(after, high[block]), after)
            before, after = nb[0, block, slot - 1], nb[1, block, slot - 1]
            nb[0, block, slot - 1] = jnp.where(here_now, pick(before, low[block]), before)
            nb[1, block, slot - 1] = jnp.where(here_now, pick(high[block], after), after)
    corner_grad = line_ends(lambda j: xs[2, j], 2, 1, pick)

    def choose(options):
        whole = all(option is not None for option in options)
        result = options[0] if whole else jnp.zeros((64, CH), BF)
        for s, option in enumerate(options):
            if option is not None and not (whole and s == 0):
                result = jnp.where(side_mask[s], option, result)
        return result

    def fill(target, block, source):
        for k, tap in enumerate(TAPS):
            target[block * 64 : block * 64 + 64, k * CH : (k + 1) * CH] = choose(
                [source(*side_frame(s, tap)) for s in range(4)]
            )

    def field_source(j):
        def source(delta, dt):
            return block_at(delta + 1, j) if dt == 0 else nb[(dt + 1) // 2, delta + 1, j]
        return source

    def grad_source(e, j):
        def source(delta, dt):
            depth = e - delta
            if depth not in (0, 1):
                return None
            return xs[2 + depth, j] if dt == 0 else nb[(1 - dt) // 2, 3 + depth, j]
        return source

    def corner_source(which, value):
        def source(delta, dt):
            return value if (delta, dt) == (-1, 2 * which - 1) else None
        return source

    order_pre = (2, 3, 1, 4)
    for block, j in enumerate(order_pre):
        fill(lp, block, field_source(j))
    order_back = [(0, 2), (0, 3), (-1, 2), (-1, 3), None, None, (0, 1), (0, 4), (-1, 1), (-1, 4)]
    for block, at in enumerate(order_back):
        fill(lg, block, corner_source(block - 4, corner_grad[block - 4]) if at is None else grad_source(*at))

    pre = mm(lp[...], w1_ref[...].reshape(9 * CH, CH))
    back = mm(lg[...], w2t[...])

    def back_block(e, j):
        block = order_back.index((e, j))
        return back[block * 64 : block * 64 + 64]

    seams = jnp.concatenate([back_block(-1, j).astype(BF) for j in range(1, 5)], axis=1)
    seams = mm(partner, seams)
    for j in range(1, 5):
        ss[j] = seams[:, (j - 1) * CH : j * CH]
    both_rows = jnp.concatenate([row_line, row_line], axis=0)

    def corner_sums(both):
        sums = mm(corner_back, (both * both_rows).astype(BF))
        return sums[:64], sums[64:]


    at_zero, at_end = corner_sums(back[256:384])
    head, tail = line_ends(lambda j: ss[j], 2, 1, pick_f)
    head, tail = head + at_zero, tail + at_end
    sides = mm(beside, jnp.concatenate([head, tail], axis=0).astype(BF))
    head, tail = head + sides[:64], tail + sides[64:]
    for slot, here_now in ((2, at_first), (4, at_last)):
        ss[slot] = jnp.where(here_now, pick_f(head, tail), ss[slot])
        ss[slot - 1] = jnp.where(here_now, pick_f(tail, head), ss[slot - 1])

    unique = {}
    hid = {}
    for block, j in enumerate(order_pre):
        value = pre[block * 64 : block * 64 + 64]
        hidden, slope = silu_parts(value)
        t = (2 * band - 2 + j) & (SPAN - 1)
        corner = jnp.logical_or(t == 0, t == SPAN - 1)
        unique[j] = jnp.where(corner, row_line, jnp.ones_like(row_line))
        grad = ((back_block(0, j) + ss[j]) * slope).astype(BF)
        gp[j] = grad
        gpu[j] = (grad.astype(F32) * unique[j]).astype(BF)
        hid[j] = hidden.astype(BF)

    mine = ((line >> 5) == (group >> 1)).astype(F32)
    edge = jnp.where(band == 0, 1.0, 0.0) * mine * row_line

    def scaled(value, factor):
        return (value.astype(F32) * factor).astype(BF)

    h_zero, h_end = pick(hid[2], hid[1]), pick(hid[1], hid[2])
    halos = mm(partner, jnp.concatenate([hid[2], hid[3]], axis=1))
    ends = mm(corner_cells, jnp.concatenate([h_zero, h_end], axis=0))
    cells = jnp.concatenate([
        scaled(hid[2], mine * unique[2]),
        scaled(hid[3], mine * unique[3]),
        scaled(halos[:, :CH], mine),
        scaled(halos[:, CH:], mine),
        scaled(ends[:64], edge),
        scaled(ends[64:], edge),
    ], axis=0)
    @pl.when((group & 1) == 0)
    def _():
        own = jnp.concatenate([scaled(gpu[2], mine), scaled(gpu[3], mine)], axis=0)
        share_ref[...] = mm_t(lp[0:128, :], own)

    @pl.when((group & 1) == 1)
    def _():
        second = mm_t(cells, lg[0:384, :])
        for k in range(9):
            share_ref[k * CH : (k + 1) * CH, :] = second[:, k * CH : (k + 1) * CH]

    inner_low = jnp.where(at_first, 0.0, 1.0)
    inner_high = jnp.where(at_last, 0.0, 1.0)

    def spread_source(e, j, ref):
        def source(delta, dt):
            if e - delta != 0:
                return None
            if dt == 0:
                return ref[j]
            before = scaled(ref[1], inner_low) if j == 2 else ref[2]
            after = ref[3] if j == 2 else scaled(ref[4], inner_high)
            return pick(before, after) if dt == 1 else pick(after, before)
        return source

    g_zero = jnp.where(at_first, gp[2], gp[4])
    g_end = jnp.where(at_first, gp[1], gp[3])
    g_zero, g_end = pick(g_zero, g_end), pick(g_end, g_zero)
    order_in = [(0, 2), (0, 3), (1, 2), (1, 3), (-1, 2), (-1, 3), None, None]
    for block, at in enumerate(order_in):
        if at is None:
            fill(lc, block, corner_source(block - 6, (g_zero, g_end)[block - 6]))
        else:
            fill(lc, block, spread_source(*at, gp if at[0] == -1 else gpu))
    back = mm(lc[...], w1t[...])
    part = [back[k * 64 : k * 64 + 64] for k in range(8)]
    at_zero, at_end = corner_sums(back[384:512])
    seams = mm(partner, jnp.concatenate([part[4], part[5]], axis=1).astype(BF))
    owe[0] = part[0] + seams[:, :CH] + pick_f(at_zero, at_end) * (1.0 - inner_low)
    owe[1] = part[2]
    owe[2] = part[1] + seams[:, CH:] + pick_f(at_end, at_zero) * (1.0 - inner_high)
    owe[3] = part[3]

    tile = jnp.concatenate([owe[k, pl.ds(pl.multiple_of(group * 16, 16), 16), :] for k in range(4)], axis=0)
    plan = [plan_ref[:, k : k + 1] for k in range(8)]
    flips = [jnp.zeros((48, 1), I32) for _ in range(2)]
    for which in range(4):
        for face_index in range(3):
            value = mirrored_in(fn_ref, rot_ref, 3 * group + face_index, which)
            for k in range(2):
                flips[k] = jnp.where(plan[6 + k] == which * 3 + face_index, value, flips[k])
    last = jnp.where(at_last, 1, 0)
    outer = jnp.logical_or(at_first, at_last)
    row_lane = jnp.where(flips[0] ^ last == plan[4], jnp.where(at_last, plan[1], plan[0]), -1)
    col_lane = jnp.where(flips[1] ^ last == plan[5], jnp.where(at_last, plan[3], plan[2]), -1)
    lanes = lax.broadcasted_iota(I32, (48, 64), 1)
    patch = (row_lane == lanes).astype(F32) + (col_lane == lanes).astype(F32)
    select = jnp.concatenate([jnp.where(outer, patch, sel_ref[0:48, :]), sel_ref[48:72, :]], axis=0)
    tail_ref[...] = mm(select.astype(BF), tile.astype(BF))


def tail_plan():
    select = np.zeros((72, 64), np.float32)
    plan = np.zeros((48, 8), np.int32)
    for pos in range(2):
        for depth in range(2):
            for face in range(3):
                lane = (pos * 2 + depth) * 16 + face
                for half in range(2):
                    select[half * 24 + (pos * 2 + depth) * 3 + face, lane + half * 3] = 1
                for side in range(2):
                    select[48 + ((pos * 2 + side) * 2 + depth) * 3 + face, lane + 6 + 3 * side] = 1
    for half in range(2):
        for side in range(2):
            for face in range(3):
                for row in range(2):
                    for col in range(2):
                        place = half * 24 + ((side * 3 + face) * 2 + row) * 2 + col
                        for last in range(2):
                            plan[place, last] = ((col ^ last) * 2 + row) * 16 + half * 3 + face
                            plan[place, 2 + last] = ((row ^ last) * 2 + col) * 16 + (2 + side) * 3 + face
                        plan[place, 4:] = side, half, half * 3 + face, (2 + side) * 3 + face
    return select, plan


def after_kernel(*refs):
    pass


def share_kernel(own_ref, other_ref, line_ref, out_ref, total):
    total[...] = own_ref[...] + other_ref[...].astype(F32) + line_ref[...]
    for i in range(BANDS):
        rows = [total[CHUNK * i : CHUNK * i + CHUNK, :], jnp.zeros((SLOT_TWO - CHUNK, CH), F32)]
        out_ref[i] = jnp.concatenate(rows, axis=0).astype(BF)


def order_selector():
    select = np.zeros((2, 64, 64), np.float32)
    for pos in range(2):
        for b in range(BANDS):
            select[0, 2 * b + pos, pos * 32 + b] = 1
            select[1, 63 - 2 * b - pos, pos * 32 + b] = 1
    return select


def reduce_kernel(in_ref, out_ref):
    total = in_ref[0].astype(F32)
    for i in range(1, BANDS):
        total = total + in_ref[i].astype(F32)
    out_ref[...] = total


def spread_kernel(factor, _order, own_ref, other_ref, tail_ref, sent, out_ref):
    total = (own_ref[...] + other_ref[...]) * factor
    for i in range(BANDS):
        start = 0 if i == 0 else 24 if i == BANDS - 1 else 48
        parts = [total, sent[i * 16 : i * 16 + 16, :], tail_ref[start : start + 24, :]]
        out_ref[i] = jnp.concatenate(parts, axis=0).astype(BF)


def sums_kernel(in_ref, out_ref):
    for i in range(BANDS):
        out_ref[i] = in_ref[i, 0:48, :].astype(F32)[0:SLOT_TWO].astype(BF)


def unpack_kernel(own_ref, other_ref, first_ref, second_ref):
    _, group = here()
    core = group & 1
    for i in range(BANDS):
        own, other = own_ref[i].astype(F32), other_ref[i].astype(F32)
        rows = slice(CHUNK * i, CHUNK * i + CHUNK)
        first_ref[rows, :] = jnp.where(core == 0, own, other)[0:CHUNK]
        second_ref[rows, :] = jnp.where(core == 0, other, own)[0:CHUNK]


def grad_kernel(fn_ref, rot_ref, sel_ref, in_ref, out_ref, wide, total):
    band, group = here()
    for i in range(BANDS):
        wide[i * 48 : i * 48 + 48, :] = in_ref[i, 32:SLOT_THREE, :].astype(F32)
    for face in range(3):
        for row in range(2):
            for q in range(8):
                piece = wide[pl.ds((4 + face) * 48 + 8 + q * 2 + row, 8, stride=144), :]
                total[row, face, pl.ds(q, 8, stride=8), :] = piece
    tiles = [wide[pl.ds(pl.multiple_of(src * 48, 16), 48), :] for src in (band, BANDS - 1 - band)]
    outer = (band == 0) | (band == BANDS - 1)

    @pl.when(~outer)
    def _():
        for side in range(2):
            for face in range(3):
                flip = mirrored_in(fn_ref, rot_ref, 3 * group + face, 2 + side) == 1
                for row in range(2):
                    for depth in range(2):
                        column = depth if side == 0 else 63 - depth
                        k, m = [24 + ((pos * 2 + side) * 2 + depth) * 3 + face for pos in (row, 1 - row)]
                        extra = jnp.where(flip, tiles[1][m : m + 1, :], tiles[0][k : k + 1, :])
                        total[row, face, column : column + 1, :] += extra

    @pl.when(outer)
    def _():
        half = jnp.where(band == 0, 0, 1)
        patches = tiles[0] + tiles[1]
        place = lax.broadcasted_iota(I32, (SPAN, CH), 0)
        inner = (place >= 2) & (place < SPAN - 2)
        for face in range(3):
            pair = [mirrored_in(fn_ref, rot_ref, 3 * group + face, side) for side in range(2)]
            order = sel_ref[jnp.where(band == 0, pair[0], pair[1])]
            for depth in range(2):
                halves = [wide[pl.ds(24 + (pos * 2 + depth) * 3 + face, BANDS, stride=48), :] for pos in range(2)]
                extra = mm(order, jnp.concatenate(halves, axis=0).astype(BF))
                total[depth ^ half, face] += jnp.where(inner, extra, 0.0)
                for side in range(2):
                    for col in range(2):
                        k = 24 + ((side * 3 + face) * 2 + depth) * 2 + col
                        column = 63 - col if side else col
                        total[depth ^ half, face, column : column + 1, :] += patches[k : k + 1, :]

    for row in range(2):
        for face in range(3):
            out_ref[face, row] = total[row, face].astype(BF)


def swapped(value, step):
    return lax.ppermute(value, "sub", [(i, i ^ step) for i in range(4)])


def body(field_in, grad_out, first_weight, second_weight, face_neighbour, seam_rotation, corner_fill):
    factor = (1.0 * 12 * SPAN * SPAN) ** -0.5
    seams = (face_neighbour.T, seam_rotation.T)
    select, plan = tail_plan()

    slots = call(
        pack_lines,
        jax.ShapeDtypeStruct((BANDS, SLOT_ONE, CH), BF),
        [
            pltpu.VMEM((2, 3, 2, SPAN, CH), BF),
            pltpu.SMEM((4, 12), I32),
            pltpu.SMEM((4, 12), I32),
            pltpu.VMEM(((SPAN + 4) * 12, CH), F32),
            pltpu.VMEM((STRIP, CH), F32),
            pltpu.SemaphoreType.DMA((4,)),
        ],
        tuple(pltpu.with_memory_space_constraint(value, pltpu.HBM) for value in (field_in, grad_out, *seams)),
        dict.fromkeys(range(4), "h"),
    )
    strips = lax.all_to_all(slots, "tile", 0, 0, tiled=True)
    lines = call(
        gather_lines,
        jax.ShapeDtypeStruct((WINDOW, ENDS, CH), BF),
        [],
        (*seams, jnp.asarray(line_selector(), BF), strips),
    )
    lines = (lines, *[swapped(lines, step) for step in (1, 2, 3)])
    tables = (corner_fill.T, jnp.asarray(plan), jnp.asarray(select, F32))
    share = jax.ShapeDtypeStruct((HALF, CH), F32)
    own, away, sent = call(
        interior_kernel,
        [share, jax.ShapeDtypeStruct((HALF, CH), BF), jax.ShapeDtypeStruct((BANDS * 16, CH), F32)],
        [
            pltpu.VMEM((2304, CH), F32),
            pltpu.VMEM((512, CH), F32),
            pltpu.VMEM((1152, CH), BF),
            pltpu.VMEM((1152, CH), BF),
            pltpu.VMEM((768, CH), F32),
            pltpu.VMEM((768, CH), F32),
            pltpu.VMEM((BANDS * UNIT, CH), F32),
        ],
        (*tables, strips, first_weight, second_weight),
    )
    away = call(after_kernel, jax.ShapeDtypeStruct((HALF, CH), BF), [], (away, *lines[1:]), dict.fromkeys((0, 1, 2, 3, "o0"), "a"), {0: 0})
    other = swapped(away, 1)

    line, tails = call(
        main_kernel,
        [share, jax.ShapeDtypeStruct((72, CH), F32)],
        [
            pltpu.VMEM((1152, CH), BF),
            pltpu.VMEM((1152, CH), BF),
            pltpu.VMEM((4, WINDOW, 64, CH), BF),
            pltpu.VMEM((WINDOW, 64, CH), BF),
            pltpu.VMEM((2, 5, 5, 64, CH), BF),
            pltpu.VMEM((256, 1152), BF),
            pltpu.VMEM((640, 1152), BF),
            pltpu.VMEM((512, 1152), BF),
            pltpu.VMEM((5, 64, CH), F32),
            pltpu.VMEM((5, 64, CH), BF),
            pltpu.VMEM((5, 64, CH), BF),
            pltpu.VMEM((4, 64, CH), F32),
        ],
        (*seams, *tables, *lines, first_weight, second_weight),
    )
    slots = call(
        share_kernel,
        jax.ShapeDtypeStruct((BANDS, SLOT_TWO, CH), BF),
        [pltpu.VMEM((HALF, CH), F32)],
        (own, other, line),
    )
    slots = lax.all_to_all(slots, "tile", 0, 0, tiled=True)
    order = jnp.asarray(order_selector(), BF)
    part = call(reduce_kernel, jax.ShapeDtypeStruct((SLOT_TWO, CH), F32), [], (slots,))
    reduced = call(
        lambda *refs: spread_kernel(factor, *refs),
        jax.ShapeDtypeStruct((BANDS, SLOT_THREE, CH), BF),
        [],
        (order, part, swapped(part, 2), tails, sent),
    )
    reduced = lax.all_to_all(reduced, "tile", 0, 0, tiled=True)
    sums = call(sums_kernel, jax.ShapeDtypeStruct((BANDS, SLOT_TWO, CH), BF), [], (reduced,))
    swap = swapped(sums, 1)
    grad_in = call(
        grad_kernel,
        jax.ShapeDtypeStruct((3, 2, SPAN, CH), BF),
        [pltpu.VMEM((BANDS * 48, CH), F32), pltpu.VMEM((2, 3, SPAN, CH), F32)],
        (*seams, order, reduced),
    )
    first, second = call(
        unpack_kernel,
        [jax.ShapeDtypeStruct((1152, CH), F32), jax.ShapeDtypeStruct((1152, CH), F32)],
        [],
        (sums, swap),
    )
    return grad_in, first.reshape(3, 3, CH, CH), second.reshape(3, 3, CH, CH)


def solution(mesh):
    return jax.shard_map(
        body,
        mesh=mesh,
        in_specs=(P("sub", "tile", None, None), P("sub", "tile", None, None), P(), P(), P(), P(), P()),
        out_specs=(P("sub", "tile", None, None), P(), P()),
        check_vma=False,
    )
```

```python
import jax
import jax.numpy as jnp
import numpy as np
from jax import lax
from jax.experimental import pallas as pl
from jax.experimental.pallas import tpu as pltpu
from jax.sharding import PartitionSpec as P

BF = jnp.bfloat16
F32 = jnp.float32
I32 = jnp.int32
BANDS = 32
SPAN = 64
CH = 128
TAPS = [(a, b) for a in range(3) for b in range(3)]
WINDOW = 6
ENDS = 48
STRIP = 12 * WINDOW
UNIT = 48
SLOT_ONE = UNIT + STRIP
HALF = 9 * CH
CHUNK = 36
SLOT_TWO = 40
SLOT_THREE = 80
VMEM_BYTES = 48 * 1024 * 1024


def mm(left, right):
    return jnp.dot(left, right, preferred_element_type=F32)


def mm_t(left, right):
    return lax.dot_general(left, right, (((0,), (0,)), ((), ())), preferred_element_type=F32)


def call(kernel, outs, scratch, operands, places=(), aliases=None):
    kinds = {"v": pltpu.VMEM, "s": pltpu.SMEM, "h": pltpu.HBM, "a": pl.ANY}
    places = dict(places)
    many = isinstance(outs, (list, tuple))
    out_specs = [pl.BlockSpec(memory_space=kinds[places.get(f"o{k}", "v")]) for k in range(len(outs) if many else 1)]
    return pl.pallas_call(
        kernel,
        out_shape=outs,
        in_specs=[pl.BlockSpec(memory_space=kinds[places.get(k, "v")]) for k in range(len(operands))],
        out_specs=out_specs if many else out_specs[0],
        scratch_shapes=scratch,
        input_output_aliases=aliases or {},
        compiler_params=pltpu.CompilerParams(vmem_limit_bytes=VMEM_BYTES),
    )(*operands)


def here():
    return lax.axis_index("tile"), lax.axis_index("sub")


def is_mirrored(fn_ref, rot_ref, face, side):
    rot = rot_ref[face, side]
    partner = 4 * fn_ref[face, side] + (rot & 3)
    return jnp.where(4 * face + side > partner, rot >> 2, 0)


def is_mirrored(fn_ref, rot_ref, face, side):
    rot = rot_ref[side, face]
    partner = 4 * fn_ref[side, face] + (rot & 3)
    return jnp.where(4 * face + side > partner, rot >> 2, 0)


def mirrored_in(fn_ref, rot_ref, face, side):
    lane = lax.broadcasted_iota(I32, (1, 12), 1) == face
    rot = jnp.sum(jnp.where(lane, rot_ref[side : side + 1, :], 0))
    partner = 4 * jnp.sum(jnp.where(lane, fn_ref[side : side + 1, :], 0)) + (rot & 3)
    return jnp.where(4 * face + side > partner, rot >> 2, 0)


def unit_of(band):
    unit = band - 4
    strip = (unit * 43) >> 7
    return strip, unit - 3 * strip


def pack_lines(f_hbm, g_hbm, fn_hbm, rot_hbm, out_ref, buf, fn_ref, rot_ref, wide, ends, sems):
    moves = ((f_hbm, buf.at[0]), (g_hbm, buf.at[1]), (fn_hbm, fn_ref), (rot_hbm, rot_ref))
    copies = [pltpu.make_async_copy(src, dst, sems.at[k]) for k, (src, dst) in enumerate(moves)]
    for copy in copies:
        copy.start()
    band, group = here()
    ends[ENDS:STRIP, :] = jnp.zeros((STRIP - ENDS, CH), F32)
    for fld in range(2):
        copies[fld].wait()
        for row in range(2):
            for face in range(3):
                block = buf[fld, face, row].astype(F32)
                wide[pl.ds(24 + fld * 6 + row * 3 + face, SPAN, stride=12), :] = block
                for edge, cols in enumerate(((0, 1), (63, 62))):
                    for depth, col in enumerate(cols):
                        place = row * 24 + fld * 12 + edge * 6 + depth * 3 + face
                        ends[place : place + 1, :] = block[col : col + 1, :]
    wide[0:24, :] = wide[SPAN * 12 : SPAN * 12 + 24, :]
    wide[SPAN * 12 + 24 : SPAN * 12 + 48, :] = wide[24:48, :]
    for copy in copies[2:]:
        copy.wait()
    side = jnp.where(band == 0, 0, 1)
    row = lax.broadcasted_iota(I32, (STRIP, CH), 0)
    row = row - 3 * ((row * 43) >> 7)
    flip = jnp.zeros((STRIP, CH), I32)
    for face in range(3):
        flip = jnp.where(row == face, is_mirrored(fn_ref, rot_ref, 3 * group + face, side), flip)
    outer = (band == 0) | (band == BANDS - 1)
    strips = [wide[24 * d : 24 * d + STRIP, :] for d in range(BANDS)]
    for d in range(BANDS):
        strip, face = unit_of(d)
        unit = wide[pl.ds(96 * strip + face, UNIT, stride=3), :] if 4 <= d < 28 else ends[0:ENDS, :]
        line = jnp.where(flip == 1, strips[BANDS - 1 - d], strips[d])
        out_ref[d] = jnp.concatenate([unit, jnp.where(outer, line, ends[...])], axis=0).astype(BF)


def line_selector():
    select = np.zeros((2, WINDOW * ENDS, 2 * STRIP + 6 * ENDS), np.float32)
    for mirrored in range(2):
        for j in range(WINDOW):
            part, parity = j // 2, j % 2
            for fld in range(2):
                for depth in range(2):
                    for face in range(3):
                        base = j * ENDS + (fld * 2 + depth) * 12 + face
                        column = (5 - j if mirrored else j) * 12 + fld * 6 + face
                        select[mirrored, base, column + depth * 3] = 1
                        select[mirrored, base + 3, STRIP + column + (1 - depth) * 3] = 1
                        for side in range(2):
                            source = 2 * STRIP + (3 * mirrored + part) * ENDS + (1 - parity if mirrored else parity) * 24
                            select[mirrored, base + 6 + 3 * side, source + fld * 12 + side * 6 + depth * 3 + face] = 1
    return select


def gather_lines(fn_ref, rot_ref, sel_ref, in_ref, out_ref):
    band, group = here()
    pieces = [in_ref[d].astype(F32)[UNIT:SLOT_ONE] for d in (0, BANDS - 1)]
    for source in [band + 31 + part for part in range(3)] + [64 - band - part for part in range(3)]:
        source = source & 31
        outer = (source == 0) | (source == BANDS - 1)
        pieces.append(jnp.where(outer, in_ref[source, 0:ENDS, :], in_ref[source, UNIT : UNIT + ENDS, :]).astype(F32))
    pieces = jnp.concatenate(pieces, axis=0).astype(BF)
    place = lax.broadcasted_iota(I32, (24, CH), 0)
    place = jnp.where(place < 12, place, place - 12)
    flip = jnp.zeros((24, CH), I32)
    lane = lax.broadcasted_iota(I32, (4, 12), 1)
    rot = rot_ref[...]
    partner = 4 * fn_ref[...] + (rot & 3)
    table = jnp.where(4 * lane + lax.broadcasted_iota(I32, (4, 12), 0) > partner, rot >> 2, 0)
    for face in range(3):
        values = jnp.sum(jnp.where(lane == 3 * group + face, table, 0), axis=1, keepdims=True)
        for side in range(4):
            flip = jnp.where(place == side * 3 + face, jnp.broadcast_to(values[side : side + 1], (24, CH)), flip)
    flip = jnp.concatenate([flip.astype(F32)] * (WINDOW * ENDS // 24), axis=0).astype(BF)
    flip = jnp.concatenate([flip] * 4, axis=1)[:, 0 : sel_ref.shape[2]] > 0.5
    picked = mm(jnp.where(flip, sel_ref[1], sel_ref[0]), pieces).astype(BF)
    for j in range(WINDOW):
        out_ref[j] = picked[j * ENDS : (j + 1) * ENDS]


def silu_parts(pre):
    logistic = 1.0 / (1.0 + jnp.exp(-pre))
    return pre * logistic, logistic * (1.0 + pre * (1.0 - logistic))


def side_frame(side, tap):
    dr, dc = tap[0] - 1, tap[1] - 1
    return ((dr, dc), (-dr, dc), (dc, dr), (-dc, dr))[side]


def transpose_weights(ref, out):
    for k, (a, b) in enumerate(TAPS):
        out[k * CH : (k + 1) * CH, :] = ref[a, b].T


def interior_kernel(
    _fill, _plan, _select, in_ref, w1_ref, w2_ref, own_ref, away_ref, sent, acc, done, w1t, w2t, f2, g2, wide
):
    band, group = here()
    strip, _ = unit_of(band)
    transpose_weights(w1_ref, w1t)
    transpose_weights(w2_ref, w2t)
    for s in range(BANDS):
        wide[s * UNIT : (s + 1) * UNIT, :] = in_ref[s, 0:UNIT, :].astype(F32)
    for q in range(12):
        for fld, target in enumerate((f2, g2)):
            for row in range(2):
                piece = wide[pl.ds(q * 4 + fld * 2 + row, BANDS, stride=UNIT), :]
                target[pl.ds(q * 64 + row, BANDS, stride=2), :] = piece

    def conv_weights(ref):
        return jnp.concatenate([ref[a].reshape(3 * CH, CH) for a in range(3)], axis=1)

    def back_weights(ref):
        columns = []
        for a in range(3):
            columns.append(jnp.concatenate([ref[(a * 3 + b) * CH : (a * 3 + b + 1) * CH, :] for b in (2, 1, 0)], axis=0))
        return jnp.concatenate(columns, axis=1)

    def up_one(value):
        return pltpu.roll(value, value.shape[0] - 1, 0)

    def down_one(value):
        return pltpu.roll(value, 1, 0)

    def three_columns(ref, first, count):
        return jnp.concatenate([ref[first + 64 * b : first + 64 * b + count, :].astype(BF) for b in range(3)], axis=1)

    y = mm(three_columns(f2, 0, 640), conv_weights(w1_ref))
    pre = down_one(y[:, :CH]) + y[:, CH : 2 * CH] + up_one(y[:, 2 * CH :])
    z = mm(three_columns(g2, 0, 640), back_weights(w2t))
    back = up_one(z[:, :CH]) + z[:, CH : 2 * CH] + down_one(z[:, 2 * CH :])
    hidden, slope = silu_parts(pre)
    index = lax.broadcasted_iota(I32, (640, CH), 0)
    col = 8 * strip - 1 + (index >> 6)
    row = index & 63
    inner = (row >= 1) & (row <= 62) & (col >= 1) & (col <= 62) & (band >= 4) & (band < 28)
    gpre = jnp.where(inner, back * slope, 0.0).astype(BF)
    hid = jnp.where(inner, hidden, 0.0)[64:576].astype(BF)

    gown = gpre[64:576].astype(F32)
    gcat = jnp.concatenate([up_one(gown).astype(BF), gpre[64:576], down_one(gown).astype(BF)], axis=1)
    first = mm_t(three_columns(f2, 64, 512), gcat)
    hown = hid.astype(F32)
    hcat = jnp.concatenate([down_one(hown).astype(BF), hid, up_one(hown).astype(BF)], axis=1)
    gback = jnp.concatenate([g2[start : start + 512, :].astype(BF) for start in (192, 128, 64)], axis=1)
    second = mm_t(hcat, gback)
    for k, (a, b) in enumerate(TAPS):
        top, low = k * CH, 1152 + k * CH
        acc[top : top + CH, :] = first[b * CH : (b + 1) * CH, a * CH : (a + 1) * CH]
        acc[low : low + CH, :] = second[a * CH : (a + 1) * CH, b * CH : (b + 1) * CH]
    core = group & 1
    own_ref[...] = acc[pl.ds(pl.multiple_of(core * HALF, CH), HALF), :]
    away_ref[...] = acc[pl.ds(pl.multiple_of((1 - core) * HALF, CH), HALF), :].astype(BF)

    gthree = jnp.concatenate([gpre[0:512], gpre[64:576], gpre[128:640]], axis=1)
    z = mm(gthree, back_weights(w1t))
    done[...] = up_one(z[:, :CH]) + z[:, CH : 2 * CH] + down_one(z[:, 2 * CH :]) + g2[128:640, :]
    for q in range(8):
        for row in range(2):
            sent[pl.ds(q * 2 + row, BANDS, stride=16), :] = done[pl.ds(q * 64 + row, BANDS, stride=2), :]


def main_kernel(
    fn_ref, rot_ref, fill_ref, plan_ref, sel_ref, own_ref, one_ref, two_ref, three_ref, w1_ref, w2_ref,
    share_ref, tail_ref,
    w1t, w2t, xs, hal, nb, lp, lg, lc, ss, gp, gpu, owe,
):
    band, group = here()
    transpose_weights(w1_ref, w1t)
    transpose_weights(w2_ref, w2t)

    line = lax.broadcasted_iota(I32, (64, 1), 0)
    place = line & 15
    side = (place >= 3).astype(I32) + (place >= 6).astype(I32) + (place >= 9).astype(I32)
    face = place - 3 * side
    home = line - place
    real = place < 12
    lane = lax.broadcasted_iota(I32, (64, 64), 1)

    def one_hot(target, keep):
        return (jnp.where(keep & real, target, -1) == lane).astype(F32).astype(BF)

    face_lane = lax.broadcasted_iota(I32, (64, 12), 1)
    faces = (jnp.where(real, 3 * (line >> 4) + face, -1) == face_lane).astype(F32).astype(BF)

    def by_line(ref, columns):
        table = ref[...].astype(F32).astype(BF)
        rows = lax.dot_general(faces, table, (((1,), (1,)), ((), ())), preferred_element_type=F32).astype(I32)
        value = rows[:, columns[0] : columns[0] + 1]
        for s in range(1, 4):
            value = jnp.where(side == s, rows[:, columns[s] : columns[s] + 1], value)
        return value

    fn = by_line(fn_ref, (0, 1, 2, 3))
    rot = by_line(rot_ref, (0, 1, 2, 3))
    fn_group = (fn * 43) >> 7
    partner = one_hot(fn_group * 16 + (rot & 3) * 3 + (fn - 3 * fn_group), real)
    number = 4 * (3 * (line >> 4) + face) + side
    flip = ((rot >> 2) == 1) & (number > 4 * fn + (rot & 3)) & real
    fills = []
    for columns in ((0, 2, 0, 1), (1, 3, 2, 3)):
        m = by_line(fill_ref, columns)
        mf = m >> 2
        mg = (mf * 43) >> 7
        target = mg * 16 + ((m >> 1) & 1) * 3 + (mf - 3 * mg)
        fills.append((one_hot(target, (m & 1) == 0), one_hot(target, (m & 1) == 1)))
    corner_cells = jnp.concatenate([jnp.concatenate(pair, axis=1) for pair in fills], axis=0)
    corner_back = corner_cells.astype(F32).T.astype(BF)
    even = (side & 1) == 0
    low_side = jnp.where(side < 2, 2, 0)
    high_side = jnp.where(side < 2, 3, 1)
    beside = jnp.concatenate([
        jnp.concatenate([one_hot(home + other * 3 + face, even), one_hot(home + other * 3 + face, ~even)], axis=1)
        for other in (low_side, high_side)
    ], axis=0)
    side_mask = [jnp.broadcast_to((side == s).astype(F32), (64, CH)).astype(BF) > 0.5 for s in range(4)]
    row_line = (side < 2).astype(F32)
    flip_f = jnp.broadcast_to(flip.astype(F32), (64, CH))
    flip_b = flip_f.astype(BF) > 0.5

    def pick(plain, mirrored):
        return jnp.where(flip_b, mirrored, plain)

    def pick_f(plain, mirrored):
        return jnp.where(flip_f > 0.5, mirrored, plain)

    arrived = (own_ref, one_ref, two_ref, three_ref)
    arrived = [jnp.concatenate([ref[j] for ref in arrived], axis=0) for j in range(WINDOW)]
    row = lax.broadcasted_iota(I32, (256, 1), 0)
    source = (((row >> 4) & 3) ^ group) * ENDS + (row >> 6) * 12 + (row & 15)
    source = jnp.where((row & 15) < 12, source, -1)
    expand = (source == lax.broadcasted_iota(I32, (256, 4 * ENDS), 1)).astype(F32).astype(BF)
    arrived = mm(expand, jnp.concatenate(arrived, axis=1)).astype(BF)
    for j in range(WINDOW):
        for block in range(4):
            xs[block, j] = arrived[block * 64 : block * 64 + 64, j * CH : (j + 1) * CH]
    halos = mm(partner, jnp.concatenate([xs[0, j] for j in range(WINDOW)], axis=1)).astype(BF)
    for j in range(WINDOW):
        hal[j] = halos[:, j * CH : (j + 1) * CH]

    def block_at(block, j):
        return hal[j] if block == 0 else xs[block - 1, j]

    for block in range(5):
        for j in range(1, 5):
            before, after = block_at(block, j - 1), block_at(block, j + 1)
            nb[0, block, j] = pick(before, after)
            nb[1, block, j] = pick(after, before)
    at_first, at_last = band == 0, band == BANDS - 1

    def line_ends(value, lower, upper, choice):
        zero = jnp.where(at_last, value(lower + 2), value(lower))
        end = jnp.where(at_last, value(upper + 2), value(upper))
        return choice(zero, end), choice(end, zero)

    h_zero, h_end = line_ends(lambda j: hal[j], 2, 1, pick)
    h_one, h_last = line_ends(lambda j: hal[j], 3, 0, pick)
    f_zero, f_end = line_ends(lambda j: xs[0, j], 2, 1, pick)
    none = jnp.zeros((64, CH), BF)
    cells = mm(corner_cells, jnp.concatenate([f_zero, f_end], axis=0)).astype(BF)
    sides = jnp.concatenate([jnp.concatenate([h_zero, h_one], axis=1), jnp.concatenate([h_end, h_last], axis=1)], axis=0)
    sides = mm(beside, sides).astype(BF)
    low = [cells[:64], sides[:64, :CH], sides[:64, CH:], none, none]
    high = [cells[64:], sides[64:, :CH], sides[64:, CH:], none, none]
    for block in range(5):
        for slot, here_now in ((2, at_first), (4, at_last)):
            before, after = nb[0, block, slot], nb[1, block, slot]
            nb[0, block, slot] = jnp.where(here_now, pick(low[block], before), before)
            nb[1, block, slot] = jnp.where(here_now, pick(after, high[block]), after)
            before, after = nb[0, block, slot - 1], nb[1, block, slot - 1]
            nb[0, block, slot - 1] = jnp.where(here_now, pick(before, low[block]), before)
            nb[1, block, slot - 1] = jnp.where(here_now, pick(high[block], after), after)
    corner_grad = line_ends(lambda j: xs[2, j], 2, 1, pick)

    def choose(options):
        whole = all(option is not None for option in options)
        result = options[0] if whole else jnp.zeros((64, CH), BF)
        for s, option in enumerate(options):
            if option is not None and not (whole and s == 0):
                result = jnp.where(side_mask[s], option, result)
        return result

    def fill(target, block, source):
        for k, tap in enumerate(TAPS):
            target[block * 64 : block * 64 + 64, k * CH : (k + 1) * CH] = choose(
                [source(*side_frame(s, tap)) for s in range(4)]
            )

    def field_source(j):
        def source(delta, dt):
            return block_at(delta + 1, j) if dt == 0 else nb[(dt + 1) // 2, delta + 1, j]
        return source

    def grad_source(e, j):
        def source(delta, dt):
            depth = e - delta
            if depth not in (0, 1):
                return None
            return xs[2 + depth, j] if dt == 0 else nb[(1 - dt) // 2, 3 + depth, j]
        return source

    def corner_source(which, value):
        def source(delta, dt):
            return value if (delta, dt) == (-1, 2 * which - 1) else None
        return source

    order_pre = (2, 3, 1, 4)
    for block, j in enumerate(order_pre):
        fill(lp, block, field_source(j))
    order_back = [(0, 2), (0, 3), (-1, 2), (-1, 3), None, None, (0, 1), (0, 4), (-1, 1), (-1, 4)]
    for block, at in enumerate(order_back):
        fill(lg, block, corner_source(block - 4, corner_grad[block - 4]) if at is None else grad_source(*at))

    pre = mm(lp[...], w1_ref[...].reshape(9 * CH, CH))
    back = mm(lg[...], w2t[...])

    def back_block(e, j):
        block = order_back.index((e, j))
        return back[block * 64 : block * 64 + 64]

    seams = jnp.concatenate([back_block(-1, j).astype(BF) for j in range(1, 5)], axis=1)
    seams = mm(partner, seams)
    for j in range(1, 5):
        ss[j] = seams[:, (j - 1) * CH : j * CH]
    both_rows = jnp.concatenate([row_line, row_line], axis=0)

    def corner_sums(both):
        sums = mm(corner_back, (both * both_rows).astype(BF))
        return sums[:64], sums[64:]


    at_zero, at_end = corner_sums(back[256:384])
    head, tail = line_ends(lambda j: ss[j], 2, 1, pick_f)
    head, tail = head + at_zero, tail + at_end
    sides = mm(beside, jnp.concatenate([head, tail], axis=0).astype(BF))
    head, tail = head + sides[:64], tail + sides[64:]
    for slot, here_now in ((2, at_first), (4, at_last)):
        ss[slot] = jnp.where(here_now, pick_f(head, tail), ss[slot])
        ss[slot - 1] = jnp.where(here_now, pick_f(tail, head), ss[slot - 1])

    unique = {}
    hid = {}
    for block, j in enumerate(order_pre):
        value = pre[block * 64 : block * 64 + 64]
        hidden, slope = silu_parts(value)
        t = (2 * band - 2 + j) & (SPAN - 1)
        corner = jnp.logical_or(t == 0, t == SPAN - 1)
        unique[j] = jnp.where(corner, row_line, jnp.ones_like(row_line))
        grad = ((back_block(0, j) + ss[j]) * slope).astype(BF)
        gp[j] = grad
        gpu[j] = (grad.astype(F32) * unique[j]).astype(BF)
        hid[j] = hidden.astype(BF)

    mine = ((line >> 5) == (group >> 1)).astype(F32)
    edge = jnp.where(band == 0, 1.0, 0.0) * mine * row_line

    def scaled(value, factor):
        return (value.astype(F32) * factor).astype(BF)

    h_zero, h_end = pick(hid[2], hid[1]), pick(hid[1], hid[2])
    halos = mm(partner, jnp.concatenate([hid[2], hid[3]], axis=1))
    ends = mm(corner_cells, jnp.concatenate([h_zero, h_end], axis=0))
    cells = jnp.concatenate([
        scaled(hid[2], mine * unique[2]),
        scaled(hid[3], mine * unique[3]),
        scaled(halos[:, :CH], mine),
        scaled(halos[:, CH:], mine),
        scaled(ends[:64], edge),
        scaled(ends[64:], edge),
    ], axis=0)
    @pl.when((group & 1) == 0)
    def _():
        own = jnp.concatenate([scaled(gpu[2], mine), scaled(gpu[3], mine)], axis=0)
        share_ref[...] = mm_t(lp[0:128, :], own)

    @pl.when((group & 1) == 1)
    def _():
        second = mm_t(cells, lg[0:384, :])
        for k in range(9):
            share_ref[k * CH : (k + 1) * CH, :] = second[:, k * CH : (k + 1) * CH]

    inner_low = jnp.where(at_first, 0.0, 1.0)
    inner_high = jnp.where(at_last, 0.0, 1.0)

    def spread_source(e, j, ref):
        def source(delta, dt):
            if e - delta != 0:
                return None
            if dt == 0:
                return ref[j]
            before = scaled(ref[1], inner_low) if j == 2 else ref[2]
            after = ref[3] if j == 2 else scaled(ref[4], inner_high)
            return pick(before, after) if dt == 1 else pick(after, before)
        return source

    g_zero = jnp.where(at_first, gp[2], gp[4])
    g_end = jnp.where(at_first, gp[1], gp[3])
    g_zero, g_end = pick(g_zero, g_end), pick(g_end, g_zero)
    order_in = [(0, 2), (0, 3), (1, 2), (1, 3), (-1, 2), (-1, 3), None, None]
    for block, at in enumerate(order_in):
        if at is None:
            fill(lc, block, corner_source(block - 6, (g_zero, g_end)[block - 6]))
        else:
            fill(lc, block, spread_source(*at, gp if at[0] == -1 else gpu))
    back = mm(lc[...], w1t[...])
    part = [back[k * 64 : k * 64 + 64] for k in range(8)]
    at_zero, at_end = corner_sums(back[384:512])
    seams = mm(partner, jnp.concatenate([part[4], part[5]], axis=1).astype(BF))
    owe[0] = part[0] + seams[:, :CH] + pick_f(at_zero, at_end) * (1.0 - inner_low)
    owe[1] = part[2]
    owe[2] = part[1] + seams[:, CH:] + pick_f(at_end, at_zero) * (1.0 - inner_high)
    owe[3] = part[3]

    tile = jnp.concatenate([owe[k, pl.ds(pl.multiple_of(group * 16, 16), 16), :] for k in range(4)], axis=0)
    plan = [plan_ref[:, k : k + 1] for k in range(8)]
    flips = [jnp.zeros((48, 1), I32) for _ in range(2)]
    table_lane = lax.broadcasted_iota(I32, (4, 12), 1)
    rotations = rot_ref[...]
    partners = 4 * fn_ref[...] + (rotations & 3)
    table = jnp.where(4 * table_lane + lax.broadcasted_iota(I32, (4, 12), 0) > partners, rotations >> 2, 0)
    for face_index in range(3):
        values = jnp.sum(jnp.where(table_lane == 3 * group + face_index, table, 0), axis=1, keepdims=True)
        for which in range(4):
            value = jnp.broadcast_to(values[which : which + 1], (48, 1))
            for k in range(2):
                flips[k] = jnp.where(plan[6 + k] == which * 3 + face_index, value, flips[k])
    last = jnp.where(at_last, 1, 0)
    outer = jnp.logical_or(at_first, at_last)
    row_lane = jnp.where(flips[0] ^ last == plan[4], jnp.where(at_last, plan[1], plan[0]), -1)
    col_lane = jnp.where(flips[1] ^ last == plan[5], jnp.where(at_last, plan[3], plan[2]), -1)
    lanes = lax.broadcasted_iota(I32, (48, 64), 1)
    patch = (row_lane == lanes).astype(F32) + (col_lane == lanes).astype(F32)
    select = jnp.concatenate([jnp.where(outer, patch, sel_ref[0:48, :]), sel_ref[48:72, :]], axis=0)
    tail_ref[...] = mm(select.astype(BF), tile.astype(BF))


def tail_plan():
    select = np.zeros((72, 64), np.float32)
    plan = np.zeros((48, 8), np.int32)
    for pos in range(2):
        for depth in range(2):
            for face in range(3):
                lane = (pos * 2 + depth) * 16 + face
                for half in range(2):
                    select[half * 24 + (pos * 2 + depth) * 3 + face, lane + half * 3] = 1
                for side in range(2):
                    select[48 + ((pos * 2 + side) * 2 + depth) * 3 + face, lane + 6 + 3 * side] = 1
    for half in range(2):
        for side in range(2):
            for face in range(3):
                for row in range(2):
                    for col in range(2):
                        place = half * 24 + ((side * 3 + face) * 2 + row) * 2 + col
                        for last in range(2):
                            plan[place, last] = ((col ^ last) * 2 + row) * 16 + half * 3 + face
                            plan[place, 2 + last] = ((row ^ last) * 2 + col) * 16 + (2 + side) * 3 + face
                        plan[place, 4:] = side, half, half * 3 + face, (2 + side) * 3 + face
    return select, plan


def after_kernel(*refs):
    pass


def share_kernel(own_ref, other_ref, line_ref, out_ref, total):
    total[...] = own_ref[...] + other_ref[...].astype(F32) + line_ref[...]
    for i in range(BANDS):
        rows = [total[CHUNK * i : CHUNK * i + CHUNK, :], jnp.zeros((SLOT_TWO - CHUNK, CH), F32)]
        out_ref[i] = jnp.concatenate(rows, axis=0).astype(BF)


def order_selector():
    select = np.zeros((2, 64, 64), np.float32)
    for pos in range(2):
        for b in range(BANDS):
            select[0, 2 * b + pos, pos * 32 + b] = 1
            select[1, 63 - 2 * b - pos, pos * 32 + b] = 1
    return select


def reduce_kernel(in_ref, out_ref):
    total = in_ref[0].astype(F32)
    for i in range(1, BANDS):
        total = total + in_ref[i].astype(F32)
    out_ref[...] = total


def spread_kernel(factor, _order, own_ref, other_ref, tail_ref, sent, out_ref):
    total = (own_ref[...] + other_ref[...]) * factor
    for i in range(BANDS):
        start = 0 if i == 0 else 24 if i == BANDS - 1 else 48
        parts = [total, sent[i * 16 : i * 16 + 16, :], tail_ref[start : start + 24, :]]
        out_ref[i] = jnp.concatenate(parts, axis=0).astype(BF)


def sums_kernel(in_ref, out_ref):
    for i in range(BANDS):
        out_ref[i] = in_ref[i, 0:48, :].astype(F32)[0:SLOT_TWO].astype(BF)


def unpack_kernel(own_ref, other_ref, first_ref, second_ref):
    _, group = here()
    core = group & 1
    for i in range(BANDS):
        own, other = own_ref[i].astype(F32), other_ref[i].astype(F32)
        rows = slice(CHUNK * i, CHUNK * i + CHUNK)
        first_ref[rows, :] = jnp.where(core == 0, own, other)[0:CHUNK]
        second_ref[rows, :] = jnp.where(core == 0, other, own)[0:CHUNK]


def grad_kernel(fn_ref, rot_ref, sel_ref, in_ref, out_ref, wide, total):
    band, group = here()
    for i in range(BANDS):
        wide[i * 48 : i * 48 + 48, :] = in_ref[i, 32:SLOT_THREE, :].astype(F32)
    for face in range(3):
        for row in range(2):
            for q in range(8):
                piece = wide[pl.ds((4 + face) * 48 + 8 + q * 2 + row, 8, stride=144), :]
                total[row, face, pl.ds(q, 8, stride=8), :] = piece
    tiles = [wide[pl.ds(pl.multiple_of(src * 48, 16), 48), :] for src in (band, BANDS - 1 - band)]
    outer = (band == 0) | (band == BANDS - 1)

    @pl.when(~outer)
    def _():
        for side in range(2):
            for face in range(3):
                flip = mirrored_in(fn_ref, rot_ref, 3 * group + face, 2 + side) == 1
                for row in range(2):
                    for depth in range(2):
                        column = depth if side == 0 else 63 - depth
                        k, m = [24 + ((pos * 2 + side) * 2 + depth) * 3 + face for pos in (row, 1 - row)]
                        extra = jnp.where(flip, tiles[1][m : m + 1, :], tiles[0][k : k + 1, :])
                        total[row, face, column : column + 1, :] += extra

    @pl.when(outer)
    def _():
        half = jnp.where(band == 0, 0, 1)
        patches = tiles[0] + tiles[1]
        place = lax.broadcasted_iota(I32, (SPAN, CH), 0)
        inner = (place >= 2) & (place < SPAN - 2)
        for face in range(3):
            pair = [mirrored_in(fn_ref, rot_ref, 3 * group + face, side) for side in range(2)]
            order = sel_ref[jnp.where(band == 0, pair[0], pair[1])]
            for depth in range(2):
                halves = [wide[pl.ds(24 + (pos * 2 + depth) * 3 + face, BANDS, stride=48), :] for pos in range(2)]
                extra = mm(order, jnp.concatenate(halves, axis=0).astype(BF))
                total[depth ^ half, face] += jnp.where(inner, extra, 0.0)
                for side in range(2):
                    for col in range(2):
                        k = 24 + ((side * 3 + face) * 2 + depth) * 2 + col
                        column = 63 - col if side else col
                        total[depth ^ half, face, column : column + 1, :] += patches[k : k + 1, :]

    for row in range(2):
        for face in range(3):
            out_ref[face, row] = total[row, face].astype(BF)


def swapped(value, step):
    return lax.ppermute(value, "sub", [(i, i ^ step) for i in range(4)])


def body(field_in, grad_out, first_weight, second_weight, face_neighbour, seam_rotation, corner_fill):
    factor = (1.0 * 12 * SPAN * SPAN) ** -0.5
    seams = (face_neighbour.T, seam_rotation.T)
    select, plan = tail_plan()

    slots = call(
        pack_lines,
        jax.ShapeDtypeStruct((BANDS, SLOT_ONE, CH), BF),
        [
            pltpu.VMEM((2, 3, 2, SPAN, CH), BF),
            pltpu.SMEM((4, 12), I32),
            pltpu.SMEM((4, 12), I32),
            pltpu.VMEM(((SPAN + 4) * 12, CH), F32),
            pltpu.VMEM((STRIP, CH), F32),
            pltpu.SemaphoreType.DMA((4,)),
        ],
        tuple(pltpu.with_memory_space_constraint(value, pltpu.HBM) for value in (field_in, grad_out, *seams)),
        dict.fromkeys(range(4), "h"),
    )
    strips = lax.all_to_all(slots, "tile", 0, 0, tiled=True)
    lines = call(
        gather_lines,
        jax.ShapeDtypeStruct((WINDOW, ENDS, CH), BF),
        [],
        (*seams, jnp.asarray(line_selector(), BF), strips),
    )
    beyond, beside = swapped(lines, 2), swapped(lines, 1)
    tables = (corner_fill.T, jnp.asarray(plan), jnp.asarray(select, F32))
    share = jax.ShapeDtypeStruct((HALF, CH), F32)
    own, away, sent = call(
        interior_kernel,
        [share, jax.ShapeDtypeStruct((HALF, CH), BF), jax.ShapeDtypeStruct((BANDS * 16, CH), F32)],
        [
            pltpu.VMEM((2304, CH), F32),
            pltpu.VMEM((512, CH), F32),
            pltpu.VMEM((1152, CH), BF),
            pltpu.VMEM((1152, CH), BF),
            pltpu.VMEM((768, CH), F32),
            pltpu.VMEM((768, CH), F32),
            pltpu.VMEM((BANDS * UNIT, CH), F32),
        ],
        (*tables, strips, first_weight, second_weight),
    )
    beyond = call(after_kernel, jax.ShapeDtypeStruct((WINDOW, ENDS, CH), BF), [], (beyond, own), dict.fromkeys((0, 1, "o0"), "a"), {0: 0})
    lines = (lines, beside, beyond, swapped(beyond, 1))
    away = call(after_kernel, jax.ShapeDtypeStruct((HALF, CH), BF), [], (away, *lines[1:]), dict.fromkeys((0, 1, 2, 3, "o0"), "a"), {0: 0})
    other = swapped(away, 1)

    line, tails = call(
        main_kernel,
        [share, jax.ShapeDtypeStruct((72, CH), F32)],
        [
            pltpu.VMEM((1152, CH), BF),
            pltpu.VMEM((1152, CH), BF),
            pltpu.VMEM((4, WINDOW, 64, CH), BF),
            pltpu.VMEM((WINDOW, 64, CH), BF),
            pltpu.VMEM((2, 5, 5, 64, CH), BF),
            pltpu.VMEM((256, 1152), BF),
            pltpu.VMEM((640, 1152), BF),
            pltpu.VMEM((512, 1152), BF),
            pltpu.VMEM((5, 64, CH), F32),
            pltpu.VMEM((5, 64, CH), BF),
            pltpu.VMEM((5, 64, CH), BF),
            pltpu.VMEM((4, 64, CH), F32),
        ],
        (*seams, *tables, *lines, first_weight, second_weight),
    )
    slots = call(
        share_kernel,
        jax.ShapeDtypeStruct((BANDS, SLOT_TWO, CH), BF),
        [pltpu.VMEM((HALF, CH), F32)],
        (own, other, line),
    )
    slots = lax.all_to_all(slots, "tile", 0, 0, tiled=True)
    order = jnp.asarray(order_selector(), BF)
    part = call(reduce_kernel, jax.ShapeDtypeStruct((SLOT_TWO, CH), F32), [], (slots,))
    reduced = call(
        lambda *refs: spread_kernel(factor, *refs),
        jax.ShapeDtypeStruct((BANDS, SLOT_THREE, CH), BF),
        [],
        (order, part, swapped(part, 2), tails, sent),
    )
    reduced = lax.all_to_all(reduced, "tile", 0, 0, tiled=True)
    sums = call(sums_kernel, jax.ShapeDtypeStruct((BANDS, SLOT_TWO, CH), BF), [], (reduced,))
    swap = swapped(sums, 1)
    grad_in = call(
        grad_kernel,
        jax.ShapeDtypeStruct((3, 2, SPAN, CH), BF),
        [pltpu.VMEM((BANDS * 48, CH), F32), pltpu.VMEM((2, 3, SPAN, CH), F32)],
        (*seams, order, reduced),
    )
    first, second = call(
        unpack_kernel,
        [jax.ShapeDtypeStruct((1152, CH), F32), jax.ShapeDtypeStruct((1152, CH), F32)],
        [],
        (sums, swap),
    )
    return grad_in, first.reshape(3, 3, CH, CH), second.reshape(3, 3, CH, CH)


def solution(mesh):
    return jax.shard_map(
        body,
        mesh=mesh,
        in_specs=(P("sub", "tile", None, None), P("sub", "tile", None, None), P(), P(), P(), P(), P()),
        out_specs=(P("sub", "tile", None, None), P(), P()),
        check_vma=False,
    )
```

```python
import jax
import jax.numpy as jnp
import numpy as np
from jax import lax
from jax.experimental import pallas as pl
from jax.experimental.pallas import tpu as pltpu
from jax.sharding import PartitionSpec as P

BF = jnp.bfloat16
F32 = jnp.float32
I32 = jnp.int32
BANDS = 32
SPAN = 64
CH = 128
TAPS = [(a, b) for a in range(3) for b in range(3)]
WINDOW = 6
ENDS = 48
STRIP = 12 * WINDOW
UNIT = 48
SLOT_ONE = UNIT + STRIP
HALF = 9 * CH
CHUNK = 36
SLOT_TWO = 40
SLOT_THREE = 80
VMEM_BYTES = 48 * 1024 * 1024


def mm(left, right):
    return jnp.dot(left, right, preferred_element_type=F32)


def mm_t(left, right):
    return lax.dot_general(left, right, (((0,), (0,)), ((), ())), preferred_element_type=F32)


def call(kernel, outs, scratch, operands, places=(), aliases=None):
    kinds = {"v": pltpu.VMEM, "s": pltpu.SMEM, "h": pltpu.HBM, "a": pl.ANY}
    places = dict(places)
    many = isinstance(outs, (list, tuple))
    out_specs = [pl.BlockSpec(memory_space=kinds[places.get(f"o{k}", "v")]) for k in range(len(outs) if many else 1)]
    return pl.pallas_call(
        kernel,
        out_shape=outs,
        in_specs=[pl.BlockSpec(memory_space=kinds[places.get(k, "v")]) for k in range(len(operands))],
        out_specs=out_specs if many else out_specs[0],
        scratch_shapes=scratch,
        input_output_aliases=aliases or {},
        compiler_params=pltpu.CompilerParams(vmem_limit_bytes=VMEM_BYTES),
    )(*operands)


def here():
    return lax.axis_index("tile"), lax.axis_index("sub")


def is_mirrored(fn_ref, rot_ref, face, side):
    rot = rot_ref[face, side]
    partner = 4 * fn_ref[face, side] + (rot & 3)
    return jnp.where(4 * face + side > partner, rot >> 2, 0)


def is_mirrored(fn_ref, rot_ref, face, side):
    rot = rot_ref[side, face]
    partner = 4 * fn_ref[side, face] + (rot & 3)
    return jnp.where(4 * face + side > partner, rot >> 2, 0)


def mirrored_in(fn_ref, rot_ref, face, side):
    lane = lax.broadcasted_iota(I32, (1, 12), 1) == face
    rot = jnp.sum(jnp.where(lane, rot_ref[side : side + 1, :], 0))
    partner = 4 * jnp.sum(jnp.where(lane, fn_ref[side : side + 1, :], 0)) + (rot & 3)
    return jnp.where(4 * face + side > partner, rot >> 2, 0)


def unit_of(band):
    unit = band - 4
    strip = (unit * 43) >> 7
    return strip, unit - 3 * strip


def pack_lines(f_hbm, g_hbm, fn_hbm, rot_hbm, out_ref, buf, fn_ref, rot_ref, wide, ends, sems):
    moves = ((f_hbm, buf.at[0]), (g_hbm, buf.at[1]), (fn_hbm, fn_ref), (rot_hbm, rot_ref))
    copies = [pltpu.make_async_copy(src, dst, sems.at[k]) for k, (src, dst) in enumerate(moves)]
    for copy in copies:
        copy.start()
    band, group = here()
    ends[ENDS:STRIP, :] = jnp.zeros((STRIP - ENDS, CH), F32)
    for fld in range(2):
        copies[fld].wait()
        for row in range(2):
            for face in range(3):
                block = buf[fld, face, row].astype(F32)
                wide[pl.ds(24 + fld * 6 + row * 3 + face, SPAN, stride=12), :] = block
                for edge, cols in enumerate(((0, 1), (63, 62))):
                    for depth, col in enumerate(cols):
                        place = row * 24 + fld * 12 + edge * 6 + depth * 3 + face
                        ends[place : place + 1, :] = block[col : col + 1, :]
    wide[0:24, :] = wide[SPAN * 12 : SPAN * 12 + 24, :]
    wide[SPAN * 12 + 24 : SPAN * 12 + 48, :] = wide[24:48, :]
    for copy in copies[2:]:
        copy.wait()
    side = jnp.where(band == 0, 0, 1)
    row = lax.broadcasted_iota(I32, (STRIP, CH), 0)
    row = row - 3 * ((row * 43) >> 7)
    flip = jnp.zeros((STRIP, CH), I32)
    for face in range(3):
        flip = jnp.where(row == face, is_mirrored(fn_ref, rot_ref, 3 * group + face, side), flip)
    outer = (band == 0) | (band == BANDS - 1)
    strips = [wide[24 * d : 24 * d + STRIP, :] for d in range(BANDS)]
    for d in range(BANDS):
        strip, face = unit_of(d)
        unit = wide[pl.ds(96 * strip + face, UNIT, stride=3), :] if 4 <= d < 28 else ends[0:ENDS, :]
        line = jnp.where(flip == 1, strips[BANDS - 1 - d], strips[d])
        out_ref[d] = jnp.concatenate([unit, jnp.where(outer, line, ends[...])], axis=0).astype(BF)


def line_selector():
    select = np.zeros((2, WINDOW * ENDS, 2 * STRIP + 6 * ENDS), np.float32)
    for mirrored in range(2):
        for j in range(WINDOW):
            part, parity = j // 2, j % 2
            for fld in range(2):
                for depth in range(2):
                    for face in range(3):
                        base = j * ENDS + (fld * 2 + depth) * 12 + face
                        column = (5 - j if mirrored else j) * 12 + fld * 6 + face
                        select[mirrored, base, column + depth * 3] = 1
                        select[mirrored, base + 3, STRIP + column + (1 - depth) * 3] = 1
                        for side in range(2):
                            source = 2 * STRIP + (3 * mirrored + part) * ENDS + (1 - parity if mirrored else parity) * 24
                            select[mirrored, base + 6 + 3 * side, source + fld * 12 + side * 6 + depth * 3 + face] = 1
    return select


def gather_lines(fn_ref, rot_ref, sel_ref, in_ref, out_ref):
    band, group = here()
    pieces = [in_ref[d].astype(F32)[UNIT:SLOT_ONE] for d in (0, BANDS - 1)]
    for source in [band + 31 + part for part in range(3)] + [64 - band - part for part in range(3)]:
        source = source & 31
        outer = (source == 0) | (source == BANDS - 1)
        pieces.append(jnp.where(outer, in_ref[source, 0:ENDS, :], in_ref[source, UNIT : UNIT + ENDS, :]).astype(F32))
    pieces = jnp.concatenate(pieces, axis=0).astype(BF)
    place = lax.broadcasted_iota(I32, (24, CH), 0)
    place = jnp.where(place < 12, place, place - 12)
    flip = jnp.zeros((24, CH), I32)
    lane = lax.broadcasted_iota(I32, (4, 12), 1)
    rot = rot_ref[...]
    partner = 4 * fn_ref[...] + (rot & 3)
    table = jnp.where(4 * lane + lax.broadcasted_iota(I32, (4, 12), 0) > partner, rot >> 2, 0)
    for face in range(3):
        values = jnp.sum(jnp.where(lane == 3 * group + face, table, 0), axis=1, keepdims=True)
        for side in range(4):
            flip = jnp.where(place == side * 3 + face, jnp.broadcast_to(values[side : side + 1], (24, CH)), flip)
    flip = jnp.concatenate([flip.astype(F32)] * (WINDOW * ENDS // 24), axis=0).astype(BF)
    flip = jnp.concatenate([flip] * 4, axis=1)[:, 0 : sel_ref.shape[2]] > 0.5
    picked = mm(jnp.where(flip, sel_ref[1], sel_ref[0]), pieces).astype(BF)
    for j in range(WINDOW):
        out_ref[j] = picked[j * ENDS : (j + 1) * ENDS]


def silu_parts(pre):
    logistic = 1.0 / (1.0 + jnp.exp(-pre))
    return pre * logistic, logistic * (1.0 + pre * (1.0 - logistic))


def side_frame(side, tap):
    dr, dc = tap[0] - 1, tap[1] - 1
    return ((dr, dc), (-dr, dc), (dc, dr), (-dc, dr))[side]


def transpose_weights(ref, out):
    for k, (a, b) in enumerate(TAPS):
        out[k * CH : (k + 1) * CH, :] = ref[a, b].T


def interior_kernel(
    _fill, _plan, _select, in_ref, w1_ref, w2_ref, own_ref, away_ref, sent, acc, done, w1t, w2t, f2, g2, wide
):
    band, group = here()
    strip, _ = unit_of(band)
    transpose_weights(w1_ref, w1t)
    transpose_weights(w2_ref, w2t)
    for s in range(BANDS):
        wide[s * UNIT : (s + 1) * UNIT, :] = in_ref[s, 0:UNIT, :].astype(F32)
    for q in range(12):
        for fld, target in enumerate((f2, g2)):
            for row in range(2):
                piece = wide[pl.ds(q * 4 + fld * 2 + row, BANDS, stride=UNIT), :]
                target[pl.ds(q * 64 + row, BANDS, stride=2), :] = piece

    def conv_weights(ref):
        return jnp.concatenate([ref[a].reshape(3 * CH, CH) for a in range(3)], axis=1)

    def back_weights(ref):
        columns = []
        for a in range(3):
            columns.append(jnp.concatenate([ref[(a * 3 + b) * CH : (a * 3 + b + 1) * CH, :] for b in (2, 1, 0)], axis=0))
        return jnp.concatenate(columns, axis=1)

    def up_one(value):
        return pltpu.roll(value, value.shape[0] - 1, 0)

    def down_one(value):
        return pltpu.roll(value, 1, 0)

    def three_columns(ref, first, count):
        return jnp.concatenate([ref[first + 64 * b : first + 64 * b + count, :].astype(BF) for b in range(3)], axis=1)

    y = mm(three_columns(f2, 0, 640), conv_weights(w1_ref))
    pre = down_one(y[:, :CH]) + y[:, CH : 2 * CH] + up_one(y[:, 2 * CH :])
    z = mm(three_columns(g2, 0, 640), back_weights(w2t))
    back = up_one(z[:, :CH]) + z[:, CH : 2 * CH] + down_one(z[:, 2 * CH :])
    hidden, slope = silu_parts(pre)
    index = lax.broadcasted_iota(I32, (640, CH), 0)
    col = 8 * strip - 1 + (index >> 6)
    row = index & 63
    inner = (row >= 1) & (row <= 62) & (col >= 1) & (col <= 62) & (band >= 4) & (band < 28)
    gpre = jnp.where(inner, back * slope, 0.0).astype(BF)
    hid = jnp.where(inner, hidden, 0.0)[64:576].astype(BF)

    gown = gpre[64:576].astype(F32)
    gcat = jnp.concatenate([up_one(gown).astype(BF), gpre[64:576], down_one(gown).astype(BF)], axis=1)
    first = mm_t(three_columns(f2, 64, 512), gcat)
    hown = hid.astype(F32)
    hcat = jnp.concatenate([down_one(hown).astype(BF), hid, up_one(hown).astype(BF)], axis=1)
    gback = jnp.concatenate([g2[start : start + 512, :].astype(BF) for start in (192, 128, 64)], axis=1)
    second = mm_t(hcat, gback)
    for k, (a, b) in enumerate(TAPS):
        top, low = k * CH, 1152 + k * CH
        acc[top : top + CH, :] = first[b * CH : (b + 1) * CH, a * CH : (a + 1) * CH]
        acc[low : low + CH, :] = second[a * CH : (a + 1) * CH, b * CH : (b + 1) * CH]
    core = group & 1
    own_ref[...] = acc[pl.ds(pl.multiple_of(core * HALF, CH), HALF), :]
    away_ref[...] = acc[pl.ds(pl.multiple_of((1 - core) * HALF, CH), HALF), :].astype(BF)

    gthree = jnp.concatenate([gpre[0:512], gpre[64:576], gpre[128:640]], axis=1)
    z = mm(gthree, back_weights(w1t))
    done[...] = up_one(z[:, :CH]) + z[:, CH : 2 * CH] + down_one(z[:, 2 * CH :]) + g2[128:640, :]
    for q in range(8):
        for row in range(2):
            sent[pl.ds(q * 2 + row, BANDS, stride=16), :] = done[pl.ds(q * 64 + row, BANDS, stride=2), :]


def main_kernel(
    fn_ref, rot_ref, fill_ref, plan_ref, sel_ref, own_ref, one_ref, two_ref, three_ref, w1_ref, w2_ref,
    share_ref, tail_ref,
    w1t, w2t, xs, hal, nb, lp, lg, lc, ss, gp, gpu, owe,
):
    band, group = here()
    transpose_weights(w1_ref, w1t)
    transpose_weights(w2_ref, w2t)

    line = lax.broadcasted_iota(I32, (64, 1), 0)
    place = line & 15
    side = (place >= 3).astype(I32) + (place >= 6).astype(I32) + (place >= 9).astype(I32)
    face = place - 3 * side
    home = line - place
    real = place < 12
    lane = lax.broadcasted_iota(I32, (64, 64), 1)

    def one_hot(target, keep):
        return (jnp.where(keep & real, target, -1) == lane).astype(F32).astype(BF)

    face_lane = lax.broadcasted_iota(I32, (64, 12), 1)
    faces = (jnp.where(real, 3 * (line >> 4) + face, -1) == face_lane).astype(F32).astype(BF)

    def by_line(ref, columns):
        table = ref[...].astype(F32).astype(BF)
        rows = lax.dot_general(faces, table, (((1,), (1,)), ((), ())), preferred_element_type=F32).astype(I32)
        value = rows[:, columns[0] : columns[0] + 1]
        for s in range(1, 4):
            value = jnp.where(side == s, rows[:, columns[s] : columns[s] + 1], value)
        return value

    fn = by_line(fn_ref, (0, 1, 2, 3))
    rot = by_line(rot_ref, (0, 1, 2, 3))
    fn_group = (fn * 43) >> 7
    partner = one_hot(fn_group * 16 + (rot & 3) * 3 + (fn - 3 * fn_group), real)
    number = 4 * (3 * (line >> 4) + face) + side
    flip = ((rot >> 2) == 1) & (number > 4 * fn + (rot & 3)) & real
    fills = []
    for columns in ((0, 2, 0, 1), (1, 3, 2, 3)):
        m = by_line(fill_ref, columns)
        mf = m >> 2
        mg = (mf * 43) >> 7
        target = mg * 16 + ((m >> 1) & 1) * 3 + (mf - 3 * mg)
        fills.append((one_hot(target, (m & 1) == 0), one_hot(target, (m & 1) == 1)))
    corner_cells = jnp.concatenate([jnp.concatenate(pair, axis=1) for pair in fills], axis=0)
    corner_back = corner_cells.astype(F32).T.astype(BF)
    even = (side & 1) == 0
    low_side = jnp.where(side < 2, 2, 0)
    high_side = jnp.where(side < 2, 3, 1)
    beside = jnp.concatenate([
        jnp.concatenate([one_hot(home + other * 3 + face, even), one_hot(home + other * 3 + face, ~even)], axis=1)
        for other in (low_side, high_side)
    ], axis=0)
    side_mask = [jnp.broadcast_to((side == s).astype(F32), (64, CH)).astype(BF) > 0.5 for s in range(4)]
    row_line = (side < 2).astype(F32)
    flip_f = jnp.broadcast_to(flip.astype(F32), (64, CH))
    flip_b = flip_f.astype(BF) > 0.5

    def pick(plain, mirrored):
        return jnp.where(flip_b, mirrored, plain)

    def pick_f(plain, mirrored):
        return jnp.where(flip_f > 0.5, mirrored, plain)

    arrived = (own_ref, one_ref, two_ref, three_ref)
    arrived = [jnp.concatenate([ref[j] for ref in arrived], axis=0) for j in range(WINDOW)]
    row = lax.broadcasted_iota(I32, (256, 1), 0)
    source = (((row >> 4) & 3) ^ group) * ENDS + (row >> 6) * 12 + (row & 15)
    source = jnp.where((row & 15) < 12, source, -1)
    expand = (source == lax.broadcasted_iota(I32, (256, 4 * ENDS), 1)).astype(F32).astype(BF)
    arrived = mm(expand, jnp.concatenate(arrived, axis=1)).astype(BF)
    for j in range(WINDOW):
        for block in range(4):
            xs[block, j] = arrived[block * 64 : block * 64 + 64, j * CH : (j + 1) * CH]
    halos = mm(partner, jnp.concatenate([xs[0, j] for j in range(WINDOW)], axis=1)).astype(BF)
    for j in range(WINDOW):
        hal[j] = halos[:, j * CH : (j + 1) * CH]

    def block_at(block, j):
        return hal[j] if block == 0 else xs[block - 1, j]

    for block in range(5):
        for j in range(1, 5):
            before, after = block_at(block, j - 1), block_at(block, j + 1)
            nb[0, block, j] = pick(before, after)
            nb[1, block, j] = pick(after, before)
    at_first, at_last = band == 0, band == BANDS - 1

    def line_ends(value, lower, upper, choice):
        zero = jnp.where(at_last, value(lower + 2), value(lower))
        end = jnp.where(at_last, value(upper + 2), value(upper))
        return choice(zero, end), choice(end, zero)

    h_zero, h_end = line_ends(lambda j: hal[j], 2, 1, pick)
    h_one, h_last = line_ends(lambda j: hal[j], 3, 0, pick)
    f_zero, f_end = line_ends(lambda j: xs[0, j], 2, 1, pick)
    none = jnp.zeros((64, CH), BF)
    cells = mm(corner_cells, jnp.concatenate([f_zero, f_end], axis=0)).astype(BF)
    sides = jnp.concatenate([jnp.concatenate([h_zero, h_one], axis=1), jnp.concatenate([h_end, h_last], axis=1)], axis=0)
    sides = mm(beside, sides).astype(BF)
    low = [cells[:64], sides[:64, :CH], sides[:64, CH:], none, none]
    high = [cells[64:], sides[64:, :CH], sides[64:, CH:], none, none]
    for block in range(5):
        for slot, here_now in ((2, at_first), (4, at_last)):
            before, after = nb[0, block, slot], nb[1, block, slot]
            nb[0, block, slot] = jnp.where(here_now, pick(low[block], before), before)
            nb[1, block, slot] = jnp.where(here_now, pick(after, high[block]), after)
            before, after = nb[0, block, slot - 1], nb[1, block, slot - 1]
            nb[0, block, slot - 1] = jnp.where(here_now, pick(before, low[block]), before)
            nb[1, block, slot - 1] = jnp.where(here_now, pick(high[block], after), after)
    corner_grad = line_ends(lambda j: xs[2, j], 2, 1, pick)

    def choose(options):
        whole = all(option is not None for option in options)
        result = options[0] if whole else jnp.zeros((64, CH), BF)
        for s, option in enumerate(options):
            if option is not None and not (whole and s == 0):
                result = jnp.where(side_mask[s], option, result)
        return result

    def fill(target, block, source):
        for k, tap in enumerate(TAPS):
            target[block * 64 : block * 64 + 64, k * CH : (k + 1) * CH] = choose(
                [source(*side_frame(s, tap)) for s in range(4)]
            )

    def field_source(j):
        def source(delta, dt):
            return block_at(delta + 1, j) if dt == 0 else nb[(dt + 1) // 2, delta + 1, j]
        return source

    def grad_source(e, j):
        def source(delta, dt):
            depth = e - delta
            if depth not in (0, 1):
                return None
            return xs[2 + depth, j] if dt == 0 else nb[(1 - dt) // 2, 3 + depth, j]
        return source

    def corner_source(which, value):
        def source(delta, dt):
            return value if (delta, dt) == (-1, 2 * which - 1) else None
        return source

    order_pre = (2, 3, 1, 4)
    for block, j in enumerate(order_pre):
        fill(lp, block, field_source(j))
    order_back = [(0, 2), (0, 3), (-1, 2), (-1, 3), None, None, (0, 1), (0, 4), (-1, 1), (-1, 4)]
    for block, at in enumerate(order_back):
        fill(lg, block, corner_source(block - 4, corner_grad[block - 4]) if at is None else grad_source(*at))

    pre = mm(lp[...], w1_ref[...].reshape(9 * CH, CH))
    back = mm(lg[...], w2t[...])

    def back_block(e, j):
        block = order_back.index((e, j))
        return back[block * 64 : block * 64 + 64]

    seams = jnp.concatenate([back_block(-1, j).astype(BF) for j in range(1, 5)], axis=1)
    seams = mm(partner, seams)
    for j in range(1, 5):
        ss[j] = seams[:, (j - 1) * CH : j * CH]
    both_rows = jnp.concatenate([row_line, row_line], axis=0)

    def corner_sums(both):
        sums = mm(corner_back, (both * both_rows).astype(BF))
        return sums[:64], sums[64:]


    at_zero, at_end = corner_sums(back[256:384])
    head, tail = line_ends(lambda j: ss[j], 2, 1, pick_f)
    head, tail = head + at_zero, tail + at_end
    sides = mm(beside, jnp.concatenate([head, tail], axis=0).astype(BF))
    head, tail = head + sides[:64], tail + sides[64:]
    for slot, here_now in ((2, at_first), (4, at_last)):
        ss[slot] = jnp.where(here_now, pick_f(head, tail), ss[slot])
        ss[slot - 1] = jnp.where(here_now, pick_f(tail, head), ss[slot - 1])

    unique = {}
    hid = {}
    for block, j in enumerate(order_pre):
        value = pre[block * 64 : block * 64 + 64]
        hidden, slope = silu_parts(value)
        t = (2 * band - 2 + j) & (SPAN - 1)
        corner = jnp.logical_or(t == 0, t == SPAN - 1)
        unique[j] = jnp.where(corner, row_line, jnp.ones_like(row_line))
        grad = ((back_block(0, j) + ss[j]) * slope).astype(BF)
        gp[j] = grad
        gpu[j] = (grad.astype(F32) * unique[j]).astype(BF)
        hid[j] = hidden.astype(BF)

    mine = ((line >> 5) == (group >> 1)).astype(F32)
    edge = jnp.where(band == 0, 1.0, 0.0) * mine * row_line

    def scaled(value, factor):
        return (value.astype(F32) * factor).astype(BF)

    h_zero, h_end = pick(hid[2], hid[1]), pick(hid[1], hid[2])
    halos = mm(partner, jnp.concatenate([hid[2], hid[3]], axis=1))
    ends = mm(corner_cells, jnp.concatenate([h_zero, h_end], axis=0))
    cells = jnp.concatenate([
        scaled(hid[2], mine * unique[2]),
        scaled(hid[3], mine * unique[3]),
        scaled(halos[:, :CH], mine),
        scaled(halos[:, CH:], mine),
        scaled(ends[:64], edge),
        scaled(ends[64:], edge),
    ], axis=0)
    @pl.when((group & 1) == 0)
    def _():
        own = jnp.concatenate([scaled(gpu[2], mine), scaled(gpu[3], mine)], axis=0)
        share_ref[...] = mm_t(lp[0:128, :], own)

    @pl.when((group & 1) == 1)
    def _():
        second = mm_t(cells, lg[0:384, :])
        for k in range(9):
            share_ref[k * CH : (k + 1) * CH, :] = second[:, k * CH : (k + 1) * CH]

    inner_low = jnp.where(at_first, 0.0, 1.0)
    inner_high = jnp.where(at_last, 0.0, 1.0)

    def spread_source(e, j, ref):
        def source(delta, dt):
            if e - delta != 0:
                return None
            if dt == 0:
                return ref[j]
            before = scaled(ref[1], inner_low) if j == 2 else ref[2]
            after = ref[3] if j == 2 else scaled(ref[4], inner_high)
            return pick(before, after) if dt == 1 else pick(after, before)
        return source

    g_zero = jnp.where(at_first, gp[2], gp[4])
    g_end = jnp.where(at_first, gp[1], gp[3])
    g_zero, g_end = pick(g_zero, g_end), pick(g_end, g_zero)
    order_in = [(0, 2), (0, 3), (1, 2), (1, 3), (-1, 2), (-1, 3), None, None]
    for block, at in enumerate(order_in):
        if at is None:
            fill(lc, block, corner_source(block - 6, (g_zero, g_end)[block - 6]))
        else:
            fill(lc, block, spread_source(*at, gp if at[0] == -1 else gpu))
    back = mm(lc[...], w1t[...])
    part = [back[k * 64 : k * 64 + 64] for k in range(8)]
    at_zero, at_end = corner_sums(back[384:512])
    seams = mm(partner, jnp.concatenate([part[4], part[5]], axis=1).astype(BF))
    owe[0] = part[0] + seams[:, :CH] + pick_f(at_zero, at_end) * (1.0 - inner_low)
    owe[1] = part[2]
    owe[2] = part[1] + seams[:, CH:] + pick_f(at_end, at_zero) * (1.0 - inner_high)
    owe[3] = part[3]

    tile = jnp.concatenate([owe[k, pl.ds(pl.multiple_of(group * 16, 16), 16), :] for k in range(4)], axis=0)
    plan = [plan_ref[:, k : k + 1] for k in range(8)]
    flips = [jnp.zeros((48, 1), I32) for _ in range(2)]
    table_lane = lax.broadcasted_iota(I32, (4, 12), 1)
    rotations = rot_ref[...]
    partners = 4 * fn_ref[...] + (rotations & 3)
    table = jnp.where(4 * table_lane + lax.broadcasted_iota(I32, (4, 12), 0) > partners, rotations >> 2, 0)
    for face_index in range(3):
        values = jnp.sum(jnp.where(table_lane == 3 * group + face_index, table, 0), axis=1, keepdims=True)
        for which in range(4):
            value = jnp.broadcast_to(values[which : which + 1], (48, 1))
            for k in range(2):
                flips[k] = jnp.where(plan[6 + k] == which * 3 + face_index, value, flips[k])
    last = jnp.where(at_last, 1, 0)
    outer = jnp.logical_or(at_first, at_last)
    row_lane = jnp.where(flips[0] ^ last == plan[4], jnp.where(at_last, plan[1], plan[0]), -1)
    col_lane = jnp.where(flips[1] ^ last == plan[5], jnp.where(at_last, plan[3], plan[2]), -1)
    lanes = lax.broadcasted_iota(I32, (48, 64), 1)
    patch = (row_lane == lanes).astype(F32) + (col_lane == lanes).astype(F32)
    select = jnp.concatenate([jnp.where(outer, patch, sel_ref[0:48, :]), sel_ref[48:72, :]], axis=0)
    tail_ref[...] = mm(select.astype(BF), tile.astype(BF))


def tail_plan():
    select = np.zeros((72, 64), np.float32)
    plan = np.zeros((48, 8), np.int32)
    for pos in range(2):
        for depth in range(2):
            for face in range(3):
                lane = (pos * 2 + depth) * 16 + face
                for half in range(2):
                    select[half * 24 + (pos * 2 + depth) * 3 + face, lane + half * 3] = 1
                for side in range(2):
                    select[48 + ((pos * 2 + side) * 2 + depth) * 3 + face, lane + 6 + 3 * side] = 1
    for half in range(2):
        for side in range(2):
            for face in range(3):
                for row in range(2):
                    for col in range(2):
                        place = half * 24 + ((side * 3 + face) * 2 + row) * 2 + col
                        for last in range(2):
                            plan[place, last] = ((col ^ last) * 2 + row) * 16 + half * 3 + face
                            plan[place, 2 + last] = ((row ^ last) * 2 + col) * 16 + (2 + side) * 3 + face
                        plan[place, 4:] = side, half, half * 3 + face, (2 + side) * 3 + face
    return select, plan


def after_kernel(*refs):
    pass


def share_kernel(own_ref, other_ref, line_ref, out_ref, total):
    total[...] = own_ref[...] + other_ref[...].astype(F32) + line_ref[...]
    for i in range(BANDS):
        rows = [total[CHUNK * i : CHUNK * i + CHUNK, :], jnp.zeros((SLOT_TWO - CHUNK, CH), F32)]
        out_ref[i] = jnp.concatenate(rows, axis=0).astype(BF)


def order_selector():
    select = np.zeros((2, 64, 64), np.float32)
    for pos in range(2):
        for b in range(BANDS):
            select[0, 2 * b + pos, pos * 32 + b] = 1
            select[1, 63 - 2 * b - pos, pos * 32 + b] = 1
    return select


def reduce_kernel(in_ref, out_ref):
    total = in_ref[0].astype(F32)
    for i in range(1, BANDS):
        total = total + in_ref[i].astype(F32)
    out_ref[...] = total


def spread_kernel(factor, _order, own_ref, other_ref, tail_ref, sent, out_ref):
    total = (own_ref[...] + other_ref[...]) * factor
    for i in range(BANDS):
        start = 0 if i == 0 else 24 if i == BANDS - 1 else 48
        parts = [total, sent[i * 16 : i * 16 + 16, :], tail_ref[start : start + 24, :]]
        out_ref[i] = jnp.concatenate(parts, axis=0).astype(BF)


def sums_kernel(in_ref, out_ref):
    for i in range(BANDS):
        out_ref[i] = in_ref[i, 0:48, :].astype(F32)[0:SLOT_TWO].astype(BF)


def unpack_kernel(own_ref, other_ref, first_ref, second_ref):
    _, group = here()
    core = group & 1
    for i in range(BANDS):
        own, other = own_ref[i].astype(F32), other_ref[i].astype(F32)
        rows = slice(CHUNK * i, CHUNK * i + CHUNK)
        first_ref[rows, :] = jnp.where(core == 0, own, other)[0:CHUNK]
        second_ref[rows, :] = jnp.where(core == 0, other, own)[0:CHUNK]


def grad_kernel(fn_ref, rot_ref, sel_ref, in_ref, out_ref, wide, total):
    band, group = here()
    for i in range(BANDS):
        wide[i * 48 : i * 48 + 48, :] = in_ref[i, 32:SLOT_THREE, :].astype(F32)
    for face in range(3):
        for row in range(2):
            for q in range(8):
                piece = wide[pl.ds((4 + face) * 48 + 8 + q * 2 + row, 8, stride=144), :]
                total[row, face, pl.ds(q, 8, stride=8), :] = piece
    tiles = [wide[pl.ds(pl.multiple_of(src * 48, 16), 48), :] for src in (band, BANDS - 1 - band)]
    outer = (band == 0) | (band == BANDS - 1)

    @pl.when(~outer)
    def _():
        for side in range(2):
            for face in range(3):
                flip = mirrored_in(fn_ref, rot_ref, 3 * group + face, 2 + side) == 1
                for row in range(2):
                    for depth in range(2):
                        column = depth if side == 0 else 63 - depth
                        k, m = [24 + ((pos * 2 + side) * 2 + depth) * 3 + face for pos in (row, 1 - row)]
                        extra = jnp.where(flip, tiles[1][m : m + 1, :], tiles[0][k : k + 1, :])
                        total[row, face, column : column + 1, :] += extra

    @pl.when(outer)
    def _():
        half = jnp.where(band == 0, 0, 1)
        patches = tiles[0] + tiles[1]
        place = lax.broadcasted_iota(I32, (SPAN, CH), 0)
        inner = (place >= 2) & (place < SPAN - 2)
        for face in range(3):
            pair = [mirrored_in(fn_ref, rot_ref, 3 * group + face, side) for side in range(2)]
            order = sel_ref[jnp.where(band == 0, pair[0], pair[1])]
            for depth in range(2):
                halves = [wide[pl.ds(24 + (pos * 2 + depth) * 3 + face, BANDS, stride=48), :] for pos in range(2)]
                extra = mm(order, jnp.concatenate(halves, axis=0).astype(BF))
                total[depth ^ half, face] += jnp.where(inner, extra, 0.0)
                for side in range(2):
                    for col in range(2):
                        k = 24 + ((side * 3 + face) * 2 + depth) * 2 + col
                        column = 63 - col if side else col
                        total[depth ^ half, face, column : column + 1, :] += patches[k : k + 1, :]

    for row in range(2):
        for face in range(3):
            out_ref[face, row] = total[row, face].astype(BF)


def swapped(value, step):
    return lax.ppermute(value, "sub", [(i, i ^ step) for i in range(4)])


def body(field_in, grad_out, first_weight, second_weight, face_neighbour, seam_rotation, corner_fill):
    factor = (1.0 * 12 * SPAN * SPAN) ** -0.5
    seams = (face_neighbour.T, seam_rotation.T)
    select, plan = tail_plan()

    slots = call(
        pack_lines,
        jax.ShapeDtypeStruct((BANDS, SLOT_ONE, CH), BF),
        [
            pltpu.VMEM((2, 3, 2, SPAN, CH), BF),
            pltpu.SMEM((4, 12), I32),
            pltpu.SMEM((4, 12), I32),
            pltpu.VMEM(((SPAN + 4) * 12, CH), F32),
            pltpu.VMEM((STRIP, CH), F32),
            pltpu.SemaphoreType.DMA((4,)),
        ],
        tuple(pltpu.with_memory_space_constraint(value, pltpu.HBM) for value in (field_in, grad_out, *seams)),
        dict.fromkeys(range(4), "h"),
    )
    strips = lax.all_to_all(slots, "tile", 0, 0, tiled=True)
    lines = call(
        gather_lines,
        jax.ShapeDtypeStruct((WINDOW, ENDS, CH), BF),
        [],
        (*seams, jnp.asarray(line_selector(), BF), strips),
    )
    beyond, beside = swapped(lines, 2), swapped(lines, 1)
    tables = (corner_fill.T, jnp.asarray(plan), jnp.asarray(select, F32))
    share = jax.ShapeDtypeStruct((HALF, CH), F32)
    own, away, sent = call(
        interior_kernel,
        [share, jax.ShapeDtypeStruct((HALF, CH), BF), jax.ShapeDtypeStruct((BANDS * 16, CH), F32)],
        [
            pltpu.VMEM((2304, CH), F32),
            pltpu.VMEM((512, CH), F32),
            pltpu.VMEM((1152, CH), BF),
            pltpu.VMEM((1152, CH), BF),
            pltpu.VMEM((768, CH), F32),
            pltpu.VMEM((768, CH), F32),
            pltpu.VMEM((BANDS * UNIT, CH), F32),
        ],
        (*tables, strips, first_weight, second_weight),
    )
    beyond = call(after_kernel, jax.ShapeDtypeStruct((WINDOW, ENDS, CH), BF), [], (beyond, own), dict.fromkeys((0, 1, "o0"), "a"), {0: 0})
    lines = (lines, beside, beyond, swapped(beyond, 1))
    away = call(after_kernel, jax.ShapeDtypeStruct((HALF, CH), BF), [], (away, *lines[1:3]), dict.fromkeys((0, 1, 2, "o0"), "a"), {0: 0})
    other = swapped(away, 1)

    line, tails = call(
        main_kernel,
        [share, jax.ShapeDtypeStruct((72, CH), F32)],
        [
            pltpu.VMEM((1152, CH), BF),
            pltpu.VMEM((1152, CH), BF),
            pltpu.VMEM((4, WINDOW, 64, CH), BF),
            pltpu.VMEM((WINDOW, 64, CH), BF),
            pltpu.VMEM((2, 5, 5, 64, CH), BF),
            pltpu.VMEM((256, 1152), BF),
            pltpu.VMEM((640, 1152), BF),
            pltpu.VMEM((512, 1152), BF),
            pltpu.VMEM((5, 64, CH), F32),
            pltpu.VMEM((5, 64, CH), BF),
            pltpu.VMEM((5, 64, CH), BF),
            pltpu.VMEM((4, 64, CH), F32),
        ],
        (*seams, *tables, *lines, first_weight, second_weight),
    )
    slots = call(
        share_kernel,
        jax.ShapeDtypeStruct((BANDS, SLOT_TWO, CH), BF),
        [pltpu.VMEM((HALF, CH), F32)],
        (own, other, line),
    )
    slots = lax.all_to_all(slots, "tile", 0, 0, tiled=True)
    order = jnp.asarray(order_selector(), BF)
    part = call(reduce_kernel, jax.ShapeDtypeStruct((SLOT_TWO, CH), F32), [], (slots,))
    reduced = call(
        lambda *refs: spread_kernel(factor, *refs),
        jax.ShapeDtypeStruct((BANDS, SLOT_THREE, CH), BF),
        [],
        (order, part, swapped(part, 2), tails, sent),
    )
    reduced = lax.all_to_all(reduced, "tile", 0, 0, tiled=True)
    sums = call(sums_kernel, jax.ShapeDtypeStruct((BANDS, SLOT_TWO, CH), BF), [], (reduced,))
    swap = swapped(sums, 1)
    grad_in = call(
        grad_kernel,
        jax.ShapeDtypeStruct((3, 2, SPAN, CH), BF),
        [pltpu.VMEM((BANDS * 48, CH), F32), pltpu.VMEM((2, 3, SPAN, CH), F32)],
        (*seams, order, reduced),
    )
    first, second = call(
        unpack_kernel,
        [jax.ShapeDtypeStruct((1152, CH), F32), jax.ShapeDtypeStruct((1152, CH), F32)],
        [],
        (sums, swap),
    )
    return grad_in, first.reshape(3, 3, CH, CH), second.reshape(3, 3, CH, CH)


def solution(mesh):
    return jax.shard_map(
        body,
        mesh=mesh,
        in_specs=(P("sub", "tile", None, None), P("sub", "tile", None, None), P(), P(), P(), P(), P()),
        out_specs=(P("sub", "tile", None, None), P(), P()),
        check_vma=False,
    )
```

```python
import jax
import jax.numpy as jnp
import numpy as np
from jax import lax
from jax.experimental import pallas as pl
from jax.experimental.pallas import tpu as pltpu
from jax.sharding import PartitionSpec as P

BF = jnp.bfloat16
F32 = jnp.float32
I32 = jnp.int32
BANDS = 32
SPAN = 64
CH = 128
TAPS = [(a, b) for a in range(3) for b in range(3)]
WINDOW = 6
ENDS = 48
STRIP = 12 * WINDOW
UNIT = 48
SLOT_ONE = UNIT + STRIP
HALF = 9 * CH
CHUNK = 36
SLOT_TWO = 40
SLOT_THREE = 80
VMEM_BYTES = 48 * 1024 * 1024


def mm(left, right):
    return jnp.dot(left, right, preferred_element_type=F32)


def mm_t(left, right):
    return lax.dot_general(left, right, (((0,), (0,)), ((), ())), preferred_element_type=F32)


def call(kernel, outs, scratch, operands, places=(), aliases=None):
    kinds = {"v": pltpu.VMEM, "s": pltpu.SMEM, "h": pltpu.HBM, "a": pl.ANY}
    places = dict(places)
    many = isinstance(outs, (list, tuple))
    out_specs = [pl.BlockSpec(memory_space=kinds[places.get(f"o{k}", "v")]) for k in range(len(outs) if many else 1)]
    return pl.pallas_call(
        kernel,
        out_shape=outs,
        in_specs=[pl.BlockSpec(memory_space=kinds[places.get(k, "v")]) for k in range(len(operands))],
        out_specs=out_specs if many else out_specs[0],
        scratch_shapes=scratch,
        input_output_aliases=aliases or {},
        compiler_params=pltpu.CompilerParams(vmem_limit_bytes=VMEM_BYTES),
    )(*operands)


def here():
    return lax.axis_index("tile"), lax.axis_index("sub")


def is_mirrored(fn_ref, rot_ref, face, side):
    rot = rot_ref[face, side]
    partner = 4 * fn_ref[face, side] + (rot & 3)
    return jnp.where(4 * face + side > partner, rot >> 2, 0)


def is_mirrored(fn_ref, rot_ref, face, side):
    rot = rot_ref[side, face]
    partner = 4 * fn_ref[side, face] + (rot & 3)
    return jnp.where(4 * face + side > partner, rot >> 2, 0)


def mirrored_in(fn_ref, rot_ref, face, side):
    lane = lax.broadcasted_iota(I32, (1, 12), 1) == face
    rot = jnp.sum(jnp.where(lane, rot_ref[side : side + 1, :], 0))
    partner = 4 * jnp.sum(jnp.where(lane, fn_ref[side : side + 1, :], 0)) + (rot & 3)
    return jnp.where(4 * face + side > partner, rot >> 2, 0)


def unit_of(band):
    unit = band - 4
    strip = (unit * 43) >> 7
    return strip, unit - 3 * strip


def pack_lines(f_hbm, g_hbm, fn_hbm, rot_hbm, out_ref, buf, fn_ref, rot_ref, wide, ends, sems):
    moves = ((f_hbm, buf.at[0]), (g_hbm, buf.at[1]), (fn_hbm, fn_ref), (rot_hbm, rot_ref))
    copies = [pltpu.make_async_copy(src, dst, sems.at[k]) for k, (src, dst) in enumerate(moves)]
    for copy in copies:
        copy.start()
    band, group = here()
    ends[ENDS:STRIP, :] = jnp.zeros((STRIP - ENDS, CH), F32)
    for fld in range(2):
        copies[fld].wait()
        for row in range(2):
            for face in range(3):
                block = buf[fld, face, row].astype(F32)
                wide[pl.ds(24 + fld * 6 + row * 3 + face, SPAN, stride=12), :] = block
                for edge, cols in enumerate(((0, 1), (63, 62))):
                    for depth, col in enumerate(cols):
                        place = row * 24 + fld * 12 + edge * 6 + depth * 3 + face
                        ends[place : place + 1, :] = block[col : col + 1, :]
    wide[0:24, :] = wide[SPAN * 12 : SPAN * 12 + 24, :]
    wide[SPAN * 12 + 24 : SPAN * 12 + 48, :] = wide[24:48, :]
    for copy in copies[2:]:
        copy.wait()
    side = jnp.where(band == 0, 0, 1)
    row = lax.broadcasted_iota(I32, (STRIP, CH), 0)
    row = row - 3 * ((row * 43) >> 7)
    flip = jnp.zeros((STRIP, CH), I32)
    for face in range(3):
        flip = jnp.where(row == face, is_mirrored(fn_ref, rot_ref, 3 * group + face, side), flip)
    outer = (band == 0) | (band == BANDS - 1)
    strips = [wide[24 * d : 24 * d + STRIP, :] for d in range(BANDS)]
    for d in range(BANDS):
        strip, face = unit_of(d)
        unit = wide[pl.ds(96 * strip + face, UNIT, stride=3), :] if 4 <= d < 28 else ends[0:ENDS, :]
        line = jnp.where(flip == 1, strips[BANDS - 1 - d], strips[d])
        out_ref[d] = jnp.concatenate([unit, jnp.where(outer, line, ends[...])], axis=0).astype(BF)


def line_selector():
    select = np.zeros((2, WINDOW * ENDS, 2 * STRIP + 6 * ENDS), np.float32)
    for mirrored in range(2):
        for j in range(WINDOW):
            part, parity = j // 2, j % 2
            for fld in range(2):
                for depth in range(2):
                    for face in range(3):
                        base = j * ENDS + (fld * 2 + depth) * 12 + face
                        column = (5 - j if mirrored else j) * 12 + fld * 6 + face
                        select[mirrored, base, column + depth * 3] = 1
                        select[mirrored, base + 3, STRIP + column + (1 - depth) * 3] = 1
                        for side in range(2):
                            source = 2 * STRIP + (3 * mirrored + part) * ENDS + (1 - parity if mirrored else parity) * 24
                            select[mirrored, base + 6 + 3 * side, source + fld * 12 + side * 6 + depth * 3 + face] = 1
    return select


def gather_lines(fn_ref, rot_ref, sel_ref, in_ref, out_ref):
    band, group = here()
    pieces = [in_ref[d].astype(F32)[UNIT:SLOT_ONE] for d in (0, BANDS - 1)]
    for source in [band + 31 + part for part in range(3)] + [64 - band - part for part in range(3)]:
        source = source & 31
        outer = (source == 0) | (source == BANDS - 1)
        pieces.append(jnp.where(outer, in_ref[source, 0:ENDS, :], in_ref[source, UNIT : UNIT + ENDS, :]).astype(F32))
    pieces = jnp.concatenate(pieces, axis=0).astype(BF)
    place = lax.broadcasted_iota(I32, (24, CH), 0)
    place = jnp.where(place < 12, place, place - 12)
    flip = jnp.zeros((24, CH), I32)
    lane = lax.broadcasted_iota(I32, (4, 12), 1)
    rot = rot_ref[...]
    partner = 4 * fn_ref[...] + (rot & 3)
    table = jnp.where(4 * lane + lax.broadcasted_iota(I32, (4, 12), 0) > partner, rot >> 2, 0)
    for face in range(3):
        values = jnp.sum(jnp.where(lane == 3 * group + face, table, 0), axis=1, keepdims=True)
        for side in range(4):
            flip = jnp.where(place == side * 3 + face, jnp.broadcast_to(values[side : side + 1], (24, CH)), flip)
    flip = jnp.concatenate([flip.astype(F32)] * (WINDOW * ENDS // 24), axis=0).astype(BF)
    flip = jnp.concatenate([flip] * 4, axis=1)[:, 0 : sel_ref.shape[2]] > 0.5
    picked = mm(jnp.where(flip, sel_ref[1], sel_ref[0]), pieces).astype(BF)
    for j in range(WINDOW):
        out_ref[j] = picked[j * ENDS : (j + 1) * ENDS]


def silu_parts(pre):
    logistic = 1.0 / (1.0 + jnp.exp(-pre))
    return pre * logistic, logistic * (1.0 + pre * (1.0 - logistic))


def side_frame(side, tap):
    dr, dc = tap[0] - 1, tap[1] - 1
    return ((dr, dc), (-dr, dc), (dc, dr), (-dc, dr))[side]


def transpose_weights(ref, out):
    for k, (a, b) in enumerate(TAPS):
        out[k * CH : (k + 1) * CH, :] = ref[a, b].T


def interior_kernel(
    _fill, _plan, _select, in_ref, w1_ref, w2_ref, own_ref, away_ref, sent, w1t, w2t, acc, done, f2, g2, wide
):
    band, group = here()
    strip, _ = unit_of(band)
    transpose_weights(w1_ref, w1t)
    transpose_weights(w2_ref, w2t)
    for s in range(BANDS):
        wide[s * UNIT : (s + 1) * UNIT, :] = in_ref[s, 0:UNIT, :].astype(F32)
    for q in range(12):
        for fld, target in enumerate((f2, g2)):
            for row in range(2):
                piece = wide[pl.ds(q * 4 + fld * 2 + row, BANDS, stride=UNIT), :]
                target[pl.ds(q * 64 + row, BANDS, stride=2), :] = piece

    def conv_weights(ref):
        return jnp.concatenate([ref[a].reshape(3 * CH, CH) for a in range(3)], axis=1)

    def back_weights(ref):
        columns = []
        for a in range(3):
            columns.append(jnp.concatenate([ref[(a * 3 + b) * CH : (a * 3 + b + 1) * CH, :] for b in (2, 1, 0)], axis=0))
        return jnp.concatenate(columns, axis=1)

    def up_one(value):
        return pltpu.roll(value, value.shape[0] - 1, 0)

    def down_one(value):
        return pltpu.roll(value, 1, 0)

    def three_columns(ref, first, count):
        return jnp.concatenate([ref[first + 64 * b : first + 64 * b + count, :].astype(BF) for b in range(3)], axis=1)

    y = mm(three_columns(f2, 0, 640), conv_weights(w1_ref))
    pre = down_one(y[:, :CH]) + y[:, CH : 2 * CH] + up_one(y[:, 2 * CH :])
    z = mm(three_columns(g2, 0, 640), back_weights(w2t))
    back = up_one(z[:, :CH]) + z[:, CH : 2 * CH] + down_one(z[:, 2 * CH :])
    hidden, slope = silu_parts(pre)
    index = lax.broadcasted_iota(I32, (640, CH), 0)
    col = 8 * strip - 1 + (index >> 6)
    row = index & 63
    inner = (row >= 1) & (row <= 62) & (col >= 1) & (col <= 62) & (band >= 4) & (band < 28)
    gpre = jnp.where(inner, back * slope, 0.0).astype(BF)
    hid = jnp.where(inner, hidden, 0.0)[64:576].astype(BF)

    gown = gpre[64:576].astype(F32)
    gcat = jnp.concatenate([up_one(gown).astype(BF), gpre[64:576], down_one(gown).astype(BF)], axis=1)
    first = mm_t(three_columns(f2, 64, 512), gcat)
    hown = hid.astype(F32)
    hcat = jnp.concatenate([down_one(hown).astype(BF), hid, up_one(hown).astype(BF)], axis=1)
    gback = jnp.concatenate([g2[start : start + 512, :].astype(BF) for start in (192, 128, 64)], axis=1)
    second = mm_t(hcat, gback)
    for k, (a, b) in enumerate(TAPS):
        top, low = k * CH, 1152 + k * CH
        acc[top : top + CH, :] = first[b * CH : (b + 1) * CH, a * CH : (a + 1) * CH]
        acc[low : low + CH, :] = second[a * CH : (a + 1) * CH, b * CH : (b + 1) * CH]
    core = group & 1
    own_ref[...] = acc[pl.ds(pl.multiple_of(core * HALF, CH), HALF), :]
    away_ref[...] = acc[pl.ds(pl.multiple_of((1 - core) * HALF, CH), HALF), :].astype(BF)

    gthree = jnp.concatenate([gpre[0:512], gpre[64:576], gpre[128:640]], axis=1)
    z = mm(gthree, back_weights(w1t))
    done[...] = up_one(z[:, :CH]) + z[:, CH : 2 * CH] + down_one(z[:, 2 * CH :]) + g2[128:640, :]
    for q in range(8):
        for row in range(2):
            sent[pl.ds(q * 2 + row, BANDS, stride=16), :] = done[pl.ds(q * 64 + row, BANDS, stride=2), :]


def main_kernel(
    fn_ref, rot_ref, fill_ref, plan_ref, sel_ref, own_ref, one_ref, two_ref, three_ref, w1_ref, w1t, w2t,
    share_ref, tail_ref,
    xs, hal, nb, lp, lg, lc, ss, gp, gpu, owe,
):
    band, group = here()

    line = lax.broadcasted_iota(I32, (64, 1), 0)
    place = line & 15
    side = (place >= 3).astype(I32) + (place >= 6).astype(I32) + (place >= 9).astype(I32)
    face = place - 3 * side
    home = line - place
    real = place < 12
    lane = lax.broadcasted_iota(I32, (64, 64), 1)

    def one_hot(target, keep):
        return (jnp.where(keep & real, target, -1) == lane).astype(F32).astype(BF)

    face_lane = lax.broadcasted_iota(I32, (64, 12), 1)
    faces = (jnp.where(real, 3 * (line >> 4) + face, -1) == face_lane).astype(F32).astype(BF)

    def by_line(ref, columns):
        table = ref[...].astype(F32).astype(BF)
        rows = lax.dot_general(faces, table, (((1,), (1,)), ((), ())), preferred_element_type=F32).astype(I32)
        value = rows[:, columns[0] : columns[0] + 1]
        for s in range(1, 4):
            value = jnp.where(side == s, rows[:, columns[s] : columns[s] + 1], value)
        return value

    fn = by_line(fn_ref, (0, 1, 2, 3))
    rot = by_line(rot_ref, (0, 1, 2, 3))
    fn_group = (fn * 43) >> 7
    partner = one_hot(fn_group * 16 + (rot & 3) * 3 + (fn - 3 * fn_group), real)
    number = 4 * (3 * (line >> 4) + face) + side
    flip = ((rot >> 2) == 1) & (number > 4 * fn + (rot & 3)) & real
    fills = []
    for columns in ((0, 2, 0, 1), (1, 3, 2, 3)):
        m = by_line(fill_ref, columns)
        mf = m >> 2
        mg = (mf * 43) >> 7
        target = mg * 16 + ((m >> 1) & 1) * 3 + (mf - 3 * mg)
        fills.append((one_hot(target, (m & 1) == 0), one_hot(target, (m & 1) == 1)))
    corner_cells = jnp.concatenate([jnp.concatenate(pair, axis=1) for pair in fills], axis=0)
    corner_back = corner_cells.astype(F32).T.astype(BF)
    even = (side & 1) == 0
    low_side = jnp.where(side < 2, 2, 0)
    high_side = jnp.where(side < 2, 3, 1)
    beside = jnp.concatenate([
        jnp.concatenate([one_hot(home + other * 3 + face, even), one_hot(home + other * 3 + face, ~even)], axis=1)
        for other in (low_side, high_side)
    ], axis=0)
    side_mask = [jnp.broadcast_to((side == s).astype(F32), (64, CH)).astype(BF) > 0.5 for s in range(4)]
    row_line = (side < 2).astype(F32)
    flip_f = jnp.broadcast_to(flip.astype(F32), (64, CH))
    flip_b = flip_f.astype(BF) > 0.5

    def pick(plain, mirrored):
        return jnp.where(flip_b, mirrored, plain)

    def pick_f(plain, mirrored):
        return jnp.where(flip_f > 0.5, mirrored, plain)

    arrived = (own_ref, one_ref, two_ref, three_ref)
    arrived = [jnp.concatenate([ref[j] for ref in arrived], axis=0) for j in range(WINDOW)]
    row = lax.broadcasted_iota(I32, (256, 1), 0)
    source = (((row >> 4) & 3) ^ group) * ENDS + (row >> 6) * 12 + (row & 15)
    source = jnp.where((row & 15) < 12, source, -1)
    expand = (source == lax.broadcasted_iota(I32, (256, 4 * ENDS), 1)).astype(F32).astype(BF)
    arrived = mm(expand, jnp.concatenate(arrived, axis=1)).astype(BF)
    for j in range(WINDOW):
        for block in range(4):
            xs[block, j] = arrived[block * 64 : block * 64 + 64, j * CH : (j + 1) * CH]
    halos = mm(partner, jnp.concatenate([xs[0, j] for j in range(WINDOW)], axis=1)).astype(BF)
    for j in range(WINDOW):
        hal[j] = halos[:, j * CH : (j + 1) * CH]

    def block_at(block, j):
        return hal[j] if block == 0 else xs[block - 1, j]

    for block in range(5):
        for j in range(1, 5):
            before, after = block_at(block, j - 1), block_at(block, j + 1)
            nb[0, block, j] = pick(before, after)
            nb[1, block, j] = pick(after, before)
    at_first, at_last = band == 0, band == BANDS - 1

    def line_ends(value, lower, upper, choice):
        zero = jnp.where(at_last, value(lower + 2), value(lower))
        end = jnp.where(at_last, value(upper + 2), value(upper))
        return choice(zero, end), choice(end, zero)

    h_zero, h_end = line_ends(lambda j: hal[j], 2, 1, pick)
    h_one, h_last = line_ends(lambda j: hal[j], 3, 0, pick)
    f_zero, f_end = line_ends(lambda j: xs[0, j], 2, 1, pick)
    none = jnp.zeros((64, CH), BF)
    cells = mm(corner_cells, jnp.concatenate([f_zero, f_end], axis=0)).astype(BF)
    sides = jnp.concatenate([jnp.concatenate([h_zero, h_one], axis=1), jnp.concatenate([h_end, h_last], axis=1)], axis=0)
    sides = mm(beside, sides).astype(BF)
    low = [cells[:64], sides[:64, :CH], sides[:64, CH:], none, none]
    high = [cells[64:], sides[64:, :CH], sides[64:, CH:], none, none]
    for block in range(5):
        for slot, here_now in ((2, at_first), (4, at_last)):
            before, after = nb[0, block, slot], nb[1, block, slot]
            nb[0, block, slot] = jnp.where(here_now, pick(low[block], before), before)
            nb[1, block, slot] = jnp.where(here_now, pick(after, high[block]), after)
            before, after = nb[0, block, slot - 1], nb[1, block, slot - 1]
            nb[0, block, slot - 1] = jnp.where(here_now, pick(before, low[block]), before)
            nb[1, block, slot - 1] = jnp.where(here_now, pick(high[block], after), after)
    corner_grad = line_ends(lambda j: xs[2, j], 2, 1, pick)

    def choose(options):
        whole = all(option is not None for option in options)
        result = options[0] if whole else jnp.zeros((64, CH), BF)
        for s, option in enumerate(options):
            if option is not None and not (whole and s == 0):
                result = jnp.where(side_mask[s], option, result)
        return result

    def fill(target, block, source):
        for k, tap in enumerate(TAPS):
            target[block * 64 : block * 64 + 64, k * CH : (k + 1) * CH] = choose(
                [source(*side_frame(s, tap)) for s in range(4)]
            )

    def field_source(j):
        def source(delta, dt):
            return block_at(delta + 1, j) if dt == 0 else nb[(dt + 1) // 2, delta + 1, j]
        return source

    def grad_source(e, j):
        def source(delta, dt):
            depth = e - delta
            if depth not in (0, 1):
                return None
            return xs[2 + depth, j] if dt == 0 else nb[(1 - dt) // 2, 3 + depth, j]
        return source

    def corner_source(which, value):
        def source(delta, dt):
            return value if (delta, dt) == (-1, 2 * which - 1) else None
        return source

    order_pre = (2, 3, 1, 4)
    for block, j in enumerate(order_pre):
        fill(lp, block, field_source(j))
    order_back = [(0, 2), (0, 3), (-1, 2), (-1, 3), None, None, (0, 1), (0, 4), (-1, 1), (-1, 4)]
    for block, at in enumerate(order_back):
        fill(lg, block, corner_source(block - 4, corner_grad[block - 4]) if at is None else grad_source(*at))

    pre = mm(lp[...], w1_ref[...].reshape(9 * CH, CH))
    back = mm(lg[...], w2t[...])

    def back_block(e, j):
        block = order_back.index((e, j))
        return back[block * 64 : block * 64 + 64]

    seams = jnp.concatenate([back_block(-1, j).astype(BF) for j in range(1, 5)], axis=1)
    seams = mm(partner, seams)
    for j in range(1, 5):
        ss[j] = seams[:, (j - 1) * CH : j * CH]
    both_rows = jnp.concatenate([row_line, row_line], axis=0)

    def corner_sums(both):
        sums = mm(corner_back, (both * both_rows).astype(BF))
        return sums[:64], sums[64:]


    at_zero, at_end = corner_sums(back[256:384])
    head, tail = line_ends(lambda j: ss[j], 2, 1, pick_f)
    head, tail = head + at_zero, tail + at_end
    sides = mm(beside, jnp.concatenate([head, tail], axis=0).astype(BF))
    head, tail = head + sides[:64], tail + sides[64:]
    for slot, here_now in ((2, at_first), (4, at_last)):
        ss[slot] = jnp.where(here_now, pick_f(head, tail), ss[slot])
        ss[slot - 1] = jnp.where(here_now, pick_f(tail, head), ss[slot - 1])

    unique = {}
    hid = {}
    for block, j in enumerate(order_pre):
        value = pre[block * 64 : block * 64 + 64]
        hidden, slope = silu_parts(value)
        t = (2 * band - 2 + j) & (SPAN - 1)
        corner = jnp.logical_or(t == 0, t == SPAN - 1)
        unique[j] = jnp.where(corner, row_line, jnp.ones_like(row_line))
        grad = ((back_block(0, j) + ss[j]) * slope).astype(BF)
        gp[j] = grad
        gpu[j] = (grad.astype(F32) * unique[j]).astype(BF)
        hid[j] = hidden.astype(BF)

    mine = ((line >> 5) == (group >> 1)).astype(F32)
    edge = jnp.where(band == 0, 1.0, 0.0) * mine * row_line

    def scaled(value, factor):
        return (value.astype(F32) * factor).astype(BF)

    h_zero, h_end = pick(hid[2], hid[1]), pick(hid[1], hid[2])
    halos = mm(partner, jnp.concatenate([hid[2], hid[3]], axis=1))
    ends = mm(corner_cells, jnp.concatenate([h_zero, h_end], axis=0))
    cells = jnp.concatenate([
        scaled(hid[2], mine * unique[2]),
        scaled(hid[3], mine * unique[3]),
        scaled(halos[:, :CH], mine),
        scaled(halos[:, CH:], mine),
        scaled(ends[:64], edge),
        scaled(ends[64:], edge),
    ], axis=0)
    @pl.when((group & 1) == 0)
    def _():
        own = jnp.concatenate([scaled(gpu[2], mine), scaled(gpu[3], mine)], axis=0)
        share_ref[...] = mm_t(lp[0:128, :], own)

    @pl.when((group & 1) == 1)
    def _():
        second = mm_t(cells, lg[0:384, :])
        for k in range(9):
            share_ref[k * CH : (k + 1) * CH, :] = second[:, k * CH : (k + 1) * CH]

    inner_low = jnp.where(at_first, 0.0, 1.0)
    inner_high = jnp.where(at_last, 0.0, 1.0)

    def spread_source(e, j, ref):
        def source(delta, dt):
            if e - delta != 0:
                return None
            if dt == 0:
                return ref[j]
            before = scaled(ref[1], inner_low) if j == 2 else ref[2]
            after = ref[3] if j == 2 else scaled(ref[4], inner_high)
            return pick(before, after) if dt == 1 else pick(after, before)
        return source

    g_zero = jnp.where(at_first, gp[2], gp[4])
    g_end = jnp.where(at_first, gp[1], gp[3])
    g_zero, g_end = pick(g_zero, g_end), pick(g_end, g_zero)
    order_in = [(0, 2), (0, 3), (1, 2), (1, 3), (-1, 2), (-1, 3), None, None]
    for block, at in enumerate(order_in):
        if at is None:
            fill(lc, block, corner_source(block - 6, (g_zero, g_end)[block - 6]))
        else:
            fill(lc, block, spread_source(*at, gp if at[0] == -1 else gpu))
    back = mm(lc[...], w1t[...])
    part = [back[k * 64 : k * 64 + 64] for k in range(8)]
    at_zero, at_end = corner_sums(back[384:512])
    seams = mm(partner, jnp.concatenate([part[4], part[5]], axis=1).astype(BF))
    owe[0] = part[0] + seams[:, :CH] + pick_f(at_zero, at_end) * (1.0 - inner_low)
    owe[1] = part[2]
    owe[2] = part[1] + seams[:, CH:] + pick_f(at_end, at_zero) * (1.0 - inner_high)
    owe[3] = part[3]

    tile = jnp.concatenate([owe[k, pl.ds(pl.multiple_of(group * 16, 16), 16), :] for k in range(4)], axis=0)
    plan = [plan_ref[:, k : k + 1] for k in range(8)]
    flips = [jnp.zeros((48, 1), I32) for _ in range(2)]
    table_lane = lax.broadcasted_iota(I32, (4, 12), 1)
    rotations = rot_ref[...]
    partners = 4 * fn_ref[...] + (rotations & 3)
    table = jnp.where(4 * table_lane + lax.broadcasted_iota(I32, (4, 12), 0) > partners, rotations >> 2, 0)
    for face_index in range(3):
        values = jnp.sum(jnp.where(table_lane == 3 * group + face_index, table, 0), axis=1, keepdims=True)
        for which in range(4):
            value = jnp.broadcast_to(values[which : which + 1], (48, 1))
            for k in range(2):
                flips[k] = jnp.where(plan[6 + k] == which * 3 + face_index, value, flips[k])
    last = jnp.where(at_last, 1, 0)
    outer = jnp.logical_or(at_first, at_last)
    row_lane = jnp.where(flips[0] ^ last == plan[4], jnp.where(at_last, plan[1], plan[0]), -1)
    col_lane = jnp.where(flips[1] ^ last == plan[5], jnp.where(at_last, plan[3], plan[2]), -1)
    lanes = lax.broadcasted_iota(I32, (48, 64), 1)
    patch = (row_lane == lanes).astype(F32) + (col_lane == lanes).astype(F32)
    select = jnp.concatenate([jnp.where(outer, patch, sel_ref[0:48, :]), sel_ref[48:72, :]], axis=0)
    tail_ref[...] = mm(select.astype(BF), tile.astype(BF))


def tail_plan():
    select = np.zeros((72, 64), np.float32)
    plan = np.zeros((48, 8), np.int32)
    for pos in range(2):
        for depth in range(2):
            for face in range(3):
                lane = (pos * 2 + depth) * 16 + face
                for half in range(2):
                    select[half * 24 + (pos * 2 + depth) * 3 + face, lane + half * 3] = 1
                for side in range(2):
                    select[48 + ((pos * 2 + side) * 2 + depth) * 3 + face, lane + 6 + 3 * side] = 1
    for half in range(2):
        for side in range(2):
            for face in range(3):
                for row in range(2):
                    for col in range(2):
                        place = half * 24 + ((side * 3 + face) * 2 + row) * 2 + col
                        for last in range(2):
                            plan[place, last] = ((col ^ last) * 2 + row) * 16 + half * 3 + face
                            plan[place, 2 + last] = ((row ^ last) * 2 + col) * 16 + (2 + side) * 3 + face
                        plan[place, 4:] = side, half, half * 3 + face, (2 + side) * 3 + face
    return select, plan


def after_kernel(*refs):
    pass


def share_kernel(own_ref, other_ref, line_ref, out_ref, total):
    total[...] = own_ref[...] + other_ref[...].astype(F32) + line_ref[...]
    for i in range(BANDS):
        rows = [total[CHUNK * i : CHUNK * i + CHUNK, :], jnp.zeros((SLOT_TWO - CHUNK, CH), F32)]
        out_ref[i] = jnp.concatenate(rows, axis=0).astype(BF)


def order_selector():
    select = np.zeros((2, 64, 64), np.float32)
    for pos in range(2):
        for b in range(BANDS):
            select[0, 2 * b + pos, pos * 32 + b] = 1
            select[1, 63 - 2 * b - pos, pos * 32 + b] = 1
    return select


def reduce_kernel(in_ref, out_ref):
    total = in_ref[0].astype(F32)
    for i in range(1, BANDS):
        total = total + in_ref[i].astype(F32)
    out_ref[...] = total


def spread_kernel(factor, _order, own_ref, other_ref, tail_ref, sent, out_ref):
    total = (own_ref[...] + other_ref[...]) * factor
    for i in range(BANDS):
        start = 0 if i == 0 else 24 if i == BANDS - 1 else 48
        parts = [total, sent[i * 16 : i * 16 + 16, :], tail_ref[start : start + 24, :]]
        out_ref[i] = jnp.concatenate(parts, axis=0).astype(BF)


def sums_kernel(in_ref, out_ref):
    for i in range(BANDS):
        out_ref[i] = in_ref[i, 0:48, :].astype(F32)[0:SLOT_TWO].astype(BF)


def unpack_kernel(own_ref, other_ref, first_ref, second_ref):
    _, group = here()
    core = group & 1
    for i in range(BANDS):
        own, other = own_ref[i].astype(F32), other_ref[i].astype(F32)
        rows = slice(CHUNK * i, CHUNK * i + CHUNK)
        first_ref[rows, :] = jnp.where(core == 0, own, other)[0:CHUNK]
        second_ref[rows, :] = jnp.where(core == 0, other, own)[0:CHUNK]


def grad_kernel(fn_ref, rot_ref, sel_ref, in_ref, out_ref, wide, total):
    band, group = here()
    for i in range(BANDS):
        wide[i * 48 : i * 48 + 48, :] = in_ref[i, 32:SLOT_THREE, :].astype(F32)
    for face in range(3):
        for row in range(2):
            for q in range(8):
                piece = wide[pl.ds((4 + face) * 48 + 8 + q * 2 + row, 8, stride=144), :]
                total[row, face, pl.ds(q, 8, stride=8), :] = piece
    tiles = [wide[pl.ds(pl.multiple_of(src * 48, 16), 48), :] for src in (band, BANDS - 1 - band)]
    outer = (band == 0) | (band == BANDS - 1)

    @pl.when(~outer)
    def _():
        for side in range(2):
            for face in range(3):
                flip = mirrored_in(fn_ref, rot_ref, 3 * group + face, 2 + side) == 1
                for row in range(2):
                    for depth in range(2):
                        column = depth if side == 0 else 63 - depth
                        k, m = [24 + ((pos * 2 + side) * 2 + depth) * 3 + face for pos in (row, 1 - row)]
                        extra = jnp.where(flip, tiles[1][m : m + 1, :], tiles[0][k : k + 1, :])
                        total[row, face, column : column + 1, :] += extra

    @pl.when(outer)
    def _():
        half = jnp.where(band == 0, 0, 1)
        patches = tiles[0] + tiles[1]
        place = lax.broadcasted_iota(I32, (SPAN, CH), 0)
        inner = (place >= 2) & (place < SPAN - 2)
        for face in range(3):
            pair = [mirrored_in(fn_ref, rot_ref, 3 * group + face, side) for side in range(2)]
            order = sel_ref[jnp.where(band == 0, pair[0], pair[1])]
            for depth in range(2):
                halves = [wide[pl.ds(24 + (pos * 2 + depth) * 3 + face, BANDS, stride=48), :] for pos in range(2)]
                extra = mm(order, jnp.concatenate(halves, axis=0).astype(BF))
                total[depth ^ half, face] += jnp.where(inner, extra, 0.0)
                for side in range(2):
                    for col in range(2):
                        k = 24 + ((side * 3 + face) * 2 + depth) * 2 + col
                        column = 63 - col if side else col
                        total[depth ^ half, face, column : column + 1, :] += patches[k : k + 1, :]

    for row in range(2):
        for face in range(3):
            out_ref[face, row] = total[row, face].astype(BF)


def swapped(value, step):
    return lax.ppermute(value, "sub", [(i, i ^ step) for i in range(4)])


def body(field_in, grad_out, first_weight, second_weight, face_neighbour, seam_rotation, corner_fill):
    factor = (1.0 * 12 * SPAN * SPAN) ** -0.5
    seams = (face_neighbour.T, seam_rotation.T)
    select, plan = tail_plan()

    slots = call(
        pack_lines,
        jax.ShapeDtypeStruct((BANDS, SLOT_ONE, CH), BF),
        [
            pltpu.VMEM((2, 3, 2, SPAN, CH), BF),
            pltpu.SMEM((4, 12), I32),
            pltpu.SMEM((4, 12), I32),
            pltpu.VMEM(((SPAN + 4) * 12, CH), F32),
            pltpu.VMEM((STRIP, CH), F32),
            pltpu.SemaphoreType.DMA((4,)),
        ],
        tuple(pltpu.with_memory_space_constraint(value, pltpu.HBM) for value in (field_in, grad_out, *seams)),
        dict.fromkeys(range(4), "h"),
    )
    strips = lax.all_to_all(slots, "tile", 0, 0, tiled=True)
    lines = call(
        gather_lines,
        jax.ShapeDtypeStruct((WINDOW, ENDS, CH), BF),
        [],
        (*seams, jnp.asarray(line_selector(), BF), strips),
    )
    beyond, beside = swapped(lines, 2), swapped(lines, 1)
    tables = (corner_fill.T, jnp.asarray(plan), jnp.asarray(select, F32))
    share = jax.ShapeDtypeStruct((HALF, CH), F32)
    turned = jax.ShapeDtypeStruct((HALF, CH), BF)
    own, away, sent, first_turned, second_turned = call(
        interior_kernel,
        [share, jax.ShapeDtypeStruct((HALF, CH), BF), jax.ShapeDtypeStruct((BANDS * 16, CH), F32), turned, turned],
        [
            pltpu.VMEM((2304, CH), F32),
            pltpu.VMEM((512, CH), F32),
            pltpu.VMEM((768, CH), F32),
            pltpu.VMEM((768, CH), F32),
            pltpu.VMEM((BANDS * UNIT, CH), F32),
        ],
        (*tables, strips, first_weight, second_weight),
    )
    beyond = call(after_kernel, jax.ShapeDtypeStruct((WINDOW, ENDS, CH), BF), [], (beyond, own), dict.fromkeys((0, 1, "o0"), "a"), {0: 0})
    lines = (lines, beside, beyond, swapped(beyond, 1))
    away = call(after_kernel, jax.ShapeDtypeStruct((HALF, CH), BF), [], (away, *lines[1:]), dict.fromkeys((0, 1, 2, 3, "o0"), "a"), {0: 0})
    other = swapped(away, 1)

    line, tails = call(
        main_kernel,
        [share, jax.ShapeDtypeStruct((72, CH), F32)],
        [
            pltpu.VMEM((4, WINDOW, 64, CH), BF),
            pltpu.VMEM((WINDOW, 64, CH), BF),
            pltpu.VMEM((2, 5, 5, 64, CH), BF),
            pltpu.VMEM((256, 1152), BF),
            pltpu.VMEM((640, 1152), BF),
            pltpu.VMEM((512, 1152), BF),
            pltpu.VMEM((5, 64, CH), F32),
            pltpu.VMEM((5, 64, CH), BF),
            pltpu.VMEM((5, 64, CH), BF),
            pltpu.VMEM((4, 64, CH), F32),
        ],
        (*seams, *tables, *lines, first_weight, first_turned, second_turned),
    )
    slots = call(
        share_kernel,
        jax.ShapeDtypeStruct((BANDS, SLOT_TWO, CH), BF),
        [pltpu.VMEM((HALF, CH), F32)],
        (own, other, line),
    )
    slots = lax.all_to_all(slots, "tile", 0, 0, tiled=True)
    order = jnp.asarray(order_selector(), BF)
    part = call(reduce_kernel, jax.ShapeDtypeStruct((SLOT_TWO, CH), F32), [], (slots,))
    reduced = call(
        lambda *refs: spread_kernel(factor, *refs),
        jax.ShapeDtypeStruct((BANDS, SLOT_THREE, CH), BF),
        [],
        (order, part, swapped(part, 2), tails, sent),
    )
    reduced = lax.all_to_all(reduced, "tile", 0, 0, tiled=True)
    sums = call(sums_kernel, jax.ShapeDtypeStruct((BANDS, SLOT_TWO, CH), BF), [], (reduced,))
    swap = swapped(sums, 1)
    grad_in = call(
        grad_kernel,
        jax.ShapeDtypeStruct((3, 2, SPAN, CH), BF),
        [pltpu.VMEM((BANDS * 48, CH), F32), pltpu.VMEM((2, 3, SPAN, CH), F32)],
        (*seams, order, reduced),
    )
    first, second = call(
        unpack_kernel,
        [jax.ShapeDtypeStruct((1152, CH), F32), jax.ShapeDtypeStruct((1152, CH), F32)],
        [],
        (sums, swap),
    )
    return grad_in, first.reshape(3, 3, CH, CH), second.reshape(3, 3, CH, CH)


def solution(mesh):
    return jax.shard_map(
        body,
        mesh=mesh,
        in_specs=(P("sub", "tile", None, None), P("sub", "tile", None, None), P(), P(), P(), P(), P()),
        out_specs=(P("sub", "tile", None, None), P(), P()),
        check_vma=False,
    )
```
